32 devices in a mesh: tile: 8 (over y, x, core), sample: 4 (over z).
Axes of the slice: x: 2, y: 2, z: 4, core: 2. Of those that a mesh axis runs over, the one named last changes fastest.
Arguments:
- features: bfloat16 [8, 9, 224, 10752], P('sample', None, 'tile'), may hold values from -6 to 6
- norm_gain: float32 [96], replicated, may hold values from 0.4 to 2.5
- conv_weight: bfloat16 [3, 3, 3, 3, 96], replicated, may hold values from -0.125 to 0.125
- patch_embed: bfloat16 [588, 1280], P(None, 'tile'), may hold values from -0.25 to 0.25
- position: bfloat16 [128, 1280], P('sample', 'tile'), may hold values from -6 to 6
- attend_in: bfloat16 [1280, 1920], P('sample', 'tile'), may hold values from -0.15625 to 0.15625
- attend_out: bfloat16 [640, 1280], P('sample', 'tile'), may hold values from -0.25 to 0.25
- reward_head: float32 [1280], replicated, may hold values from -0.24 to 0.24
- group_index: int32 [8], P('sample'), may hold values from 0 to 1, as said below
- frame_pick: int32 [8, 8], P('sample'), may hold values from 0 to 8, as said below
Outputs:
- feature_grad: bfloat16 [8, 9, 224, 10752], P('sample', None, 'tile')
The draws below stay inside these ranges and needn't reach their ends.
Inputs may be any that keep to these rules, and one draw needn't show every extreme that they name: `group_index`: each prompt number is the prompt of exactly 4 samples. `frame_pick`: the 8 frames of one sample are all different.
All inputs are finite; a program needn't handle non-finite values.
Results may differ from the reference program's by a relative error of at most 0.02.
Values may be sent and summed in bfloat16 or wider, within the bound.
No kernel may reach another device: no remote copies, remote signals or barrier semaphores. Data moves between devices by JAX's collectives and lax.ppermute only.
A program may use at most 192 MiB of HBM per device.

```python
import math
import jax
import jax.numpy as jnp
from jax import lax

C = 96
FRAMES = 9
SCORED = 8
PATCH = 14
D = 1280
HEADS = 8
HD = 80
GROUP = 4
SAMPLES = 8
FH = 224
FW = 112
NP = 128
HQ = 640
PATCH_IN = 588


def draw_group_index(key, part):
    order = jax.random.permutation(key, SAMPLES)
    return (order // GROUP).astype(jnp.int32)


def draw_frame_pick(key, part):
    keys = jax.random.split(jax.random.fold_in(key, 7), SAMPLES)
    picks = jax.vmap(lambda one_key: jax.random.permutation(one_key, FRAMES)[:SCORED])(keys)
    return picks.astype(jnp.int32)


def block_levels(stream_key, shape, cuts, smallest, top_value):
    level, own = 1.0, jax.random.fold_in(stream_key, 6)
    for axis_at, shards_of in cuts:
        steps = jnp.exp(jax.random.uniform(jax.random.fold_in(own, axis_at), (shards_of,), jnp.float32, smallest / len(cuts), top_value / len(cuts)))
        level = level * jnp.repeat(steps, shape[axis_at] // shards_of).reshape([-1 if axis == axis_at else 1 for axis in range(len(shape))])
    return level


def normal_values(key, shape, scale, bound, shards=(), held_as=jnp.bfloat16):
    loudness = block_levels(key, shape, shards, -0.22, 0.18) if shards else 1.0
    values = jax.random.normal(key, shape, jnp.float32) * scale * loudness
    return jnp.minimum(jnp.maximum(values, -bound), bound).astype(held_as)


def setup_inputs(seed: int = 0) -> dict:
    splits = jax.random.split(jax.random.key(seed), 11)
    features = normal_values(splits[0], (SAMPLES, FRAMES, FH, C * FW), 1.0, 6.0, ((0, 4), (2, 8)))
    norm_gain = jnp.clip(jnp.exp(jax.random.uniform(splits[1], (C,), jnp.float32, math.log(0.4), math.log(2.5))), 0.4, 2.5)
    conv_weight = normal_values(splits[2], (3, 3, 3, 3, C), (27 * C) ** -0.5, 0.125)
    patch_embed = normal_values(splits[3], (PATCH_IN, D), PATCH_IN ** -0.5, 0.25, ((1, 8),))
    position = normal_values(splits[4], (NP, D), 1.0, 6.0, ((0, 4), (1, 8)))
    attend_in = normal_values(splits[5], (D, 3 * HQ), D ** -0.5, 0.15625, ((0, 4), (1, 8)))
    attend_out = normal_values(splits[6], (HQ, D), HQ ** -0.5, 0.25, ((0, 4), (1, 8)))
    reward_head = normal_values(splits[7], (D,), 0.04, 0.24, (), jnp.float32)
    group_index = draw_group_index(jax.random.fold_in(splits[10], 71), 0)
    frame_pick = draw_frame_pick(jax.random.fold_in(splits[10], 71), 0)
    return {"features": features, "norm_gain": norm_gain, "conv_weight": conv_weight, "patch_embed": patch_embed, "position": position, "attend_in": attend_in, "attend_out": attend_out, "reward_head": reward_head, "group_index": group_index, "frame_pick": frame_pick}


LOSS_SCALE = 16384.0
SMOOTH = 0.01

def normed_silu(inputs, norm_gain):
    second = lax.optimization_barrier(jnp.mean(inputs * inputs, axis=-4, keepdims=True))
    scaled = inputs * lax.rsqrt(second + 1e-06) * norm_gain[:, None, None, None]
    return jax.nn.silu(scaled)

def conv_forward(padded, conv_weight, frame_count, row_count, column_count):
    channels = padded.shape[0]
    tap_weights = conv_weight.reshape(27, 3, channels).astype(jnp.float32)
    spread = jnp.einsum('koc,ctrw->kotrw', tap_weights, padded.astype(jnp.float32), precision=lax.Precision.HIGHEST)
    summed = jnp.zeros((3, frame_count, row_count, column_count), jnp.float32)
    for step_time in range(3):
        for step_row in range(3):
            for step_column in range(3):
                tap_index = step_time * 9 + step_row * 3 + step_column
                summed = summed + spread[tap_index, :, step_time:step_time + frame_count, step_row:step_row + row_count, step_column:step_column + column_count]
    return summed

def conv_backward(grad_pad, conv_weight, frame_count, row_count, column_count):
    channels = conv_weight.shape[-1]
    tap_weights = conv_weight.reshape(27, 3, channels).astype(jnp.float32)
    pieces = []
    for step_time in range(3):
        for step_row in range(3):
            for step_column in range(3):
                pieces.append(grad_pad[:, 2 - step_time:2 - step_time + frame_count, 2 - step_row:2 - step_row + row_count, 2 - step_column:2 - step_column + column_count])
    stacked = jnp.stack(pieces, axis=0).astype(jnp.float32)
    return jnp.einsum('koc,kotrw->ctrw', tap_weights, stacked, precision=lax.Precision.HIGHEST)

def frame_score(frame_one, patch_embed, position, attend_in, attend_out, reward_head):
    row_count = frame_one.shape[1] // PATCH
    column_count = frame_one.shape[2] // PATCH
    patches = frame_one.reshape(3, row_count, PATCH, column_count, PATCH).transpose(1, 3, 0, 2, 4).reshape(row_count * column_count, 3 * PATCH * PATCH)
    tokens = jnp.dot(patches, patch_embed, preferred_element_type=jnp.float32) + position.astype(jnp.float32)
    centered = tokens - lax.optimization_barrier(jnp.mean(tokens, axis=-1, keepdims=True))
    normed = (centered * lax.rsqrt(lax.optimization_barrier(jnp.mean(centered * centered, axis=-1, keepdims=True)) + 1e-05)).astype(jnp.bfloat16)
    mixed_rows = jnp.dot(normed, attend_in, preferred_element_type=jnp.float32).astype(jnp.bfloat16)
    inner_width = HEADS * HD
    query_rows = mixed_rows[:, :inner_width].reshape(-1, HEADS, HD)
    key_rows = mixed_rows[:, inner_width:2 * inner_width].reshape(-1, HEADS, HD)
    values = mixed_rows[:, 2 * inner_width:].reshape(-1, HEADS, HD)
    scores = jnp.einsum('qhd,khd->hqk', query_rows, key_rows, preferred_element_type=jnp.float32) * HD ** (-0.5)
    weights = jax.nn.softmax(scores, axis=-1).astype(jnp.bfloat16)
    attended = jnp.einsum('hqk,khd->qhd', weights, values, preferred_element_type=jnp.float32)
    attended = attended.reshape(-1, inner_width).astype(jnp.bfloat16)
    residual = tokens + jnp.dot(attended, attend_out, preferred_element_type=jnp.float32)
    pooled = lax.optimization_barrier(jnp.mean(residual, axis=0))
    pooled_centered = pooled - jnp.mean(pooled)
    pooled_normed = pooled_centered * lax.rsqrt(jnp.mean(pooled_centered * pooled_centered) + 1e-05)
    return jnp.sum(pooled_normed * reward_head)

def reference(features, norm_gain, conv_weight, patch_embed, position, attend_in, attend_out, reward_head, group_index, frame_pick):
    sample_count, frame_count, row_count, merged = features.shape
    channels = norm_gain.shape[0]
    column_count = merged // channels
    layered = features.reshape(sample_count, frame_count, row_count, channels, column_count).transpose(0, 3, 1, 2, 4)
    scored = frame_pick.shape[1]
    prompts = sample_count // GROUP

    def decode(clip_one):
        activation = normed_silu(clip_one.astype(jnp.float32), norm_gain).astype(jnp.bfloat16)
        padded = jnp.pad(activation, ((0, 0), (2, 0), (1, 1), (1, 1)))
        return conv_forward(padded, conv_weight, frame_count, row_count, column_count).astype(jnp.bfloat16)
    decoded = lax.map(decode, layered)
    picked = jax.vmap(lambda clip_one, pick_one: jnp.take(clip_one, pick_one, axis=1))(decoded, frame_pick)
    entries = jnp.transpose(picked, (0, 2, 1, 3, 4)).reshape(sample_count * scored, 3, row_count, column_count)

    def score_one(frame_one):
        return frame_score(frame_one, patch_embed, position, attend_in, attend_out, reward_head)
    scores = lax.map(score_one, entries).reshape(sample_count, scored)
    rewards = lax.optimization_barrier(jnp.sum(scores, axis=1)) / scored
    member = (group_index[:, None] == jnp.arange(prompts, dtype=jnp.int32)[None, :]).astype(jnp.float32)
    group_sum = lax.optimization_barrier(jnp.sum(member * rewards[:, None], axis=0))
    group_square = lax.optimization_barrier(jnp.sum(member * (rewards * rewards)[:, None], axis=0))
    mean_group = group_sum / GROUP
    second_group = group_square / GROUP - mean_group * mean_group
    sample_mean = lax.optimization_barrier(jnp.sum(member * mean_group[None, :], axis=1))
    sample_second = lax.optimization_barrier(jnp.sum(member * second_group[None, :], axis=1))
    advantage = (rewards - sample_mean) * lax.rsqrt(sample_second + SMOOTH)
    cotangent = jnp.repeat(-LOSS_SCALE * advantage / scored, scored)

    def grad_one(paired):
        frame_one, weight_one = paired
        unused, pullback = jax.vjp(score_one, frame_one)
        return pullback(weight_one)[0]
    gradients = lax.map(grad_one, (entries, cotangent)).reshape(sample_count, scored, 3, row_count, column_count)
    chosen = (frame_pick[:, :, None] == jnp.arange(frame_count, dtype=jnp.int32)[None, None, :]).astype(jnp.float32)
    frame_grad = jnp.einsum('sjf,sjcrw->scfrw', chosen, gradients.astype(jnp.float32), precision=lax.Precision.HIGHEST).astype(jnp.bfloat16)

    def restore(paired):
        grad_frames, clip_one = paired
        grad_pad = jnp.pad(grad_frames, ((0, 0), (0, 2), (1, 1), (1, 1)))
        activation_grad = conv_backward(grad_pad, conv_weight, frame_count, row_count, column_count)
        unused, pullback = jax.vjp(lambda inputs: normed_silu(inputs, norm_gain), clip_one.astype(jnp.float32))
        return pullback(activation_grad)[0].astype(jnp.bfloat16)
    result = lax.map(restore, (frame_grad, layered))
    return result.transpose(0, 2, 3, 1, 4).reshape(sample_count, frame_count, row_count, merged)
```

```python
import functools

import jax
import jax.numpy as jnp
from jax import lax
from jax.experimental import pallas as pl
from jax.experimental.pallas import tpu as pltpu
from jax.sharding import PartitionSpec as P

SCORED = 8
PATCH = 14
HEADS = 8
HD = 80
GROUP = 4
LOSS_SCALE = 16384.0
SMOOTH = 0.01

CH = 96
COLS = 112
SPAN = 8 * COLS
SPANS = CH // 8
OUT_ROWS = 27 * 16
IN_ROWS = CH * 8
NT = 8
NZ = 4
PACK = 1120
KIN = 896
D = 1280
NTOK = 128
F32 = jnp.float32
BF16 = jnp.bfloat16


def lane_iota(rows):
    return lax.broadcasted_iota(jnp.int32, (rows, 128), 1)


def left(value, amount):
    amount = amount % 128
    return value if amount == 0 else pltpu.roll(value, 128 - amount, 1)


def to_channels(tiles, lane):
    found = []
    for k in range(8):
        start = COLS * k
        q, off = divmod(start, 128)
        head = left(tiles[q], off)
        if 128 - off < COLS:
            head = jnp.where(lane < 128 - off, head, left(tiles[q + 1], off))
        found.append(head)
    return found


def to_tiles(channels, lane):
    found = []
    for q in range(7):
        cut = COLS - 16 * q
        found.append(
            jnp.where(lane < cut, left(channels[q], 16 * q), left(channels[q + 1], 128 - cut))
        )
    return found


def spread_all(value, lane):
    return to_tiles([value] * 8, lane)


def fold_all(tiles, lane):
    parts = to_channels(tiles, lane)
    while len(parts) > 1:
        parts = [parts[i] + parts[i + 1] for i in range(0, len(parts), 2)]
    return parts[0]


def load_rows(ref, row, count, lane):
    value = ref[0, 0, row : row + count, lane : lane + SPAN].astype(F32)
    if count < 16:
        value = jnp.concatenate([value, jnp.zeros((16 - count, SPAN), F32)], axis=0)
    return value


def lane_tiles(value):
    return [value[:, 128 * q : 128 * q + 128] for q in range(7)]


def banded(weight_ref, transposed):
    pick = (
        lax.broadcasted_iota(jnp.int32, (OUT_ROWS, 32), 0) // 16
        == lax.broadcasted_iota(jnp.int32, (OUT_ROWS, 32), 1)
    ).astype(BF16)
    if transposed:
        shape, p_dim, r_dim = (IN_ROWS, OUT_ROWS), 1, 0
        grow = (
            lax.broadcasted_iota(jnp.int32, (IN_ROWS, CH), 0) // 8
            == lax.broadcasted_iota(jnp.int32, (IN_ROWS, CH), 1)
        ).astype(BF16)
    else:
        shape, p_dim, r_dim = (OUT_ROWS, IN_ROWS), 0, 1
        grow = (
            lax.broadcasted_iota(jnp.int32, (CH, IN_ROWS), 1) // 8
            == lax.broadcasted_iota(jnp.int32, (CH, IN_ROWS), 0)
        ).astype(BF16)
    p_at = lax.broadcasted_iota(jnp.int32, shape, p_dim) % 16
    r_at = lax.broadcasted_iota(jnp.int32, shape, r_dim) % 8
    total = jnp.zeros(shape, F32)
    for b in range(3):
        rows = jnp.dot(pick, weight_ref[b], preferred_element_type=F32).astype(BF16)
        if transposed:
            full = lax.dot_general(
                grow, rows, (((1,), (1,)), ((), ())), preferred_element_type=F32
            )
        else:
            full = jnp.dot(rows, grow, preferred_element_type=F32)
        total = jnp.where(p_at == r_at + 2 - b, full, total)
    return total.astype(BF16)


def decode_kernel(row_count, slot_ref, live_ref, x_ref, gain_ref, weight_ref, out_ref, inv_ref, band, operand, acc):
    s, t = pl.program_id(0), pl.program_id(1)
    frames = pl.num_programs(1)
    slabs = -(-row_count // 16)
    lane = lane_iota(16)

    @pl.when((s == 0) & (t == 0))
    def _():
        band[...] = banded(weight_ref, False)

    @pl.when(t == 0)
    def _():
        acc[...] = jnp.zeros(acc.shape, F32)

    for slab in range(slabs):
        row = 16 * slab
        count = min(16, row_count - row)
        square = jnp.zeros((16, SPAN), F32)
        for g in range(SPANS):
            value = load_rows(x_ref, row, count, g * SPAN)
            square = square + value * value
        second = fold_all(lane_tiles(square), lane) * (1.0 / CH)
        inv = jnp.concatenate(spread_all(lax.rsqrt(second + 1e-06), lane), axis=1)
        inv_ref[0, 0, row : row + 16, :] = inv
        for g in range(SPANS):
            value = load_rows(x_ref, row, count, g * SPAN)
            half = value * inv * gain_ref[:, g * SPAN : g * SPAN + SPAN]
            act = half + half * jnp.tanh(half)
            found = to_channels(lane_tiles(act), lane)
            for m in range(4):
                at = (g * 8 + 2 * m) * 8
                one, two = found[2 * m], found[2 * m + 1]
                operand[slab, at : at + 16, 0:128] = jnp.concatenate(
                    [one[:8], two[:8]], axis=0
                ).astype(BF16)
                operand[slab, at : at + 16, 128:256] = jnp.concatenate(
                    [one[8:], two[8:]], axis=0
                ).astype(BF16)
        spread = jnp.dot(band[...], operand[slab], preferred_element_type=F32)
        lane_out = lane_iota(144)
        for half_at in range(2):
            k = 2 * slab + half_at
            part = spread[:, 128 * half_at : 128 * half_at + 128]
            low, mid, high = part[0:144], part[144:288], part[288:432]
            low = jnp.where(lane_out == 0, 0.0, pltpu.roll(low, 1, 1))
            high = jnp.where(lane_out == COLS - 1, 0.0, pltpu.roll(high, 127, 1))
            total = low + mid + high
            for a in range(3):
                for o in range(3):
                    at = (a * 3 + o) * 16
                    acc[2 - a, o, 8 * k : 8 * k + 16, :] += total[at : at + 16]

    @pl.when(live_ref[s * frames + t] > 0)
    def _():
        rows = out_ref.shape[3]
        keep = lane_iota(rows) < COLS
        for o in range(3):
            out_ref[0, 0, o] = jnp.where(keep, acc[0, o, 0:rows, :], 0.0).astype(BF16)

    acc[0] = acc[1]
    acc[1] = acc[2]
    acc[2] = jnp.zeros(acc.shape[1:], F32)


def restore_kernel(row_count, entry_ref, x_ref, inv_ref, gain_ref, weight_ref, grad_ref, scale_ref, out_ref, band, shifted, operand, coming, inner):
    s, t = pl.program_id(0), pl.program_id(1)
    frames = pl.num_programs(1)
    slabs = -(-row_count // 16)
    lane = lane_iota(16)
    lane8 = lane_iota(8)
    rows = grad_ref.shape[3]

    @pl.when((s == 0) & (t == 0))
    def _():
        band[...] = banded(weight_ref, True)
        shifted[...] = jnp.zeros(shifted.shape, F32)

    @pl.when(t == 0)
    def _():
        lane_rows = lane_iota(rows)

        def one_frame(frame, carry):
            entry = entry_ref[s * frames + frame]
            scale = jnp.where(entry >= 0, scale_ref[s], 0.0)
            source = jnp.maximum(entry, 0)
            for o in range(3):
                value = grad_ref[source, s, o].astype(F32) * scale
                value = jnp.where(lane_rows < COLS, value, 0.0).astype(BF16).astype(F32)
                shifted[frame, 0, o, 0:rows, :] = pltpu.roll(value, 127, 1)
                shifted[frame, 1, o, 0:rows, :] = value
                shifted[frame, 2, o, 0:rows, :] = pltpu.roll(value, 1, 1)
            return carry

        lax.fori_loop(0, frames, one_frame, 0)

    for slab in range(slabs):
        row = 16 * slab
        count = min(16, row_count - row)
        for e in range(3):
            for a in range(3):
                for o in range(3):
                    at = ((e * 3 + a) * 3 + o) * 16
                    for half_at in range(2):
                        k = 2 * slab + half_at
                        operand[slab, at : at + 16, 128 * half_at : 128 * half_at + 128] = shifted[
                            t + 2 - a, e, o, 8 * k : 8 * k + 16, :
                        ].astype(BF16)
        coming[slab] = jnp.dot(band[...], operand[slab], preferred_element_type=F32)
        inv = inv_ref[0, 0, row : row + 16, :]
        total = jnp.zeros((16, SPAN), F32)
        for g in range(SPANS):
            halves = []
            for half_at in range(2):
                channels = [
                    coming[slab, (g * 8 + k) * 8 : (g * 8 + k) * 8 + 8, 128 * half_at : 128 * half_at + 128]
                    for k in range(8)
                ]
                halves.append(jnp.concatenate(to_tiles(channels, lane8), axis=1))
            cot = jnp.concatenate(halves, axis=0)
            value = load_rows(x_ref, row, count, g * SPAN)
            gain = gain_ref[:, g * SPAN : g * SPAN + SPAN]
            half = value * inv * gain
            th = jnp.tanh(half)
            out = cot * gain * (1.0 + th) * (1.0 + half * (1.0 - th))
            total = total + out * value
            inner[slab, :, g * SPAN : g * SPAN + SPAN] = out
        folded = fold_all(lane_tiles(total), lane) * (1.0 / CH)
        factor = jnp.concatenate(spread_all(folded, lane), axis=1) * inv * inv * inv
        for g in range(SPANS):
            value = load_rows(x_ref, row, count, g * SPAN)
            result = inner[slab, :, g * SPAN : g * SPAN + SPAN] * inv - value * factor
            out_ref[0, 0, row : row + count, g * SPAN : g * SPAN + SPAN] = result[:count].astype(BF16)


def nt_dot(one, two):
    return lax.dot_general(one, two, (((1,), (1,)), ((), ())), preferred_element_type=F32)


def tn_dot(one, two):
    return lax.dot_general(one, two, (((0,), (0,)), ((), ())), preferred_element_type=F32)


def nn_dot(one, two):
    return jnp.dot(one, two, preferred_element_type=F32)


def split_two(value):
    high = value.astype(BF16)
    low = (value - high.astype(F32)).astype(BF16)
    return jnp.concatenate([high, low], axis=0)


def reward_kernel(
    row_count, tiles, samples,
    part_ref, pack_ref, head_ref,
    out_ref, score_ref,
    frame, flip, embed, outw, place, patches, tokens, normed, normed16, slots, weights, dslots, dnormed, rows8, abar,
):
    height = row_count * tiles
    patch_rows = height // PATCH
    lane64 = lane_iota(8) < 64
    lane = lane_iota(NTOK)
    count = samples * NTOK

    embed[...] = jnp.zeros(embed.shape, BF16)
    lane96 = lane_iota(96)
    for z in range(NZ):
        for i in range(NT):
            source = pack_ref.at[i * NZ + z]
            for xx in range(4):
                x = 4 * z + xx
                if x < PATCH:
                    embed[64 * x : 64 * x + 48, 128 * i : 128 * i + 128] = source[640 + 48 * xx : 688 + 48 * xx, :]
            outw[160 * z : 160 * z + 160, 128 * i : 128 * i + 128] = source[832:992, :]
            place[32 * z : 32 * z + 32, 128 * i : 128 * i + 128] = source[992:1024, :]
        for ib in range(2):
            sources = [pack_ref[(4 * ib + j) * NZ + z, 1024:1120, :].astype(F32) for j in range(4)]
            rolled = [[sources[j] if d == 0 else pltpu.roll(sources[j], 32 * d, 1) for d in range(4)] for j in range(4)]
            at = 1024 + 128 * ib
            for q in range(4):
                found = rolled[0][(0 - q) % 4]
                for j in range(1, 4):
                    found = jnp.where(lane96 >= 32 * j, rolled[j][(j - q) % 4], found)
                found = found.astype(BF16)
                if q < 2:
                    for xx in range(2):
                        x = 4 * z + 2 * q + xx
                        if x < PATCH:
                            embed[64 * x : 64 * x + 48, at : at + 128] = found[48 * xx : 48 * xx + 48]
                elif q == 2:
                    outw[160 * z : 160 * z + 96, at : at + 128] = found
                else:
                    outw[160 * z + 96 : 160 * z + 160, at : at + 128] = found[:64]
                    place[32 * z : 32 * z + 32, at : at + 128] = found[64:96]

    flip[...] = jnp.zeros(flip.shape, F32)
    for f in range(samples):
        frame[...] = jnp.zeros(frame.shape, F32)
        for i in range(tiles):
            at = row_count * i + 7
            for o in range(3):
                frame[o, at : at + row_count + 2, :] += part_ref[i, f, o, 0 : row_count + 2, :].astype(F32)
        for pair in range(patch_rows // 2):
            for local in range(2):
                at = 8 + PATCH * (2 * pair + local)
                for o in range(3):
                    flip[0, 64 * local + PATCH * o : 64 * local + PATCH * o + PATCH, :] = (
                        frame[o, at : at + PATCH, :].astype(BF16).astype(F32)
                    )
            flip[1] = flip[0].T
            token = f * NTOK + pair * 16
            for y in range(PATCH // 2):
                even = flip[1, pl.ds(2 * y, 8, stride=PATCH), :]
                odd = flip[1, pl.ds(2 * y + 1, 8, stride=PATCH), :]
                patches[token : token + 8, 128 * y : 128 * y + 128] = jnp.where(lane64, even, pltpu.roll(odd, 64, 1))
                patches[token + 8 : token + 16, 128 * y : 128 * y + 128] = jnp.where(lane64, pltpu.roll(even, 64, 1), odd)

    token_value = nn_dot(patches[...].astype(BF16), embed[...])
    rows8[...] = jnp.zeros(rows8.shape, F32)
    abar[...] = jnp.zeros(abar.shape, F32)
    place_value = place[...].astype(F32)
    for f in range(samples):
        value = token_value[f * NTOK : f * NTOK + NTOK] + place_value
        rows8[0, f : f + 1, :] = jnp.mean(value, axis=0, keepdims=True)
        centered = value - jnp.mean(value, axis=-1, keepdims=True)
        scale = lax.rsqrt(jnp.mean(centered * centered, axis=-1, keepdims=True) + 1e-05)
        value = centered * scale
        normed[f * NTOK : f * NTOK + NTOK, :] = value
        normed16[f * NTOK : f * NTOK + NTOK, :] = value.astype(BF16)
        tokens[f * NTOK : f * NTOK + NTOK, :] = jnp.broadcast_to(scale, (NTOK, 128))

    def weight_part(i, z):
        source = pack_ref.at[i * NZ + z]
        return jnp.concatenate([source[0:256, :], source[320:576, :]], axis=1)

    def weight_rest(i):
        return jnp.concatenate(
            [
                jnp.concatenate([pack_ref[i * NZ + z, 256:320, :], pack_ref[i * NZ + z, 576:640, :]], axis=1)
                for z in range(NZ)
            ],
            axis=0,
        )

    lane_all = lane_iota(count)
    for i in range(NT):
        mixed = nn_dot(normed16[:, 1024:1280], weight_rest(i))
        for z in range(NZ):
            mixed = mixed + nn_dot(normed16[:, 256 * z : 256 * z + 256], weight_part(i, z))
        first, second = mixed[:, 0:128], mixed[:, 128:256]
        found = (
            first,
            jnp.where(lane_all < 48, pltpu.roll(first, 48, 1), pltpu.roll(second, 48, 1)),
            pltpu.roll(second, 96, 1),
        )
        for m in range(3):
            slots[3 * i + m] = jnp.where(lane_all < HD, found[m], 0.0).astype(BF16)

    for h in range(HEADS):
        for f in range(samples):
            span = slice(f * NTOK, f * NTOK + NTOK)
            logits = nt_dot(slots[h, span, :], slots[HEADS + h, span, :]) * HD ** (-0.5)
            logits = jnp.exp(logits - jnp.max(logits, axis=-1, keepdims=True))
            prob = logits / jnp.sum(logits, axis=-1, keepdims=True)
            weights[h * samples + f] = prob
            attended = nn_dot(prob.astype(BF16), slots[2 * HEADS + h, span, :]).astype(BF16)
            abar[h, f : f + 1, :] = jnp.mean(attended.astype(F32), axis=0, keepdims=True)

    pooled = rows8[0]
    for h in range(HEADS):
        part = nn_dot(split_two(abar[h])[:, 0:HD], outw[HD * h : HD * h + HD, :])
        pooled = pooled + part[0:8] + part[8:16]
    pooled = pooled - jnp.mean(pooled, axis=-1, keepdims=True)
    scale = lax.rsqrt(jnp.mean(pooled * pooled, axis=-1, keepdims=True) + 1e-05)
    pooled = pooled * scale
    head = head_ref[...]
    score_ref[...] = jnp.broadcast_to(jnp.sum(pooled * head, axis=-1, keepdims=True), (8, 128))
    dpooled = scale * (
        head - jnp.mean(head, axis=-1, keepdims=True) - pooled * jnp.mean(pooled * head, axis=-1, keepdims=True)
    )
    dres = dpooled * (1.0 / NTOK)
    rows8[1] = dres
    dres_two = split_two(dres)

    for h in range(HEADS):
        datt = nt_dot(dres_two, outw[HD * h : HD * h + HD, :])
        datt = (datt[0:8] + datt[8:16]).astype(BF16)
        datt = jnp.concatenate([datt, jnp.zeros((8, 128 - HD), BF16)], axis=1)
        for f in range(samples):
            span = slice(f * NTOK, f * NTOK + NTOK)
            prob = weights[h * samples + f]
            row = datt[f : f + 1, :]
            dweight = nt_dot(datt, slots[2 * HEADS + h, span, :])[f : f + 1, :].astype(BF16).astype(F32)
            inner = jnp.sum(prob * dweight, axis=-1, keepdims=True)
            dlogit = (prob * (dweight - inner) * HD ** (-0.5)).astype(BF16)
            dslots[h, span, :] = nn_dot(dlogit, slots[HEADS + h, span, :])
            dslots[HEADS + h, span, :] = tn_dot(dlogit, slots[h, span, :])
            dslots[2 * HEADS + h, span, :] = tn_dot(
                prob.astype(BF16), jnp.broadcast_to(row.astype(F32), (NTOK, 128)).astype(BF16)
            )

    dnormed[...] = jnp.zeros(dnormed.shape, F32)
    for i in range(NT):
        one, two, three = dslots[3 * i], dslots[3 * i + 1], dslots[3 * i + 2]
        two = pltpu.roll(two, 80, 1)
        three = pltpu.roll(three, 32, 1)
        first = jnp.where(lane_all < HD, one, two)
        second = jnp.where(lane_all < 32, two, jnp.where(lane_all < COLS, three, 0.0))
        dmixed = jnp.concatenate([first, second], axis=1).astype(BF16)
        for z in range(NZ):
            dnormed[:, 256 * z : 256 * z + 256] += nt_dot(dmixed, weight_part(i, z))
        dnormed[:, 1024:1280] += nt_dot(dmixed, weight_rest(i))

    for f in range(samples):
        span = slice(f * NTOK, f * NTOK + NTOK)
        value, dvalue = normed[span, :], dnormed[span, :]
        scale = tokens[span, 0:1]
        dvalue = scale * (
            dvalue
            - jnp.mean(dvalue, axis=-1, keepdims=True)
            - value * jnp.mean(dvalue * value, axis=-1, keepdims=True)
        )
        normed16[span, :] = (dvalue + rows8[1, f : f + 1, :]).astype(BF16)
    patches[...] = nt_dot(normed16[...], embed[...])

    frame[...] = jnp.zeros(frame.shape, F32)
    rows = out_ref.shape[3]
    flip[...] = jnp.zeros(flip.shape, F32)
    for f in range(samples):
        for pair in range(patch_rows // 2):
            token = f * NTOK + pair * 16
            for y in range(PATCH // 2):
                one = patches[token : token + 8, 128 * y : 128 * y + 128]
                two = patches[token + 8 : token + 16, 128 * y : 128 * y + 128]
                flip[1, pl.ds(2 * y, 8, stride=PATCH), :] = jnp.where(lane64, one, pltpu.roll(two, 64, 1))
                flip[1, pl.ds(2 * y + 1, 8, stride=PATCH), :] = jnp.where(lane64, pltpu.roll(one, 64, 1), two)
            flip[0] = flip[1].T
            for local in range(2):
                at = 8 + PATCH * (2 * pair + local)
                for o in range(3):
                    frame[o, at : at + PATCH, :] = flip[0, 64 * local + PATCH * o : 64 * local + PATCH * o + PATCH, :]
        for i in range(tiles):
            at = row_count * i + 7
            for o in range(3):
                out_ref[i, f, o] = frame[o, at : at + rows, :].astype(BF16)


def pack_part(rows_in, embed_part, out_part, place_part):
    ordered = jnp.concatenate([rows_in[0:128], rows_in[160:288], rows_in[128:160], rows_in[288:320]], axis=0)
    upper = jnp.pad(ordered[:, 128:240], ((0, 0), (0, 16)))
    other = jnp.concatenate([embed_part, out_part, place_part], axis=0)
    rest = other[:, 128:160].reshape(4, 96, 32)
    rest = jnp.concatenate([rest[q] for q in range(4)], axis=1)
    return jnp.concatenate([ordered[:, 0:128], upper, other[:, 0:128], rest], axis=0)


def embed_rows(patch_embed):
    columns = patch_embed.shape[1]
    ordered = patch_embed.reshape(3 * PATCH, PATCH, columns).transpose(1, 0, 2)
    ordered = jnp.pad(ordered, ((0, 16 - PATCH), (0, 48 - 3 * PATCH), (0, 0)))
    return ordered.reshape(16 * 48, columns)


def packed_weights(patch_embed, position, attend_in, attend_out):
    tiles, parts = lax.axis_size("tile"), lax.axis_size("sample")
    if tiles == NT and parts == NZ:
        z = lax.axis_index("sample")
        embed_part = lax.dynamic_slice_in_dim(embed_rows(patch_embed), z * 192, 192, axis=0)
        mine = pack_part(attend_in, embed_part, attend_out, position)
        return lax.all_gather(mine, ("tile", "sample"), axis=0)

    def whole(value):
        value = lax.all_gather(value, "sample", axis=0, tiled=True)
        return lax.all_gather(value, "tile", axis=1, tiled=True)

    embed_full = embed_rows(lax.all_gather(patch_embed, "tile", axis=1, tiled=True))
    split = [
        value.reshape(NZ, value.shape[0] // NZ, NT, value.shape[1] // NT).transpose(2, 0, 1, 3)
        for value in (whole(attend_in), embed_full, whole(attend_out), whole(position))
    ]
    split = [value.reshape((NT * NZ,) + value.shape[2:]) for value in split]
    return jax.vmap(pack_part)(*split)


def params(mib=48):
    return pltpu.CompilerParams(vmem_limit_bytes=mib * 1024 * 1024)


def local(
    features,
    norm_gain,
    conv_weight,
    patch_embed,
    position,
    attend_in,
    attend_out,
    reward_head,
    group_index,
    frame_pick,
):
    samples, frames, row_count, merged = features.shape
    tiles, parts = lax.axis_size("tile"), lax.axis_size("sample")
    slabs = -(-row_count // 16)
    sent_rows = -(-(row_count + 2) // 16) * 16
    acc_rows = max(16 * slabs + 8, sent_rows)
    packed = packed_weights(patch_embed, position, attend_in, attend_out)
    half_gain = jnp.repeat(0.5 * norm_gain, COLS)[None, :]
    taps = jnp.pad(
        conv_weight.transpose(1, 2, 0, 3, 4).reshape(3, 27, CH), ((0, 0), (0, 5), (0, 0))
    )

    is_entry = frame_pick[:, None, :] == jnp.arange(frames, dtype=jnp.int32)[None, :, None]
    entry_at = jnp.arange(SCORED, dtype=jnp.int32)[None, None, :]
    live = jnp.any(is_entry, axis=2).astype(jnp.int32)
    entry = jnp.sum(jnp.where(is_entry, entry_at, 0), axis=2) - (1 - live)
    following = jnp.concatenate([entry[:, 1:], entry[:, -2:-1]], axis=1)
    slot = jnp.where(entry >= 0, entry, following).reshape(-1)
    live = live.reshape(-1)

    x_spec = pl.BlockSpec((1, 1, row_count, merged), lambda s, t, *_: (s, t, 0, 0))
    inv_spec = pl.BlockSpec((1, 1, 16 * slabs, SPAN), lambda s, t, *_: (s, t, 0, 0))
    gain_spec = pl.BlockSpec((1, merged), lambda s, t, *_: (0, 0))
    taps_spec = pl.BlockSpec((3, 32, CH), lambda s, t, *_: (0, 0, 0))
    decoded, inverse = pl.pallas_call(
        functools.partial(decode_kernel, row_count),
        grid_spec=pltpu.PrefetchScalarGridSpec(
            num_scalar_prefetch=2,
            grid=(samples, frames),
            in_specs=[x_spec, gain_spec, taps_spec],
            out_specs=[
                pl.BlockSpec(
                    (1, 1, 3, sent_rows, 128),
                    lambda s, t, slot_ref, live_ref: (slot_ref[s * frames + t], s, 0, 0, 0),
                ),
                inv_spec,
            ],
            scratch_shapes=[
                pltpu.VMEM((OUT_ROWS, IN_ROWS), BF16),
                pltpu.VMEM((slabs, IN_ROWS, 256), BF16),
                pltpu.VMEM((3, 3, acc_rows, 128), F32),
            ],
        ),
        out_shape=[
            jax.ShapeDtypeStruct((SCORED, samples, 3, sent_rows, 128), BF16),
            jax.ShapeDtypeStruct((samples, frames, 16 * slabs, SPAN), F32),
        ],
        compiler_params=params(),
        name="decode",
    )(slot, live, features, half_gain, taps)

    if tiles > SCORED:
        decoded = jnp.pad(decoded, ((0, tiles - SCORED),) + ((0, 0),) * 4)
    owned = lax.all_to_all(decoded, "tile", split_axis=0, concat_axis=0, tiled=True)

    head = reward_head.reshape(NT, D // NT)
    head = jnp.concatenate([head[:, :128].reshape(-1), head[:, 128:].reshape(-1)])[None, :]
    height = row_count * tiles
    count = samples * NTOK
    grads, scores = pl.pallas_call(
        functools.partial(reward_kernel, row_count, tiles, samples),
        out_shape=[
            jax.ShapeDtypeStruct((tiles, samples, 3, sent_rows, 128), BF16),
            jax.ShapeDtypeStruct((8, 128), F32),
        ],
        scratch_shapes=[
            pltpu.VMEM((3, height + 48, 128), F32),
            pltpu.VMEM((2, 128, 128), F32),
            pltpu.VMEM((KIN, D), BF16),
            pltpu.VMEM((HEADS * HD, D), BF16),
            pltpu.VMEM((NTOK, D), BF16),
            pltpu.VMEM((count, KIN), F32),
            pltpu.VMEM((count, 128), F32),
            pltpu.VMEM((count, D), F32),
            pltpu.VMEM((count, D), BF16),
            pltpu.VMEM((3 * HEADS, count, 128), BF16),
            pltpu.VMEM((HEADS * samples, NTOK, NTOK), F32),
            pltpu.VMEM((3 * HEADS, count, 128), F32),
            pltpu.VMEM((count, D), F32),
            pltpu.VMEM((2, 8, D), F32),
            pltpu.VMEM((HEADS, 8, 128), F32),
        ],
        compiler_params=params(),
        name="reward",
    )(owned, packed, head)

    mine = jnp.concatenate([scores[:samples, 0], group_index.astype(F32)])
    gathered = [mine]
    for shift in range(1, parts):
        ring = [(z, (z + shift) % parts) for z in range(parts)]
        gathered.append(lax.ppermute(mine, "sample", ring))
    gathered = jnp.stack(gathered)
    groups = gathered[:, samples:].reshape(-1)
    score_row = gathered[:, :samples].reshape(-1)
    high = score_row.astype(BF16)
    low = score_row - high.astype(F32)
    mid = low.astype(BF16)
    low = (low - mid.astype(F32)).astype(BF16)
    total = parts * samples
    carried = jnp.concatenate([high, mid, low])
    grads = grads.at[:, 0, 0, sent_rows - 1, 0 : 3 * total].set(
        jnp.broadcast_to(carried, (tiles, 3 * total))
    )
    returned = lax.all_to_all(grads, "tile", split_axis=0, concat_axis=0, tiled=True)
    returned = returned[:SCORED]

    got = returned[:, 0, 0, sent_rows - 1, 0 : 3 * total].astype(F32).reshape(SCORED, 3, total)
    entry_scores = got[:, 0] + (got[:, 1] + got[:, 2])
    rewards = jnp.sum(entry_scores, axis=0) / SCORED
    member = (groups[:samples, None] == groups[None, :]).astype(F32)
    mean_group = jnp.sum(member * rewards[None, :], axis=1) / GROUP
    second_group = jnp.sum(member * (rewards * rewards)[None, :], axis=1) / GROUP - mean_group * mean_group
    advantage = (rewards[:samples] - mean_group) * lax.rsqrt(second_group + SMOOTH)
    cotangent = -LOSS_SCALE * advantage / SCORED

    return pl.pallas_call(
        functools.partial(restore_kernel, row_count),
        grid_spec=pltpu.PrefetchScalarGridSpec(
            num_scalar_prefetch=1,
            grid=(samples, frames),
            in_specs=[
                x_spec,
                inv_spec,
                gain_spec,
                taps_spec,
                pl.BlockSpec((SCORED, samples, 3, sent_rows, 128), lambda s, t, *_: (0, 0, 0, 0, 0)),
                pl.BlockSpec(memory_space=pltpu.SMEM),
            ],
            out_specs=x_spec,
            scratch_shapes=[
                pltpu.VMEM((IN_ROWS, OUT_ROWS), BF16),
                pltpu.VMEM((frames + 2, 3, 3, acc_rows, 128), F32),
                pltpu.VMEM((slabs, OUT_ROWS, 256), BF16),
                pltpu.VMEM((slabs, IN_ROWS, 256), F32),
                pltpu.VMEM((slabs, 16, merged), F32),
            ],
        ),
        out_shape=jax.ShapeDtypeStruct(features.shape, BF16),
        compiler_params=params(),
        name="restore",
    )(entry.reshape(-1), features, inverse, half_gain, taps, returned, cotangent)


def solution(mesh):
    in_specs = (
        P("sample", None, "tile", None),
        P(),
        P(),
        P(None, "tile"),
        P("sample", "tile"),
        P("sample", "tile"),
        P("sample", "tile"),
        P(),
        P("sample"),
        P("sample", None),
    )
    out_specs = P("sample", None, "tile", None)
    return jax.shard_map(local, mesh=mesh, in_specs=in_specs, out_specs=out_specs, check_vma=False)
```

```python
import functools

import jax
import jax.numpy as jnp
from jax import lax
from jax.experimental import pallas as pl
from jax.experimental.pallas import tpu as pltpu
from jax.experimental.layout import Layout, with_layout_constraint
from jax.sharding import Mesh, PartitionSpec as P

SCORED = 8
PATCH = 14
HEADS = 8
HD = 80
GROUP = 4
LOSS_SCALE = 16384.0
SMOOTH = 0.01

TILE = ("chip", "core")
CH = 96
COLS = 112
SPANS = CH // 8
OUT_ROWS = 27 * 16
NT = 8
NZ = 4
PACK = 1120
CYCLE = [
    (2 * chip + core) * NZ + z
    for chip, heights in ((0, (0, 1, 2, 3)), (1, (3, 2, 1, 0)), (3, (0, 1, 2, 3)), (2, (3, 2, 1, 0)))
    for z in heights
    for core in range(2)
]
PLACES = [[CYCLE.index(i * NZ + z) for z in range(NZ)] for i in range(NT)]
KIN = 896
D = 1280
NTOK = 128
F32 = jnp.float32
BF16 = jnp.bfloat16


def lane_iota(rows):
    return lax.broadcasted_iota(jnp.int32, (rows, 128), 1)


def sub_iota(rows):
    return lax.broadcasted_iota(jnp.int32, (rows, 128), 0)


def channels_of(raw, at, group, sample):
    start = 8 + 14 * group + sample
    here = raw[at, pl.ds(start, 8, stride=2), :]
    before = raw[at, pl.ds(start - 2, 8, stride=2), :]
    joined = jnp.where(lane_iota(8) < 128 - 16 * sub_iota(8), here, before)
    return pltpu.roll(joined, 0, 1, stride=16, stride_axis=0)


def tiles_of(value):
    turned = jnp.take_along_axis(value, (lane_iota(8) + 16 * sub_iota(8)) % 128, axis=1)
    return jnp.where(lane_iota(8) < COLS - 16 * sub_iota(8), turned, pltpu.roll(turned, 7, 0))


def banded(weight_ref, taps, row_block, transposed):
    taps[...] = jnp.zeros(taps.shape, F32)
    for a in range(3):
        for b in range(3):
            for e in range(3):
                for o in range(3):
                    at = (a * 3 + e) * 3 + o
                    taps[b, at : at + 1, :] = weight_ref[a, b, e, o : o + 1, :].astype(F32)
    inner = row_block * CH
    pick = (
        lax.broadcasted_iota(jnp.int32, (OUT_ROWS, 32), 0) // 16
        == lax.broadcasted_iota(jnp.int32, (OUT_ROWS, 32), 1)
    ).astype(BF16)
    if transposed:
        shape, p_dim, r_dim = (inner, OUT_ROWS), 1, 0
        grow_shape, grow_dim = (inner, CH), 0
    else:
        shape, p_dim, r_dim = (OUT_ROWS, inner), 0, 1
        grow_shape, grow_dim = (CH, inner), 1
    at = lax.broadcasted_iota(jnp.int32, grow_shape, grow_dim)
    at = at - CH * ((at.astype(F32) + 0.5) * (1.0 / CH)).astype(jnp.int32)
    grow = (at == lax.broadcasted_iota(jnp.int32, grow_shape, 1 - grow_dim)).astype(BF16)
    p_at = lax.broadcasted_iota(jnp.int32, shape, p_dim) % 16
    r_at = lax.broadcasted_iota(jnp.int32, shape, r_dim)
    r_at = ((r_at.astype(F32) + 0.5) * (1.0 / CH)).astype(jnp.int32)
    total = jnp.zeros(shape, F32)
    for b in range(3):
        rows = jnp.dot(pick, taps[b].astype(BF16), preferred_element_type=F32).astype(BF16)
        if transposed:
            full = lax.dot_general(
                grow, rows, (((1,), (1,)), ((), ())), preferred_element_type=F32
            )
        else:
            full = jnp.dot(rows, grow, preferred_element_type=F32)
        total = jnp.where(p_at == r_at + 2 - b, full, total)
    return total.astype(BF16)


def half_gains(gain_ref):
    rows = jnp.concatenate([gain_ref[0:1, :], jnp.zeros((1, 128 - CH), F32)], axis=1)
    return 0.5 * jnp.broadcast_to(rows, (128, 128)).T


def entry_of(pick_ref, sample, frame):
    found = jnp.int32(-1)
    for j in range(SCORED):
        found = jnp.where(pick_ref[sample, j] == frame, jnp.int32(j), found)
    return found


def decode_kernel(row_block, pick_ref, x_ref, gain_ref, weight_ref, out_ref, band, taps, gains, raw, operand, acc, final):
    t = pl.program_id(0)
    blocks = x_ref.shape[1] // row_block
    rows = out_ref.shape[3]

    @pl.when(t == 0)
    def _():
        band[...] = banded(weight_ref, taps, row_block, False)
        gains[...] = half_gains(gain_ref)
        acc[...] = jnp.zeros(acc.shape, F32)
        raw[...] = jnp.zeros(raw.shape, F32)

    for k in range(blocks):

        def one_row(row, at):
            raw[at, 8:176, :] = x_ref[0, k * row_block + row].astype(F32)
            for s in range(2):
                found = [channels_of(raw, at, g, s) for g in range(SPANS)]
                square = found[0] * found[0]
                for g in range(1, SPANS):
                    square = square + found[g] * found[g]
                second = jnp.sum(square, axis=0, keepdims=True) * (1.0 / CH)
                inv = lax.rsqrt(second + 1e-06)
                for m in range(SPANS // 2):
                    acts = []
                    for g in (2 * m, 2 * m + 1):
                        half = found[g] * inv * gains[8 * g : 8 * g + 8, :]
                        acts.append(half + half * jnp.tanh(half))
                    start = row * CH + 16 * m
                    operand[k, start : start + 16, 128 * s : 128 * s + 128] = jnp.concatenate(
                        acts, axis=0
                    ).astype(BF16)

        for row in range(row_block):
            one_row(row, row)
        spread = jnp.dot(band[...], operand[k], preferred_element_type=F32)
        lane = lane_iota(48)
        for s in range(2):
            part = spread[:, 128 * s : 128 * s + 128]
            for a in range(3):
                low, mid, high = (part[144 * a + 48 * e : 144 * a + 48 * e + 48] for e in range(3))
                low = jnp.where(lane == 0, 0.0, pltpu.roll(low, 1, 1))
                high = jnp.where(lane == COLS - 1, 0.0, pltpu.roll(high, 127, 1))
                acc[k, 2 - a, s] += low + mid + high

    keep = lane_iota(rows) < COLS
    for s in range(2):
        entry = entry_of(pick_ref, s, t)

        @pl.when(entry >= 0)
        def _():
            for o in range(3):
                final[...] = jnp.zeros(final.shape, F32)
                for k in range(blocks):
                    start = k * row_block
                    final[start : start + 16, :] += acc[k, 0, s, 16 * o : 16 * o + 16, :]
                out_ref[jnp.maximum(entry, 0), s, o] = jnp.where(keep, final[0:rows, :], 0.0).astype(BF16)

    for k in range(blocks):
        acc[k, 0] = acc[k, 1]
        acc[k, 1] = acc[k, 2]
        acc[k, 2] = jnp.zeros(acc.shape[2:], F32)


def restore_kernel(row_block, pick_ref, scale_ref, x_ref, gain_ref, weight_ref, grad_ref, out_ref, band, taps, gains, raw, back, shifted, coming):
    t = pl.program_id(0)
    frames = pl.num_programs(0)
    blocks = x_ref.shape[1] // row_block
    rows = grad_ref.shape[3]

    @pl.when(t == 0)
    def _():
        band[...] = banded(weight_ref, taps, row_block, True)
        gains[...] = half_gains(gain_ref)
        raw[...] = jnp.zeros(raw.shape, F32)
        shifted[...] = jnp.zeros(shifted.shape, BF16)
        lane = lane_iota(rows)

        def one_frame(frame, carry):
            for s in range(2):
                entry = entry_of(pick_ref, s, frame)
                scale = jnp.where(entry >= 0, scale_ref[s], 0.0)
                source = jnp.maximum(entry, 0)
                for o in range(3):
                    value = grad_ref[source, s, o].astype(F32) * scale
                    value = jnp.where(lane < COLS, value, 0.0)
                    for e, moved in enumerate((pltpu.roll(value, 127, 1), value, pltpu.roll(value, 1, 1))):
                        for k in range(blocks):
                            start = k * row_block
                            shifted[frame, k, 48 * e + 16 * o : 48 * e + 16 * o + 16, 128 * s : 128 * s + 128] = moved[
                                start : start + 16
                            ].astype(BF16)
            return carry

        lax.fori_loop(0, frames, one_frame, 0)

    for k in range(blocks):
        operand = jnp.concatenate([shifted[t + 2 - a, k] for a in range(3)], axis=0)
        coming[k] = jnp.dot(band[...], operand, preferred_element_type=F32)

        def one_row(row, at):
            raw[at, 8:176, :] = x_ref[0, k * row_block + row].astype(F32)
            for s in range(2):
                found = [channels_of(raw, at, g, s) for g in range(SPANS)]
                square = found[0] * found[0]
                for g in range(1, SPANS):
                    square = square + found[g] * found[g]
                inv = lax.rsqrt(jnp.sum(square, axis=0, keepdims=True) * (1.0 / CH) + 1e-06)
                outs, total = [], None
                for g in range(SPANS):
                    gain = gains[8 * g : 8 * g + 8, :]
                    half = found[g] * inv * gain
                    th = jnp.tanh(half)
                    start = row * CH + 8 * g
                    cot = coming[k, start : start + 8, 128 * s : 128 * s + 128]
                    out = cot * gain * (1.0 + th) * (1.0 + half * (1.0 - th))
                    outs.append(out)
                    total = out * found[g] if g == 0 else total + out * found[g]
                factor = jnp.sum(total, axis=0, keepdims=True) * (1.0 / CH) * inv * inv * inv
                for g in range(SPANS):
                    result = tiles_of(outs[g] * inv - found[g] * factor)
                    back[at, pl.ds(14 * g + s, 7, stride=2), :] = result[0:7]
            out_ref[0, k * row_block + row] = back[at].astype(BF16)

        for row in range(row_block):
            one_row(row, row)


def nt_dot(one, two):
    return lax.dot_general(one, two, (((1,), (1,)), ((), ())), preferred_element_type=F32)


def tn_dot(one, two):
    return lax.dot_general(one, two, (((0,), (0,)), ((), ())), preferred_element_type=F32)


def nn_dot(one, two):
    return jnp.dot(one, two, preferred_element_type=F32)


def split_two(value):
    high = value.astype(BF16)
    low = (value - high.astype(F32)).astype(BF16)
    return jnp.concatenate([high, low], axis=0)


def reward_kernel(
    row_count, tiles, samples,
    part_ref, packed_ref, head_ref,
    out_ref, score_ref,
    pack, arrived, frame, flip, embed, outw, place, patches, tokens, normed, normed16, slots, weights, dslots, dnormed, rows8, abar,
):
    height = row_count * tiles
    patch_rows = height // PATCH
    lane64 = lane_iota(8) < 64
    lane = lane_iota(NTOK)
    count = samples * NTOK

    copy = pltpu.make_async_copy(packed_ref, pack, arrived)
    copy.start()

    flip[...] = jnp.zeros(flip.shape, F32)
    for f in range(samples):
        frame[...] = jnp.zeros(frame.shape, F32)
        for i in range(tiles):
            at = row_count * i + 7
            for o in range(3):
                frame[o, at : at + row_count + 2, :] += part_ref[i, f, o, 0 : row_count + 2, :].astype(F32)
        for pair in range(patch_rows // 2):
            for local in range(2):
                at = 8 + PATCH * (2 * pair + local)
                for o in range(3):
                    flip[0, 64 * local + PATCH * o : 64 * local + PATCH * o + PATCH, :] = (
                        frame[o, at : at + PATCH, :].astype(BF16).astype(F32)
                    )
            flip[1] = flip[0].T
            token = f * NTOK + pair * 16
            for y in range(PATCH // 2):
                even = flip[1, pl.ds(2 * y, 8, stride=PATCH), :]
                odd = flip[1, pl.ds(2 * y + 1, 8, stride=PATCH), :]
                patches[token : token + 8, 128 * y : 128 * y + 128] = jnp.where(lane64, even, pltpu.roll(odd, 64, 1))
                patches[token + 8 : token + 16, 128 * y : 128 * y + 128] = jnp.where(lane64, pltpu.roll(even, 64, 1), odd)

    copy.wait()

    embed[...] = jnp.zeros(embed.shape, BF16)
    lane96 = lane_iota(96)
    for z in range(NZ):
        for i in range(NT):
            source = pack.at[PLACES[i][z]]
            for xx in range(4):
                x = 4 * z + xx
                if x < PATCH:
                    embed[64 * x : 64 * x + 48, 128 * i : 128 * i + 128] = source[640 + 48 * xx : 688 + 48 * xx, :]
            outw[160 * z : 160 * z + 160, 128 * i : 128 * i + 128] = source[832:992, :]
            place[32 * z : 32 * z + 32, 128 * i : 128 * i + 128] = source[992:1024, :]
        for ib in range(2):
            sources = [pack[PLACES[4 * ib + j][z], 1024:1120, :].astype(F32) for j in range(4)]
            rolled = [[sources[j] if d == 0 else pltpu.roll(sources[j], 32 * d, 1) for d in range(4)] for j in range(4)]
            at = 1024 + 128 * ib
            for q in range(4):
                found = rolled[0][(0 - q) % 4]
                for j in range(1, 4):
                    found = jnp.where(lane96 >= 32 * j, rolled[j][(j - q) % 4], found)
                found = found.astype(BF16)
                if q < 2:
                    for xx in range(2):
                        x = 4 * z + 2 * q + xx
                        if x < PATCH:
                            embed[64 * x : 64 * x + 48, at : at + 128] = found[48 * xx : 48 * xx + 48]
                elif q == 2:
                    outw[160 * z : 160 * z + 96, at : at + 128] = found
                else:
                    outw[160 * z + 96 : 160 * z + 160, at : at + 128] = found[:64]
                    place[32 * z : 32 * z + 32, at : at + 128] = found[64:96]

    token_value = nn_dot(patches[...].astype(BF16), embed[...])
    rows8[...] = jnp.zeros(rows8.shape, F32)
    abar[...] = jnp.zeros(abar.shape, F32)
    place_value = place[...].astype(F32)
    for f in range(samples):
        value = token_value[f * NTOK : f * NTOK + NTOK] + place_value
        rows8[0, f : f + 1, :] = jnp.mean(value, axis=0, keepdims=True)
        centered = value - jnp.mean(value, axis=-1, keepdims=True)
        scale = lax.rsqrt(jnp.mean(centered * centered, axis=-1, keepdims=True) + 1e-05)
        value = centered * scale
        normed[f * NTOK : f * NTOK + NTOK, :] = value
        normed16[f * NTOK : f * NTOK + NTOK, :] = value.astype(BF16)
        tokens[f * NTOK : f * NTOK + NTOK, :] = jnp.broadcast_to(scale, (NTOK, 128))

    def weight_part(i, z):
        source = pack.at[PLACES[i][z]]
        return jnp.concatenate([source[0:256, :], source[320:576, :]], axis=1)

    def weight_rest(i):
        return jnp.concatenate(
            [
                jnp.concatenate([pack[PLACES[i][z], 256:320, :], pack[PLACES[i][z], 576:640, :]], axis=1)
                for z in range(NZ)
            ],
            axis=0,
        )

    lane_all = lane_iota(count)
    for i in range(NT):
        mixed = nn_dot(normed16[:, 1024:1280], weight_rest(i))
        for z in range(NZ):
            mixed = mixed + nn_dot(normed16[:, 256 * z : 256 * z + 256], weight_part(i, z))
        first, second = mixed[:, 0:128], mixed[:, 128:256]
        found = (
            first,
            jnp.where(lane_all < 48, pltpu.roll(first, 48, 1), pltpu.roll(second, 48, 1)),
            pltpu.roll(second, 96, 1),
        )
        for m in range(3):
            slots[3 * i + m] = jnp.where(lane_all < HD, found[m], 0.0).astype(BF16)

    for h in range(HEADS):
        for f in range(samples):
            span = slice(f * NTOK, f * NTOK + NTOK)
            logits = nt_dot(slots[h, span, :], slots[HEADS + h, span, :]) * HD ** (-0.5)
            logits = jnp.exp(logits - jnp.max(logits, axis=-1, keepdims=True))
            prob = logits / jnp.sum(logits, axis=-1, keepdims=True)
            weights[h * samples + f] = prob
            attended = nn_dot(prob.astype(BF16), slots[2 * HEADS + h, span, :]).astype(BF16)
            abar[h, f : f + 1, :] = jnp.mean(attended.astype(F32), axis=0, keepdims=True)

    pooled = rows8[0]
    for h in range(HEADS):
        part = nn_dot(split_two(abar[h])[:, 0:HD], outw[HD * h : HD * h + HD, :])
        pooled = pooled + part[0:8] + part[8:16]
    pooled = pooled - jnp.mean(pooled, axis=-1, keepdims=True)
    scale = lax.rsqrt(jnp.mean(pooled * pooled, axis=-1, keepdims=True) + 1e-05)
    pooled = pooled * scale
    head = head_ref[...]
    score_ref[...] = jnp.broadcast_to(jnp.sum(pooled * head, axis=-1, keepdims=True), (8, 128))
    dpooled = scale * (
        head - jnp.mean(head, axis=-1, keepdims=True) - pooled * jnp.mean(pooled * head, axis=-1, keepdims=True)
    )
    dres = dpooled * (1.0 / NTOK)
    rows8[1] = dres
    dres_two = split_two(dres)

    for h in range(HEADS):
        datt = nt_dot(dres_two, outw[HD * h : HD * h + HD, :])
        datt = (datt[0:8] + datt[8:16]).astype(BF16)
        datt = jnp.concatenate([datt, jnp.zeros((8, 128 - HD), BF16)], axis=1)
        for f in range(samples):
            span = slice(f * NTOK, f * NTOK + NTOK)
            prob = weights[h * samples + f]
            row = datt[f : f + 1, :]
            dweight = nt_dot(datt, slots[2 * HEADS + h, span, :])[f : f + 1, :].astype(BF16).astype(F32)
            inner = jnp.sum(prob * dweight, axis=-1, keepdims=True)
            dlogit = (prob * (dweight - inner) * HD ** (-0.5)).astype(BF16)
            dslots[h, span, :] = nn_dot(dlogit, slots[HEADS + h, span, :])
            dslots[HEADS + h, span, :] = tn_dot(dlogit, slots[h, span, :])
            dslots[2 * HEADS + h, span, :] = tn_dot(
                prob.astype(BF16), jnp.broadcast_to(row.astype(F32), (NTOK, 128)).astype(BF16)
            )

    dnormed[...] = jnp.zeros(dnormed.shape, F32)
    for i in range(NT):
        one, two, three = dslots[3 * i], dslots[3 * i + 1], dslots[3 * i + 2]
        two = pltpu.roll(two, 80, 1)
        three = pltpu.roll(three, 32, 1)
        first = jnp.where(lane_all < HD, one, two)
        second = jnp.where(lane_all < 32, two, jnp.where(lane_all < COLS, three, 0.0))
        dmixed = jnp.concatenate([first, second], axis=1).astype(BF16)
        for z in range(NZ):
            dnormed[:, 256 * z : 256 * z + 256] += nt_dot(dmixed, weight_part(i, z))
        dnormed[:, 1024:1280] += nt_dot(dmixed, weight_rest(i))

    for f in range(samples):
        span = slice(f * NTOK, f * NTOK + NTOK)
        value, dvalue = normed[span, :], dnormed[span, :]
        scale = tokens[span, 0:1]
        dvalue = scale * (
            dvalue
            - jnp.mean(dvalue, axis=-1, keepdims=True)
            - value * jnp.mean(dvalue * value, axis=-1, keepdims=True)
        )
        normed16[span, :] = (dvalue + rows8[1, f : f + 1, :]).astype(BF16)
    patches[...] = nt_dot(normed16[...], embed[...])

    frame[...] = jnp.zeros(frame.shape, F32)
    rows = out_ref.shape[3]
    flip[...] = jnp.zeros(flip.shape, F32)
    for f in range(samples):
        for pair in range(patch_rows // 2):
            token = f * NTOK + pair * 16
            for y in range(PATCH // 2):
                one = patches[token : token + 8, 128 * y : 128 * y + 128]
                two = patches[token + 8 : token + 16, 128 * y : 128 * y + 128]
                flip[1, pl.ds(2 * y, 8, stride=PATCH), :] = jnp.where(lane64, one, pltpu.roll(two, 64, 1))
                flip[1, pl.ds(2 * y + 1, 8, stride=PATCH), :] = jnp.where(lane64, pltpu.roll(one, 64, 1), two)
            flip[0] = flip[1].T
            for local in range(2):
                at = 8 + PATCH * (2 * pair + local)
                for o in range(3):
                    frame[o, at : at + PATCH, :] = flip[0, 64 * local + PATCH * o : 64 * local + PATCH * o + PATCH, :]
        for i in range(tiles):
            at = row_count * i + 7
            for o in range(3):
                out_ref[i, f, o] = frame[o, at : at + rows, :].astype(BF16)


def pack_part(rows_in, embed_part, out_part, place_part):
    ordered = jnp.concatenate([rows_in[0:128], rows_in[160:288], rows_in[128:160], rows_in[288:320]], axis=0)
    upper = jnp.pad(ordered[:, 128:240], ((0, 0), (0, 16)))
    other = jnp.concatenate([embed_part, out_part, place_part], axis=0)
    rest = other[:, 128:160].reshape(4, 96, 32)
    rest = jnp.concatenate([rest[q] for q in range(4)], axis=1)
    return jnp.concatenate([ordered[:, 0:128], upper, other[:, 0:128], rest], axis=0)


def pack_kernel(z_ref, rows_ref, embed_ref, out_ref, place_ref, packed_ref):
    for source, target, count in ((0, 0, 128), (160, 128, 128), (128, 256, 32), (288, 288, 32)):
        packed_ref[target : target + count, :] = rows_ref[source : source + count, 0:128]
        packed_ref[320 + target : 320 + target + count, :] = jnp.concatenate(
            [rows_ref[source : source + count, 128:240], jnp.zeros((count, 16), BF16)], axis=1
        )
    packed_ref[832:992, :] = out_ref[:, 0:128]
    packed_ref[992:1024, :] = place_ref[:, 0:128]
    width = embed_ref.shape[1]
    pixel = lax.broadcasted_iota(jnp.int32, (48, width), 0)
    lane = lax.broadcasted_iota(jnp.int32, (48, width), 1)
    parts = []
    for local in range(4):
        x = 4 * z_ref[0] + local
        hit = (lane == pixel * PATCH + x) & (pixel < 3 * PATCH) & (x < PATCH)
        parts.append(nt_dot(hit.astype(BF16), embed_ref[...]))
    embed_part = jnp.concatenate(parts, axis=0)
    packed_ref[640:832, :] = embed_part[:, 0:128].astype(BF16)
    tail = out_ref[:, 128:160].astype(F32)
    last = place_ref[:, 128:160].astype(F32)
    packed_ref[1024:1120, :] = jnp.concatenate(
        [
            embed_part[0:96, 128:160],
            embed_part[96:192, 128:160],
            tail[0:96],
            jnp.concatenate([tail[96:160], last], axis=0),
        ],
        axis=1,
    ).astype(BF16)


def embed_rows(patch_embed):
    columns = patch_embed.shape[1]
    ordered = patch_embed.reshape(3 * PATCH, PATCH, columns).transpose(1, 0, 2)
    ordered = jnp.pad(ordered, ((0, 16 - PATCH), (0, 48 - 3 * PATCH), (0, 0)))
    return ordered.reshape(16 * 48, columns)


def packed_weights(patch_embed, position, attend_in, attend_out):
    if lax.axis_size(TILE) == NT and lax.axis_size("sample") == NZ:
        z = lax.axis_index("sample").astype(jnp.int32).reshape(1)
        mine = pl.pallas_call(
            pack_kernel,
            in_specs=[pl.BlockSpec(memory_space=pltpu.SMEM)] + [pl.BlockSpec(memory_space=pltpu.VMEM)] * 4,
            out_shape=jax.ShapeDtypeStruct((PACK, 128), BF16),
            compiler_params=params(16),
            name="pack",
        )(z, attend_in, patch_embed.T, attend_out, position)
        return lax.all_gather(mine, TILE + ("sample",), axis=0, axis_index_groups=[CYCLE])

    def whole(value):
        value = lax.all_gather(value, "sample", axis=0, tiled=True)
        return lax.all_gather(value, TILE, axis=1, tiled=True)

    embed_full = embed_rows(lax.all_gather(patch_embed, TILE, axis=1, tiled=True))
    split = [
        value.reshape(NZ, value.shape[0] // NZ, NT, value.shape[1] // NT).transpose(2, 0, 1, 3)
        for value in (whole(attend_in), embed_full, whole(attend_out), whole(position))
    ]
    split = [value.reshape((NT * NZ,) + value.shape[2:])[jnp.array(CYCLE)] for value in split]
    return jax.vmap(pack_part)(*split)


def params(mib=48):
    return pltpu.CompilerParams(vmem_limit_bytes=mib * 1024 * 1024)


def local(
    features,
    norm_gain,
    conv_weight,
    patch_embed,
    position,
    attend_in,
    attend_out,
    reward_head,
    group_index,
    frame_pick,
):
    samples, frames, row_count, merged = features.shape
    tiles, parts = lax.axis_size(TILE), lax.axis_size("sample")
    sent_rows = -(-(row_count + 2) // 16) * 16
    row_block = row_count if row_count <= 14 else 14
    blocks = row_count // row_block
    inner = row_block * CH
    packed = packed_weights(patch_embed, position, attend_in, attend_out)
    order = Layout((1, 2, 3, 0, 4))
    split = (samples, frames, row_count, merged // 128, 128)
    view = with_layout_constraint(features.reshape(split), order).transpose(1, 2, 3, 0, 4)
    view = view.reshape(frames, row_count, samples * merged // 128, 128)
    gain = norm_gain[None, :]

    smem = pl.BlockSpec(memory_space=pltpu.SMEM)
    view_spec = pl.BlockSpec((1,) + view.shape[1:], lambda t: (t, 0, 0, 0))
    gain_spec = pl.BlockSpec((1, CH), lambda t: (0, 0))
    taps_spec = pl.BlockSpec((3, 3, 3, 3, CH), lambda t: (0, 0, 0, 0, 0))
    sent = (SCORED, samples, 3, sent_rows, 128)
    sent_spec = pl.BlockSpec(sent, lambda t: (0, 0, 0, 0, 0))
    decoded = pl.pallas_call(
        functools.partial(decode_kernel, row_block),
        grid=(frames,),
        in_specs=[smem, view_spec, gain_spec, taps_spec],
        out_specs=sent_spec,
        scratch_shapes=[
            pltpu.VMEM((OUT_ROWS, inner), BF16),
            pltpu.VMEM((3, 32, CH), F32),
            pltpu.VMEM((128, 128), F32),
            pltpu.VMEM((row_block, 192, 128), F32),
            pltpu.VMEM((blocks, inner, 256), BF16),
            pltpu.VMEM((blocks, 3, samples, 48, 128), F32),
            pltpu.VMEM((sent_rows + 16, 128), F32),
        ],
        out_shape=jax.ShapeDtypeStruct(sent, BF16),
        compiler_params=params(32),
        name="decode",
    )(frame_pick, view, gain, conv_weight)

    if tiles > SCORED:
        decoded = jnp.pad(decoded, ((0, tiles - SCORED),) + ((0, 0),) * 4)
    owned = lax.all_to_all(decoded, TILE, split_axis=0, concat_axis=0, tiled=True)

    head = reward_head.reshape(NT, D // NT)
    head = jnp.concatenate([head[:, :128].reshape(-1), head[:, 128:].reshape(-1)])[None, :]
    height = row_count * tiles
    count = samples * NTOK
    grads, scores = pl.pallas_call(
        functools.partial(reward_kernel, row_count, tiles, samples),
        out_shape=[
            jax.ShapeDtypeStruct((tiles, samples, 3, sent_rows, 128), BF16),
            jax.ShapeDtypeStruct((8, 128), F32),
        ],
        in_specs=[
            pl.BlockSpec(memory_space=pltpu.VMEM),
            pl.BlockSpec(memory_space=pl.ANY),
            pl.BlockSpec(memory_space=pltpu.VMEM),
        ],
        scratch_shapes=[
            pltpu.VMEM(packed.shape, BF16),
            pltpu.SemaphoreType.DMA,
            pltpu.VMEM((3, height + 48, 128), F32),
            pltpu.VMEM((2, 128, 128), F32),
            pltpu.VMEM((KIN, D), BF16),
            pltpu.VMEM((HEADS * HD, D), BF16),
            pltpu.VMEM((NTOK, D), BF16),
            pltpu.VMEM((count, KIN), F32),
            pltpu.VMEM((count, 128), F32),
            pltpu.VMEM((count, D), F32),
            pltpu.VMEM((count, D), BF16),
            pltpu.VMEM((3 * HEADS, count, 128), BF16),
            pltpu.VMEM((HEADS * samples, NTOK, NTOK), F32),
            pltpu.VMEM((3 * HEADS, count, 128), F32),
            pltpu.VMEM((count, D), F32),
            pltpu.VMEM((2, 8, D), F32),
            pltpu.VMEM((HEADS, 8, 128), F32),
        ],
        compiler_params=params(),
        name="reward",
    )(owned, packed, head)

    mine = jnp.concatenate([scores[:samples, 0], group_index.astype(F32)])
    gathered = [mine]
    for shift in range(1, parts):
        ring = [(z, (z + shift) % parts) for z in range(parts)]
        gathered.append(lax.ppermute(mine, "sample", ring))
    gathered = jnp.stack(gathered)
    groups = gathered[:, samples:].reshape(-1)
    score_row = gathered[:, :samples].reshape(-1)
    high = score_row.astype(BF16)
    low = score_row - high.astype(F32)
    mid = low.astype(BF16)
    low = (low - mid.astype(F32)).astype(BF16)
    total = parts * samples
    carried = jnp.concatenate([high, mid, low])
    grads = grads.at[:, 0, 0, sent_rows - 1, 0 : 3 * total].set(
        jnp.broadcast_to(carried, (tiles, 3 * total))
    )
    returned = lax.all_to_all(grads, TILE, split_axis=0, concat_axis=0, tiled=True)
    returned = returned[:SCORED]

    got = returned[:, 0, 0, sent_rows - 1, 0 : 3 * total].astype(F32).reshape(SCORED, 3, total)
    entry_scores = got[:, 0] + (got[:, 1] + got[:, 2])
    rewards = jnp.sum(entry_scores, axis=0) / SCORED
    member = (groups[:samples, None] == groups[None, :]).astype(F32)
    mean_group = jnp.sum(member * rewards[None, :], axis=1) / GROUP
    second_group = jnp.sum(member * (rewards * rewards)[None, :], axis=1) / GROUP - mean_group * mean_group
    advantage = (rewards[:samples] - mean_group) * lax.rsqrt(second_group + SMOOTH)
    cotangent = -LOSS_SCALE * advantage / SCORED

    result = pl.pallas_call(
        functools.partial(restore_kernel, row_block),
        grid=(frames,),
        in_specs=[smem, smem, view_spec, gain_spec, taps_spec, sent_spec],
        out_specs=view_spec,
        scratch_shapes=[
            pltpu.VMEM((inner, OUT_ROWS), BF16),
            pltpu.VMEM((3, 32, CH), F32),
            pltpu.VMEM((128, 128), F32),
            pltpu.VMEM((row_block, 192, 128), F32),
            pltpu.VMEM((row_block, samples * merged // 128, 128), F32),
            pltpu.VMEM((frames + 2, blocks, 144, 256), BF16),
            pltpu.VMEM((blocks, inner, 256), F32),
        ],
        out_shape=jax.ShapeDtypeStruct(view.shape, BF16),
        compiler_params=params(),
        name="restore",
    )(frame_pick, cotangent, view, gain, conv_weight, returned)
    result = result.reshape(frames, row_count, merged // 128, samples, 128).transpose(3, 0, 1, 2, 4)
    return with_layout_constraint(result, order).reshape(features.shape)


def solution(mesh):
    tiles, parts = mesh.devices.shape
    split = Mesh(mesh.devices.reshape(tiles // 2, 2, parts), ("chip", "core", "sample"))
    in_specs = (
        P("sample", None, TILE, None),
        P(),
        P(),
        P(None, TILE),
        P("sample", TILE),
        P("sample", TILE),
        P("sample", TILE),
        P(),
        P("sample"),
        P("sample", None),
    )
    out_specs = P("sample", None, TILE, None)
    return jax.shard_map(local, mesh=split, in_specs=in_specs, out_specs=out_specs, check_vma=False)
```

```python
import functools

import jax
import jax.numpy as jnp
from jax import lax
from jax.experimental import pallas as pl
from jax.experimental.pallas import tpu as pltpu
from jax.experimental.layout import Layout, with_layout_constraint
from jax.sharding import Mesh, PartitionSpec as P

SCORED = 8
PATCH = 14
HEADS = 8
HD = 80
GROUP = 4
LOSS_SCALE = 16384.0
SMOOTH = 0.01

TILE = ("chip", "core")
CH = 96
COLS = 112
SPANS = CH // 8
OUT_ROWS = 27 * 16
NT = 8
NZ = 4
PACK = 880
CYCLE = [
    (2 * chip + core) * NZ + z
    for chip, heights in ((0, (0, 1, 2, 3)), (1, (3, 2, 1, 0)), (3, (0, 1, 2, 3)), (2, (3, 2, 1, 0)))
    for z in heights
    for core in range(2)
]
PLACES = [[CYCLE.index(i * NZ + z) for z in range(NZ)] for i in range(NT)]
KIN = 896
D = 1280
NTOK = 128
F32 = jnp.float32
BF16 = jnp.bfloat16


def lane_iota(rows):
    return lax.broadcasted_iota(jnp.int32, (rows, 128), 1)


def sub_iota(rows):
    return lax.broadcasted_iota(jnp.int32, (rows, 128), 0)


def channels_of(raw, at, group, sample):
    start = 8 + 14 * group + sample
    here = raw[at, pl.ds(start, 8, stride=2), :]
    before = raw[at, pl.ds(start - 2, 8, stride=2), :]
    joined = jnp.where(lane_iota(8) < 128 - 16 * sub_iota(8), here, before)
    return pltpu.roll(joined, 0, 1, stride=16, stride_axis=0)


def tiles_of(value):
    turned = jnp.take_along_axis(value, (lane_iota(8) + 16 * sub_iota(8)) % 128, axis=1)
    return jnp.where(lane_iota(8) < COLS - 16 * sub_iota(8), turned, pltpu.roll(turned, 7, 0))


def banded(weight_ref, taps, row_block, transposed):
    taps[...] = jnp.zeros(taps.shape, F32)
    for a in range(3):
        for b in range(3):
            for e in range(3):
                for o in range(3):
                    at = (a * 3 + e) * 3 + o
                    taps[b, at : at + 1, :] = weight_ref[a, b, e, o : o + 1, :].astype(F32)
    inner = row_block * CH
    pick = (
        lax.broadcasted_iota(jnp.int32, (OUT_ROWS, 32), 0) // 16
        == lax.broadcasted_iota(jnp.int32, (OUT_ROWS, 32), 1)
    ).astype(BF16)
    if transposed:
        shape, p_dim, r_dim = (inner, OUT_ROWS), 1, 0
        grow_shape, grow_dim = (inner, CH), 0
    else:
        shape, p_dim, r_dim = (OUT_ROWS, inner), 0, 1
        grow_shape, grow_dim = (CH, inner), 1
    at = lax.broadcasted_iota(jnp.int32, grow_shape, grow_dim)
    at = at - CH * ((at.astype(F32) + 0.5) * (1.0 / CH)).astype(jnp.int32)
    grow = (at == lax.broadcasted_iota(jnp.int32, grow_shape, 1 - grow_dim)).astype(BF16)
    p_at = lax.broadcasted_iota(jnp.int32, shape, p_dim) % 16
    r_at = lax.broadcasted_iota(jnp.int32, shape, r_dim)
    r_at = ((r_at.astype(F32) + 0.5) * (1.0 / CH)).astype(jnp.int32)
    total = jnp.zeros(shape, F32)
    for b in range(3):
        rows = jnp.dot(pick, taps[b].astype(BF16), preferred_element_type=F32).astype(BF16)
        if transposed:
            full = lax.dot_general(
                grow, rows, (((1,), (1,)), ((), ())), preferred_element_type=F32
            )
        else:
            full = jnp.dot(rows, grow, preferred_element_type=F32)
        total = jnp.where(p_at == r_at + 2 - b, full, total)
    return total.astype(BF16)


def half_gains(gain_ref):
    rows = jnp.concatenate([gain_ref[0:1, :], jnp.zeros((1, 128 - CH), F32)], axis=1)
    return 0.5 * jnp.broadcast_to(rows, (128, 128)).T


def entry_of(pick_ref, sample, frame):
    found = jnp.int32(-1)
    for j in range(SCORED):
        found = jnp.where(pick_ref[sample, j] == frame, jnp.int32(j), found)
    return found


def decode_kernel(row_block, pick_ref, x_ref, gain_ref, weight_ref, out_ref, x_out, inv_out, band, taps, gains, raw, operand, acc, final):
    t = pl.program_id(0)
    blocks = x_ref.shape[1] // row_block
    rows = out_ref.shape[3]

    @pl.when(t == 0)
    def _():
        band[...] = banded(weight_ref, taps, row_block, False)
        gains[...] = half_gains(gain_ref)
        acc[...] = jnp.zeros(acc.shape, F32)
        raw[...] = jnp.zeros(raw.shape, F32)

    for k in range(blocks):

        def one_row(row, at):
            raw[at, 8:176, :] = x_ref[0, k * row_block + row].astype(F32)
            for s in range(2):
                found = [channels_of(raw, at, g, s) for g in range(SPANS)]
                square = found[0] * found[0]
                for g in range(1, SPANS):
                    square = square + found[g] * found[g]
                second = jnp.sum(square, axis=0, keepdims=True) * (1.0 / CH)
                inv = lax.rsqrt(second + 1e-06)
                inv_out[0, k * row_block + row, s : s + 1, :] = inv
                for m in range(SPANS // 2):
                    x_out[0, k * row_block + row, s, 16 * m : 16 * m + 16, :] = jnp.concatenate(
                        [found[2 * m], found[2 * m + 1]], axis=0
                    ).astype(BF16)
                    acts = []
                    for g in (2 * m, 2 * m + 1):
                        half = found[g] * inv * gains[8 * g : 8 * g + 8, :]
                        acts.append(half + half * jnp.tanh(half))
                    start = row * CH + 16 * m
                    operand[k, start : start + 16, 128 * s : 128 * s + 128] = jnp.concatenate(
                        acts, axis=0
                    ).astype(BF16)

        for row in range(row_block):
            one_row(row, row)
        spread = jnp.dot(band[...], operand[k], preferred_element_type=F32)
        lane = lane_iota(48)
        for s in range(2):
            part = spread[:, 128 * s : 128 * s + 128]
            for a in range(3):
                low, mid, high = (part[144 * a + 48 * e : 144 * a + 48 * e + 48] for e in range(3))
                low = jnp.where(lane == 0, 0.0, pltpu.roll(low, 1, 1))
                high = jnp.where(lane == COLS - 1, 0.0, pltpu.roll(high, 127, 1))
                acc[k, 2 - a, s] += low + mid + high

    keep = lane_iota(rows) < COLS
    for s in range(2):
        entry = entry_of(pick_ref, s, t)

        @pl.when(entry >= 0)
        def _():
            for o in range(3):
                final[...] = jnp.zeros(final.shape, F32)
                for k in range(blocks):
                    start = k * row_block
                    final[start : start + 16, :] += acc[k, 0, s, 16 * o : 16 * o + 16, :]
                out_ref[jnp.maximum(entry, 0), s, o] = jnp.where(keep, final[0:rows, :], 0.0).astype(BF16)

    for k in range(blocks):
        acc[k, 0] = acc[k, 1]
        acc[k, 1] = acc[k, 2]
        acc[k, 2] = jnp.zeros(acc.shape[2:], F32)


def restore_kernel(row_block, pick_ref, scale_ref, x_ref, inv_ref, gain_ref, weight_ref, grad_ref, out_ref, band, taps, gains, back, shifted, coming):
    t = pl.program_id(0)
    frames = pl.num_programs(0)
    blocks = x_ref.shape[1] // row_block
    rows = grad_ref.shape[3]

    @pl.when(t == 0)
    def _():
        band[...] = banded(weight_ref, taps, row_block, True)
        gains[...] = half_gains(gain_ref)
        shifted[...] = jnp.zeros(shifted.shape, BF16)
        lane = lane_iota(rows)

        def one_frame(frame, carry):
            for s in range(2):
                entry = entry_of(pick_ref, s, frame)
                scale = jnp.where(entry >= 0, scale_ref[s], 0.0)
                source = jnp.maximum(entry, 0)
                for o in range(3):
                    value = grad_ref[source, s, o].astype(F32) * scale
                    value = jnp.where(lane < COLS, value, 0.0)
                    for e, moved in enumerate((pltpu.roll(value, 127, 1), value, pltpu.roll(value, 1, 1))):
                        for k in range(blocks):
                            start = k * row_block
                            shifted[frame, k, 48 * e + 16 * o : 48 * e + 16 * o + 16, 128 * s : 128 * s + 128] = moved[
                                start : start + 16
                            ].astype(BF16)
            return carry

        lax.fori_loop(0, frames, one_frame, 0)

    for k in range(blocks):
        operand = jnp.concatenate([shifted[t + 2 - a, k] for a in range(3)], axis=0)
        coming[k] = jnp.dot(band[...], operand, preferred_element_type=F32)

        def one_row(row, at):
            for s in range(2):
                inv = inv_ref[0, k * row_block + row, s : s + 1, :]
                outs, units, total = [], [], None
                for m in range(SPANS // 2):
                    pair = x_ref[0, k * row_block + row, s, 16 * m : 16 * m + 16, :].astype(F32)
                    for local in range(2):
                        g = 2 * m + local
                        unit = pair[8 * local : 8 * local + 8] * inv
                        gain = gains[8 * g : 8 * g + 8, :]
                        half = unit * gain
                        th = jnp.tanh(half)
                        start = row * CH + 8 * g
                        cot = coming[k, start : start + 8, 128 * s : 128 * s + 128]
                        out = cot * gain * (1.0 + th) * (1.0 + half * (1.0 - th))
                        outs.append(out)
                        units.append(unit)
                        total = out * unit if g == 0 else total + out * unit
                factor = jnp.sum(total, axis=0, keepdims=True) * (1.0 / CH)
                for g in range(SPANS):
                    result = tiles_of((outs[g] - units[g] * factor) * inv)
                    back[at, pl.ds(14 * g + s, 7, stride=2), :] = result[0:7]
            out_ref[0, k * row_block + row] = back[at].astype(BF16)

        for row in range(row_block):
            one_row(row, row)


def nt_dot(one, two):
    return lax.dot_general(one, two, (((1,), (1,)), ((), ())), preferred_element_type=F32)


def tn_dot(one, two):
    return lax.dot_general(one, two, (((0,), (0,)), ((), ())), preferred_element_type=F32)


def nn_dot(one, two):
    return jnp.dot(one, two, preferred_element_type=F32)


def split_two(value):
    high = value.astype(BF16)
    low = (value - high.astype(F32)).astype(BF16)
    return jnp.concatenate([high, low], axis=0)


def reward_kernel(
    row_count, tiles, samples,
    part_ref, embed_ref, packed_ref, head_ref,
    out_ref, score_ref,
    pack, arrived, frame, flip, embed, outw, place, patches, tokens, normed, normed16, slots, weights, dslots, dnormed, rows8, abar, order,
):
    height = row_count * tiles
    patch_rows = height // PATCH
    lane64 = lane_iota(8) < 64
    lane = lane_iota(NTOK)
    count = samples * NTOK

    copy = pltpu.make_async_copy(packed_ref, pack, arrived)
    copy.start()

    inputs = 3 * PATCH * PATCH
    for i in range(NT):
        embed[128 * i : 128 * i + 128, :] = embed_ref[i, 0:128, :]
        embed[1024 + 32 * i : 1056 + 32 * i, :] = embed_ref[i, 128:160, :]
    pixel = lax.broadcasted_iota(jnp.int32, (64, inputs), 0)
    column = lax.broadcasted_iota(jnp.int32, (64, inputs), 1)
    for x in range(PATCH):
        order[64 * x : 64 * x + 64, :] = (
            (column == pixel * PATCH + x) & (pixel < 3 * PATCH)
        ).astype(BF16)

    flip[...] = jnp.zeros(flip.shape, F32)
    frame[...] = jnp.zeros(frame.shape, F32)
    for f in range(samples):
        for i in range(tiles):
            at = row_count * i + 7
            for o in range(3):
                frame[f, o, at : at + row_count + 2, :] += part_ref[i, f, o, 0 : row_count + 2, :].astype(F32)
    for f in range(samples):
        for pair in range(patch_rows // 2):
            turn = flip.at[f * (patch_rows // 2) + pair]
            for local in range(2):
                at = 8 + PATCH * (2 * pair + local)
                for o in range(3):
                    turn[0, 64 * local + PATCH * o : 64 * local + PATCH * o + PATCH, :] = (
                        frame[f, o, at : at + PATCH, :].astype(BF16).astype(F32)
                    )
            turn[1] = turn[0].T
            token = f * NTOK + pair * 16
            for y in range(PATCH // 2):
                even = turn[1, pl.ds(2 * y, 8, stride=PATCH), :]
                odd = turn[1, pl.ds(2 * y + 1, 8, stride=PATCH), :]
                patches[token : token + 8, 128 * y : 128 * y + 128] = jnp.where(lane64, even, pltpu.roll(odd, 64, 1))
                patches[token + 8 : token + 16, 128 * y : 128 * y + 128] = jnp.where(lane64, pltpu.roll(even, 64, 1), odd)

    copy.wait()

    lane48 = lane_iota(48)
    for z in range(NZ):
        for i in range(NT):
            source = pack.at[PLACES[i][z]]
            outw[160 * z : 160 * z + 160, 128 * i : 128 * i + 128] = source[640:800, :]
            place[32 * z : 32 * z + 32, 128 * i : 128 * i + 128] = source[800:832, :]
        for ib in range(2):
            sources = [pack[PLACES[4 * ib + j][z], 832:880, :].astype(F32) for j in range(4)]
            rolled = [[sources[j] if d == 0 else pltpu.roll(sources[j], 32 * d, 1) for d in range(4)] for j in range(4)]
            at = 1024 + 128 * ib
            for q in range(4):
                found = rolled[0][(0 - q) % 4]
                for j in range(1, 4):
                    found = jnp.where(lane48 >= 32 * j, rolled[j][(j - q) % 4], found)
                found = found.astype(BF16)
                if q < 3:
                    outw[160 * z + 48 * q : 160 * z + 48 * q + 48, at : at + 128] = found
                else:
                    outw[160 * z + 144 : 160 * z + 160, at : at + 128] = found[:16]
                    place[32 * z : 32 * z + 32, at : at + 128] = found[16:48]

    patches16 = nn_dot(patches[...].astype(BF16), order[...]).astype(BF16)
    token_value = nt_dot(patches16, embed[...])
    rows8[...] = jnp.zeros(rows8.shape, F32)
    abar[...] = jnp.zeros(abar.shape, F32)
    place_value = place[...].astype(F32)
    for f in range(samples):
        value = token_value[f * NTOK : f * NTOK + NTOK] + place_value
        rows8[0, f : f + 1, :] = jnp.mean(value, axis=0, keepdims=True)
        centered = value - jnp.mean(value, axis=-1, keepdims=True)
        scale = lax.rsqrt(jnp.mean(centered * centered, axis=-1, keepdims=True) + 1e-05)
        value = centered * scale
        normed[f * NTOK : f * NTOK + NTOK, :] = value
        normed16[f * NTOK : f * NTOK + NTOK, :] = value.astype(BF16)
        tokens[f * NTOK : f * NTOK + NTOK, :] = jnp.broadcast_to(scale, (NTOK, 128))

    def weight_part(i, z):
        source = pack.at[PLACES[i][z]]
        return jnp.concatenate([source[0:256, :], source[320:576, :]], axis=1)

    def weight_rest(i):
        return jnp.concatenate(
            [
                jnp.concatenate([pack[PLACES[i][z], 256:320, :], pack[PLACES[i][z], 576:640, :]], axis=1)
                for z in range(NZ)
            ],
            axis=0,
        )

    lane_all = lane_iota(count)
    for i in range(NT):
        mixed = nn_dot(
            normed16[...], jnp.concatenate([weight_part(i, z) for z in range(NZ)] + [weight_rest(i)], axis=0)
        )
        first, second = mixed[:, 0:128], mixed[:, 128:256]
        found = (
            first,
            jnp.where(lane_all < 48, pltpu.roll(first, 48, 1), pltpu.roll(second, 48, 1)),
            pltpu.roll(second, 96, 1),
        )
        for m in range(3):
            slots[3 * i + m] = jnp.where(lane_all < HD, found[m], 0.0).astype(BF16)

    for h in range(HEADS):
        for f in range(samples):
            span = slice(f * NTOK, f * NTOK + NTOK)
            logits = nt_dot(slots[h, span, :], slots[HEADS + h, span, :]) * HD ** (-0.5)
            logits = jnp.exp(logits - jnp.max(logits, axis=-1, keepdims=True))
            prob = logits / jnp.sum(logits, axis=-1, keepdims=True)
            weights[h * samples + f] = prob
            attended = nn_dot(prob.astype(BF16), slots[2 * HEADS + h, span, :]).astype(BF16)
            abar[h, f : f + 1, :] = jnp.mean(attended.astype(F32), axis=0, keepdims=True)

    pooled = rows8[0]
    for h in range(HEADS):
        part = nn_dot(split_two(abar[h])[:, 0:HD], outw[HD * h : HD * h + HD, :])
        pooled = pooled + part[0:8] + part[8:16]
    pooled = pooled - jnp.mean(pooled, axis=-1, keepdims=True)
    scale = lax.rsqrt(jnp.mean(pooled * pooled, axis=-1, keepdims=True) + 1e-05)
    pooled = pooled * scale
    head = head_ref[...]
    score_ref[...] = jnp.broadcast_to(jnp.sum(pooled * head, axis=-1, keepdims=True), (8, 128))
    dpooled = scale * (
        head - jnp.mean(head, axis=-1, keepdims=True) - pooled * jnp.mean(pooled * head, axis=-1, keepdims=True)
    )
    dres = dpooled * (1.0 / NTOK)
    rows8[1] = dres
    dres_two = split_two(dres)

    for h in range(HEADS):
        datt = nt_dot(dres_two, outw[HD * h : HD * h + HD, :])
        datt = (datt[0:8] + datt[8:16]).astype(BF16)
        datt = jnp.concatenate([datt, jnp.zeros((8, 128 - HD), BF16)], axis=1)
        for f in range(samples):
            span = slice(f * NTOK, f * NTOK + NTOK)
            prob = weights[h * samples + f]
            row = datt[f : f + 1, :]
            dweight = nt_dot(datt, slots[2 * HEADS + h, span, :])[f : f + 1, :].astype(BF16).astype(F32)
            inner = jnp.sum(prob * dweight, axis=-1, keepdims=True)
            dlogit = (prob * (dweight - inner) * HD ** (-0.5)).astype(BF16)
            dslots[h, span, :] = nn_dot(dlogit, slots[HEADS + h, span, :])
            dslots[HEADS + h, span, :] = tn_dot(dlogit, slots[h, span, :])
            dslots[2 * HEADS + h, span, :] = tn_dot(
                prob.astype(BF16), jnp.broadcast_to(row.astype(F32), (NTOK, 128)).astype(BF16)
            )

    parts = []
    for i in range(NT):
        one, two, three = dslots[3 * i], dslots[3 * i + 1], dslots[3 * i + 2]
        two = pltpu.roll(two, 80, 1)
        three = pltpu.roll(three, 32, 1)
        first = jnp.where(lane_all < HD, one, two)
        second = jnp.where(lane_all < 32, two, jnp.where(lane_all < COLS, three, 0.0))
        parts += [first.astype(BF16), second.astype(BF16)]
    dmixed = jnp.concatenate(parts, axis=1)
    for z in range(NZ):
        wide = jnp.concatenate([weight_part(i, z) for i in range(NT)], axis=1)
        dnormed[:, 256 * z : 256 * z + 256] = nt_dot(dmixed, wide)
    wide = jnp.concatenate([weight_rest(i) for i in range(NT)], axis=1)
    dnormed[:, 1024:1280] = nt_dot(dmixed, wide)

    for f in range(samples):
        span = slice(f * NTOK, f * NTOK + NTOK)
        value, dvalue = normed[span, :], dnormed[span, :]
        scale = tokens[span, 0:1]
        dvalue = scale * (
            dvalue
            - jnp.mean(dvalue, axis=-1, keepdims=True)
            - value * jnp.mean(dvalue * value, axis=-1, keepdims=True)
        )
        normed16[span, :] = (dvalue + rows8[1, f : f + 1, :]).astype(BF16)
    patches[...] = nt_dot(nn_dot(normed16[...], embed[...]).astype(BF16), order[...])

    frame[...] = jnp.zeros(frame.shape, F32)
    rows = out_ref.shape[3]
    for f in range(samples):
        for pair in range(patch_rows // 2):
            turn = flip.at[f * (patch_rows // 2) + pair]
            token = f * NTOK + pair * 16
            for y in range(PATCH // 2):
                one = patches[token : token + 8, 128 * y : 128 * y + 128]
                two = patches[token + 8 : token + 16, 128 * y : 128 * y + 128]
                turn[1, pl.ds(2 * y, 8, stride=PATCH), :] = jnp.where(lane64, one, pltpu.roll(two, 64, 1))
                turn[1, pl.ds(2 * y + 1, 8, stride=PATCH), :] = jnp.where(lane64, pltpu.roll(one, 64, 1), two)
            turn[0] = turn[1].T
            for local in range(2):
                at = 8 + PATCH * (2 * pair + local)
                for o in range(3):
                    frame[f, o, at : at + PATCH, :] = turn[0, 64 * local + PATCH * o : 64 * local + PATCH * o + PATCH, :]
    for f in range(samples):
        for i in range(tiles):
            at = row_count * i + 7
            for o in range(3):
                out_ref[i, f, o] = frame[f, o, at : at + rows, :].astype(BF16)


def pack_part(rows_in, out_part, place_part):
    ordered = jnp.concatenate([rows_in[0:128], rows_in[160:288], rows_in[128:160], rows_in[288:320]], axis=0)
    upper = jnp.pad(ordered[:, 128:240], ((0, 0), (0, 16)))
    other = jnp.concatenate([out_part, place_part], axis=0)
    rest = other[:, 128:160].reshape(4, 48, 32)
    rest = jnp.concatenate([rest[q] for q in range(4)], axis=1)
    return jnp.concatenate([ordered[:, 0:128], upper, other[:, 0:128], rest], axis=0)


def pack_kernel(rows_ref, out_ref, place_ref, packed_ref):
    for source, target, count in ((0, 0, 128), (160, 128, 128), (128, 256, 32), (288, 288, 32)):
        packed_ref[target : target + count, :] = rows_ref[source : source + count, 0:128]
        packed_ref[320 + target : 320 + target + count, :] = jnp.concatenate(
            [rows_ref[source : source + count, 128:240], jnp.zeros((count, 16), BF16)], axis=1
        )
    packed_ref[640:800, :] = out_ref[:, 0:128]
    packed_ref[800:832, :] = place_ref[:, 0:128]
    tail = out_ref[:, 128:160].astype(F32)
    last = place_ref[:, 128:160].astype(F32)
    packed_ref[832:880, :] = jnp.concatenate(
        [tail[0:48], tail[48:96], tail[96:144], jnp.concatenate([tail[144:160], last], axis=0)],
        axis=1,
    ).astype(BF16)


def packed_weights(position, attend_in, attend_out):
    if lax.axis_size(TILE) == NT and lax.axis_size("sample") == NZ:
        mine = pl.pallas_call(
            pack_kernel,
            out_shape=jax.ShapeDtypeStruct((PACK, 128), BF16),
            compiler_params=params(),
            name="pack",
        )(attend_in, attend_out, position)
        return lax.all_gather(mine, TILE + ("sample",), axis=0, axis_index_groups=[CYCLE])

    def whole(value):
        value = lax.all_gather(value, "sample", axis=0, tiled=True)
        return lax.all_gather(value, TILE, axis=1, tiled=True)

    split = [
        value.reshape(NZ, value.shape[0] // NZ, NT, value.shape[1] // NT).transpose(2, 0, 1, 3)
        for value in (whole(attend_in), whole(attend_out), whole(position))
    ]
    split = [value.reshape((NT * NZ,) + value.shape[2:])[jnp.array(CYCLE)] for value in split]
    return jax.vmap(pack_part)(*split)


def embed_parts(patch_embed):
    tiles = lax.axis_size(TILE)
    copies = jnp.broadcast_to(patch_embed.T[None], (tiles,) + patch_embed.shape[::-1])
    found = lax.all_to_all(copies, TILE, split_axis=0, concat_axis=0, tiled=True)
    return found.reshape(NT, D // NT, patch_embed.shape[0])


def params(mib=58):
    return pltpu.CompilerParams(vmem_limit_bytes=mib * 1024 * 1024)


def local(
    features,
    norm_gain,
    conv_weight,
    patch_embed,
    position,
    attend_in,
    attend_out,
    reward_head,
    group_index,
    frame_pick,
):
    samples, frames, row_count, merged = features.shape
    tiles, parts = lax.axis_size(TILE), lax.axis_size("sample")
    sent_rows = -(-(row_count + 2) // 16) * 16
    row_block = row_count if row_count <= 14 else 14
    blocks = row_count // row_block
    inner = row_block * CH
    packed = packed_weights(position, attend_in, attend_out)
    embed = embed_parts(patch_embed)
    order = Layout((1, 2, 3, 0, 4))
    split = (samples, frames, row_count, merged // 128, 128)
    view = with_layout_constraint(features.reshape(split), order).transpose(1, 2, 3, 0, 4)
    view = view.reshape(frames, row_count, samples * merged // 128, 128)
    gain = norm_gain[None, :]

    smem = pl.BlockSpec(memory_space=pltpu.SMEM)
    view_spec = pl.BlockSpec((1,) + view.shape[1:], lambda t: (t, 0, 0, 0))
    gain_spec = pl.BlockSpec((1, CH), lambda t: (0, 0))
    taps_spec = pl.BlockSpec((3, 3, 3, 3, CH), lambda t: (0, 0, 0, 0, 0))
    sent = (SCORED, samples, 3, sent_rows, 128)
    sent_spec = pl.BlockSpec(sent, lambda t: (0, 0, 0, 0, 0))
    aligned = (frames, row_count, samples, CH, 128)
    aligned_spec = pl.BlockSpec((1,) + aligned[1:], lambda t: (t, 0, 0, 0, 0))
    inv_spec = pl.BlockSpec((1, row_count, samples, 128), lambda t: (t, 0, 0, 0))
    decoded, x_aligned, inverse = pl.pallas_call(
        functools.partial(decode_kernel, row_block),
        grid=(frames,),
        in_specs=[smem, view_spec, gain_spec, taps_spec],
        out_specs=[sent_spec, aligned_spec, inv_spec],
        scratch_shapes=[
            pltpu.VMEM((OUT_ROWS, inner), BF16),
            pltpu.VMEM((3, 32, CH), F32),
            pltpu.VMEM((128, 128), F32),
            pltpu.VMEM((row_block, 192, 128), F32),
            pltpu.VMEM((blocks, inner, 256), BF16),
            pltpu.VMEM((blocks, 3, samples, 48, 128), F32),
            pltpu.VMEM((sent_rows + 16, 128), F32),
        ],
        out_shape=[
            jax.ShapeDtypeStruct(sent, BF16),
            jax.ShapeDtypeStruct(aligned, BF16),
            jax.ShapeDtypeStruct((frames, row_count, samples, 128), F32),
        ],
        compiler_params=params(),
        name="decode",
    )(frame_pick, view, gain, conv_weight)

    if tiles > SCORED:
        decoded = jnp.pad(decoded, ((0, tiles - SCORED),) + ((0, 0),) * 4)
    owned = lax.all_to_all(decoded, TILE, split_axis=0, concat_axis=0, tiled=True)

    head = reward_head.reshape(NT, D // NT)
    head = jnp.concatenate([head[:, :128].reshape(-1), head[:, 128:].reshape(-1)])[None, :]
    height = row_count * tiles
    count = samples * NTOK
    grads, scores = pl.pallas_call(
        functools.partial(reward_kernel, row_count, tiles, samples),
        out_shape=[
            jax.ShapeDtypeStruct((tiles, samples, 3, sent_rows, 128), BF16),
            jax.ShapeDtypeStruct((8, 128), F32),
        ],
        in_specs=[
            pl.BlockSpec(memory_space=pltpu.VMEM),
            pl.BlockSpec(memory_space=pltpu.VMEM),
            pl.BlockSpec(memory_space=pl.ANY),
            pl.BlockSpec(memory_space=pltpu.VMEM),
        ],
        scratch_shapes=[
            pltpu.VMEM(packed.shape, BF16),
            pltpu.SemaphoreType.DMA,
            pltpu.VMEM((samples, 3, height + 48, 128), F32),
            pltpu.VMEM((samples * height // (2 * PATCH), 2, 128, 128), F32),
            pltpu.VMEM((D, embed.shape[2]), BF16),
            pltpu.VMEM((HEADS * HD, D), BF16),
            pltpu.VMEM((NTOK, D), BF16),
            pltpu.VMEM((count, KIN), F32),
            pltpu.VMEM((count, 128), F32),
            pltpu.VMEM((count, D), F32),
            pltpu.VMEM((count, D), BF16),
            pltpu.VMEM((3 * HEADS, count, 128), BF16),
            pltpu.VMEM((HEADS * samples, NTOK, NTOK), F32),
            pltpu.VMEM((3 * HEADS, count, 128), F32),
            pltpu.VMEM((count, D), F32),
            pltpu.VMEM((2, 8, D), F32),
            pltpu.VMEM((HEADS, 8, 128), F32),
            pltpu.VMEM((KIN, embed.shape[2]), BF16),
        ],
        compiler_params=params(),
        name="reward",
    )(owned, embed, packed, head)

    mine = jnp.concatenate([scores[:samples, 0], group_index.astype(F32)])
    gathered = [mine]
    for shift in range(1, parts):
        ring = [(z, (z + shift) % parts) for z in range(parts)]
        gathered.append(lax.ppermute(mine, "sample", ring))
    gathered = jnp.stack(gathered)
    groups = gathered[:, samples:].reshape(-1)
    score_row = gathered[:, :samples].reshape(-1)
    high = score_row.astype(BF16)
    low = score_row - high.astype(F32)
    mid = low.astype(BF16)
    low = (low - mid.astype(F32)).astype(BF16)
    total = parts * samples
    carried = jnp.concatenate([high, mid, low])
    grads = grads.at[:, 0, 0, sent_rows - 1, 0 : 3 * total].set(
        jnp.broadcast_to(carried, (tiles, 3 * total))
    )
    returned = lax.all_to_all(grads, TILE, split_axis=0, concat_axis=0, tiled=True)
    returned = returned[:SCORED]

    got = returned[:, 0, 0, sent_rows - 1, 0 : 3 * total].astype(F32).reshape(SCORED, 3, total)
    entry_scores = got[:, 0] + (got[:, 1] + got[:, 2])
    rewards = jnp.sum(entry_scores, axis=0) / SCORED
    member = (groups[:samples, None] == groups[None, :]).astype(F32)
    mean_group = jnp.sum(member * rewards[None, :], axis=1) / GROUP
    second_group = jnp.sum(member * (rewards * rewards)[None, :], axis=1) / GROUP - mean_group * mean_group
    advantage = (rewards[:samples] - mean_group) * lax.rsqrt(second_group + SMOOTH)
    cotangent = -LOSS_SCALE * advantage / SCORED

    result = pl.pallas_call(
        functools.partial(restore_kernel, row_block),
        grid=(frames,),
        in_specs=[smem, smem, aligned_spec, inv_spec, gain_spec, taps_spec, sent_spec],
        out_specs=view_spec,
        scratch_shapes=[
            pltpu.VMEM((inner, OUT_ROWS), BF16),
            pltpu.VMEM((3, 32, CH), F32),
            pltpu.VMEM((128, 128), F32),
            pltpu.VMEM((row_block, samples * merged // 128, 128), F32),
            pltpu.VMEM((frames + 2, blocks, 144, 256), BF16),
            pltpu.VMEM((blocks, inner, 256), F32),
        ],
        out_shape=jax.ShapeDtypeStruct(view.shape, BF16),
        compiler_params=params(),
        name="restore",
    )(frame_pick, cotangent, x_aligned, inverse, gain, conv_weight, returned)
    result = result.reshape(frames, row_count, merged // 128, samples, 128).transpose(3, 0, 1, 2, 4)
    return with_layout_constraint(result, order).reshape(features.shape)


def solution(mesh):
    tiles, parts = mesh.devices.shape
    split = Mesh(mesh.devices.reshape(tiles // 2, 2, parts), ("chip", "core", "sample"))
    in_specs = (
        P("sample", None, TILE, None),
        P(),
        P(),
        P(None, TILE),
        P("sample", TILE),
        P("sample", TILE),
        P("sample", TILE),
        P(),
        P("sample"),
        P("sample", None),
    )
    out_specs = P("sample", None, TILE, None)
    return jax.shard_map(local, mesh=split, in_specs=in_specs, out_specs=out_specs, check_vma=False)
```

```python
import functools

import jax
import jax.numpy as jnp
from jax import lax
from jax.experimental import pallas as pl
from jax.experimental.pallas import tpu as pltpu
from jax.experimental.layout import Layout, with_layout_constraint
from jax.sharding import Mesh, PartitionSpec as P

SCORED = 8
PATCH = 14
HEADS = 8
HD = 80
GROUP = 4
LOSS_SCALE = 16384.0
SMOOTH = 0.01

TILE = ("chip", "core")
CH = 96
COLS = 112
SPANS = CH // 8
OUT_ROWS = 27 * 16
NT = 8
NZ = 4
PACK = 1120
CYCLE = [
    (chip, z)
    for chip, heights in ((0, (0, 1, 2, 3)), (1, (3, 2, 1, 0)), (3, (0, 1, 2, 3)), (2, (3, 2, 1, 0)))
    for z in heights
]
RINGS = (CYCLE, CYCLE[::-1])
PLACES = [[RINGS[i % 2].index((i // 2, z)) for z in range(NZ)] for i in range(NT)]
STARTS = (0, 48, 96, 112)
KIN = 896
D = 1280
NTOK = 128
F32 = jnp.float32
BF16 = jnp.bfloat16


def lane_iota(rows):
    return lax.broadcasted_iota(jnp.int32, (rows, 128), 1)


def sub_iota(rows):
    return lax.broadcasted_iota(jnp.int32, (rows, 128), 0)


def channels_of(raw, at, group, sample):
    start = 8 + 14 * group + sample
    here = raw[at, pl.ds(start, 8, stride=2), :]
    before = raw[at, pl.ds(start - 2, 8, stride=2), :]
    joined = jnp.where(lane_iota(8) < 128 - 16 * sub_iota(8), here, before)
    return pltpu.roll(joined, 0, 1, stride=16, stride_axis=0)


def tiles_of(value):
    turned = jnp.take_along_axis(value, (lane_iota(8) + 16 * sub_iota(8)) % 128, axis=1)
    return jnp.where(lane_iota(8) < COLS - 16 * sub_iota(8), turned, pltpu.roll(turned, 7, 0))


def banded(weight_ref, taps, row_block, transposed):
    taps[...] = jnp.zeros(taps.shape, F32)
    for a in range(3):
        for b in range(3):
            for e in range(3):
                for o in range(3):
                    at = (a * 3 + e) * 3 + o
                    taps[b, at : at + 1, :] = weight_ref[a, b, e, o : o + 1, :].astype(F32)
    inner = row_block * CH
    pick = (
        lax.broadcasted_iota(jnp.int32, (OUT_ROWS, 32), 0) // 16
        == lax.broadcasted_iota(jnp.int32, (OUT_ROWS, 32), 1)
    ).astype(BF16)
    if transposed:
        shape, p_dim, r_dim = (inner, OUT_ROWS), 1, 0
        grow_shape, grow_dim = (inner, CH), 0
    else:
        shape, p_dim, r_dim = (OUT_ROWS, inner), 0, 1
        grow_shape, grow_dim = (CH, inner), 1
    at = lax.broadcasted_iota(jnp.int32, grow_shape, grow_dim)
    at = at - CH * ((at.astype(F32) + 0.5) * (1.0 / CH)).astype(jnp.int32)
    grow = (at == lax.broadcasted_iota(jnp.int32, grow_shape, 1 - grow_dim)).astype(BF16)
    p_at = lax.broadcasted_iota(jnp.int32, shape, p_dim) % 16
    r_at = lax.broadcasted_iota(jnp.int32, shape, r_dim)
    r_at = ((r_at.astype(F32) + 0.5) * (1.0 / CH)).astype(jnp.int32)
    total = jnp.zeros(shape, F32)
    for b in range(3):
        rows = jnp.dot(pick, taps[b].astype(BF16), preferred_element_type=F32).astype(BF16)
        if transposed:
            full = lax.dot_general(
                grow, rows, (((1,), (1,)), ((), ())), preferred_element_type=F32
            )
        else:
            full = jnp.dot(rows, grow, preferred_element_type=F32)
        total = jnp.where(p_at == r_at + 2 - b, full, total)
    return total.astype(BF16)


def half_gains(gain_ref):
    rows = jnp.concatenate([gain_ref[0:1, :], jnp.zeros((1, 128 - CH), F32)], axis=1)
    return 0.5 * jnp.broadcast_to(rows, (128, 128)).T


def entry_of(pick_ref, sample, frame):
    found = jnp.int32(-1)
    for j in range(SCORED):
        found = jnp.where(pick_ref[sample, j] == frame, jnp.int32(j), found)
    return found


def decode_kernel(row_block, pick_ref, x_ref, gain_ref, weight_ref, out_ref, x_out, inv_out, band, taps, gains, raw, operand, acc, final):
    t = pl.program_id(0)
    blocks = x_ref.shape[1] // row_block
    rows = out_ref.shape[3]

    @pl.when(t == 0)
    def _():
        band[...] = banded(weight_ref, taps, row_block, False)
        gains[...] = half_gains(gain_ref)
        acc[...] = jnp.zeros(acc.shape, F32)
        raw[...] = jnp.zeros(raw.shape, F32)

    for k in range(blocks):

        def one_row(row, at):
            raw[at, 8:176, :] = x_ref[0, k * row_block + row].astype(F32)
            for s in range(2):
                found = [channels_of(raw, at, g, s) for g in range(SPANS)]
                square = found[0] * found[0]
                for g in range(1, SPANS):
                    square = square + found[g] * found[g]
                second = jnp.sum(square, axis=0, keepdims=True) * (1.0 / CH)
                inv = lax.rsqrt(second + 1e-06)
                inv_out[0, k * row_block + row, s : s + 1, :] = inv
                for m in range(SPANS // 2):
                    x_out[0, k * row_block + row, s, 16 * m : 16 * m + 16, :] = jnp.concatenate(
                        [found[2 * m], found[2 * m + 1]], axis=0
                    ).astype(BF16)
                    acts = []
                    for g in (2 * m, 2 * m + 1):
                        half = found[g] * inv * gains[8 * g : 8 * g + 8, :]
                        acts.append(half + half * jnp.tanh(half))
                    start = row * CH + 16 * m
                    operand[k, start : start + 16, 128 * s : 128 * s + 128] = jnp.concatenate(
                        acts, axis=0
                    ).astype(BF16)

        for row in range(row_block):
            one_row(row, row)
        spread = jnp.dot(band[...], operand[k], preferred_element_type=F32)
        lane = lane_iota(48)
        for s in range(2):
            part = spread[:, 128 * s : 128 * s + 128]
            for a in range(3):
                low, mid, high = (part[144 * a + 48 * e : 144 * a + 48 * e + 48] for e in range(3))
                low = jnp.where(lane == 0, 0.0, pltpu.roll(low, 1, 1))
                high = jnp.where(lane == COLS - 1, 0.0, pltpu.roll(high, 127, 1))
                acc[k, 2 - a, s] += low + mid + high

    keep = lane_iota(rows) < COLS
    for s in range(2):
        entry = entry_of(pick_ref, s, t)

        @pl.when(entry >= 0)
        def _():
            for o in range(3):
                final[...] = jnp.zeros(final.shape, F32)
                for k in range(blocks):
                    start = k * row_block
                    final[start : start + 16, :] += acc[k, 0, s, 16 * o : 16 * o + 16, :]
                out_ref[jnp.maximum(entry, 0), s, o] = jnp.where(keep, final[0:rows, :], 0.0).astype(BF16)

    for k in range(blocks):
        acc[k, 0] = acc[k, 1]
        acc[k, 1] = acc[k, 2]
        acc[k, 2] = jnp.zeros(acc.shape[2:], F32)


def restore_kernel(row_block, pick_ref, scale_ref, x_ref, inv_ref, gain_ref, weight_ref, grad_ref, out_ref, band, taps, gains, back, shifted, coming):
    t = pl.program_id(0)
    frames = pl.num_programs(0)
    blocks = x_ref.shape[1] // row_block
    rows = grad_ref.shape[3]

    @pl.when(t == 0)
    def _():
        band[...] = banded(weight_ref, taps, row_block, True)
        gains[...] = half_gains(gain_ref)
        shifted[...] = jnp.zeros(shifted.shape, BF16)
        lane = lane_iota(rows)

        def one_frame(frame, carry):
            for s in range(2):
                entry = entry_of(pick_ref, s, frame)
                scale = jnp.where(entry >= 0, scale_ref[s], 0.0)
                source = jnp.maximum(entry, 0)
                for o in range(3):
                    value = grad_ref[source, s, o].astype(F32) * scale
                    value = jnp.where(lane < COLS, value, 0.0)
                    for e, moved in enumerate((pltpu.roll(value, 127, 1), value, pltpu.roll(value, 1, 1))):
                        for k in range(blocks):
                            start = k * row_block
                            shifted[frame, k, 48 * e + 16 * o : 48 * e + 16 * o + 16, 128 * s : 128 * s + 128] = moved[
                                start : start + 16
                            ].astype(BF16)
            return carry

        lax.fori_loop(0, frames, one_frame, 0)

    for k in range(blocks):
        operand = jnp.concatenate([shifted[t + 2 - a, k] for a in range(3)], axis=0)
        coming[k] = jnp.dot(band[...], operand, preferred_element_type=F32)

        def one_row(row, at):
            for s in range(2):
                inv = inv_ref[0, k * row_block + row, s : s + 1, :]
                outs, units, total = [], [], None
                for m in range(SPANS // 2):
                    pair = x_ref[0, k * row_block + row, s, 16 * m : 16 * m + 16, :].astype(F32)
                    for local in range(2):
                        g = 2 * m + local
                        unit = pair[8 * local : 8 * local + 8] * inv
                        gain = gains[8 * g : 8 * g + 8, :]
                        half = unit * gain
                        th = jnp.tanh(half)
                        start = row * CH + 8 * g
                        cot = coming[k, start : start + 8, 128 * s : 128 * s + 128]
                        out = cot * gain * (1.0 + th) * (1.0 + half * (1.0 - th))
                        outs.append(out)
                        units.append(unit)
                        total = out * unit if g == 0 else total + out * unit
                factor = jnp.sum(total, axis=0, keepdims=True) * (1.0 / CH)
                for g in range(SPANS):
                    result = tiles_of((outs[g] - units[g] * factor) * inv)
                    back[at, pl.ds(14 * g + s, 7, stride=2), :] = result[0:7]
            out_ref[0, k * row_block + row] = back[at].astype(BF16)

        for row in range(row_block):
            one_row(row, row)


def nt_dot(one, two):
    return lax.dot_general(one, two, (((1,), (1,)), ((), ())), preferred_element_type=F32)


def tn_dot(one, two):
    return lax.dot_general(one, two, (((0,), (0,)), ((), ())), preferred_element_type=F32)


def nn_dot(one, two):
    return jnp.dot(one, two, preferred_element_type=F32)


def split_two(value):
    high = value.astype(BF16)
    low = (value - high.astype(F32)).astype(BF16)
    return jnp.concatenate([high, low], axis=0)


def reward_kernel(
    row_count, tiles, samples,
    core_ref, part_ref, mine_ref, other_ref, head_ref,
    out_ref, score_ref,
    pack, arrived, frame, flip, embed, outw, place, patches, tokens, normed, normed16, slots, weights, dslots, dnormed, rows8, abar, order,
):
    height = row_count * tiles
    patch_rows = height // PATCH
    lane64 = lane_iota(8) < 64
    lane = lane_iota(NTOK)
    count = samples * NTOK

    core = core_ref[0]
    copies = []
    for part, (begin, end) in enumerate(((880, 1120), (640, 880), (0, 640))):
        copies.append(
            [
                pltpu.make_async_copy(
                    source.at[:, begin:end, :], pack.at[at, :, begin:end, :], arrived.at[part, which]
                )
                for which, (source, at) in enumerate(((mine_ref, core), (other_ref, 1 - core)))
            ]
        )
        for copy in copies[-1]:
            copy.start()

    inputs = order.shape[1]
    pixel = lax.broadcasted_iota(jnp.int32, (64, inputs), 0)
    column = lax.broadcasted_iota(jnp.int32, (64, inputs), 1)
    for x in range(PATCH):
        order[64 * x : 64 * x + 64, :] = (
            (column == pixel * PATCH + x) & (pixel < 3 * PATCH)
        ).astype(BF16)

    flip[...] = jnp.zeros(flip.shape, F32)
    frame[...] = jnp.zeros(frame.shape, F32)
    for f in range(samples):
        for i in range(tiles):
            at = row_count * i + 7
            for o in range(3):
                frame[f, o, at : at + row_count + 2, :] += part_ref[i, f, o, 0 : row_count + 2, :].astype(F32)
    for f in range(samples):
        for pair in range(patch_rows // 2):
            turn = flip.at[f * (patch_rows // 2) + pair]
            for local in range(2):
                at = 8 + PATCH * (2 * pair + local)
                for o in range(3):
                    turn[0, 64 * local + PATCH * o : 64 * local + PATCH * o + PATCH, :] = (
                        frame[f, o, at : at + PATCH, :].astype(BF16).astype(F32)
                    )
            turn[1] = turn[0].T
            token = f * NTOK + pair * 16
            for y in range(PATCH // 2):
                even = turn[1, pl.ds(2 * y, 8, stride=PATCH), :]
                odd = turn[1, pl.ds(2 * y + 1, 8, stride=PATCH), :]
                patches[token : token + 8, 128 * y : 128 * y + 128] = jnp.where(lane64, even, pltpu.roll(odd, 64, 1))
                patches[token + 8 : token + 16, 128 * y : 128 * y + 128] = jnp.where(lane64, pltpu.roll(even, 64, 1), odd)

    for copy in copies[0] + copies[1]:
        copy.wait()

    for i in range(NT):
        for z, (begin, height, target) in enumerate(
            ((0, 48, 128 * i), (0, 48, 128 * i + 48), (0, 32, 128 * i + 96), (16, 32, 1024 + 32 * i))
        ):
            source = pack.at[i % 2, PLACES[i][z]]
            for part in range(5):
                at = 880 + 48 * part + begin
                embed[target : target + height, 128 * part : 128 * part + 128] = source[at : at + height, :]
    lane48 = lane_iota(48)
    for h in range(HEADS):
        outw[128 * h + HD : 128 * h + 128, :] = jnp.zeros((128 - HD, D), BF16)
    for z in range(NZ):
        for i in range(NT):
            source = pack.at[i % 2, PLACES[i][z]]
            for local in range(2):
                at, begin = 128 * (2 * z + local), 640 + HD * local
                outw[at : at + HD, 128 * i : 128 * i + 128] = source[begin : begin + HD, :]
            place[32 * z : 32 * z + 32, 128 * i : 128 * i + 128] = source[800:832, :]
        for ib in range(2):
            sources = [pack[j % 2, PLACES[4 * ib + j][z], 832:880, :].astype(F32) for j in range(4)]
            rolled = [[sources[j] if d == 0 else pltpu.roll(sources[j], 32 * d, 1) for d in range(4)] for j in range(4)]
            at = 1024 + 128 * ib
            for q in range(4):
                found = rolled[0][(0 - q) % 4]
                for j in range(1, 4):
                    found = jnp.where(lane48 >= 32 * j, rolled[j][(j - q) % 4], found)
                found = found.astype(BF16)
                for begin, end, row in (
                    ((0, 48, 0),),
                    ((0, 32, 48), (32, 48, 128)),
                    ((0, 48, 144),),
                    ((0, 16, 192),),
                )[q]:
                    row = 256 * z + row
                    outw[row : row + end - begin, at : at + 128] = found[begin:end]
                if q == 3:
                    place[32 * z : 32 * z + 32, at : at + 128] = found[16:48]

    patches16 = nn_dot(patches[...].astype(BF16), order[...]).astype(BF16)
    token_value = nt_dot(patches16, embed[...])
    rows8[...] = jnp.zeros(rows8.shape, F32)
    abar[...] = jnp.zeros(abar.shape, F32)
    place_value = place[...].astype(F32)
    for f in range(samples):
        value = token_value[f * NTOK : f * NTOK + NTOK] + place_value
        rows8[0, f : f + 1, :] = jnp.mean(value, axis=0, keepdims=True)
        centered = value - jnp.mean(value, axis=-1, keepdims=True)
        scale = lax.rsqrt(jnp.mean(centered * centered, axis=-1, keepdims=True) + 1e-05)
        value = centered * scale
        normed[f * NTOK : f * NTOK + NTOK, :] = value
        normed16[f * NTOK : f * NTOK + NTOK, :] = value.astype(BF16)
        tokens[f * NTOK : f * NTOK + NTOK, :] = jnp.broadcast_to(scale, (NTOK, 128))

    def weight_part(i, z):
        source = pack.at[i % 2, PLACES[i][z]]
        return jnp.concatenate([source[0:256, :], source[320:576, :]], axis=1)

    def weight_rest(i):
        return jnp.concatenate(
            [
                jnp.concatenate(
                    [pack[i % 2, PLACES[i][z], 256:320, :], pack[i % 2, PLACES[i][z], 576:640, :]], axis=1
                )
                for z in range(NZ)
            ],
            axis=0,
        )

    lane_all = lane_iota(count)
    for copy in copies[2]:
        copy.wait()
    for i in range(NT):
        mixed = nn_dot(
            normed16[...], jnp.concatenate([weight_part(i, z) for z in range(NZ)] + [weight_rest(i)], axis=0)
        )
        first, second = mixed[:, 0:128], mixed[:, 128:256]
        found = (
            first,
            jnp.where(lane_all < 48, pltpu.roll(first, 48, 1), pltpu.roll(second, 48, 1)),
            pltpu.roll(second, 96, 1),
        )
        for m in range(3):
            slots[3 * i + m] = jnp.where(lane_all < HD, found[m], 0.0).astype(BF16)

    for h in range(HEADS):
        for f in range(samples):
            span = slice(f * NTOK, f * NTOK + NTOK)
            logits = nt_dot(slots[h, span, :], slots[HEADS + h, span, :]) * HD ** (-0.5)
            logits = jnp.exp(logits - jnp.max(logits, axis=-1, keepdims=True))
            prob = logits / jnp.sum(logits, axis=-1, keepdims=True)
            weights[h * samples + f] = prob
            attended = nn_dot(prob.astype(BF16), slots[2 * HEADS + h, span, :]).astype(BF16)
            abar[f : f + 1, 128 * h : 128 * h + 128] = jnp.mean(attended.astype(F32), axis=0, keepdims=True)

    part = nn_dot(split_two(abar[...]), outw[...])
    pooled = rows8[0] + part[0:8] + part[8:16]
    pooled = pooled - jnp.mean(pooled, axis=-1, keepdims=True)
    scale = lax.rsqrt(jnp.mean(pooled * pooled, axis=-1, keepdims=True) + 1e-05)
    pooled = pooled * scale
    head = head_ref[...]
    score_ref[...] = jnp.broadcast_to(jnp.sum(pooled * head, axis=-1, keepdims=True), (8, 128))
    dpooled = scale * (
        head - jnp.mean(head, axis=-1, keepdims=True) - pooled * jnp.mean(pooled * head, axis=-1, keepdims=True)
    )
    dres = dpooled * (1.0 / NTOK)
    rows8[1] = dres
    datts = nt_dot(split_two(dres), outw[...])
    datts = (datts[0:8] + datts[8:16]).astype(BF16)

    for h in range(HEADS):
        datt = datts[:, 128 * h : 128 * h + 128]
        for f in range(samples):
            span = slice(f * NTOK, f * NTOK + NTOK)
            prob = weights[h * samples + f]
            row = datt[f : f + 1, :]
            dweight = nt_dot(datt, slots[2 * HEADS + h, span, :])[f : f + 1, :].astype(BF16).astype(F32)
            inner = jnp.sum(prob * dweight, axis=-1, keepdims=True)
            dlogit = (prob * (dweight - inner) * HD ** (-0.5)).astype(BF16)
            dslots[h, span, :] = nn_dot(dlogit, slots[HEADS + h, span, :])
            dslots[HEADS + h, span, :] = tn_dot(dlogit, slots[h, span, :])
            dslots[2 * HEADS + h, span, :] = tn_dot(
                prob.astype(BF16), jnp.broadcast_to(row.astype(F32), (NTOK, 128)).astype(BF16)
            )

    parts = []
    for i in range(NT):
        one, two, three = dslots[3 * i], dslots[3 * i + 1], dslots[3 * i + 2]
        two = pltpu.roll(two, 80, 1)
        three = pltpu.roll(three, 32, 1)
        first = jnp.where(lane_all < HD, one, two)
        second = jnp.where(lane_all < 32, two, jnp.where(lane_all < COLS, three, 0.0))
        parts += [first.astype(BF16), second.astype(BF16)]
    dmixed = jnp.concatenate(parts, axis=1)
    for z in range(NZ):
        wide = jnp.concatenate([weight_part(i, z) for i in range(NT)], axis=1)
        dnormed[:, 256 * z : 256 * z + 256] = nt_dot(dmixed, wide)
    wide = jnp.concatenate([weight_rest(i) for i in range(NT)], axis=1)
    dnormed[:, 1024:1280] = nt_dot(dmixed, wide)

    for f in range(samples):
        span = slice(f * NTOK, f * NTOK + NTOK)
        value, dvalue = normed[span, :], dnormed[span, :]
        scale = tokens[span, 0:1]
        dvalue = scale * (
            dvalue
            - jnp.mean(dvalue, axis=-1, keepdims=True)
            - value * jnp.mean(dvalue * value, axis=-1, keepdims=True)
        )
        normed16[span, :] = (dvalue + rows8[1, f : f + 1, :]).astype(BF16)
    patches[...] = nt_dot(nn_dot(normed16[...], embed[...]).astype(BF16), order[...])

    frame[...] = jnp.zeros(frame.shape, F32)
    rows = out_ref.shape[3]
    for f in range(samples):
        for pair in range(patch_rows // 2):
            turn = flip.at[f * (patch_rows // 2) + pair]
            token = f * NTOK + pair * 16
            for y in range(PATCH // 2):
                one = patches[token : token + 8, 128 * y : 128 * y + 128]
                two = patches[token + 8 : token + 16, 128 * y : 128 * y + 128]
                turn[1, pl.ds(2 * y, 8, stride=PATCH), :] = jnp.where(lane64, one, pltpu.roll(two, 64, 1))
                turn[1, pl.ds(2 * y + 1, 8, stride=PATCH), :] = jnp.where(lane64, pltpu.roll(one, 64, 1), two)
            turn[0] = turn[1].T
            for local in range(2):
                at = 8 + PATCH * (2 * pair + local)
                for o in range(3):
                    frame[f, o, at : at + PATCH, :] = turn[0, 64 * local + PATCH * o : 64 * local + PATCH * o + PATCH, :]
    for f in range(samples):
        for i in range(tiles):
            at = row_count * i + 7
            for o in range(3):
                out_ref[i, f, o] = frame[f, o, at : at + rows, :].astype(BF16)


def pack_part(rows_in, out_part, place_part, embed_part):
    ordered = jnp.concatenate([rows_in[0:128], rows_in[160:288], rows_in[128:160], rows_in[288:320]], axis=0)
    upper = jnp.pad(ordered[:, 128:240], ((0, 0), (0, 16)))
    other = jnp.concatenate([out_part, place_part], axis=0)
    rest = other[:, 128:160].reshape(4, 48, 32)
    rest = jnp.concatenate([rest[q] for q in range(4)], axis=1)
    embed_part = jnp.pad(embed_part, ((0, 0), (0, 640 - embed_part.shape[1])))
    embed_part = embed_part.reshape(48, 5, 128).transpose(1, 0, 2).reshape(240, 128)
    return jnp.concatenate([ordered[:, 0:128], upper, other[:, 0:128], rest, embed_part], axis=0)


def pack_kernel(z_ref, rows_ref, out_ref, place_ref, embed_ref, packed_ref):
    for source, target, count in ((0, 0, 128), (160, 128, 128), (128, 256, 32), (288, 288, 32)):
        packed_ref[target : target + count, :] = rows_ref[source : source + count, 0:128]
        packed_ref[320 + target : 320 + target + count, :] = jnp.concatenate(
            [rows_ref[source : source + count, 128:240], jnp.zeros((count, 16), BF16)], axis=1
        )
    packed_ref[640:800, :] = out_ref[:, 0:128]
    packed_ref[800:832, :] = place_ref[:, 0:128]
    tail = out_ref[:, 128:160].astype(F32)
    last = place_ref[:, 128:160].astype(F32)
    packed_ref[832:880, :] = jnp.concatenate(
        [tail[0:48], tail[48:96], tail[96:144], jnp.concatenate([tail[144:160], last], axis=0)],
        axis=1,
    ).astype(BF16)
    width = embed_ref.shape[1]
    start = pl.multiple_of(jnp.where(z_ref[0] == NZ - 1, STARTS[-1], 48 * z_ref[0]), 16)
    for part in range(5):
        count = min(128, width - 128 * part)
        value = embed_ref[pl.ds(start, 48), 128 * part : 128 * part + count]
        if count < 128:
            value = jnp.concatenate([value, jnp.zeros((48, 128 - count), BF16)], axis=1)
        packed_ref[880 + 48 * part : 928 + 48 * part, :] = value


def packed_weights(patch_embed, position, attend_in, attend_out):
    if lax.axis_size(TILE) == NT and lax.axis_size("sample") == NZ:
        z = lax.axis_index("sample").astype(jnp.int32).reshape(1)
        mine = pl.pallas_call(
            pack_kernel,
            in_specs=[pl.BlockSpec(memory_space=pltpu.SMEM)] + [pl.BlockSpec(memory_space=pltpu.VMEM)] * 4,
            out_shape=jax.ShapeDtypeStruct((PACK, 128), BF16),
            compiler_params=params(),
            name="pack",
        )(z, attend_in, attend_out, position, patch_embed.T)
        groups = [[(2 * chip + core) * NZ + z for chip, z in RINGS[core]] for core in range(2)]
        mine = lax.all_gather(mine, TILE + ("sample",), axis=0, axis_index_groups=groups)
        return mine, None, lax.axis_index("core").astype(jnp.int32).reshape(1)

    def whole(value):
        value = lax.all_gather(value, "sample", axis=0, tiled=True)
        return lax.all_gather(value, TILE, axis=1, tiled=True)

    split = [
        value.reshape(NZ, value.shape[0] // NZ, NT, value.shape[1] // NT).transpose(2, 0, 1, 3)
        for value in (whole(attend_in), whole(attend_out), whole(position))
    ]
    columns = lax.all_gather(patch_embed.T, TILE, axis=0, tiled=True).reshape(NT, D // NT, -1)
    split.append(jnp.stack([columns[:, start : start + 48] for start in STARTS], axis=1))
    packed = jax.vmap(jax.vmap(pack_part))(*split)
    mine, other = (
        jnp.stack([packed[2 * chip + core, z] for chip, z in RINGS[core]]) for core in range(2)
    )
    return mine, other, jnp.zeros(1, jnp.int32)


def params(mib=58):
    return pltpu.CompilerParams(vmem_limit_bytes=mib * 1024 * 1024)


def local(
    features,
    norm_gain,
    conv_weight,
    patch_embed,
    position,
    attend_in,
    attend_out,
    reward_head,
    group_index,
    frame_pick,
):
    samples, frames, row_count, merged = features.shape
    tiles, parts = lax.axis_size(TILE), lax.axis_size("sample")
    sent_rows = -(-(row_count + 2) // 16) * 16
    row_block = row_count if row_count <= 14 else 14
    blocks = row_count // row_block
    inner = row_block * CH
    packed, other, core = packed_weights(patch_embed, position, attend_in, attend_out)
    order = Layout((1, 2, 3, 0, 4))
    split = (samples, frames, row_count, merged // 128, 128)
    view = with_layout_constraint(features.reshape(split), order).transpose(1, 2, 3, 0, 4)
    view = view.reshape(frames, row_count, samples * merged // 128, 128)
    gain = norm_gain[None, :]

    smem = pl.BlockSpec(memory_space=pltpu.SMEM)
    view_spec = pl.BlockSpec((1,) + view.shape[1:], lambda t: (t, 0, 0, 0))
    gain_spec = pl.BlockSpec((1, CH), lambda t: (0, 0))
    taps_spec = pl.BlockSpec((3, 3, 3, 3, CH), lambda t: (0, 0, 0, 0, 0))
    sent = (SCORED, samples, 3, sent_rows, 128)
    sent_spec = pl.BlockSpec(sent, lambda t: (0, 0, 0, 0, 0))
    aligned = (frames, row_count, samples, CH, 128)
    aligned_spec = pl.BlockSpec((1,) + aligned[1:], lambda t: (t, 0, 0, 0, 0))
    inv_spec = pl.BlockSpec((1, row_count, samples, 128), lambda t: (t, 0, 0, 0))
    decoded, x_aligned, inverse = pl.pallas_call(
        functools.partial(decode_kernel, row_block),
        grid=(frames,),
        in_specs=[smem, view_spec, gain_spec, taps_spec],
        out_specs=[sent_spec, aligned_spec, inv_spec],
        scratch_shapes=[
            pltpu.VMEM((OUT_ROWS, inner), BF16),
            pltpu.VMEM((3, 32, CH), F32),
            pltpu.VMEM((128, 128), F32),
            pltpu.VMEM((row_block, 192, 128), F32),
            pltpu.VMEM((blocks, inner, 256), BF16),
            pltpu.VMEM((blocks, 3, samples, 48, 128), F32),
            pltpu.VMEM((sent_rows + 16, 128), F32),
        ],
        out_shape=[
            jax.ShapeDtypeStruct(sent, BF16),
            jax.ShapeDtypeStruct(aligned, BF16),
            jax.ShapeDtypeStruct((frames, row_count, samples, 128), F32),
        ],
        compiler_params=params(),
        name="decode",
    )(frame_pick, view, gain, conv_weight)

    if tiles > SCORED:
        decoded = jnp.pad(decoded, ((0, tiles - SCORED),) + ((0, 0),) * 4)
    owned = lax.all_to_all(decoded, TILE, split_axis=0, concat_axis=0, tiled=True)
    if other is None:
        packed, owned = lax.optimization_barrier((packed, owned))
        other = lax.ppermute(packed, "core", [(0, 1), (1, 0)])

    head = reward_head.reshape(NT, D // NT)
    head = jnp.concatenate([head[:, :128].reshape(-1), head[:, 128:].reshape(-1)])[None, :]
    height = row_count * tiles
    count = samples * NTOK
    grads, scores = pl.pallas_call(
        functools.partial(reward_kernel, row_count, tiles, samples),
        out_shape=[
            jax.ShapeDtypeStruct((tiles, samples, 3, sent_rows, 128), BF16),
            jax.ShapeDtypeStruct((8, 128), F32),
        ],
        in_specs=[
            smem,
            pl.BlockSpec(memory_space=pltpu.VMEM),
            pl.BlockSpec(memory_space=pl.ANY),
            pl.BlockSpec(memory_space=pl.ANY),
            pl.BlockSpec(memory_space=pltpu.VMEM),
        ],
        scratch_shapes=[
            pltpu.VMEM((2,) + packed.shape, BF16),
            pltpu.SemaphoreType.DMA((3, 2)),
            pltpu.VMEM((samples, 3, height + 48, 128), F32),
            pltpu.VMEM((samples * height // (2 * PATCH), 2, 128, 128), F32),
            pltpu.VMEM((D, 640), BF16),
            pltpu.VMEM((HEADS * 128, D), BF16),
            pltpu.VMEM((NTOK, D), BF16),
            pltpu.VMEM((count, KIN), F32),
            pltpu.VMEM((count, 128), F32),
            pltpu.VMEM((count, D), F32),
            pltpu.VMEM((count, D), BF16),
            pltpu.VMEM((3 * HEADS, count, 128), BF16),
            pltpu.VMEM((HEADS * samples, NTOK, NTOK), F32),
            pltpu.VMEM((3 * HEADS, count, 128), F32),
            pltpu.VMEM((count, D), F32),
            pltpu.VMEM((2, 8, D), F32),
            pltpu.VMEM((8, HEADS * 128), F32),
            pltpu.VMEM((KIN, 640), BF16),
        ],
        compiler_params=params(),
        name="reward",
    )(core, owned, packed, other, head)

    mine = jnp.concatenate([scores[:samples, 0], group_index.astype(F32)])
    mine = jnp.broadcast_to(mine[None], (tiles * parts, 2 * samples))
    everyone = lax.all_to_all(mine, TILE + ("sample",), split_axis=0, concat_axis=0, tiled=True)
    everyone = everyone.reshape(tiles, parts, 2, samples)
    returned = lax.all_to_all(grads, TILE, split_axis=0, concat_axis=0, tiled=True)
    returned = returned[:SCORED]

    rewards = jnp.sum(everyone[:SCORED, :, 0], axis=0).reshape(-1) / SCORED
    groups = everyone[0, :, 1].reshape(-1)
    here = (lax.axis_index("sample") * samples).astype(jnp.int32)
    own_rewards = lax.dynamic_slice_in_dim(rewards, here, samples)
    own_groups = lax.dynamic_slice_in_dim(groups, here, samples)
    member = (own_groups[:, None] == groups[None, :]).astype(F32)
    mean_group = jnp.sum(member * rewards[None, :], axis=1) / GROUP
    second_group = jnp.sum(member * (rewards * rewards)[None, :], axis=1) / GROUP - mean_group * mean_group
    advantage = (own_rewards - mean_group) * lax.rsqrt(second_group + SMOOTH)
    cotangent = -LOSS_SCALE * advantage / SCORED

    result = pl.pallas_call(
        functools.partial(restore_kernel, row_block),
        grid=(frames,),
        in_specs=[smem, smem, aligned_spec, inv_spec, gain_spec, taps_spec, sent_spec],
        out_specs=view_spec,
        scratch_shapes=[
            pltpu.VMEM((inner, OUT_ROWS), BF16),
            pltpu.VMEM((3, 32, CH), F32),
            pltpu.VMEM((128, 128), F32),
            pltpu.VMEM((row_block, samples * merged // 128, 128), F32),
            pltpu.VMEM((frames + 2, blocks, 144, 256), BF16),
            pltpu.VMEM((blocks, inner, 256), F32),
        ],
        out_shape=jax.ShapeDtypeStruct(view.shape, BF16),
        compiler_params=params(),
        name="restore",
    )(frame_pick, cotangent, x_aligned, inverse, gain, conv_weight, returned)
    result = result.reshape(frames, row_count, merged // 128, samples, 128).transpose(3, 0, 1, 2, 4)
    return with_layout_constraint(result, order).reshape(features.shape)


def solution(mesh):
    tiles, parts = mesh.devices.shape
    split = Mesh(mesh.devices.reshape(tiles // 2, 2, parts), ("chip", "core", "sample"))
    in_specs = (
        P("sample", None, TILE, None),
        P(),
        P(),
        P(None, TILE),
        P("sample", TILE),
        P("sample", TILE),
        P("sample", TILE),
        P(),
        P("sample"),
        P("sample", None),
    )
    out_specs = P("sample", None, TILE, None)
    return jax.shard_map(local, mesh=split, in_specs=in_specs, out_specs=out_specs, check_vma=False)
```

```python
import functools

import jax
import jax.numpy as jnp
from jax import lax
from jax.experimental import pallas as pl
from jax.experimental.pallas import tpu as pltpu
from jax.experimental.layout import Layout, with_layout_constraint
from jax.sharding import Mesh, PartitionSpec as P

SCORED = 8
PATCH = 14
HEADS = 8
HD = 80
GROUP = 4
LOSS_SCALE = 16384.0
SMOOTH = 0.01

TILE = ("chip", "core")
CH = 96
COLS = 112
SPANS = CH // 8
OUT_ROWS = 27 * 16
NT = 8
NZ = 4
PACK = 1120
CYCLE = [
    (2 * chip + core, z)
    for chip, heights in ((0, (0, 1, 2, 3)), (1, (3, 2, 1, 0)), (3, (0, 1, 2, 3)), (2, (3, 2, 1, 0)))
    for z in heights
    for core in range(2)
]
PLACES = [[CYCLE.index((i, z)) for z in range(NZ)] for i in range(NT)]
STARTS = (0, 48, 96, 112)
KIN = 896
D = 1280
NTOK = 128
F32 = jnp.float32
BF16 = jnp.bfloat16


def lane_iota(rows):
    return lax.broadcasted_iota(jnp.int32, (rows, 128), 1)


def sub_iota(rows):
    return lax.broadcasted_iota(jnp.int32, (rows, 128), 0)


def channels_of(raw, at, group, sample):
    start = 8 + 14 * group + sample
    here = raw[at, pl.ds(start, 8, stride=2), :]
    before = raw[at, pl.ds(start - 2, 8, stride=2), :]
    joined = jnp.where(lane_iota(8) < 128 - 16 * sub_iota(8), here, before)
    return pltpu.roll(joined, 0, 1, stride=16, stride_axis=0)


def tiles_of(value):
    turned = jnp.take_along_axis(value, (lane_iota(8) + 16 * sub_iota(8)) % 128, axis=1)
    return jnp.where(lane_iota(8) < COLS - 16 * sub_iota(8), turned, pltpu.roll(turned, 7, 0))


def banded(weight_ref, taps, row_block, transposed):
    taps[...] = jnp.zeros(taps.shape, F32)
    for a in range(3):
        for b in range(3):
            for e in range(3):
                for o in range(3):
                    at = (a * 3 + e) * 3 + o
                    taps[b, at : at + 1, :] = weight_ref[a, b, e, o : o + 1, :].astype(F32)
    inner = row_block * CH
    pick = (
        lax.broadcasted_iota(jnp.int32, (OUT_ROWS, 32), 0) // 16
        == lax.broadcasted_iota(jnp.int32, (OUT_ROWS, 32), 1)
    ).astype(BF16)
    if transposed:
        shape, p_dim, r_dim = (inner, OUT_ROWS), 1, 0
        grow_shape, grow_dim = (inner, CH), 0
    else:
        shape, p_dim, r_dim = (OUT_ROWS, inner), 0, 1
        grow_shape, grow_dim = (CH, inner), 1
    at = lax.broadcasted_iota(jnp.int32, grow_shape, grow_dim)
    at = at - CH * ((at.astype(F32) + 0.5) * (1.0 / CH)).astype(jnp.int32)
    grow = (at == lax.broadcasted_iota(jnp.int32, grow_shape, 1 - grow_dim)).astype(BF16)
    p_at = lax.broadcasted_iota(jnp.int32, shape, p_dim) % 16
    r_at = lax.broadcasted_iota(jnp.int32, shape, r_dim)
    r_at = ((r_at.astype(F32) + 0.5) * (1.0 / CH)).astype(jnp.int32)
    total = jnp.zeros(shape, F32)
    for b in range(3):
        rows = jnp.dot(pick, taps[b].astype(BF16), preferred_element_type=F32).astype(BF16)
        if transposed:
            full = lax.dot_general(
                grow, rows, (((1,), (1,)), ((), ())), preferred_element_type=F32
            )
        else:
            full = jnp.dot(rows, grow, preferred_element_type=F32)
        total = jnp.where(p_at == r_at + 2 - b, full, total)
    return total.astype(BF16)


def half_gains(gain_ref):
    rows = jnp.concatenate([gain_ref[0:1, :], jnp.zeros((1, 128 - CH), F32)], axis=1)
    return 0.5 * jnp.broadcast_to(rows, (128, 128)).T


def entry_of(pick_ref, sample, frame):
    found = jnp.int32(-1)
    for j in range(SCORED):
        found = jnp.where(pick_ref[sample, j] == frame, jnp.int32(j), found)
    return found


def decode_kernel(row_block, pick_ref, x_ref, gain_ref, weight_ref, out_ref, x_out, inv_out, slope_out, turned_out, band, taps, gains, raw, operand, acc, final):
    t = pl.program_id(0)
    blocks = x_ref.shape[1] // row_block
    rows = out_ref.shape[3]

    @pl.when(t == 0)
    def _():
        band[...] = banded(weight_ref, taps, row_block, False)
        turned_out[...] = banded(weight_ref, taps, row_block, True)
        gains[...] = half_gains(gain_ref)
        acc[...] = jnp.zeros(acc.shape, F32)
        raw[...] = jnp.zeros(raw.shape, F32)

    for k in range(blocks):

        def one_row(row, at):
            raw[at, 8:176, :] = x_ref[0, k * row_block + row].astype(F32)
            for s in range(2):
                found = [channels_of(raw, at, g, s) for g in range(SPANS)]
                square = found[0] * found[0]
                for g in range(1, SPANS):
                    square = square + found[g] * found[g]
                second = jnp.sum(square, axis=0, keepdims=True) * (1.0 / CH)
                inv = lax.rsqrt(second + 1e-06)
                inv_out[0, k * row_block + row, s : s + 1, :] = inv
                for m in range(SPANS // 2):
                    x_out[0, k * row_block + row, s, 16 * m : 16 * m + 16, :] = jnp.concatenate(
                        [found[2 * m], found[2 * m + 1]], axis=0
                    ).astype(BF16)
                    acts, slopes = [], []
                    for g in (2 * m, 2 * m + 1):
                        gain = gains[8 * g : 8 * g + 8, :]
                        half = found[g] * inv * gain
                        th = jnp.tanh(half)
                        rest = half - half * th
                        acts.append(half + half * th)
                        slopes.append((gain + gain * th) * (1.0 + rest))
                    slope_out[0, k * row_block + row, s, 16 * m : 16 * m + 16, :] = jnp.concatenate(
                        slopes, axis=0
                    ).astype(BF16)
                    start = row * CH + 16 * m
                    operand[k, start : start + 16, 128 * s : 128 * s + 128] = jnp.concatenate(
                        acts, axis=0
                    ).astype(BF16)

        for row in range(row_block):
            one_row(row, row)
        spread = jnp.dot(band[...], operand[k], preferred_element_type=F32)
        lane = lane_iota(48)
        for s in range(2):
            part = spread[:, 128 * s : 128 * s + 128]
            for a in range(3):
                low, mid, high = (part[144 * a + 48 * e : 144 * a + 48 * e + 48] for e in range(3))
                low = jnp.where(lane == 0, 0.0, pltpu.roll(low, 1, 1))
                high = jnp.where(lane == COLS - 1, 0.0, pltpu.roll(high, 127, 1))
                acc[k, 2 - a, s] += low + mid + high

    keep = lane_iota(rows) < COLS
    for s in range(2):
        entry = entry_of(pick_ref, s, t)

        @pl.when(entry >= 0)
        def _():
            for o in range(3):
                final[...] = jnp.zeros(final.shape, F32)
                for k in range(blocks):
                    start = k * row_block
                    final[start : start + 16, :] += acc[k, 0, s, 16 * o : 16 * o + 16, :]
                out_ref[jnp.maximum(entry, 0), s, o] = jnp.where(keep, final[0:rows, :], 0.0).astype(BF16)

    for k in range(blocks):
        acc[k, 0] = acc[k, 1]
        acc[k, 1] = acc[k, 2]
        acc[k, 2] = jnp.zeros(acc.shape[2:], F32)


def restore_kernel(row_block, pick_ref, scale_ref, x_ref, inv_ref, slope_ref, band, grad_ref, out_ref, back, shifted, coming):
    t = pl.program_id(0)
    frames = pl.num_programs(0)
    blocks = x_ref.shape[1] // row_block
    rows = grad_ref.shape[3]

    @pl.when(t == 0)
    def _():
        shifted[...] = jnp.zeros(shifted.shape, BF16)
        lane = lane_iota(rows)

        def one_frame(frame, carry):
            for s in range(2):
                entry = entry_of(pick_ref, s, frame)
                scale = jnp.where(entry >= 0, scale_ref[s], 0.0)
                source = jnp.maximum(entry, 0)
                for o in range(3):
                    value = grad_ref[source, s, o].astype(F32) * scale
                    value = jnp.where(lane < COLS, value, 0.0)
                    for e, moved in enumerate((pltpu.roll(value, 127, 1), value, pltpu.roll(value, 1, 1))):
                        for k in range(blocks):
                            start = k * row_block
                            shifted[frame, k, 48 * e + 16 * o : 48 * e + 16 * o + 16, 128 * s : 128 * s + 128] = moved[
                                start : start + 16
                            ].astype(BF16)
            return carry

        lax.fori_loop(0, frames, one_frame, 0)

    for k in range(blocks):
        operand = jnp.concatenate([shifted[t + 2 - a, k] for a in range(3)], axis=0)
        coming[k] = jnp.dot(band[...], operand, preferred_element_type=F32)

        def one_row(row, at):
            for s in range(2):
                inv = inv_ref[0, k * row_block + row, s : s + 1, :]
                outs, units, total = [], [], None
                for m in range(SPANS // 2):
                    pair = x_ref[0, k * row_block + row, s, 16 * m : 16 * m + 16, :].astype(F32)
                    slopes = slope_ref[0, k * row_block + row, s, 16 * m : 16 * m + 16, :].astype(F32)
                    for local in range(2):
                        g = 2 * m + local
                        unit = pair[8 * local : 8 * local + 8] * inv
                        start = row * CH + 8 * g
                        cot = coming[k, start : start + 8, 128 * s : 128 * s + 128]
                        out = cot * slopes[8 * local : 8 * local + 8]
                        outs.append(out)
                        units.append(unit)
                        total = out * unit if g == 0 else total + out * unit
                factor = jnp.sum(total, axis=0, keepdims=True) * (1.0 / CH)
                for g in range(SPANS):
                    result = tiles_of((outs[g] - units[g] * factor) * inv)
                    back[at, pl.ds(14 * g + s, 7, stride=2), :] = result[0:7]
            out_ref[0, k * row_block + row] = back[at].astype(BF16)

        for row in range(row_block):
            one_row(row, row)


def nt_dot(one, two):
    return lax.dot_general(one, two, (((1,), (1,)), ((), ())), preferred_element_type=F32)


def tn_dot(one, two):
    return lax.dot_general(one, two, (((0,), (0,)), ((), ())), preferred_element_type=F32)


def nn_dot(one, two):
    return jnp.dot(one, two, preferred_element_type=F32)


def split_two(value):
    high = value.astype(BF16)
    low = (value - high.astype(F32)).astype(BF16)
    return jnp.concatenate([high, low], axis=0)


def reward_kernel(
    row_count, tiles, samples,
    part_ref, packed_ref, head_ref,
    out_ref, score_ref,
    pack, arrived, frame, flip, embed, outw, place, patches, tokens, normed, normed16, slots, weights, dslots, dnormed, rows8, abar, order,
):
    height = row_count * tiles
    patch_rows = height // PATCH
    lane64 = lane_iota(8) < 64
    lane = lane_iota(NTOK)
    count = samples * NTOK

    copies = []
    for part, (begin, end) in enumerate(((880, 1120), (640, 880), (0, 640))):
        copies.append(
            pltpu.make_async_copy(
                packed_ref.at[:, begin:end, :], pack.at[:, begin:end, :], arrived.at[part]
            )
        )
        copies[-1].start()

    inputs = order.shape[1]
    pixel = lax.broadcasted_iota(jnp.int32, (64, inputs), 0)
    column = lax.broadcasted_iota(jnp.int32, (64, inputs), 1)
    for x in range(PATCH):
        order[64 * x : 64 * x + 64, :] = (
            (column == pixel * PATCH + x) & (pixel < 3 * PATCH)
        ).astype(BF16)

    flip[...] = jnp.zeros(flip.shape, F32)
    frame[...] = jnp.zeros(frame.shape, F32)
    for f in range(samples):
        for i in range(tiles):
            at = row_count * i + 7
            for o in range(3):
                frame[f, o, at : at + row_count + 2, :] += part_ref[i, f, o, 0 : row_count + 2, :].astype(F32)
    for f in range(samples):
        for pair in range(patch_rows // 2):
            turn = flip.at[f * (patch_rows // 2) + pair]
            for local in range(2):
                at = 8 + PATCH * (2 * pair + local)
                for o in range(3):
                    turn[0, 64 * local + PATCH * o : 64 * local + PATCH * o + PATCH, :] = (
                        frame[f, o, at : at + PATCH, :].astype(BF16).astype(F32)
                    )
            turn[1] = turn[0].T
            token = f * NTOK + pair * 16
            for y in range(PATCH // 2):
                even = turn[1, pl.ds(2 * y, 8, stride=PATCH), :]
                odd = turn[1, pl.ds(2 * y + 1, 8, stride=PATCH), :]
                patches[token : token + 8, 128 * y : 128 * y + 128] = jnp.where(lane64, even, pltpu.roll(odd, 64, 1))
                patches[token + 8 : token + 16, 128 * y : 128 * y + 128] = jnp.where(lane64, pltpu.roll(even, 64, 1), odd)

    copies[0].wait()
    copies[1].wait()

    for i in range(NT):
        for z, (begin, height, target) in enumerate(
            ((0, 48, 128 * i), (0, 48, 128 * i + 48), (0, 32, 128 * i + 96), (16, 32, 1024 + 32 * i))
        ):
            source = pack.at[PLACES[i][z]]
            for part in range(5):
                at = 880 + 48 * part + begin
                embed[target : target + height, 128 * part : 128 * part + 128] = source[at : at + height, :]
    lane48 = lane_iota(48)
    for h in range(HEADS):
        outw[128 * h + HD : 128 * h + 128, :] = jnp.zeros((128 - HD, D), BF16)
    for z in range(NZ):
        for i in range(NT):
            source = pack.at[PLACES[i][z]]
            for local in range(2):
                at, begin = 128 * (2 * z + local), 640 + HD * local
                outw[at : at + HD, 128 * i : 128 * i + 128] = source[begin : begin + HD, :]
            place[32 * z : 32 * z + 32, 128 * i : 128 * i + 128] = source[800:832, :]
        for ib in range(2):
            sources = [pack[PLACES[4 * ib + j][z], 832:880, :].astype(F32) for j in range(4)]
            rolled = [[sources[j] if d == 0 else pltpu.roll(sources[j], 32 * d, 1) for d in range(4)] for j in range(4)]
            at = 1024 + 128 * ib
            for q in range(4):
                found = rolled[0][(0 - q) % 4]
                for j in range(1, 4):
                    found = jnp.where(lane48 >= 32 * j, rolled[j][(j - q) % 4], found)
                found = found.astype(BF16)
                for begin, end, row in (
                    ((0, 48, 0),),
                    ((0, 32, 48), (32, 48, 128)),
                    ((0, 48, 144),),
                    ((0, 16, 192),),
                )[q]:
                    row = 256 * z + row
                    outw[row : row + end - begin, at : at + 128] = found[begin:end]
                if q == 3:
                    place[32 * z : 32 * z + 32, at : at + 128] = found[16:48]

    patches16 = nn_dot(patches[...].astype(BF16), order[...]).astype(BF16)
    token_value = nt_dot(patches16, embed[...])
    rows8[...] = jnp.zeros(rows8.shape, F32)
    abar[...] = jnp.zeros(abar.shape, F32)
    place_value = place[...].astype(F32)
    for f in range(samples):
        value = token_value[f * NTOK : f * NTOK + NTOK] + place_value
        rows8[0, f : f + 1, :] = jnp.mean(value, axis=0, keepdims=True)
        centered = value - jnp.mean(value, axis=-1, keepdims=True)
        scale = lax.rsqrt(jnp.mean(centered * centered, axis=-1, keepdims=True) + 1e-05)
        value = centered * scale
        normed[f * NTOK : f * NTOK + NTOK, :] = value
        normed16[f * NTOK : f * NTOK + NTOK, :] = value.astype(BF16)
        tokens[f * NTOK : f * NTOK + NTOK, :] = jnp.broadcast_to(scale, (NTOK, 128))

    def weight_part(i, z):
        source = pack.at[PLACES[i][z]]
        return jnp.concatenate([source[0:256, :], source[320:576, :]], axis=1)

    def weight_rest(i):
        return jnp.concatenate(
            [
                jnp.concatenate([pack[PLACES[i][z], 256:320, :], pack[PLACES[i][z], 576:640, :]], axis=1)
                for z in range(NZ)
            ],
            axis=0,
        )

    lane_all = lane_iota(count)
    copies[2].wait()
    for i in range(NT):
        mixed = nn_dot(
            normed16[...], jnp.concatenate([weight_part(i, z) for z in range(NZ)] + [weight_rest(i)], axis=0)
        )
        first, second = mixed[:, 0:128], mixed[:, 128:256]
        found = (
            first,
            jnp.where(lane_all < 48, pltpu.roll(first, 48, 1), pltpu.roll(second, 48, 1)),
            pltpu.roll(second, 96, 1),
        )
        for m in range(3):
            slots[3 * i + m] = jnp.where(lane_all < HD, found[m], 0.0).astype(BF16)

    for h in range(HEADS):
        for f in range(samples):
            span = slice(f * NTOK, f * NTOK + NTOK)
            logits = nt_dot(slots[h, span, :], slots[HEADS + h, span, :]) * HD ** (-0.5)
            logits = jnp.exp(logits - jnp.max(logits, axis=-1, keepdims=True))
            prob = logits / jnp.sum(logits, axis=-1, keepdims=True)
            weights[h * samples + f] = prob
            attended = nn_dot(prob.astype(BF16), slots[2 * HEADS + h, span, :]).astype(BF16)
            abar[f : f + 1, 128 * h : 128 * h + 128] = jnp.mean(attended.astype(F32), axis=0, keepdims=True)

    part = nn_dot(split_two(abar[...]), outw[...])
    pooled = rows8[0] + part[0:8] + part[8:16]
    pooled = pooled - jnp.mean(pooled, axis=-1, keepdims=True)
    scale = lax.rsqrt(jnp.mean(pooled * pooled, axis=-1, keepdims=True) + 1e-05)
    pooled = pooled * scale
    head = head_ref[...]
    score_ref[...] = jnp.broadcast_to(jnp.sum(pooled * head, axis=-1, keepdims=True), (8, 128))
    dpooled = scale * (
        head - jnp.mean(head, axis=-1, keepdims=True) - pooled * jnp.mean(pooled * head, axis=-1, keepdims=True)
    )
    dres = dpooled * (1.0 / NTOK)
    rows8[1] = dres
    datts = nt_dot(split_two(dres), outw[...])
    datts = (datts[0:8] + datts[8:16]).astype(BF16)

    for h in range(HEADS):
        datt = datts[:, 128 * h : 128 * h + 128]
        for f in range(samples):
            span = slice(f * NTOK, f * NTOK + NTOK)
            prob = weights[h * samples + f]
            row = datt[f : f + 1, :]
            dweight = nt_dot(datt, slots[2 * HEADS + h, span, :])[f : f + 1, :].astype(BF16).astype(F32)
            inner = jnp.sum(prob * dweight, axis=-1, keepdims=True)
            dlogit = (prob * (dweight - inner) * HD ** (-0.5)).astype(BF16)
            dslots[h, span, :] = nn_dot(dlogit, slots[HEADS + h, span, :])
            dslots[HEADS + h, span, :] = tn_dot(dlogit, slots[h, span, :])
            dslots[2 * HEADS + h, span, :] = tn_dot(
                prob.astype(BF16), jnp.broadcast_to(row.astype(F32), (NTOK, 128)).astype(BF16)
            )

    parts = []
    for i in range(NT):
        one, two, three = dslots[3 * i], dslots[3 * i + 1], dslots[3 * i + 2]
        two = pltpu.roll(two, 80, 1)
        three = pltpu.roll(three, 32, 1)
        first = jnp.where(lane_all < HD, one, two)
        second = jnp.where(lane_all < 32, two, jnp.where(lane_all < COLS, three, 0.0))
        parts += [first.astype(BF16), second.astype(BF16)]
    dmixed = jnp.concatenate(parts, axis=1)
    for z in range(NZ):
        wide = jnp.concatenate([weight_part(i, z) for i in range(NT)], axis=1)
        dnormed[:, 256 * z : 256 * z + 256] = nt_dot(dmixed, wide)
    wide = jnp.concatenate([weight_rest(i) for i in range(NT)], axis=1)
    dnormed[:, 1024:1280] = nt_dot(dmixed, wide)

    for f in range(samples):
        span = slice(f * NTOK, f * NTOK + NTOK)
        value, dvalue = normed[span, :], dnormed[span, :]
        scale = tokens[span, 0:1]
        dvalue = scale * (
            dvalue
            - jnp.mean(dvalue, axis=-1, keepdims=True)
            - value * jnp.mean(dvalue * value, axis=-1, keepdims=True)
        )
        normed16[span, :] = (dvalue + rows8[1, f : f + 1, :]).astype(BF16)
    patches[...] = nt_dot(nn_dot(normed16[...], embed[...]).astype(BF16), order[...])

    frame[...] = jnp.zeros(frame.shape, F32)
    rows = out_ref.shape[3]
    for f in range(samples):
        for pair in range(patch_rows // 2):
            turn = flip.at[f * (patch_rows // 2) + pair]
            token = f * NTOK + pair * 16
            for y in range(PATCH // 2):
                one = patches[token : token + 8, 128 * y : 128 * y + 128]
                two = patches[token + 8 : token + 16, 128 * y : 128 * y + 128]
                turn[1, pl.ds(2 * y, 8, stride=PATCH), :] = jnp.where(lane64, one, pltpu.roll(two, 64, 1))
                turn[1, pl.ds(2 * y + 1, 8, stride=PATCH), :] = jnp.where(lane64, pltpu.roll(one, 64, 1), two)
            turn[0] = turn[1].T
            for local in range(2):
                at = 8 + PATCH * (2 * pair + local)
                for o in range(3):
                    frame[f, o, at : at + PATCH, :] = turn[0, 64 * local + PATCH * o : 64 * local + PATCH * o + PATCH, :]
    for f in range(samples):
        for i in range(tiles):
            at = row_count * i + 7
            for o in range(3):
                out_ref[i, f, o] = frame[f, o, at : at + rows, :].astype(BF16)


def pack_part(rows_in, out_part, place_part, embed_part):
    ordered = jnp.concatenate([rows_in[0:128], rows_in[160:288], rows_in[128:160], rows_in[288:320]], axis=0)
    upper = jnp.pad(ordered[:, 128:240], ((0, 0), (0, 16)))
    other = jnp.concatenate([out_part, place_part], axis=0)
    rest = other[:, 128:160].reshape(4, 48, 32)
    rest = jnp.concatenate([rest[q] for q in range(4)], axis=1)
    embed_part = jnp.pad(embed_part, ((0, 0), (0, 640 - embed_part.shape[1])))
    embed_part = embed_part.reshape(48, 5, 128).transpose(1, 0, 2).reshape(240, 128)
    return jnp.concatenate([ordered[:, 0:128], upper, other[:, 0:128], rest, embed_part], axis=0)


def pack_kernel(z_ref, rows_ref, out_ref, place_ref, embed_ref, packed_ref):
    for source, target, count in ((0, 0, 128), (160, 128, 128), (128, 256, 32), (288, 288, 32)):
        packed_ref[target : target + count, :] = rows_ref[source : source + count, 0:128]
        packed_ref[320 + target : 320 + target + count, :] = jnp.concatenate(
            [rows_ref[source : source + count, 128:240], jnp.zeros((count, 16), BF16)], axis=1
        )
    packed_ref[640:800, :] = out_ref[:, 0:128]
    packed_ref[800:832, :] = place_ref[:, 0:128]
    tail = out_ref[:, 128:160].astype(F32)
    last = place_ref[:, 128:160].astype(F32)
    packed_ref[832:880, :] = jnp.concatenate(
        [tail[0:48], tail[48:96], tail[96:144], jnp.concatenate([tail[144:160], last], axis=0)],
        axis=1,
    ).astype(BF16)
    width = embed_ref.shape[1]
    start = pl.multiple_of(jnp.where(z_ref[0] == NZ - 1, STARTS[-1], 48 * z_ref[0]), 16)
    for part in range(5):
        count = min(128, width - 128 * part)
        value = embed_ref[pl.ds(start, 48), 128 * part : 128 * part + count]
        if count < 128:
            value = jnp.concatenate([value, jnp.zeros((48, 128 - count), BF16)], axis=1)
        packed_ref[880 + 48 * part : 928 + 48 * part, :] = value


def packed_weights(patch_embed, position, attend_in, attend_out):
    if lax.axis_size(TILE) == NT and lax.axis_size("sample") == NZ:
        z = lax.axis_index("sample").astype(jnp.int32).reshape(1)
        mine = pl.pallas_call(
            pack_kernel,
            in_specs=[pl.BlockSpec(memory_space=pltpu.SMEM)] + [pl.BlockSpec(memory_space=pltpu.VMEM)] * 4,
            out_shape=jax.ShapeDtypeStruct((PACK, 128), BF16),
            compiler_params=params(),
            name="pack",
        )(z, attend_in, attend_out, position, patch_embed.T)
        group = [i * NZ + z for i, z in CYCLE]
        return lax.all_gather(mine, TILE + ("sample",), axis=0, axis_index_groups=[group])

    def whole(value):
        value = lax.all_gather(value, "sample", axis=0, tiled=True)
        return lax.all_gather(value, TILE, axis=1, tiled=True)

    split = [
        value.reshape(NZ, value.shape[0] // NZ, NT, value.shape[1] // NT).transpose(2, 0, 1, 3)
        for value in (whole(attend_in), whole(attend_out), whole(position))
    ]
    columns = lax.all_gather(patch_embed.T, TILE, axis=0, tiled=True).reshape(NT, D // NT, -1)
    split.append(jnp.stack([columns[:, start : start + 48] for start in STARTS], axis=1))
    packed = jax.vmap(jax.vmap(pack_part))(*split)
    return jnp.stack([packed[i, z] for i, z in CYCLE])


def params(mib=58):
    return pltpu.CompilerParams(vmem_limit_bytes=mib * 1024 * 1024)


def local(
    features,
    norm_gain,
    conv_weight,
    patch_embed,
    position,
    attend_in,
    attend_out,
    reward_head,
    group_index,
    frame_pick,
):
    samples, frames, row_count, merged = features.shape
    tiles, parts = lax.axis_size(TILE), lax.axis_size("sample")
    sent_rows = -(-(row_count + 2) // 16) * 16
    row_block = row_count if row_count <= 14 else 14
    blocks = row_count // row_block
    inner = row_block * CH
    packed = packed_weights(patch_embed, position, attend_in, attend_out)
    order = Layout((1, 2, 3, 0, 4))
    split = (samples, frames, row_count, merged // 128, 128)
    view = with_layout_constraint(features.reshape(split), order).transpose(1, 2, 3, 0, 4)
    view = view.reshape(frames, row_count, samples * merged // 128, 128)
    gain = norm_gain[None, :]

    smem = pl.BlockSpec(memory_space=pltpu.SMEM)
    view_spec = pl.BlockSpec((1,) + view.shape[1:], lambda t: (t, 0, 0, 0))
    gain_spec = pl.BlockSpec((1, CH), lambda t: (0, 0))
    taps_spec = pl.BlockSpec((3, 3, 3, 3, CH), lambda t: (0, 0, 0, 0, 0))
    sent = (SCORED, samples, 3, sent_rows, 128)
    sent_spec = pl.BlockSpec(sent, lambda t: (0, 0, 0, 0, 0))
    aligned = (frames, row_count, samples, CH, 128)
    aligned_spec = pl.BlockSpec((1,) + aligned[1:], lambda t: (t, 0, 0, 0, 0))
    inv_spec = pl.BlockSpec((1, row_count, samples, 128), lambda t: (t, 0, 0, 0))
    band_spec = pl.BlockSpec((inner, OUT_ROWS), lambda t: (0, 0))
    decoded, x_aligned, inverse, slopes, band = pl.pallas_call(
        functools.partial(decode_kernel, row_block),
        grid=(frames,),
        in_specs=[smem, view_spec, gain_spec, taps_spec],
        out_specs=[sent_spec, aligned_spec, inv_spec, aligned_spec, band_spec],
        scratch_shapes=[
            pltpu.VMEM((OUT_ROWS, inner), BF16),
            pltpu.VMEM((3, 32, CH), F32),
            pltpu.VMEM((128, 128), F32),
            pltpu.VMEM((row_block, 192, 128), F32),
            pltpu.VMEM((blocks, inner, 256), BF16),
            pltpu.VMEM((blocks, 3, samples, 48, 128), F32),
            pltpu.VMEM((sent_rows + 16, 128), F32),
        ],
        out_shape=[
            jax.ShapeDtypeStruct(sent, BF16),
            jax.ShapeDtypeStruct(aligned, BF16),
            jax.ShapeDtypeStruct((frames, row_count, samples, 128), F32),
            jax.ShapeDtypeStruct(aligned, BF16),
            jax.ShapeDtypeStruct((inner, OUT_ROWS), BF16),
        ],
        compiler_params=params(),
        name="decode",
    )(frame_pick, view, gain, conv_weight)

    if tiles > SCORED:
        decoded = jnp.pad(decoded, ((0, tiles - SCORED),) + ((0, 0),) * 4)
    owned = lax.all_to_all(decoded, TILE, split_axis=0, concat_axis=0, tiled=True)

    head = reward_head.reshape(NT, D // NT)
    head = jnp.concatenate([head[:, :128].reshape(-1), head[:, 128:].reshape(-1)])[None, :]
    height = row_count * tiles
    count = samples * NTOK
    grads, scores = pl.pallas_call(
        functools.partial(reward_kernel, row_count, tiles, samples),
        out_shape=[
            jax.ShapeDtypeStruct((tiles, samples, 3, sent_rows, 128), BF16),
            jax.ShapeDtypeStruct((8, 128), F32),
        ],
        in_specs=[
            pl.BlockSpec(memory_space=pltpu.VMEM),
            pl.BlockSpec(memory_space=pl.ANY),
            pl.BlockSpec(memory_space=pltpu.VMEM),
        ],
        scratch_shapes=[
            pltpu.VMEM(packed.shape, BF16),
            pltpu.SemaphoreType.DMA((3,)),
            pltpu.VMEM((samples, 3, height + 48, 128), F32),
            pltpu.VMEM((samples * height // (2 * PATCH), 2, 128, 128), F32),
            pltpu.VMEM((D, 640), BF16),
            pltpu.VMEM((HEADS * 128, D), BF16),
            pltpu.VMEM((NTOK, D), BF16),
            pltpu.VMEM((count, KIN), F32),
            pltpu.VMEM((count, 128), F32),
            pltpu.VMEM((count, D), F32),
            pltpu.VMEM((count, D), BF16),
            pltpu.VMEM((3 * HEADS, count, 128), BF16),
            pltpu.VMEM((HEADS * samples, NTOK, NTOK), F32),
            pltpu.VMEM((3 * HEADS, count, 128), F32),
            pltpu.VMEM((count, D), F32),
            pltpu.VMEM((2, 8, D), F32),
            pltpu.VMEM((8, HEADS * 128), F32),
            pltpu.VMEM((KIN, 640), BF16),
        ],
        compiler_params=params(),
        name="reward",
    )(owned, packed, head)

    mine = jnp.concatenate([scores[:samples, 0], group_index.astype(F32)])
    mine = jnp.broadcast_to(mine[None], (tiles * parts, 2 * samples))
    everyone = lax.all_to_all(mine, TILE + ("sample",), split_axis=0, concat_axis=0, tiled=True)
    everyone = everyone.reshape(tiles, parts, 2, samples)
    returned = lax.all_to_all(grads, TILE, split_axis=0, concat_axis=0, tiled=True)
    returned = returned[:SCORED]

    rewards = jnp.sum(everyone[:SCORED, :, 0], axis=0).reshape(-1) / SCORED
    groups = everyone[0, :, 1].reshape(-1)
    here = (lax.axis_index("sample") * samples).astype(jnp.int32)
    own_rewards = lax.dynamic_slice_in_dim(rewards, here, samples)
    own_groups = lax.dynamic_slice_in_dim(groups, here, samples)
    member = (own_groups[:, None] == groups[None, :]).astype(F32)
    mean_group = jnp.sum(member * rewards[None, :], axis=1) / GROUP
    second_group = jnp.sum(member * (rewards * rewards)[None, :], axis=1) / GROUP - mean_group * mean_group
    advantage = (own_rewards - mean_group) * lax.rsqrt(second_group + SMOOTH)
    cotangent = -LOSS_SCALE * advantage / SCORED

    result = pl.pallas_call(
        functools.partial(restore_kernel, row_block),
        grid=(frames,),
        in_specs=[smem, smem, aligned_spec, inv_spec, aligned_spec, band_spec, sent_spec],
        out_specs=view_spec,
        scratch_shapes=[
            pltpu.VMEM((row_block, samples * merged // 128, 128), F32),
            pltpu.VMEM((frames + 2, blocks, 144, 256), BF16),
            pltpu.VMEM((blocks, inner, 256), F32),
        ],
        out_shape=jax.ShapeDtypeStruct(view.shape, BF16),
        compiler_params=params(),
        name="restore",
    )(frame_pick, cotangent, x_aligned, inverse, slopes, band, returned)
    result = result.reshape(frames, row_count, merged // 128, samples, 128).transpose(3, 0, 1, 2, 4)
    return with_layout_constraint(result, order).reshape(features.shape)


def solution(mesh):
    tiles, parts = mesh.devices.shape
    split = Mesh(mesh.devices.reshape(tiles // 2, 2, parts), ("chip", "core", "sample"))
    in_specs = (
        P("sample", None, TILE, None),
        P(),
        P(),
        P(None, TILE),
        P("sample", TILE),
        P("sample", TILE),
        P("sample", TILE),
        P(),
        P("sample"),
        P("sample", None),
    )
    out_specs = P("sample", None, TILE, None)
    return jax.shard_map(local, mesh=split, in_specs=in_specs, out_specs=out_specs, check_vma=False)
```

```python
import functools

import jax
import jax.numpy as jnp
from jax import lax
from jax.experimental import pallas as pl
from jax.experimental.pallas import tpu as pltpu
from jax.experimental.layout import Layout, with_layout_constraint
from jax.sharding import Mesh, PartitionSpec as P

SCORED = 8
PATCH = 14
HEADS = 8
HD = 80
GROUP = 4
LOSS_SCALE = 16384.0
SMOOTH = 0.01

TILE = ("chip", "core")
CH = 96
COLS = 112
SPANS = CH // 8
OUT_ROWS = 27 * 16
NT = 8
NZ = 4
PACK = 1120
ROWS_IN = 640
CYCLE = [
    (2 * chip + core, z)
    for chip, heights in ((0, (0, 1, 2, 3)), (1, (3, 2, 1, 0)), (3, (0, 1, 2, 3)), (2, (3, 2, 1, 0)))
    for z in heights
    for core in range(2)
]
PLACES = [[CYCLE.index((i, z)) for z in range(NZ)] for i in range(NT)]
STARTS = (0, 48, 96, 112)
KIN = 896
D = 1280
NTOK = 128
F32 = jnp.float32
BF16 = jnp.bfloat16


def lane_iota(rows):
    return lax.broadcasted_iota(jnp.int32, (rows, 128), 1)


def sub_iota(rows):
    return lax.broadcasted_iota(jnp.int32, (rows, 128), 0)


def channels_of(raw, at, group, sample):
    start = 8 + 14 * group + sample
    here = raw[at, pl.ds(start, 8, stride=2), :]
    before = raw[at, pl.ds(start - 2, 8, stride=2), :]
    joined = jnp.where(lane_iota(8) < 128 - 16 * sub_iota(8), here, before)
    return pltpu.roll(joined, 0, 1, stride=16, stride_axis=0)


def tiles_of(value):
    turned = jnp.take_along_axis(value, (lane_iota(8) + 16 * sub_iota(8)) % 128, axis=1)
    return jnp.where(lane_iota(8) < COLS - 16 * sub_iota(8), turned, pltpu.roll(turned, 7, 0))


def banded(weight_ref, taps, row_block, transposed):
    taps[...] = jnp.zeros(taps.shape, F32)
    for a in range(3):
        for b in range(3):
            for e in range(3):
                for o in range(3):
                    at = (a * 3 + e) * 3 + o
                    taps[b, at : at + 1, :] = weight_ref[a, b, e, o : o + 1, :].astype(F32)
    inner = row_block * CH
    pick = (
        lax.broadcasted_iota(jnp.int32, (OUT_ROWS, 32), 0) // 16
        == lax.broadcasted_iota(jnp.int32, (OUT_ROWS, 32), 1)
    ).astype(BF16)
    if transposed:
        shape, p_dim, r_dim = (inner, OUT_ROWS), 1, 0
        grow_shape, grow_dim = (inner, CH), 0
    else:
        shape, p_dim, r_dim = (OUT_ROWS, inner), 0, 1
        grow_shape, grow_dim = (CH, inner), 1
    at = lax.broadcasted_iota(jnp.int32, grow_shape, grow_dim)
    at = at - CH * ((at.astype(F32) + 0.5) * (1.0 / CH)).astype(jnp.int32)
    grow = (at == lax.broadcasted_iota(jnp.int32, grow_shape, 1 - grow_dim)).astype(BF16)
    p_at = lax.broadcasted_iota(jnp.int32, shape, p_dim) % 16
    r_at = lax.broadcasted_iota(jnp.int32, shape, r_dim)
    r_at = ((r_at.astype(F32) + 0.5) * (1.0 / CH)).astype(jnp.int32)
    total = jnp.zeros(shape, F32)
    for b in range(3):
        rows = jnp.dot(pick, taps[b].astype(BF16), preferred_element_type=F32).astype(BF16)
        if transposed:
            full = lax.dot_general(
                grow, rows, (((1,), (1,)), ((), ())), preferred_element_type=F32
            )
        else:
            full = jnp.dot(rows, grow, preferred_element_type=F32)
        total = jnp.where(p_at == r_at + 2 - b, full, total)
    return total.astype(BF16)


def half_gains(gain_ref):
    rows = jnp.concatenate([gain_ref[0:1, :], jnp.zeros((1, 128 - CH), F32)], axis=1)
    return 0.5 * jnp.broadcast_to(rows, (128, 128)).T


def entry_of(pick_ref, sample, frame):
    found = jnp.int32(-1)
    for j in range(SCORED):
        found = jnp.where(pick_ref[sample, j] == frame, jnp.int32(j), found)
    return found


def decode_kernel(row_block, pick_ref, x_ref, gain_ref, weight_ref, out_ref, x_out, inv_out, slope_out, turned_out, band, taps, gains, raw, operand, acc, final):
    t = pl.program_id(0)
    blocks = x_ref.shape[1] // row_block
    rows = out_ref.shape[3]

    @pl.when(t == 0)
    def _():
        band[...] = banded(weight_ref, taps, row_block, False)
        turned_out[...] = banded(weight_ref, taps, row_block, True)
        gains[...] = half_gains(gain_ref)
        acc[...] = jnp.zeros(acc.shape, F32)
        raw[...] = jnp.zeros(raw.shape, F32)

    for k in range(blocks):

        def one_row(row, at):
            raw[at, 8:176, :] = x_ref[0, k * row_block + row].astype(F32)
            for s in range(2):
                found = [channels_of(raw, at, g, s) for g in range(SPANS)]
                square = found[0] * found[0]
                for g in range(1, SPANS):
                    square = square + found[g] * found[g]
                second = jnp.sum(square, axis=0, keepdims=True) * (1.0 / CH)
                inv = lax.rsqrt(second + 1e-06)
                inv_out[0, k * row_block + row, s : s + 1, :] = inv
                for m in range(SPANS // 2):
                    x_out[0, k * row_block + row, s, 16 * m : 16 * m + 16, :] = jnp.concatenate(
                        [found[2 * m], found[2 * m + 1]], axis=0
                    ).astype(BF16)
                    acts, slopes = [], []
                    for g in (2 * m, 2 * m + 1):
                        gain = gains[8 * g : 8 * g + 8, :]
                        half = found[g] * inv * gain
                        th = jnp.tanh(half)
                        rest = half - half * th
                        acts.append(half + half * th)
                        slopes.append((gain + gain * th) * (1.0 + rest))
                    slope_out[0, k * row_block + row, s, 16 * m : 16 * m + 16, :] = jnp.concatenate(
                        slopes, axis=0
                    ).astype(BF16)
                    start = row * CH + 16 * m
                    operand[k, start : start + 16, 128 * s : 128 * s + 128] = jnp.concatenate(
                        acts, axis=0
                    ).astype(BF16)

        for row in range(row_block):
            one_row(row, row)
        spread = jnp.dot(band[...], operand[k], preferred_element_type=F32)
        lane = lane_iota(48)
        for s in range(2):
            part = spread[:, 128 * s : 128 * s + 128]
            for a in range(3):
                low, mid, high = (part[144 * a + 48 * e : 144 * a + 48 * e + 48] for e in range(3))
                low = jnp.where(lane == 0, 0.0, pltpu.roll(low, 1, 1))
                high = jnp.where(lane == COLS - 1, 0.0, pltpu.roll(high, 127, 1))
                acc[k, 2 - a, s] += low + mid + high

    keep = lane_iota(rows) < COLS
    for s in range(2):
        entry = entry_of(pick_ref, s, t)

        @pl.when(entry >= 0)
        def _():
            for o in range(3):
                final[...] = jnp.zeros(final.shape, F32)
                for k in range(blocks):
                    start = k * row_block
                    final[start : start + 16, :] += acc[k, 0, s, 16 * o : 16 * o + 16, :]
                out_ref[jnp.maximum(entry, 0), s, o] = jnp.where(keep, final[0:rows, :], 0.0).astype(BF16)

    for k in range(blocks):
        acc[k, 0] = acc[k, 1]
        acc[k, 1] = acc[k, 2]
        acc[k, 2] = jnp.zeros(acc.shape[2:], F32)


def restore_kernel(row_block, pick_ref, scale_ref, x_ref, inv_ref, slope_ref, band, grad_ref, out_ref, back, shifted, coming):
    t = pl.program_id(0)
    frames = pl.num_programs(0)
    blocks = x_ref.shape[1] // row_block
    rows = grad_ref.shape[3]

    @pl.when(t == 0)
    def _():
        shifted[...] = jnp.zeros(shifted.shape, BF16)
        lane = lane_iota(rows)

        def one_frame(frame, carry):
            for s in range(2):
                entry = entry_of(pick_ref, s, frame)
                scale = jnp.where(entry >= 0, scale_ref[s], 0.0)
                source = jnp.maximum(entry, 0)
                for o in range(3):
                    value = grad_ref[source, s, o].astype(F32) * scale
                    value = jnp.where(lane < COLS, value, 0.0)
                    for e, moved in enumerate((pltpu.roll(value, 127, 1), value, pltpu.roll(value, 1, 1))):
                        for k in range(blocks):
                            start = k * row_block
                            shifted[frame, k, 48 * e + 16 * o : 48 * e + 16 * o + 16, 128 * s : 128 * s + 128] = moved[
                                start : start + 16
                            ].astype(BF16)
            return carry

        lax.fori_loop(0, frames, one_frame, 0)

    for k in range(blocks):
        operand = jnp.concatenate([shifted[t + 2 - a, k] for a in range(3)], axis=0)
        coming[k] = jnp.dot(band[...], operand, preferred_element_type=F32)

        def one_row(row, at):
            for s in range(2):
                inv = inv_ref[0, k * row_block + row, s : s + 1, :]
                outs, units, total = [], [], None
                for m in range(SPANS // 2):
                    pair = x_ref[0, k * row_block + row, s, 16 * m : 16 * m + 16, :].astype(F32)
                    slopes = slope_ref[0, k * row_block + row, s, 16 * m : 16 * m + 16, :].astype(F32)
                    for local in range(2):
                        g = 2 * m + local
                        unit = pair[8 * local : 8 * local + 8] * inv
                        start = row * CH + 8 * g
                        cot = coming[k, start : start + 8, 128 * s : 128 * s + 128]
                        out = cot * slopes[8 * local : 8 * local + 8]
                        outs.append(out)
                        units.append(unit)
                        total = out * unit if g == 0 else total + out * unit
                factor = jnp.sum(total, axis=0, keepdims=True) * (1.0 / CH)
                for g in range(SPANS):
                    result = tiles_of((outs[g] - units[g] * factor) * inv)
                    back[at, pl.ds(14 * g + s, 7, stride=2), :] = result[0:7]
            out_ref[0, k * row_block + row] = back[at].astype(BF16)

        for row in range(row_block):
            one_row(row, row)


def nt_dot(one, two):
    return lax.dot_general(one, two, (((1,), (1,)), ((), ())), preferred_element_type=F32)


def tn_dot(one, two):
    return lax.dot_general(one, two, (((0,), (0,)), ((), ())), preferred_element_type=F32)


def nn_dot(one, two):
    return jnp.dot(one, two, preferred_element_type=F32)


def split_two(value):
    high = value.astype(BF16)
    low = (value - high.astype(F32)).astype(BF16)
    return jnp.concatenate([high, low], axis=0)


def token_kernel(
    row_count, tiles, samples,
    part_ref, pack_ref,
    normed, normed16, scales, rows8, embed, outw, order,
    frame, flip, place, patches,
):
    height = row_count * tiles
    patch_rows = height // PATCH
    lane64 = lane_iota(8) < 64
    inputs = order.shape[1]
    pixel = lax.broadcasted_iota(jnp.int32, (64, inputs), 0)
    column = lax.broadcasted_iota(jnp.int32, (64, inputs), 1)
    for x in range(PATCH):
        order[64 * x : 64 * x + 64, :] = (
            (column == pixel * PATCH + x) & (pixel < 3 * PATCH)
        ).astype(BF16)

    flip[...] = jnp.zeros(flip.shape, F32)
    frame[...] = jnp.zeros(frame.shape, F32)
    for f in range(samples):
        for i in range(tiles):
            at = row_count * i + 7
            for o in range(3):
                frame[f, o, at : at + row_count + 2, :] += part_ref[i, f, o, 0 : row_count + 2, :].astype(F32)
    for f in range(samples):
        for pair in range(patch_rows // 2):
            turn = flip.at[f * (patch_rows // 2) + pair]
            for local in range(2):
                at = 8 + PATCH * (2 * pair + local)
                for o in range(3):
                    turn[0, 64 * local + PATCH * o : 64 * local + PATCH * o + PATCH, :] = (
                        frame[f, o, at : at + PATCH, :].astype(BF16).astype(F32)
                    )
            turn[1] = turn[0].T
            token = f * NTOK + pair * 16
            for y in range(PATCH // 2):
                even = turn[1, pl.ds(2 * y, 8, stride=PATCH), :]
                odd = turn[1, pl.ds(2 * y + 1, 8, stride=PATCH), :]
                patches[token : token + 8, 128 * y : 128 * y + 128] = jnp.where(lane64, even, pltpu.roll(odd, 64, 1))
                patches[token + 8 : token + 16, 128 * y : 128 * y + 128] = jnp.where(lane64, pltpu.roll(even, 64, 1), odd)

    for i in range(NT):
        for z, (begin, tall, target) in enumerate(
            ((0, 48, 128 * i), (0, 48, 128 * i + 48), (0, 32, 128 * i + 96), (16, 32, 1024 + 32 * i))
        ):
            source = pack_ref.at[PLACES[i][z]]
            for part in range(5):
                at = 240 + 48 * part + begin
                embed[target : target + tall, 128 * part : 128 * part + 128] = source[at : at + tall, :]
    lane48 = lane_iota(48)
    for h in range(HEADS):
        outw[128 * h + HD : 128 * h + 128, :] = jnp.zeros((128 - HD, D), BF16)
    for z in range(NZ):
        for i in range(NT):
            source = pack_ref.at[PLACES[i][z]]
            for local in range(2):
                at, begin = 128 * (2 * z + local), HD * local
                outw[at : at + HD, 128 * i : 128 * i + 128] = source[begin : begin + HD, :]
            place[32 * z : 32 * z + 32, 128 * i : 128 * i + 128] = source[160:192, :]
        for ib in range(2):
            sources = [pack_ref[PLACES[4 * ib + j][z], 192:240, :].astype(F32) for j in range(4)]
            rolled = [[sources[j] if d == 0 else pltpu.roll(sources[j], 32 * d, 1) for d in range(4)] for j in range(4)]
            at = 1024 + 128 * ib
            for q in range(4):
                found = rolled[0][(0 - q) % 4]
                for j in range(1, 4):
                    found = jnp.where(lane48 >= 32 * j, rolled[j][(j - q) % 4], found)
                found = found.astype(BF16)
                for begin, end, row in (
                    ((0, 48, 0),),
                    ((0, 32, 48), (32, 48, 128)),
                    ((0, 48, 144),),
                    ((0, 16, 192),),
                )[q]:
                    row = 256 * z + row
                    outw[row : row + end - begin, at : at + 128] = found[begin:end]
                if q == 3:
                    place[32 * z : 32 * z + 32, at : at + 128] = found[16:48]

    patches16 = nn_dot(patches[...].astype(BF16), order[...]).astype(BF16)
    token_value = nt_dot(patches16, embed[...])
    rows8[...] = jnp.zeros(rows8.shape, F32)
    place_value = place[...].astype(F32)
    for f in range(samples):
        value = token_value[f * NTOK : f * NTOK + NTOK] + place_value
        rows8[f : f + 1, :] = jnp.mean(value, axis=0, keepdims=True)
        centered = value - jnp.mean(value, axis=-1, keepdims=True)
        scale = lax.rsqrt(jnp.mean(centered * centered, axis=-1, keepdims=True) + 1e-05)
        value = centered * scale
        normed[f * NTOK : f * NTOK + NTOK, :] = value
        normed16[f * NTOK : f * NTOK + NTOK, :] = value.astype(BF16)
        scales[f * NTOK : f * NTOK + NTOK, :] = jnp.broadcast_to(scale, (NTOK, 128))


def weight_part(pack, i, z):
    source = pack.at[PLACES[i][z]]
    return jnp.concatenate([source[0:256, :], source[320:576, :]], axis=1)


def weight_rest(pack, i):
    return jnp.concatenate(
        [
            jnp.concatenate([pack[PLACES[i][z], 256:320, :], pack[PLACES[i][z], 576:640, :]], axis=1)
            for z in range(NZ)
        ],
        axis=0,
    )


def forward_kernel(
    samples,
    normed16, rows8, outw, packed_ref, head_ref,
    slots, weights, datts_ref, dres_ref, score_ref,
    pack, arrived, abar,
):
    count = samples * NTOK
    copies = [
        [
            pltpu.make_async_copy(packed_ref.at[PLACES[i][z]], pack.at[PLACES[i][z]], arrived.at[i, z])
            for z in range(NZ)
        ]
        for i in range(NT)
    ]
    for some in copies:
        for copy in some:
            copy.start()
    lane_all = lane_iota(count)
    abar[...] = jnp.zeros(abar.shape, F32)
    for i in range(NT):
        for copy in copies[i]:
            copy.wait()
        mixed = nn_dot(
            normed16[...], jnp.concatenate([weight_part(pack, i, z) for z in range(NZ)] + [weight_rest(pack, i)], axis=0)
        )
        first, second = mixed[:, 0:128], mixed[:, 128:256]
        found = (
            first,
            jnp.where(lane_all < 48, pltpu.roll(first, 48, 1), pltpu.roll(second, 48, 1)),
            pltpu.roll(second, 96, 1),
        )
        for m in range(3):
            slots[3 * i + m] = jnp.where(lane_all < HD, found[m], 0.0).astype(BF16)

    for h in range(HEADS):
        for f in range(samples):
            span = slice(f * NTOK, f * NTOK + NTOK)
            logits = nt_dot(slots[h, span, :], slots[HEADS + h, span, :]) * HD ** (-0.5)
            logits = jnp.exp(logits - jnp.max(logits, axis=-1, keepdims=True))
            prob = logits / jnp.sum(logits, axis=-1, keepdims=True)
            weights[h * samples + f] = prob
            attended = nn_dot(prob.astype(BF16), slots[2 * HEADS + h, span, :]).astype(BF16)
            abar[f : f + 1, 128 * h : 128 * h + 128] = jnp.mean(attended.astype(F32), axis=0, keepdims=True)

    part = nn_dot(split_two(abar[...]), outw[...])
    pooled = rows8[...] + part[0:8] + part[8:16]
    pooled = pooled - jnp.mean(pooled, axis=-1, keepdims=True)
    scale = lax.rsqrt(jnp.mean(pooled * pooled, axis=-1, keepdims=True) + 1e-05)
    pooled = pooled * scale
    head = head_ref[...]
    score_ref[...] = jnp.broadcast_to(jnp.sum(pooled * head, axis=-1, keepdims=True), (8, 128))
    dpooled = scale * (
        head - jnp.mean(head, axis=-1, keepdims=True) - pooled * jnp.mean(pooled * head, axis=-1, keepdims=True)
    )
    dres = dpooled * (1.0 / NTOK)
    dres_ref[...] = dres
    datts = nt_dot(split_two(dres), outw[...])
    datts_ref[...] = (datts[0:8] + datts[8:16]).astype(BF16)


def backward_kernel(
    row_count, tiles, samples,
    slots, weights, datts_ref, dres_ref, packed_ref, embed_ref, order_ref, normed_ref, scales,
    out_ref,
    pack, embed, order, normed, arrived, frame, flip, patches, dslots, dnormed, dtokens,
):
    height = row_count * tiles
    patch_rows = height // PATCH
    lane64 = lane_iota(8) < 64
    lane_all = lane_iota(samples * NTOK)
    copies = [
        pltpu.make_async_copy(source, target, arrived.at[at])
        for at, (source, target) in enumerate(
            ((packed_ref, pack), (normed_ref, normed), (embed_ref, embed), (order_ref, order))
        )
    ]
    for copy in copies:
        copy.start()

    for h in range(HEADS):
        datt = datts_ref[:, 128 * h : 128 * h + 128]
        for f in range(samples):
            span = slice(f * NTOK, f * NTOK + NTOK)
            prob = weights[h * samples + f]
            row = datt[f : f + 1, :]
            dweight = nt_dot(datt, slots[2 * HEADS + h, span, :])[f : f + 1, :].astype(BF16).astype(F32)
            inner = jnp.sum(prob * dweight, axis=-1, keepdims=True)
            dlogit = (prob * (dweight - inner) * HD ** (-0.5)).astype(BF16)
            dslots[h, span, :] = nn_dot(dlogit, slots[HEADS + h, span, :])
            dslots[HEADS + h, span, :] = tn_dot(dlogit, slots[h, span, :])
            dslots[2 * HEADS + h, span, :] = tn_dot(
                prob.astype(BF16), jnp.broadcast_to(row.astype(F32), (NTOK, 128)).astype(BF16)
            )

    copies[0].wait()
    parts = []
    for i in range(NT):
        one, two, three = dslots[3 * i], dslots[3 * i + 1], dslots[3 * i + 2]
        two = pltpu.roll(two, 80, 1)
        three = pltpu.roll(three, 32, 1)
        first = jnp.where(lane_all < HD, one, two)
        second = jnp.where(lane_all < 32, two, jnp.where(lane_all < COLS, three, 0.0))
        parts += [first.astype(BF16), second.astype(BF16)]
    dmixed = jnp.concatenate(parts, axis=1)
    for z in range(NZ):
        wide = jnp.concatenate([weight_part(pack, i, z) for i in range(NT)], axis=1)
        dnormed[:, 256 * z : 256 * z + 256] = nt_dot(dmixed, wide)
    wide = jnp.concatenate([weight_rest(pack, i) for i in range(NT)], axis=1)
    dnormed[:, 1024:1280] = nt_dot(dmixed, wide)

    copies[1].wait()
    for f in range(samples):
        span = slice(f * NTOK, f * NTOK + NTOK)
        value, dvalue = normed[span, :], dnormed[span, :]
        scale = scales[span, 0:1]
        dvalue = scale * (
            dvalue
            - jnp.mean(dvalue, axis=-1, keepdims=True)
            - value * jnp.mean(dvalue * value, axis=-1, keepdims=True)
        )
        dtokens[span, :] = (dvalue + dres_ref[f : f + 1, :]).astype(BF16)
    copies[2].wait()
    copies[3].wait()
    patches[...] = nt_dot(nn_dot(dtokens[...], embed[...]).astype(BF16), order[...])

    frame[...] = jnp.zeros(frame.shape, F32)
    flip[...] = jnp.zeros(flip.shape, F32)
    rows = out_ref.shape[3]
    for f in range(samples):
        for pair in range(patch_rows // 2):
            turn = flip.at[f * (patch_rows // 2) + pair]
            token = f * NTOK + pair * 16
            for y in range(PATCH // 2):
                one = patches[token : token + 8, 128 * y : 128 * y + 128]
                two = patches[token + 8 : token + 16, 128 * y : 128 * y + 128]
                turn[1, pl.ds(2 * y, 8, stride=PATCH), :] = jnp.where(lane64, one, pltpu.roll(two, 64, 1))
                turn[1, pl.ds(2 * y + 1, 8, stride=PATCH), :] = jnp.where(lane64, pltpu.roll(one, 64, 1), two)
            turn[0] = turn[1].T
            for local in range(2):
                at = 8 + PATCH * (2 * pair + local)
                for o in range(3):
                    frame[f, o, at : at + PATCH, :] = turn[0, 64 * local + PATCH * o : 64 * local + PATCH * o + PATCH, :]
    for f in range(samples):
        for i in range(tiles):
            at = row_count * i + 7
            for o in range(3):
                out_ref[i, f, o] = frame[f, o, at : at + rows, :].astype(BF16)


def pack_part(rows_in, out_part, place_part, embed_part):
    ordered = jnp.concatenate([rows_in[0:128], rows_in[160:288], rows_in[128:160], rows_in[288:320]], axis=0)
    upper = jnp.pad(ordered[:, 128:240], ((0, 0), (0, 16)))
    other = jnp.concatenate([out_part, place_part], axis=0)
    rest = other[:, 128:160].reshape(4, 48, 32)
    rest = jnp.concatenate([rest[q] for q in range(4)], axis=1)
    embed_part = jnp.pad(embed_part, ((0, 0), (0, 640 - embed_part.shape[1])))
    embed_part = embed_part.reshape(48, 5, 128).transpose(1, 0, 2).reshape(240, 128)
    return jnp.concatenate([ordered[:, 0:128], upper, other[:, 0:128], rest, embed_part], axis=0)


def pack_kernel(z_ref, rows_ref, out_ref, place_ref, embed_ref, first_ref, second_ref):
    for source, target, count in ((0, 0, 128), (160, 128, 128), (128, 256, 32), (288, 288, 32)):
        second_ref[target : target + count, :] = rows_ref[source : source + count, 0:128]
        second_ref[320 + target : 320 + target + count, :] = jnp.concatenate(
            [rows_ref[source : source + count, 128:240], jnp.zeros((count, 16), BF16)], axis=1
        )
    first_ref[0:160, :] = out_ref[:, 0:128]
    first_ref[160:192, :] = place_ref[:, 0:128]
    tail = out_ref[:, 128:160].astype(F32)
    last = place_ref[:, 128:160].astype(F32)
    first_ref[192:240, :] = jnp.concatenate(
        [tail[0:48], tail[48:96], tail[96:144], jnp.concatenate([tail[144:160], last], axis=0)],
        axis=1,
    ).astype(BF16)
    width = embed_ref.shape[1]
    start = pl.multiple_of(jnp.where(z_ref[0] == NZ - 1, STARTS[-1], 48 * z_ref[0]), 16)
    for part in range(5):
        count = min(128, width - 128 * part)
        value = embed_ref[pl.ds(start, 48), 128 * part : 128 * part + count]
        if count < 128:
            value = jnp.concatenate([value, jnp.zeros((48, 128 - count), BF16)], axis=1)
        first_ref[240 + 48 * part : 288 + 48 * part, :] = value


def packed_weights(patch_embed, position, attend_in, attend_out):
    if lax.axis_size(TILE) == NT and lax.axis_size("sample") == NZ:
        z = lax.axis_index("sample").astype(jnp.int32).reshape(1)
        mine = pl.pallas_call(
            pack_kernel,
            in_specs=[pl.BlockSpec(memory_space=pltpu.SMEM)] + [pl.BlockSpec(memory_space=pltpu.VMEM)] * 4,
            out_shape=[jax.ShapeDtypeStruct((rows, 128), BF16) for rows in (PACK - ROWS_IN, ROWS_IN)],
            compiler_params=params(),
            name="pack",
        )(z, attend_in, attend_out, position, patch_embed.T)
        group = [i * NZ + z for i, z in CYCLE]
        return [
            lax.all_gather(value, TILE + ("sample",), axis=0, axis_index_groups=[group])
            for value in mine
        ]

    def whole(value):
        value = lax.all_gather(value, "sample", axis=0, tiled=True)
        return lax.all_gather(value, TILE, axis=1, tiled=True)

    split = [
        value.reshape(NZ, value.shape[0] // NZ, NT, value.shape[1] // NT).transpose(2, 0, 1, 3)
        for value in (whole(attend_in), whole(attend_out), whole(position))
    ]
    columns = lax.all_gather(patch_embed.T, TILE, axis=0, tiled=True).reshape(NT, D // NT, -1)
    split.append(jnp.stack([columns[:, start : start + 48] for start in STARTS], axis=1))
    packed = jax.vmap(jax.vmap(pack_part))(*split)
    packed = jnp.stack([packed[i, z] for i, z in CYCLE])
    return packed[:, ROWS_IN:], packed[:, :ROWS_IN]


def params(mib=58):
    return pltpu.CompilerParams(vmem_limit_bytes=mib * 1024 * 1024)


def local(
    features,
    norm_gain,
    conv_weight,
    patch_embed,
    position,
    attend_in,
    attend_out,
    reward_head,
    group_index,
    frame_pick,
):
    samples, frames, row_count, merged = features.shape
    tiles, parts = lax.axis_size(TILE), lax.axis_size("sample")
    sent_rows = -(-(row_count + 2) // 16) * 16
    row_block = row_count if row_count <= 14 else 14
    blocks = row_count // row_block
    inner = row_block * CH
    packed, packed_in = packed_weights(patch_embed, position, attend_in, attend_out)
    order = Layout((1, 2, 3, 0, 4))
    split = (samples, frames, row_count, merged // 128, 128)
    view = with_layout_constraint(features.reshape(split), order).transpose(1, 2, 3, 0, 4)
    view = view.reshape(frames, row_count, samples * merged // 128, 128)
    gain = norm_gain[None, :]

    smem = pl.BlockSpec(memory_space=pltpu.SMEM)
    view_spec = pl.BlockSpec((1,) + view.shape[1:], lambda t: (t, 0, 0, 0))
    gain_spec = pl.BlockSpec((1, CH), lambda t: (0, 0))
    taps_spec = pl.BlockSpec((3, 3, 3, 3, CH), lambda t: (0, 0, 0, 0, 0))
    sent = (SCORED, samples, 3, sent_rows, 128)
    sent_spec = pl.BlockSpec(sent, lambda t: (0, 0, 0, 0, 0))
    aligned = (frames, row_count, samples, CH, 128)
    aligned_spec = pl.BlockSpec((1,) + aligned[1:], lambda t: (t, 0, 0, 0, 0))
    inv_spec = pl.BlockSpec((1, row_count, samples, 128), lambda t: (t, 0, 0, 0))
    band_spec = pl.BlockSpec((inner, OUT_ROWS), lambda t: (0, 0))
    decoded, x_aligned, inverse, slopes, band = pl.pallas_call(
        functools.partial(decode_kernel, row_block),
        grid=(frames,),
        in_specs=[smem, view_spec, gain_spec, taps_spec],
        out_specs=[sent_spec, aligned_spec, inv_spec, aligned_spec, band_spec],
        scratch_shapes=[
            pltpu.VMEM((OUT_ROWS, inner), BF16),
            pltpu.VMEM((3, 32, CH), F32),
            pltpu.VMEM((128, 128), F32),
            pltpu.VMEM((row_block, 192, 128), F32),
            pltpu.VMEM((blocks, inner, 256), BF16),
            pltpu.VMEM((blocks, 3, samples, 48, 128), F32),
            pltpu.VMEM((sent_rows + 16, 128), F32),
        ],
        out_shape=[
            jax.ShapeDtypeStruct(sent, BF16),
            jax.ShapeDtypeStruct(aligned, BF16),
            jax.ShapeDtypeStruct((frames, row_count, samples, 128), F32),
            jax.ShapeDtypeStruct(aligned, BF16),
            jax.ShapeDtypeStruct((inner, OUT_ROWS), BF16),
        ],
        compiler_params=params(),
        name="decode",
    )(frame_pick, view, gain, conv_weight)

    if tiles > SCORED:
        decoded = jnp.pad(decoded, ((0, tiles - SCORED),) + ((0, 0),) * 4)
    owned = lax.all_to_all(decoded, TILE, split_axis=0, concat_axis=0, tiled=True)

    head = reward_head.reshape(NT, D // NT)
    head = jnp.concatenate([head[:, :128].reshape(-1), head[:, 128:].reshape(-1)])[None, :]
    height = row_count * tiles
    count = samples * NTOK
    vmem = pl.BlockSpec(memory_space=pltpu.VMEM)
    hbm = pl.BlockSpec(memory_space=pl.ANY)
    frame_scratch = pltpu.VMEM((samples, 3, height + 48, 128), F32)
    flip_scratch = pltpu.VMEM((samples * height // (2 * PATCH), 2, 128, 128), F32)
    normed, normed16, scales, means, embed, outw, inputs = pl.pallas_call(
        functools.partial(token_kernel, row_count, tiles, samples),
        out_shape=[
            jax.ShapeDtypeStruct((count, D), F32),
            jax.ShapeDtypeStruct((count, D), BF16),
            jax.ShapeDtypeStruct((count, 128), F32),
            jax.ShapeDtypeStruct((8, D), F32),
            jax.ShapeDtypeStruct((D, 640), BF16),
            jax.ShapeDtypeStruct((HEADS * 128, D), BF16),
            jax.ShapeDtypeStruct((KIN, 640), BF16),
        ],
        scratch_shapes=[frame_scratch, flip_scratch, pltpu.VMEM((NTOK, D), BF16), pltpu.VMEM((count, KIN), F32)],
        compiler_params=params(),
        name="tokens",
    )(owned, packed)
    slots, weights, datts, dres, scores = pl.pallas_call(
        functools.partial(forward_kernel, samples),
        out_shape=[
            jax.ShapeDtypeStruct((3 * HEADS, count, 128), BF16),
            jax.ShapeDtypeStruct((HEADS * samples, NTOK, NTOK), F32),
            jax.ShapeDtypeStruct((8, HEADS * 128), BF16),
            jax.ShapeDtypeStruct((8, D), F32),
            jax.ShapeDtypeStruct((8, 128), F32),
        ],
        in_specs=[vmem, vmem, vmem, hbm, vmem],
        scratch_shapes=[
            pltpu.VMEM(packed_in.shape, BF16),
            pltpu.SemaphoreType.DMA((NT, NZ)),
            pltpu.VMEM((8, HEADS * 128), F32),
        ],
        compiler_params=params(),
        name="forward",
    )(normed16, means, outw, packed_in, head)
    grads = pl.pallas_call(
        functools.partial(backward_kernel, row_count, tiles, samples),
        out_shape=jax.ShapeDtypeStruct((tiles, samples, 3, sent_rows, 128), BF16),
        in_specs=[vmem, vmem, vmem, vmem, hbm, hbm, hbm, hbm, vmem],
        scratch_shapes=[
            pltpu.VMEM(packed_in.shape, BF16),
            pltpu.VMEM((D, 640), BF16),
            pltpu.VMEM((KIN, 640), BF16),
            pltpu.VMEM((count, D), F32),
            pltpu.SemaphoreType.DMA((4,)),
            frame_scratch,
            flip_scratch,
            pltpu.VMEM((count, KIN), F32),
            pltpu.VMEM((3 * HEADS, count, 128), F32),
            pltpu.VMEM((count, D), F32),
            pltpu.VMEM((count, D), BF16),
        ],
        compiler_params=params(),
        name="backward",
    )(slots, weights, datts, dres, packed_in, embed, inputs, normed, scales)

    mine = jnp.concatenate([scores[:samples, 0], group_index.astype(F32)])
    mine = jnp.broadcast_to(mine[None], (tiles * parts, 2 * samples))
    everyone = lax.all_to_all(mine, TILE + ("sample",), split_axis=0, concat_axis=0, tiled=True)
    everyone = everyone.reshape(tiles, parts, 2, samples)
    returned = lax.all_to_all(grads, TILE, split_axis=0, concat_axis=0, tiled=True)
    returned = returned[:SCORED]

    rewards = jnp.sum(everyone[:SCORED, :, 0], axis=0).reshape(-1) / SCORED
    groups = everyone[0, :, 1].reshape(-1)
    here = (lax.axis_index("sample") * samples).astype(jnp.int32)
    own_rewards = lax.dynamic_slice_in_dim(rewards, here, samples)
    own_groups = lax.dynamic_slice_in_dim(groups, here, samples)
    member = (own_groups[:, None] == groups[None, :]).astype(F32)
    mean_group = jnp.sum(member * rewards[None, :], axis=1) / GROUP
    second_group = jnp.sum(member * (rewards * rewards)[None, :], axis=1) / GROUP - mean_group * mean_group
    advantage = (own_rewards - mean_group) * lax.rsqrt(second_group + SMOOTH)
    cotangent = -LOSS_SCALE * advantage / SCORED

    result = pl.pallas_call(
        functools.partial(restore_kernel, row_block),
        grid=(frames,),
        in_specs=[smem, smem, aligned_spec, inv_spec, aligned_spec, band_spec, sent_spec],
        out_specs=view_spec,
        scratch_shapes=[
            pltpu.VMEM((row_block, samples * merged // 128, 128), F32),
            pltpu.VMEM((frames + 2, blocks, 144, 256), BF16),
            pltpu.VMEM((blocks, inner, 256), F32),
        ],
        out_shape=jax.ShapeDtypeStruct(view.shape, BF16),
        compiler_params=params(),
        name="restore",
    )(frame_pick, cotangent, x_aligned, inverse, slopes, band, returned)
    result = result.reshape(frames, row_count, merged // 128, samples, 128).transpose(3, 0, 1, 2, 4)
    return with_layout_constraint(result, order).reshape(features.shape)


def solution(mesh):
    tiles, parts = mesh.devices.shape
    split = Mesh(mesh.devices.reshape(tiles // 2, 2, parts), ("chip", "core", "sample"))
    in_specs = (
        P("sample", None, TILE, None),
        P(),
        P(),
        P(None, TILE),
        P("sample", TILE),
        P("sample", TILE),
        P("sample", TILE),
        P(),
        P("sample"),
        P("sample", None),
    )
    out_specs = P("sample", None, TILE, None)
    return jax.shard_map(local, mesh=split, in_specs=in_specs, out_specs=out_specs, check_vma=False)
```

```python
import functools

import jax
import jax.numpy as jnp
from jax import lax
from jax.experimental import pallas as pl
from jax.experimental.pallas import tpu as pltpu
from jax.experimental.layout import Layout, with_layout_constraint
from jax.sharding import Mesh, PartitionSpec as P

SCORED = 8
PATCH = 14
HEADS = 8
HD = 80
GROUP = 4
LOSS_SCALE = 16384.0
SMOOTH = 0.01

TILE = ("chip", "core")
CH = 96
COLS = 112
SPANS = CH // 8
OUT_ROWS = 27 * 16
BACK = 6
BACK_ROWS = 3 * 80
NT = 8
NZ = 4
PACK = 1120
CYCLE = [
    (2 * chip + core, z)
    for chip, heights in ((0, (0, 1, 2, 3)), (1, (3, 2, 1, 0)), (3, (0, 1, 2, 3)), (2, (3, 2, 1, 0)))
    for z in heights
    for core in range(2)
]
PLACES = [[CYCLE.index((i, z)) for z in range(NZ)] for i in range(NT)]
STARTS = (0, 48, 96, 112)
KIN = 896
D = 1280
NTOK = 128
F32 = jnp.float32
BF16 = jnp.bfloat16


def lane_iota(rows):
    return lax.broadcasted_iota(jnp.int32, (rows, 128), 1)


def sub_iota(rows):
    return lax.broadcasted_iota(jnp.int32, (rows, 128), 0)


def channels_of(raw, at, group, sample):
    start = 8 + 14 * group + sample
    here = raw[at, pl.ds(start, 8, stride=2), :]
    before = raw[at, pl.ds(start - 2, 8, stride=2), :]
    joined = jnp.where(lane_iota(8) < 128 - 16 * sub_iota(8), here, before)
    return pltpu.roll(joined, 0, 1, stride=16, stride_axis=0)


def tiles_of(value):
    turned = jnp.take_along_axis(value, (lane_iota(8) + 16 * sub_iota(8)) % 128, axis=1)
    return jnp.where(lane_iota(8) < COLS - 16 * sub_iota(8), turned, pltpu.roll(turned, 7, 0))


def load_taps(weight_ref, taps):
    taps[...] = jnp.zeros(taps.shape, F32)
    for a in range(3):
        for b in range(3):
            for e in range(3):
                for o in range(3):
                    at = (a * 3 + e) * 3 + o
                    taps[b, at : at + 1, :] = weight_ref[a, b, e, o : o + 1, :].astype(F32)


def row_of(shape, dim):
    at = lax.broadcasted_iota(jnp.int32, shape, dim)
    return ((at.astype(F32) + 0.5) * (1.0 / CH)).astype(jnp.int32)


def banded(taps, row_block):
    inner = row_block * CH
    pick = (
        lax.broadcasted_iota(jnp.int32, (OUT_ROWS, 32), 0) // 16
        == lax.broadcasted_iota(jnp.int32, (OUT_ROWS, 32), 1)
    ).astype(BF16)
    at = lax.broadcasted_iota(jnp.int32, (CH, inner), 1) - CH * row_of((CH, inner), 1)
    grow = (at == lax.broadcasted_iota(jnp.int32, (CH, inner), 0)).astype(BF16)
    shape = (OUT_ROWS, inner)
    p_at = lax.broadcasted_iota(jnp.int32, shape, 0) % 16
    r_at = row_of(shape, 1)
    total = jnp.zeros(shape, F32)
    for b in range(3):
        rows = nn_dot(pick, taps[b].astype(BF16)).astype(BF16)
        total = jnp.where(p_at == r_at + 2 - b, nn_dot(rows, grow), total)
    return total.astype(BF16)


def banded_back(taps):
    inner = BACK * CH

    def column_of(shape, dim):
        at = lax.broadcasted_iota(jnp.int32, shape, dim)
        a = (at >= 80).astype(jnp.int32) + (at >= 160).astype(jnp.int32)
        return a, at - 80 * a

    a, rest = column_of((BACK_ROWS, 32), 0)
    tap = jnp.where(rest // 8 < 9, 9 * a + rest // 8, 31)
    pick = (tap == lax.broadcasted_iota(jnp.int32, (BACK_ROWS, 32), 1)).astype(BF16)
    at = lax.broadcasted_iota(jnp.int32, (inner, CH), 0) - CH * row_of((inner, CH), 0)
    grow = (at == lax.broadcasted_iota(jnp.int32, (inner, CH), 1)).astype(BF16)
    shape = (inner, BACK_ROWS)
    p_at = column_of(shape, 1)[1] % 8
    r_at = row_of(shape, 0)
    total = jnp.zeros(shape, F32)
    for b in range(3):
        rows = nn_dot(pick, taps[b].astype(BF16)).astype(BF16)
        total = jnp.where(p_at == r_at + 2 - b, nt_dot(grow, rows), total)
    return total.astype(BF16)


def half_gains(gain_ref):
    rows = jnp.concatenate([gain_ref[0:1, :], jnp.zeros((1, 128 - CH), F32)], axis=1)
    return 0.5 * jnp.broadcast_to(rows, (128, 128)).T


def entry_of(pick_ref, sample, frame):
    found = jnp.int32(-1)
    for j in range(SCORED):
        found = jnp.where(pick_ref[sample, j] == frame, jnp.int32(j), found)
    return found


def decode_kernel(row_block, pick_ref, x_ref, gain_ref, weight_ref, out_ref, x_out, slope_out, turned_out, band, taps, gains, raw, operand, acc, final):
    t = pl.program_id(0)
    blocks = x_ref.shape[1] // row_block
    rows = out_ref.shape[3]

    @pl.when(t == 0)
    def _():
        load_taps(weight_ref, taps)
        band[...] = banded(taps, row_block)
        turned_out[...] = banded_back(taps)
        gains[...] = half_gains(gain_ref)
        acc[...] = jnp.zeros(acc.shape, F32)
        raw[...] = jnp.zeros(raw.shape, F32)

    for k in range(blocks):

        def one_row(row, at):
            raw[at, 8:176, :] = x_ref[0, k * row_block + row].astype(F32)
            for s in range(2):
                found = [channels_of(raw, at, g, s) for g in range(SPANS)]
                square = found[0] * found[0]
                for g in range(1, SPANS):
                    square = square + found[g] * found[g]
                second = jnp.sum(square, axis=0, keepdims=True) * (1.0 / CH)
                inv = lax.rsqrt(second + 1e-06)
                for m in range(SPANS // 2):
                    x_out[0, k * row_block + row, s, 16 * m : 16 * m + 16, :] = jnp.concatenate(
                        [found[2 * m] * inv, found[2 * m + 1] * inv], axis=0
                    ).astype(BF16)
                    acts, slopes = [], []
                    for g in (2 * m, 2 * m + 1):
                        gain = gains[8 * g : 8 * g + 8, :]
                        half = found[g] * inv * gain
                        th = jnp.tanh(half)
                        rest = half - half * th
                        acts.append(half + half * th)
                        slopes.append((gain * inv) * (1.0 + th) * (1.0 + rest))
                    slope_out[0, k * row_block + row, s, 16 * m : 16 * m + 16, :] = jnp.concatenate(
                        slopes, axis=0
                    ).astype(BF16)
                    start = row * CH + 16 * m
                    operand[k, start : start + 16, 128 * s : 128 * s + 128] = jnp.concatenate(
                        acts, axis=0
                    ).astype(BF16)

        for row in range(row_block):
            one_row(row, row)
        spread = jnp.dot(band[...], operand[k], preferred_element_type=F32)
        lane = lane_iota(48)
        for s in range(2):
            part = spread[:, 128 * s : 128 * s + 128]
            for a in range(3):
                low, mid, high = (part[144 * a + 48 * e : 144 * a + 48 * e + 48] for e in range(3))
                low = jnp.where(lane == 0, 0.0, pltpu.roll(low, 1, 1))
                high = jnp.where(lane == COLS - 1, 0.0, pltpu.roll(high, 127, 1))
                acc[k, 2 - a, s] += low + mid + high

    keep = lane_iota(rows) < COLS
    for s in range(2):
        entry = entry_of(pick_ref, s, t)

        @pl.when(entry >= 0)
        def _():
            for o in range(3):
                final[...] = jnp.zeros(final.shape, F32)
                for k in range(blocks):
                    start = k * row_block
                    final[start : start + 16, :] += acc[k, 0, s, 16 * o : 16 * o + 16, :]
                out_ref[jnp.maximum(entry, 0), s, o] = jnp.where(keep, final[0:rows, :], 0.0).astype(BF16)

    for k in range(blocks):
        acc[k, 0] = acc[k, 1]
        acc[k, 1] = acc[k, 2]
        acc[k, 2] = jnp.zeros(acc.shape[2:], F32)


def restore_kernel(pick_ref, scale_ref, x_ref, slope_ref, band, grad_ref, out_ref, back, shifted, coming):
    t = pl.program_id(0)
    frames = pl.num_programs(0)
    row_count = x_ref.shape[1]
    starts = range(0, row_count, BACK)
    rows = grad_ref.shape[3]

    @pl.when(t == 0)
    def _():
        shifted[...] = jnp.zeros(shifted.shape, BF16)
        lane = lane_iota(rows)
        blank = jnp.zeros((8, 128), F32)

        def one_frame(frame, carry):
            for s in range(2):
                entry = entry_of(pick_ref, s, frame)
                scale = jnp.where(entry >= 0, scale_ref[s], 0.0)
                source = jnp.maximum(entry, 0)
                moved = [[], [], []]
                for o in range(3):
                    value = grad_ref[source, s, o].astype(F32) * scale
                    value = jnp.where(lane < COLS, value, 0.0)
                    for e, turned in enumerate((pltpu.roll(value, 127, 1), value, pltpu.roll(value, 1, 1))):
                        moved[e].append(turned)
                for k, start in enumerate(starts):
                    block = [turned[start : start + 8] for some in moved for turned in some]
                    shifted[frame, k, :, 128 * s : 128 * s + 128] = jnp.concatenate(
                        block + [blank], axis=0
                    ).astype(BF16)
            return carry

        lax.fori_loop(0, frames, one_frame, 0)

    for k, start in enumerate(starts):
        count = min(BACK, row_count - start)
        operand = jnp.concatenate([shifted[t + 2 - a, k] for a in range(3)], axis=0)
        coming[k, 0 : count * CH, :] = nn_dot(band[0 : count * CH, :], operand)
        for local in range(count):
            row = start + local
            for s in range(2):
                outs, units, total = [], [], None
                for m in range(SPANS // 2):
                    pair = x_ref[0, row, s, 16 * m : 16 * m + 16, :].astype(F32)
                    slopes = slope_ref[0, row, s, 16 * m : 16 * m + 16, :].astype(F32)
                    for part in range(2):
                        g = 2 * m + part
                        unit = pair[8 * part : 8 * part + 8]
                        at = local * CH + 8 * g
                        out = coming[k, at : at + 8, 128 * s : 128 * s + 128] * slopes[8 * part : 8 * part + 8]
                        outs.append(out)
                        units.append(unit)
                        total = out * unit if g == 0 else total + out * unit
                factor = jnp.sum(total, axis=0, keepdims=True) * (1.0 / CH)
                for g in range(SPANS):
                    result = tiles_of(outs[g] - units[g] * factor)
                    back[row % back.shape[0], pl.ds(14 * g + s, 7, stride=2), :] = result[0:7]
            out_ref[0, row] = back[row % back.shape[0]].astype(BF16)


def nt_dot(one, two):
    return lax.dot_general(one, two, (((1,), (1,)), ((), ())), preferred_element_type=F32)


def tn_dot(one, two):
    return lax.dot_general(one, two, (((0,), (0,)), ((), ())), preferred_element_type=F32)


def nn_dot(one, two):
    return jnp.dot(one, two, preferred_element_type=F32)


def split_two(value):
    high = value.astype(BF16)
    low = (value - high.astype(F32)).astype(BF16)
    return jnp.concatenate([high, low], axis=0)


def patch_kernel(row_count, tiles, samples, part_ref, inputs_ref, order, frame, flip, patches):
    height = row_count * tiles
    patch_rows = height // PATCH
    lane64 = lane_iota(8) < 64
    inputs = order.shape[1]
    pixel = lax.broadcasted_iota(jnp.int32, (64, inputs), 0)
    column = lax.broadcasted_iota(jnp.int32, (64, inputs), 1)
    for x in range(PATCH):
        order[64 * x : 64 * x + 64, :] = (
            (column == pixel * PATCH + x) & (pixel < 3 * PATCH)
        ).astype(BF16)

    flip[...] = jnp.zeros(flip.shape, F32)
    frame[...] = jnp.zeros(frame.shape, F32)
    for f in range(samples):
        for i in range(tiles):
            at = row_count * i + 7
            for o in range(3):
                frame[f, o, at : at + row_count + 2, :] += part_ref[i, f, o, 0 : row_count + 2, :].astype(F32)
    for f in range(samples):
        for pair in range(patch_rows // 2):
            turn = flip.at[f * (patch_rows // 2) + pair]
            for local in range(2):
                at = 8 + PATCH * (2 * pair + local)
                for o in range(3):
                    turn[0, 64 * local + PATCH * o : 64 * local + PATCH * o + PATCH, :] = (
                        frame[f, o, at : at + PATCH, :].astype(BF16).astype(F32)
                    )
            turn[1] = turn[0].T
            token = f * NTOK + pair * 16
            for y in range(PATCH // 2):
                even = turn[1, pl.ds(2 * y, 8, stride=PATCH), :]
                odd = turn[1, pl.ds(2 * y + 1, 8, stride=PATCH), :]
                patches[token : token + 8, 128 * y : 128 * y + 128] = jnp.where(lane64, even, pltpu.roll(odd, 64, 1))
                patches[token + 8 : token + 16, 128 * y : 128 * y + 128] = jnp.where(lane64, pltpu.roll(even, 64, 1), odd)

    inputs_ref[...] = nn_dot(patches[...].astype(BF16), order[...]).astype(BF16)


def reward_kernel(
    row_count, tiles, samples,
    inputs_ref, order, packed_ref, head_ref,
    out_ref, score_ref,
    pack, arrived, frame, flip, embed, outw, place, patches, tokens, normed, normed16, slots, weights, dslots, dnormed, rows8, abar,
):
    height = row_count * tiles
    patch_rows = height // PATCH
    lane64 = lane_iota(8) < 64
    lane = lane_iota(NTOK)
    count = samples * NTOK

    copies = []
    for part, (begin, end) in enumerate(((880, 1120), (640, 880), (0, 640))):
        copies.append(
            pltpu.make_async_copy(
                packed_ref.at[:, begin:end, :], pack.at[:, begin:end, :], arrived.at[part]
            )
        )
        copies[-1].start()

    flip[...] = jnp.zeros(flip.shape, F32)
    copies[0].wait()
    copies[1].wait()

    for i in range(NT):
        for z, (begin, height, target) in enumerate(
            ((0, 48, 128 * i), (0, 48, 128 * i + 48), (0, 32, 128 * i + 96), (16, 32, 1024 + 32 * i))
        ):
            source = pack.at[PLACES[i][z]]
            for part in range(5):
                at = 880 + 48 * part + begin
                embed[target : target + height, 128 * part : 128 * part + 128] = source[at : at + height, :]
    lane48 = lane_iota(48)
    for h in range(HEADS):
        outw[128 * h + HD : 128 * h + 128, :] = jnp.zeros((128 - HD, D), BF16)
    for z in range(NZ):
        for i in range(NT):
            source = pack.at[PLACES[i][z]]
            for local in range(2):
                at, begin = 128 * (2 * z + local), 640 + HD * local
                outw[at : at + HD, 128 * i : 128 * i + 128] = source[begin : begin + HD, :]
            place[32 * z : 32 * z + 32, 128 * i : 128 * i + 128] = source[800:832, :]
        for ib in range(2):
            sources = [pack[PLACES[4 * ib + j][z], 832:880, :].astype(F32) for j in range(4)]
            rolled = [[sources[j] if d == 0 else pltpu.roll(sources[j], 32 * d, 1) for d in range(4)] for j in range(4)]
            at = 1024 + 128 * ib
            for q in range(4):
                found = rolled[0][(0 - q) % 4]
                for j in range(1, 4):
                    found = jnp.where(lane48 >= 32 * j, rolled[j][(j - q) % 4], found)
                found = found.astype(BF16)
                for begin, end, row in (
                    ((0, 48, 0),),
                    ((0, 32, 48), (32, 48, 128)),
                    ((0, 48, 144),),
                    ((0, 16, 192),),
                )[q]:
                    row = 256 * z + row
                    outw[row : row + end - begin, at : at + 128] = found[begin:end]
                if q == 3:
                    place[32 * z : 32 * z + 32, at : at + 128] = found[16:48]

    token_value = nt_dot(inputs_ref[...], embed[...])
    rows8[...] = jnp.zeros(rows8.shape, F32)
    abar[...] = jnp.zeros(abar.shape, F32)
    place_value = place[...].astype(F32)
    for f in range(samples):
        value = token_value[f * NTOK : f * NTOK + NTOK] + place_value
        rows8[0, f : f + 1, :] = jnp.mean(value, axis=0, keepdims=True)
        centered = value - jnp.mean(value, axis=-1, keepdims=True)
        scale = lax.rsqrt(jnp.mean(centered * centered, axis=-1, keepdims=True) + 1e-05)
        value = centered * scale
        normed[f * NTOK : f * NTOK + NTOK, :] = value
        normed16[f * NTOK : f * NTOK + NTOK, :] = value.astype(BF16)
        tokens[f * NTOK : f * NTOK + NTOK, :] = jnp.broadcast_to(scale, (NTOK, 128))

    def weight_part(i, z):
        source = pack.at[PLACES[i][z]]
        return jnp.concatenate([source[0:256, :], source[320:576, :]], axis=1)

    def weight_rest(i):
        return jnp.concatenate(
            [
                jnp.concatenate([pack[PLACES[i][z], 256:320, :], pack[PLACES[i][z], 576:640, :]], axis=1)
                for z in range(NZ)
            ],
            axis=0,
        )

    lane_all = lane_iota(count)
    copies[2].wait()
    for i in range(NT):
        mixed = nn_dot(
            normed16[...], jnp.concatenate([weight_part(i, z) for z in range(NZ)] + [weight_rest(i)], axis=0)
        )
        first, second = mixed[:, 0:128], mixed[:, 128:256]
        found = (
            first,
            jnp.where(lane_all < 48, pltpu.roll(first, 48, 1), pltpu.roll(second, 48, 1)),
            pltpu.roll(second, 96, 1),
        )
        for m in range(3):
            slots[3 * i + m] = jnp.where(lane_all < HD, found[m], 0.0).astype(BF16)

    for h in range(HEADS):
        for f in range(samples):
            span = slice(f * NTOK, f * NTOK + NTOK)
            logits = nt_dot(slots[h, span, :], slots[HEADS + h, span, :]) * HD ** (-0.5)
            logits = jnp.exp(logits - jnp.max(logits, axis=-1, keepdims=True))
            prob = logits / jnp.sum(logits, axis=-1, keepdims=True)
            weights[h * samples + f] = prob
            attended = nn_dot(prob.astype(BF16), slots[2 * HEADS + h, span, :]).astype(BF16)
            abar[f : f + 1, 128 * h : 128 * h + 128] = jnp.mean(attended.astype(F32), axis=0, keepdims=True)

    part = nn_dot(split_two(abar[...]), outw[...])
    pooled = rows8[0] + part[0:8] + part[8:16]
    pooled = pooled - jnp.mean(pooled, axis=-1, keepdims=True)
    scale = lax.rsqrt(jnp.mean(pooled * pooled, axis=-1, keepdims=True) + 1e-05)
    pooled = pooled * scale
    head = head_ref[...]
    score_ref[...] = jnp.broadcast_to(jnp.sum(pooled * head, axis=-1, keepdims=True), (8, 128))
    dpooled = scale * (
        head - jnp.mean(head, axis=-1, keepdims=True) - pooled * jnp.mean(pooled * head, axis=-1, keepdims=True)
    )
    dres = dpooled * (1.0 / NTOK)
    rows8[1] = dres
    datts = nt_dot(split_two(dres), outw[...])
    datts = (datts[0:8] + datts[8:16]).astype(BF16)

    for h in range(HEADS):
        datt = datts[:, 128 * h : 128 * h + 128]
        for f in range(samples):
            span = slice(f * NTOK, f * NTOK + NTOK)
            prob = weights[h * samples + f]
            row = datt[f : f + 1, :]
            dweight = nt_dot(datt, slots[2 * HEADS + h, span, :])[f : f + 1, :].astype(BF16).astype(F32)
            inner = jnp.sum(prob * dweight, axis=-1, keepdims=True)
            dlogit = (prob * (dweight - inner) * HD ** (-0.5)).astype(BF16)
            dslots[h, span, :] = nn_dot(dlogit, slots[HEADS + h, span, :])
            dslots[HEADS + h, span, :] = tn_dot(dlogit, slots[h, span, :])
            dslots[2 * HEADS + h, span, :] = tn_dot(
                prob.astype(BF16), jnp.broadcast_to(row.astype(F32), (NTOK, 128)).astype(BF16)
            )

    parts = []
    for i in range(NT):
        one, two, three = dslots[3 * i], dslots[3 * i + 1], dslots[3 * i + 2]
        two = pltpu.roll(two, 80, 1)
        three = pltpu.roll(three, 32, 1)
        first = jnp.where(lane_all < HD, one, two)
        second = jnp.where(lane_all < 32, two, jnp.where(lane_all < COLS, three, 0.0))
        parts += [first.astype(BF16), second.astype(BF16)]
    dmixed = jnp.concatenate(parts, axis=1)
    for z in range(NZ):
        wide = jnp.concatenate([weight_part(i, z) for i in range(NT)], axis=1)
        dnormed[:, 256 * z : 256 * z + 256] = nt_dot(dmixed, wide)
    wide = jnp.concatenate([weight_rest(i) for i in range(NT)], axis=1)
    dnormed[:, 1024:1280] = nt_dot(dmixed, wide)

    for f in range(samples):
        span = slice(f * NTOK, f * NTOK + NTOK)
        value, dvalue = normed[span, :], dnormed[span, :]
        scale = tokens[span, 0:1]
        dvalue = scale * (
            dvalue
            - jnp.mean(dvalue, axis=-1, keepdims=True)
            - value * jnp.mean(dvalue * value, axis=-1, keepdims=True)
        )
        normed16[span, :] = (dvalue + rows8[1, f : f + 1, :]).astype(BF16)
    patches[...] = nt_dot(nn_dot(normed16[...], embed[...]).astype(BF16), order[...])

    frame[...] = jnp.zeros(frame.shape, F32)
    rows = out_ref.shape[3]
    for f in range(samples):
        for pair in range(patch_rows // 2):
            turn = flip.at[f * (patch_rows // 2) + pair]
            token = f * NTOK + pair * 16
            for y in range(PATCH // 2):
                one = patches[token : token + 8, 128 * y : 128 * y + 128]
                two = patches[token + 8 : token + 16, 128 * y : 128 * y + 128]
                turn[1, pl.ds(2 * y, 8, stride=PATCH), :] = jnp.where(lane64, one, pltpu.roll(two, 64, 1))
                turn[1, pl.ds(2 * y + 1, 8, stride=PATCH), :] = jnp.where(lane64, pltpu.roll(one, 64, 1), two)
            turn[0] = turn[1].T
            for local in range(2):
                at = 8 + PATCH * (2 * pair + local)
                for o in range(3):
                    frame[f, o, at : at + PATCH, :] = turn[0, 64 * local + PATCH * o : 64 * local + PATCH * o + PATCH, :]
    for f in range(samples):
        for i in range(tiles):
            at = row_count * i + 7
            for o in range(3):
                out_ref[i, f, o] = frame[f, o, at : at + rows, :].astype(BF16)


def pack_part(rows_in, out_part, place_part, embed_part):
    ordered = jnp.concatenate([rows_in[0:128], rows_in[160:288], rows_in[128:160], rows_in[288:320]], axis=0)
    upper = jnp.pad(ordered[:, 128:240], ((0, 0), (0, 16)))
    other = jnp.concatenate([out_part, place_part], axis=0)
    rest = other[:, 128:160].reshape(4, 48, 32)
    rest = jnp.concatenate([rest[q] for q in range(4)], axis=1)
    embed_part = jnp.pad(embed_part, ((0, 0), (0, 640 - embed_part.shape[1])))
    embed_part = embed_part.reshape(48, 5, 128).transpose(1, 0, 2).reshape(240, 128)
    return jnp.concatenate([ordered[:, 0:128], upper, other[:, 0:128], rest, embed_part], axis=0)


def pack_kernel(z_ref, rows_ref, out_ref, place_ref, embed_ref, packed_ref):
    for source, target, count in ((0, 0, 128), (160, 128, 128), (128, 256, 32), (288, 288, 32)):
        packed_ref[target : target + count, :] = rows_ref[source : source + count, 0:128]
        packed_ref[320 + target : 320 + target + count, :] = jnp.concatenate(
            [rows_ref[source : source + count, 128:240], jnp.zeros((count, 16), BF16)], axis=1
        )
    packed_ref[640:800, :] = out_ref[:, 0:128]
    packed_ref[800:832, :] = place_ref[:, 0:128]
    tail = out_ref[:, 128:160].astype(F32)
    last = place_ref[:, 128:160].astype(F32)
    packed_ref[832:880, :] = jnp.concatenate(
        [tail[0:48], tail[48:96], tail[96:144], jnp.concatenate([tail[144:160], last], axis=0)],
        axis=1,
    ).astype(BF16)
    width = embed_ref.shape[1]
    start = pl.multiple_of(jnp.where(z_ref[0] == NZ - 1, STARTS[-1], 48 * z_ref[0]), 16)
    for part in range(5):
        count = min(128, width - 128 * part)
        value = embed_ref[pl.ds(start, 48), 128 * part : 128 * part + count]
        if count < 128:
            value = jnp.concatenate([value, jnp.zeros((48, 128 - count), BF16)], axis=1)
        packed_ref[880 + 48 * part : 928 + 48 * part, :] = value


def packed_weights(patch_embed, position, attend_in, attend_out):
    if lax.axis_size(TILE) == NT and lax.axis_size("sample") == NZ:
        z = lax.axis_index("sample").astype(jnp.int32).reshape(1)
        mine = pl.pallas_call(
            pack_kernel,
            in_specs=[pl.BlockSpec(memory_space=pltpu.SMEM)] + [pl.BlockSpec(memory_space=pltpu.VMEM)] * 4,
            out_shape=jax.ShapeDtypeStruct((PACK, 128), BF16),
            compiler_params=params(),
            name="pack",
        )(z, attend_in, attend_out, position, patch_embed.T)
        group = [i * NZ + z for i, z in CYCLE]
        return lax.all_gather(mine, TILE + ("sample",), axis=0, axis_index_groups=[group])

    def whole(value):
        value = lax.all_gather(value, "sample", axis=0, tiled=True)
        return lax.all_gather(value, TILE, axis=1, tiled=True)

    split = [
        value.reshape(NZ, value.shape[0] // NZ, NT, value.shape[1] // NT).transpose(2, 0, 1, 3)
        for value in (whole(attend_in), whole(attend_out), whole(position))
    ]
    columns = lax.all_gather(patch_embed.T, TILE, axis=0, tiled=True).reshape(NT, D // NT, -1)
    split.append(jnp.stack([columns[:, start : start + 48] for start in STARTS], axis=1))
    packed = jax.vmap(jax.vmap(pack_part))(*split)
    return jnp.stack([packed[i, z] for i, z in CYCLE])


def params(mib=58):
    return pltpu.CompilerParams(vmem_limit_bytes=mib * 1024 * 1024)


def local(
    features,
    norm_gain,
    conv_weight,
    patch_embed,
    position,
    attend_in,
    attend_out,
    reward_head,
    group_index,
    frame_pick,
):
    samples, frames, row_count, merged = features.shape
    tiles, parts = lax.axis_size(TILE), lax.axis_size("sample")
    sent_rows = -(-(row_count + 2) // 16) * 16
    row_block = row_count if row_count <= 14 else 14
    blocks = row_count // row_block
    inner = row_block * CH
    packed = packed_weights(patch_embed, position, attend_in, attend_out)
    order = Layout((1, 2, 3, 0, 4))
    split = (samples, frames, row_count, merged // 128, 128)
    view = with_layout_constraint(features.reshape(split), order).transpose(1, 2, 3, 0, 4)
    view = view.reshape(frames, row_count, samples * merged // 128, 128)
    gain = norm_gain[None, :]

    smem = pl.BlockSpec(memory_space=pltpu.SMEM)
    view_spec = pl.BlockSpec((1,) + view.shape[1:], lambda t: (t, 0, 0, 0))
    gain_spec = pl.BlockSpec((1, CH), lambda t: (0, 0))
    taps_spec = pl.BlockSpec((3, 3, 3, 3, CH), lambda t: (0, 0, 0, 0, 0))
    sent = (SCORED, samples, 3, sent_rows, 128)
    sent_spec = pl.BlockSpec(sent, lambda t: (0, 0, 0, 0, 0))
    aligned = (frames, row_count, samples, CH, 128)
    aligned_spec = pl.BlockSpec((1,) + aligned[1:], lambda t: (t, 0, 0, 0, 0))
    band_spec = pl.BlockSpec((BACK * CH, BACK_ROWS), lambda t: (0, 0))
    decoded, x_aligned, slopes, band = pl.pallas_call(
        functools.partial(decode_kernel, row_block),
        grid=(frames,),
        in_specs=[smem, view_spec, gain_spec, taps_spec],
        out_specs=[sent_spec, aligned_spec, aligned_spec, band_spec],
        scratch_shapes=[
            pltpu.VMEM((OUT_ROWS, inner), BF16),
            pltpu.VMEM((3, 32, CH), F32),
            pltpu.VMEM((128, 128), F32),
            pltpu.VMEM((row_block, 192, 128), F32),
            pltpu.VMEM((blocks, inner, 256), BF16),
            pltpu.VMEM((blocks, 3, samples, 48, 128), F32),
            pltpu.VMEM((sent_rows + 16, 128), F32),
        ],
        out_shape=[
            jax.ShapeDtypeStruct(sent, BF16),
            jax.ShapeDtypeStruct(aligned, BF16),
            jax.ShapeDtypeStruct(aligned, BF16),
            jax.ShapeDtypeStruct((BACK * CH, BACK_ROWS), BF16),
        ],
        compiler_params=params(),
        name="decode",
    )(frame_pick, view, gain, conv_weight)

    if tiles > SCORED:
        decoded = jnp.pad(decoded, ((0, tiles - SCORED),) + ((0, 0),) * 4)
    owned = lax.all_to_all(decoded, TILE, split_axis=0, concat_axis=0, tiled=True)

    head = reward_head.reshape(NT, D // NT)
    head = jnp.concatenate([head[:, :128].reshape(-1), head[:, 128:].reshape(-1)])[None, :]
    height = row_count * tiles
    count = samples * NTOK
    frame_scratch = pltpu.VMEM((samples, 3, height + 48, 128), F32)
    flip_scratch = pltpu.VMEM((samples * height // (2 * PATCH), 2, 128, 128), F32)
    inputs, input_order = pl.pallas_call(
        functools.partial(patch_kernel, row_count, tiles, samples),
        out_shape=[jax.ShapeDtypeStruct((count, 640), BF16), jax.ShapeDtypeStruct((KIN, 640), BF16)],
        scratch_shapes=[frame_scratch, flip_scratch, pltpu.VMEM((count, KIN), F32)],
        compiler_params=params(),
        name="patches",
    )(owned)
    grads, scores = pl.pallas_call(
        functools.partial(reward_kernel, row_count, tiles, samples),
        out_shape=[
            jax.ShapeDtypeStruct((tiles, samples, 3, sent_rows, 128), BF16),
            jax.ShapeDtypeStruct((8, 128), F32),
        ],
        in_specs=[
            pl.BlockSpec(memory_space=pltpu.VMEM),
            pl.BlockSpec(memory_space=pltpu.VMEM),
            pl.BlockSpec(memory_space=pl.ANY),
            pl.BlockSpec(memory_space=pltpu.VMEM),
        ],
        scratch_shapes=[
            pltpu.VMEM(packed.shape, BF16),
            pltpu.SemaphoreType.DMA((3,)),
            frame_scratch,
            flip_scratch,
            pltpu.VMEM((D, 640), BF16),
            pltpu.VMEM((HEADS * 128, D), BF16),
            pltpu.VMEM((NTOK, D), BF16),
            pltpu.VMEM((count, KIN), F32),
            pltpu.VMEM((count, 128), F32),
            pltpu.VMEM((count, D), F32),
            pltpu.VMEM((count, D), BF16),
            pltpu.VMEM((3 * HEADS, count, 128), BF16),
            pltpu.VMEM((HEADS * samples, NTOK, NTOK), F32),
            pltpu.VMEM((3 * HEADS, count, 128), F32),
            pltpu.VMEM((count, D), F32),
            pltpu.VMEM((2, 8, D), F32),
            pltpu.VMEM((8, HEADS * 128), F32),
        ],
        compiler_params=params(),
        name="reward",
    )(inputs, input_order, packed, head)

    mine = jnp.concatenate([scores[:samples, 0], group_index.astype(F32)])
    mine = jnp.broadcast_to(mine[None], (tiles * parts, 2 * samples))
    everyone = lax.all_to_all(mine, TILE + ("sample",), split_axis=0, concat_axis=0, tiled=True)
    everyone = everyone.reshape(tiles, parts, 2, samples)
    returned = lax.all_to_all(grads, TILE, split_axis=0, concat_axis=0, tiled=True)
    returned = returned[:SCORED]

    rewards = jnp.sum(everyone[:SCORED, :, 0], axis=0).reshape(-1) / SCORED
    groups = everyone[0, :, 1].reshape(-1)
    here = (lax.axis_index("sample") * samples).astype(jnp.int32)
    own_rewards = lax.dynamic_slice_in_dim(rewards, here, samples)
    own_groups = lax.dynamic_slice_in_dim(groups, here, samples)
    member = (own_groups[:, None] == groups[None, :]).astype(F32)
    mean_group = jnp.sum(member * rewards[None, :], axis=1) / GROUP
    second_group = jnp.sum(member * (rewards * rewards)[None, :], axis=1) / GROUP - mean_group * mean_group
    advantage = (own_rewards - mean_group) * lax.rsqrt(second_group + SMOOTH)
    cotangent = -LOSS_SCALE * advantage / SCORED

    result = pl.pallas_call(
        restore_kernel,
        grid=(frames,),
        in_specs=[smem, smem, aligned_spec, aligned_spec, band_spec, sent_spec],
        out_specs=view_spec,
        scratch_shapes=[
            pltpu.VMEM((row_block, samples * merged // 128, 128), F32),
            pltpu.VMEM((frames + 2, -(-row_count // BACK), 80, 256), BF16),
            pltpu.VMEM((-(-row_count // BACK), BACK * CH, 256), F32),
        ],
        out_shape=jax.ShapeDtypeStruct(view.shape, BF16),
        compiler_params=params(),
        name="restore",
    )(frame_pick, cotangent, x_aligned, slopes, band, returned)
    result = result.reshape(frames, row_count, merged // 128, samples, 128).transpose(3, 0, 1, 2, 4)
    return with_layout_constraint(result, order).reshape(features.shape)


def solution(mesh):
    tiles, parts = mesh.devices.shape
    split = Mesh(mesh.devices.reshape(tiles // 2, 2, parts), ("chip", "core", "sample"))
    in_specs = (
        P("sample", None, TILE, None),
        P(),
        P(),
        P(None, TILE),
        P("sample", TILE),
        P("sample", TILE),
        P("sample", TILE),
        P(),
        P("sample"),
        P("sample", None),
    )
    out_specs = P("sample", None, TILE, None)
    return jax.shard_map(local, mesh=split, in_specs=in_specs, out_specs=out_specs, check_vma=False)
```

```python
import functools

import jax
import jax.numpy as jnp
from jax import lax
from jax.experimental import pallas as pl
from jax.experimental.pallas import tpu as pltpu
from jax.experimental.layout import Layout, with_layout_constraint
from jax.sharding import Mesh, PartitionSpec as P

SCORED = 8
PATCH = 14
HEADS = 8
HD = 80
GROUP = 4
LOSS_SCALE = 16384.0
SMOOTH = 0.01

TILE = ("chip", "core")
CH = 96
COLS = 112
SPANS = CH // 8
OUT_ROWS = 27 * 16
BACK = 6
BACK_ROWS = 3 * 80
NT = 8
NZ = 4
PACK = 1120
CYCLE = [
    (2 * chip + core, z)
    for chip, heights in ((0, (0, 1, 2, 3)), (1, (3, 2, 1, 0)), (3, (0, 1, 2, 3)), (2, (3, 2, 1, 0)))
    for z in heights
    for core in range(2)
]
PLACES = [[CYCLE.index((i, z)) for z in range(NZ)] for i in range(NT)]
STARTS = (0, 48, 96, 112)
KIN = 896
D = 1280
NTOK = 128
F32 = jnp.float32
BF16 = jnp.bfloat16


def lane_iota(rows):
    return lax.broadcasted_iota(jnp.int32, (rows, 128), 1)


def left(value, amount):
    return pltpu.roll(value, 128 - amount, 1)


def sub_iota(rows):
    return lax.broadcasted_iota(jnp.int32, (rows, 128), 0)


def channels_of(raw, at, group, sample):
    start = 8 + 14 * group + sample
    here = raw[at, pl.ds(start, 8, stride=2), :]
    before = raw[at, pl.ds(start - 2, 8, stride=2), :]
    joined = jnp.where(lane_iota(8) < 128 - 16 * sub_iota(8), here, before)
    return pltpu.roll(joined, 0, 1, stride=16, stride_axis=0)


def tiles_of(value):
    turned = jnp.take_along_axis(value, (lane_iota(8) + 16 * sub_iota(8)) % 128, axis=1)
    return jnp.where(lane_iota(8) < COLS - 16 * sub_iota(8), turned, pltpu.roll(turned, 7, 0))


def load_taps(weight_ref, taps):
    taps[...] = jnp.zeros(taps.shape, F32)
    for a in range(3):
        for b in range(3):
            for e in range(3):
                for o in range(3):
                    at = (a * 3 + e) * 3 + o
                    taps[b, at : at + 1, :] = weight_ref[a, b, e, o : o + 1, :].astype(F32)


def row_of(shape, dim):
    at = lax.broadcasted_iota(jnp.int32, shape, dim)
    return ((at.astype(F32) + 0.5) * (1.0 / CH)).astype(jnp.int32)


def banded(taps, row_block):
    inner = row_block * CH
    pick = (
        lax.broadcasted_iota(jnp.int32, (OUT_ROWS, 32), 0) // 16
        == lax.broadcasted_iota(jnp.int32, (OUT_ROWS, 32), 1)
    ).astype(BF16)
    at = lax.broadcasted_iota(jnp.int32, (CH, inner), 1) - CH * row_of((CH, inner), 1)
    grow = (at == lax.broadcasted_iota(jnp.int32, (CH, inner), 0)).astype(BF16)
    shape = (OUT_ROWS, inner)
    p_at = lax.broadcasted_iota(jnp.int32, shape, 0) % 16
    r_at = row_of(shape, 1)
    total = jnp.zeros(shape, F32)
    for b in range(3):
        rows = nn_dot(pick, taps[b].astype(BF16)).astype(BF16)
        total = jnp.where(p_at == r_at + 2 - b, nn_dot(rows, grow), total)
    return total.astype(BF16)


def banded_back(taps):
    inner = BACK * CH

    def column_of(shape, dim):
        at = lax.broadcasted_iota(jnp.int32, shape, dim)
        a = (at >= 80).astype(jnp.int32) + (at >= 160).astype(jnp.int32)
        return a, at - 80 * a

    a, rest = column_of((BACK_ROWS, 32), 0)
    tap = jnp.where(rest // 8 < 9, 9 * a + rest // 8, 31)
    pick = (tap == lax.broadcasted_iota(jnp.int32, (BACK_ROWS, 32), 1)).astype(BF16)
    at = lax.broadcasted_iota(jnp.int32, (inner, CH), 0) - CH * row_of((inner, CH), 0)
    grow = (at == lax.broadcasted_iota(jnp.int32, (inner, CH), 1)).astype(BF16)
    shape = (inner, BACK_ROWS)
    p_at = column_of(shape, 1)[1] % 8
    r_at = row_of(shape, 0)
    total = jnp.zeros(shape, F32)
    for b in range(3):
        rows = nn_dot(pick, taps[b].astype(BF16)).astype(BF16)
        total = jnp.where(p_at == r_at + 2 - b, nt_dot(grow, rows), total)
    return total.astype(BF16)


def half_gains(gain_ref):
    rows = jnp.concatenate([gain_ref[0:1, :], jnp.zeros((1, 128 - CH), F32)], axis=1)
    return 0.5 * jnp.broadcast_to(rows, (128, 128)).T


def entry_of(pick_ref, sample, frame):
    found = jnp.int32(-1)
    for j in range(SCORED):
        found = jnp.where(pick_ref[sample, j] == frame, jnp.int32(j), found)
    return found


def decode_kernel(row_block, pick_ref, x_ref, gain_ref, weight_ref, out_ref, x_out, slope_out, turned_out, band, taps, gains, raw, operand, acc, final):
    t = pl.program_id(0)
    blocks = x_ref.shape[1] // row_block
    rows = out_ref.shape[3]

    @pl.when(t == 0)
    def _():
        load_taps(weight_ref, taps)
        band[...] = banded(taps, row_block)
        turned_out[...] = banded_back(taps)
        gains[...] = half_gains(gain_ref)
        acc[...] = jnp.zeros(acc.shape, F32)
        raw[...] = jnp.zeros(raw.shape, F32)

    for k in range(blocks):

        def one_row(row, at):
            raw[at, 8:176, :] = x_ref[0, k * row_block + row].astype(F32)
            for s in range(2):
                found = [channels_of(raw, at, g, s) for g in range(SPANS)]
                square = found[0] * found[0]
                for g in range(1, SPANS):
                    square = square + found[g] * found[g]
                second = jnp.sum(square, axis=0, keepdims=True) * (1.0 / CH)
                inv = lax.rsqrt(second + 1e-06)
                for m in range(SPANS // 2):
                    x_out[0, k * row_block + row, s, 16 * m : 16 * m + 16, :] = jnp.concatenate(
                        [found[2 * m] * inv, found[2 * m + 1] * inv], axis=0
                    ).astype(BF16)
                    acts, slopes = [], []
                    for g in (2 * m, 2 * m + 1):
                        gain = gains[8 * g : 8 * g + 8, :]
                        half = found[g] * inv * gain
                        th = jnp.tanh(half)
                        rest = half - half * th
                        acts.append(half + half * th)
                        slopes.append((gain * inv) * (1.0 + th) * (1.0 + rest))
                    slope_out[0, k * row_block + row, s, 16 * m : 16 * m + 16, :] = jnp.concatenate(
                        slopes, axis=0
                    ).astype(BF16)
                    start = row * CH + 16 * m
                    operand[k, start : start + 16, 128 * s : 128 * s + 128] = jnp.concatenate(
                        acts, axis=0
                    ).astype(BF16)

        for row in range(row_block):
            one_row(row, row)
        spread = jnp.dot(band[...], operand[k], preferred_element_type=F32)
        lane = lane_iota(48)
        for s in range(2):
            part = spread[:, 128 * s : 128 * s + 128]
            for a in range(3):
                low, mid, high = (part[144 * a + 48 * e : 144 * a + 48 * e + 48] for e in range(3))
                low = jnp.where(lane == 0, 0.0, pltpu.roll(low, 1, 1))
                high = jnp.where(lane == COLS - 1, 0.0, pltpu.roll(high, 127, 1))
                acc[k, 2 - a, s] += low + mid + high

    keep = lane_iota(rows) < COLS
    for s in range(2):
        entry = entry_of(pick_ref, s, t)

        @pl.when(entry >= 0)
        def _():
            for o in range(3):
                final[...] = jnp.zeros(final.shape, F32)
                for k in range(blocks):
                    start = k * row_block
                    final[start : start + 16, :] += acc[k, 0, s, 16 * o : 16 * o + 16, :]
                out_ref[jnp.maximum(entry, 0), s, o] = jnp.where(keep, final[0:rows, :], 0.0).astype(BF16)

    for k in range(blocks):
        acc[k, 0] = acc[k, 1]
        acc[k, 1] = acc[k, 2]
        acc[k, 2] = jnp.zeros(acc.shape[2:], F32)


def cotangents(parts, here, everyone):
    row = lax.broadcasted_iota(jnp.int32, everyone.shape, 0)
    own = jnp.zeros((1, 128), F32)
    layers = []
    for z in range(parts):
        mine = (row % parts == z) & (row < SCORED * parts)
        found = jnp.sum(jnp.where(mine, everyone, 0.0), axis=0, keepdims=True) / SCORED
        own = jnp.where(here == z, found, own)
        layers.append(found)
    prompt = left(own, 2)
    total = jnp.zeros((1, 128), F32)
    square = jnp.zeros((1, 128), F32)
    for found in layers:
        for s in range(2):
            member = prompt == found[:, 2 + s : 3 + s]
            reward = found[:, s : s + 1]
            total = total + jnp.where(member, reward, 0.0)
            square = square + jnp.where(member, reward * reward, 0.0)
    mean = total / GROUP
    second = square / GROUP - mean * mean
    return -LOSS_SCALE * ((own - mean) * lax.rsqrt(second + SMOOTH)) / SCORED


def restore_kernel(parts, pick_ref, here_ref, everyone_ref, x_ref, slope_ref, band, grad_ref, out_ref, back, shifted, coming):
    t = pl.program_id(0)
    frames = pl.num_programs(0)
    row_count = x_ref.shape[1]
    starts = range(0, row_count, BACK)
    rows = grad_ref.shape[3]

    @pl.when(t == 0)
    def _():
        shifted[...] = jnp.zeros(shifted.shape, BF16)
        lane = lane_iota(rows)
        blank = jnp.zeros((8, 128), F32)
        scales = cotangents(parts, here_ref[0], everyone_ref[...])

        def one_frame(frame, carry):
            for s in range(2):
                entry = entry_of(pick_ref, s, frame)
                scale = jnp.where(entry >= 0, scales[:, s : s + 1], 0.0)
                source = jnp.maximum(entry, 0)
                moved = [[], [], []]
                for o in range(3):
                    value = grad_ref[source, s, o].astype(F32) * scale
                    value = jnp.where(lane < COLS, value, 0.0)
                    for e, turned in enumerate((pltpu.roll(value, 127, 1), value, pltpu.roll(value, 1, 1))):
                        moved[e].append(turned)
                for k, start in enumerate(starts):
                    block = [turned[start : start + 8] for some in moved for turned in some]
                    shifted[frame, k, :, 128 * s : 128 * s + 128] = jnp.concatenate(
                        block + [blank], axis=0
                    ).astype(BF16)
            return carry

        lax.fori_loop(0, frames, one_frame, 0)

    for k, start in enumerate(starts):
        count = min(BACK, row_count - start)
        operand = jnp.concatenate([shifted[t + 2 - a, k] for a in range(3)], axis=0)
        coming[k, 0 : count * CH, :] = nn_dot(band[0 : count * CH, :], operand)
        for local in range(count):
            row = start + local
            for s in range(2):
                outs, units, total = [], [], None
                for m in range(SPANS // 2):
                    pair = x_ref[0, row, s, 16 * m : 16 * m + 16, :].astype(F32)
                    slopes = slope_ref[0, row, s, 16 * m : 16 * m + 16, :].astype(F32)
                    for part in range(2):
                        g = 2 * m + part
                        unit = pair[8 * part : 8 * part + 8]
                        at = local * CH + 8 * g
                        out = coming[k, at : at + 8, 128 * s : 128 * s + 128] * slopes[8 * part : 8 * part + 8]
                        outs.append(out)
                        units.append(unit)
                        total = out * unit if g == 0 else total + out * unit
                factor = jnp.sum(total, axis=0, keepdims=True) * (1.0 / CH)
                for g in range(SPANS):
                    result = tiles_of(outs[g] - units[g] * factor)
                    back[row % back.shape[0], pl.ds(14 * g + s, 7, stride=2), :] = result[0:7]
            out_ref[0, row] = back[row % back.shape[0]].astype(BF16)


def nt_dot(one, two):
    return lax.dot_general(one, two, (((1,), (1,)), ((), ())), preferred_element_type=F32)


def tn_dot(one, two):
    return lax.dot_general(one, two, (((0,), (0,)), ((), ())), preferred_element_type=F32)


def nn_dot(one, two):
    return jnp.dot(one, two, preferred_element_type=F32)


def split_two(value):
    high = value.astype(BF16)
    low = (value - high.astype(F32)).astype(BF16)
    return jnp.concatenate([high, low], axis=0)


def patch_kernel(row_count, tiles, samples, part_ref, inputs_ref, order, frame, flip, patches):
    height = row_count * tiles
    patch_rows = height // PATCH
    lane64 = lane_iota(8) < 64
    inputs = order.shape[1]
    pixel = lax.broadcasted_iota(jnp.int32, (64, inputs), 0)
    column = lax.broadcasted_iota(jnp.int32, (64, inputs), 1)
    for x in range(PATCH):
        order[64 * x : 64 * x + 64, :] = (
            (column == pixel * PATCH + x) & (pixel < 3 * PATCH)
        ).astype(BF16)

    flip[...] = jnp.zeros(flip.shape, F32)
    frame[...] = jnp.zeros(frame.shape, F32)
    for f in range(samples):
        for i in range(tiles):
            at = row_count * i + 7
            for o in range(3):
                frame[f, o, at : at + row_count + 2, :] += part_ref[i, f, o, 0 : row_count + 2, :].astype(F32)
    for f in range(samples):
        for pair in range(patch_rows // 2):
            turn = flip.at[f * (patch_rows // 2) + pair]
            for local in range(2):
                at = 8 + PATCH * (2 * pair + local)
                for o in range(3):
                    turn[0, 64 * local + PATCH * o : 64 * local + PATCH * o + PATCH, :] = (
                        frame[f, o, at : at + PATCH, :].astype(BF16).astype(F32)
                    )
            turn[1] = turn[0].T
            token = f * NTOK + pair * 16
            for y in range(PATCH // 2):
                even = turn[1, pl.ds(2 * y, 8, stride=PATCH), :]
                odd = turn[1, pl.ds(2 * y + 1, 8, stride=PATCH), :]
                patches[token : token + 8, 128 * y : 128 * y + 128] = jnp.where(lane64, even, pltpu.roll(odd, 64, 1))
                patches[token + 8 : token + 16, 128 * y : 128 * y + 128] = jnp.where(lane64, pltpu.roll(even, 64, 1), odd)

    inputs_ref[...] = nn_dot(patches[...].astype(BF16), order[...]).astype(BF16)


def reward_kernel(
    row_count, tiles, samples,
    group_ref, inputs_ref, order, packed_ref, head_ref,
    out_ref, score_ref,
    pack, arrived, frame, flip, embed, outw, place, patches, tokens, normed, normed16, slots, weights, dslots, dnormed, rows8, abar, both,
):
    height = row_count * tiles
    patch_rows = height // PATCH
    lane64 = lane_iota(8) < 64
    lane = lane_iota(NTOK)
    count = samples * NTOK

    copies = []
    for part, (begin, end) in enumerate(((880, 1120), (640, 880), (0, 640))):
        copies.append(
            pltpu.make_async_copy(
                packed_ref.at[:, begin:end, :], pack.at[:, begin:end, :], arrived.at[part]
            )
        )
        copies[-1].start()

    flip[...] = jnp.zeros(flip.shape, F32)
    copies[0].wait()
    copies[1].wait()

    for i in range(NT):
        for z, (begin, height, target) in enumerate(
            ((0, 48, 128 * i), (0, 48, 128 * i + 48), (0, 32, 128 * i + 96), (16, 32, 1024 + 32 * i))
        ):
            source = pack.at[PLACES[i][z]]
            for part in range(5):
                at = 880 + 48 * part + begin
                embed[target : target + height, 128 * part : 128 * part + 128] = source[at : at + height, :]
    lane48 = lane_iota(48)
    for h in range(HEADS):
        outw[128 * h + HD : 128 * h + 128, :] = jnp.zeros((128 - HD, D), BF16)
    for z in range(NZ):
        for i in range(NT):
            source = pack.at[PLACES[i][z]]
            for local in range(2):
                at, begin = 128 * (2 * z + local), 640 + HD * local
                outw[at : at + HD, 128 * i : 128 * i + 128] = source[begin : begin + HD, :]
            place[32 * z : 32 * z + 32, 128 * i : 128 * i + 128] = source[800:832, :]
        for ib in range(2):
            sources = [pack[PLACES[4 * ib + j][z], 832:880, :].astype(F32) for j in range(4)]
            rolled = [[sources[j] if d == 0 else pltpu.roll(sources[j], 32 * d, 1) for d in range(4)] for j in range(4)]
            at = 1024 + 128 * ib
            for q in range(4):
                found = rolled[0][(0 - q) % 4]
                for j in range(1, 4):
                    found = jnp.where(lane48 >= 32 * j, rolled[j][(j - q) % 4], found)
                found = found.astype(BF16)
                for begin, end, row in (
                    ((0, 48, 0),),
                    ((0, 32, 48), (32, 48, 128)),
                    ((0, 48, 144),),
                    ((0, 16, 192),),
                )[q]:
                    row = 256 * z + row
                    outw[row : row + end - begin, at : at + 128] = found[begin:end]
                if q == 3:
                    place[32 * z : 32 * z + 32, at : at + 128] = found[16:48]

    token_value = nt_dot(inputs_ref[...], embed[...])
    rows8[...] = jnp.zeros(rows8.shape, F32)
    abar[...] = jnp.zeros(abar.shape, F32)
    place_value = place[...].astype(F32)
    for f in range(samples):
        value = token_value[f * NTOK : f * NTOK + NTOK] + place_value
        rows8[0, f : f + 1, :] = jnp.mean(value, axis=0, keepdims=True)
        centered = value - jnp.mean(value, axis=-1, keepdims=True)
        scale = lax.rsqrt(jnp.mean(centered * centered, axis=-1, keepdims=True) + 1e-05)
        value = centered * scale
        normed[f * NTOK : f * NTOK + NTOK, :] = value
        normed16[f * NTOK : f * NTOK + NTOK, :] = value.astype(BF16)
        tokens[f * NTOK : f * NTOK + NTOK, :] = jnp.broadcast_to(scale, (NTOK, 128))

    def weight_part(i, z):
        source = pack.at[PLACES[i][z]]
        return jnp.concatenate([source[0:256, :], source[320:576, :]], axis=1)

    def weight_rest(i):
        return jnp.concatenate(
            [
                jnp.concatenate([pack[PLACES[i][z], 256:320, :], pack[PLACES[i][z], 576:640, :]], axis=1)
                for z in range(NZ)
            ],
            axis=0,
        )

    lane_all = lane_iota(count)
    copies[2].wait()
    for i in range(NT):
        mixed = nn_dot(
            normed16[...], jnp.concatenate([weight_part(i, z) for z in range(NZ)] + [weight_rest(i)], axis=0)
        )
        first, second = mixed[:, 0:128], mixed[:, 128:256]
        found = (
            first,
            jnp.where(lane_all < 48, pltpu.roll(first, 48, 1), pltpu.roll(second, 48, 1)),
            pltpu.roll(second, 96, 1),
        )
        for m in range(3):
            slots[3 * i + m] = jnp.where(lane_all < HD, found[m], 0.0).astype(BF16)

    for h in range(HEADS):
        for f in range(samples):
            span = slice(f * NTOK, f * NTOK + NTOK)
            logits = nt_dot(slots[h, span, :], slots[HEADS + h, span, :]) * HD ** (-0.5)
            logits = jnp.exp(logits - jnp.max(logits, axis=-1, keepdims=True))
            prob = logits / jnp.sum(logits, axis=-1, keepdims=True)
            weights[h * samples + f] = prob
            sums = jnp.sum(prob.astype(BF16).astype(F32), axis=0, keepdims=True)
            sums = split_two(jnp.broadcast_to(sums, (8, 128)))
            both[h * samples + f] = sums
            mean = nn_dot(sums, slots[2 * HEADS + h, span, :]) * (1.0 / NTOK)
            abar[f : f + 1, 128 * h : 128 * h + 128] = mean[0:1] + mean[8:9]

    part = nn_dot(split_two(abar[...]), outw[...])
    pooled = rows8[0] + part[0:8] + part[8:16]
    pooled = pooled - jnp.mean(pooled, axis=-1, keepdims=True)
    scale = lax.rsqrt(jnp.mean(pooled * pooled, axis=-1, keepdims=True) + 1e-05)
    pooled = pooled * scale
    head = head_ref[...]
    score = jnp.sum(pooled * head, axis=-1, keepdims=True)
    lane1 = lane_iota(1)
    sent = jnp.zeros((1, 128), F32)
    for f in range(samples):
        sent = jnp.where(lane1 == f, score[f : f + 1], sent)
        sent = jnp.where(lane1 == samples + f, group_ref[f].astype(F32), sent)
    score_ref[...] = jnp.broadcast_to(sent, score_ref.shape)
    dpooled = scale * (
        head - jnp.mean(head, axis=-1, keepdims=True) - pooled * jnp.mean(pooled * head, axis=-1, keepdims=True)
    )
    dres = dpooled * (1.0 / NTOK)
    rows8[1] = dres
    datts = nt_dot(split_two(dres), outw[...])
    datts = (datts[0:8] + datts[8:16]).astype(BF16)

    first_rows = sub_iota(16) % 8 == 0
    for h in range(HEADS):
        datt = datts[:, 128 * h : 128 * h + 128]
        for f in range(samples):
            span = slice(f * NTOK, f * NTOK + NTOK)
            prob = weights[h * samples + f]
            row = datt[f : f + 1, :]
            dweight = nt_dot(datt, slots[2 * HEADS + h, span, :])[f : f + 1, :].astype(BF16).astype(F32)
            inner = jnp.sum(prob * dweight, axis=-1, keepdims=True)
            dlogit = (prob * (dweight - inner) * HD ** (-0.5)).astype(BF16)
            dslots[h, span, :] = nn_dot(dlogit, slots[HEADS + h, span, :])
            dslots[HEADS + h, span, :] = tn_dot(dlogit, slots[h, span, :])
            pair = jnp.where(first_rows, jnp.broadcast_to(row.astype(F32), (16, 128)), 0.0).astype(BF16)
            dslots[2 * HEADS + h, span, :] = tn_dot(both[h * samples + f], pair)

    parts = []
    for i in range(NT):
        one, two, three = dslots[3 * i], dslots[3 * i + 1], dslots[3 * i + 2]
        two = pltpu.roll(two, 80, 1)
        three = pltpu.roll(three, 32, 1)
        first = jnp.where(lane_all < HD, one, two)
        second = jnp.where(lane_all < 32, two, jnp.where(lane_all < COLS, three, 0.0))
        parts += [first.astype(BF16), second.astype(BF16)]
    dmixed = jnp.concatenate(parts, axis=1)
    for z in range(NZ):
        wide = jnp.concatenate([weight_part(i, z) for i in range(NT)], axis=1)
        dnormed[:, 256 * z : 256 * z + 256] = nt_dot(dmixed, wide)
    wide = jnp.concatenate([weight_rest(i) for i in range(NT)], axis=1)
    dnormed[:, 1024:1280] = nt_dot(dmixed, wide)

    for f in range(samples):
        span = slice(f * NTOK, f * NTOK + NTOK)
        value, dvalue = normed[span, :], dnormed[span, :]
        scale = tokens[span, 0:1]
        dvalue = scale * (
            dvalue
            - jnp.mean(dvalue, axis=-1, keepdims=True)
            - value * jnp.mean(dvalue * value, axis=-1, keepdims=True)
        )
        normed16[span, :] = (dvalue + rows8[1, f : f + 1, :]).astype(BF16)
    patches[...] = nt_dot(nn_dot(normed16[...], embed[...]).astype(BF16), order[...])

    frame[...] = jnp.zeros(frame.shape, F32)
    rows = out_ref.shape[3]
    for f in range(samples):
        for pair in range(patch_rows // 2):
            turn = flip.at[f * (patch_rows // 2) + pair]
            token = f * NTOK + pair * 16
            for y in range(PATCH // 2):
                one = patches[token : token + 8, 128 * y : 128 * y + 128]
                two = patches[token + 8 : token + 16, 128 * y : 128 * y + 128]
                turn[1, pl.ds(2 * y, 8, stride=PATCH), :] = jnp.where(lane64, one, pltpu.roll(two, 64, 1))
                turn[1, pl.ds(2 * y + 1, 8, stride=PATCH), :] = jnp.where(lane64, pltpu.roll(one, 64, 1), two)
            turn[0] = turn[1].T
            for local in range(2):
                at = 8 + PATCH * (2 * pair + local)
                for o in range(3):
                    frame[f, o, at : at + PATCH, :] = turn[0, 64 * local + PATCH * o : 64 * local + PATCH * o + PATCH, :]
    for f in range(samples):
        for i in range(tiles):
            at = row_count * i + 7
            for o in range(3):
                out_ref[i, f, o] = frame[f, o, at : at + rows, :].astype(BF16)


def pack_part(rows_in, out_part, place_part, embed_part):
    ordered = jnp.concatenate([rows_in[0:128], rows_in[160:288], rows_in[128:160], rows_in[288:320]], axis=0)
    upper = jnp.pad(ordered[:, 128:240], ((0, 0), (0, 16)))
    other = jnp.concatenate([out_part, place_part], axis=0)
    rest = other[:, 128:160].reshape(4, 48, 32)
    rest = jnp.concatenate([rest[q] for q in range(4)], axis=1)
    embed_part = jnp.pad(embed_part, ((0, 0), (0, 640 - embed_part.shape[1])))
    embed_part = embed_part.reshape(48, 5, 128).transpose(1, 0, 2).reshape(240, 128)
    return jnp.concatenate([ordered[:, 0:128], upper, other[:, 0:128], rest, embed_part], axis=0)


def pack_kernel(z_ref, rows_ref, out_ref, place_ref, embed_ref, packed_ref):
    for source, target, count in ((0, 0, 128), (160, 128, 128), (128, 256, 32), (288, 288, 32)):
        packed_ref[target : target + count, :] = rows_ref[source : source + count, 0:128]
        packed_ref[320 + target : 320 + target + count, :] = jnp.concatenate(
            [rows_ref[source : source + count, 128:240], jnp.zeros((count, 16), BF16)], axis=1
        )
    packed_ref[640:800, :] = out_ref[:, 0:128]
    packed_ref[800:832, :] = place_ref[:, 0:128]
    tail = out_ref[:, 128:160].astype(F32)
    last = place_ref[:, 128:160].astype(F32)
    packed_ref[832:880, :] = jnp.concatenate(
        [tail[0:48], tail[48:96], tail[96:144], jnp.concatenate([tail[144:160], last], axis=0)],
        axis=1,
    ).astype(BF16)
    width = embed_ref.shape[1]
    start = pl.multiple_of(jnp.where(z_ref[0] == NZ - 1, STARTS[-1], 48 * z_ref[0]), 16)
    for part in range(5):
        count = min(128, width - 128 * part)
        value = embed_ref[pl.ds(start, 48), 128 * part : 128 * part + count]
        if count < 128:
            value = jnp.concatenate([value, jnp.zeros((48, 128 - count), BF16)], axis=1)
        packed_ref[880 + 48 * part : 928 + 48 * part, :] = value


def packed_weights(patch_embed, position, attend_in, attend_out):
    if lax.axis_size(TILE) == NT and lax.axis_size("sample") == NZ:
        z = lax.axis_index("sample").astype(jnp.int32).reshape(1)
        mine = pl.pallas_call(
            pack_kernel,
            in_specs=[pl.BlockSpec(memory_space=pltpu.SMEM)] + [pl.BlockSpec(memory_space=pltpu.VMEM)] * 4,
            out_shape=jax.ShapeDtypeStruct((PACK, 128), BF16),
            compiler_params=params(),
            name="pack",
        )(z, attend_in, attend_out, position, patch_embed.T)
        group = [i * NZ + z for i, z in CYCLE]
        return lax.all_gather(mine, TILE + ("sample",), axis=0, axis_index_groups=[group])

    def whole(value):
        value = lax.all_gather(value, "sample", axis=0, tiled=True)
        return lax.all_gather(value, TILE, axis=1, tiled=True)

    split = [
        value.reshape(NZ, value.shape[0] // NZ, NT, value.shape[1] // NT).transpose(2, 0, 1, 3)
        for value in (whole(attend_in), whole(attend_out), whole(position))
    ]
    columns = lax.all_gather(patch_embed.T, TILE, axis=0, tiled=True).reshape(NT, D // NT, -1)
    split.append(jnp.stack([columns[:, start : start + 48] for start in STARTS], axis=1))
    packed = jax.vmap(jax.vmap(pack_part))(*split)
    return jnp.stack([packed[i, z] for i, z in CYCLE])


def params(mib=58):
    return pltpu.CompilerParams(vmem_limit_bytes=mib * 1024 * 1024)


def local(
    features,
    norm_gain,
    conv_weight,
    patch_embed,
    position,
    attend_in,
    attend_out,
    reward_head,
    group_index,
    frame_pick,
):
    samples, frames, row_count, merged = features.shape
    tiles, parts = lax.axis_size(TILE), lax.axis_size("sample")
    sent_rows = -(-(row_count + 2) // 16) * 16
    row_block = row_count if row_count <= 14 else 14
    blocks = row_count // row_block
    inner = row_block * CH
    packed = packed_weights(patch_embed, position, attend_in, attend_out)
    order = Layout((1, 2, 3, 0, 4))
    split = (samples, frames, row_count, merged // 128, 128)
    view = with_layout_constraint(features.reshape(split), order).transpose(1, 2, 3, 0, 4)
    view = view.reshape(frames, row_count, samples * merged // 128, 128)
    gain = norm_gain[None, :]

    smem = pl.BlockSpec(memory_space=pltpu.SMEM)
    view_spec = pl.BlockSpec((1,) + view.shape[1:], lambda t: (t, 0, 0, 0))
    gain_spec = pl.BlockSpec((1, CH), lambda t: (0, 0))
    taps_spec = pl.BlockSpec((3, 3, 3, 3, CH), lambda t: (0, 0, 0, 0, 0))
    sent = (SCORED, samples, 3, sent_rows, 128)
    sent_spec = pl.BlockSpec(sent, lambda t: (0, 0, 0, 0, 0))
    aligned = (frames, row_count, samples, CH, 128)
    aligned_spec = pl.BlockSpec((1,) + aligned[1:], lambda t: (t, 0, 0, 0, 0))
    band_spec = pl.BlockSpec((BACK * CH, BACK_ROWS), lambda t: (0, 0))
    decoded, x_aligned, slopes, band = pl.pallas_call(
        functools.partial(decode_kernel, row_block),
        grid=(frames,),
        in_specs=[smem, view_spec, gain_spec, taps_spec],
        out_specs=[sent_spec, aligned_spec, aligned_spec, band_spec],
        scratch_shapes=[
            pltpu.VMEM((OUT_ROWS, inner), BF16),
            pltpu.VMEM((3, 32, CH), F32),
            pltpu.VMEM((128, 128), F32),
            pltpu.VMEM((row_block, 192, 128), F32),
            pltpu.VMEM((blocks, inner, 256), BF16),
            pltpu.VMEM((blocks, 3, samples, 48, 128), F32),
            pltpu.VMEM((sent_rows + 16, 128), F32),
        ],
        out_shape=[
            jax.ShapeDtypeStruct(sent, BF16),
            jax.ShapeDtypeStruct(aligned, BF16),
            jax.ShapeDtypeStruct(aligned, BF16),
            jax.ShapeDtypeStruct((BACK * CH, BACK_ROWS), BF16),
        ],
        compiler_params=params(),
        name="decode",
    )(frame_pick, view, gain, conv_weight)

    if tiles > SCORED:
        decoded = jnp.pad(decoded, ((0, tiles - SCORED),) + ((0, 0),) * 4)
    owned = lax.all_to_all(decoded, TILE, split_axis=0, concat_axis=0, tiled=True)

    head = reward_head.reshape(NT, D // NT)
    head = jnp.concatenate([head[:, :128].reshape(-1), head[:, 128:].reshape(-1)])[None, :]
    height = row_count * tiles
    count = samples * NTOK
    frame_scratch = pltpu.VMEM((samples, 3, height + 48, 128), F32)
    flip_scratch = pltpu.VMEM((samples * height // (2 * PATCH), 2, 128, 128), F32)
    inputs, input_order = pl.pallas_call(
        functools.partial(patch_kernel, row_count, tiles, samples),
        out_shape=[jax.ShapeDtypeStruct((count, 640), BF16), jax.ShapeDtypeStruct((KIN, 640), BF16)],
        scratch_shapes=[frame_scratch, flip_scratch, pltpu.VMEM((count, KIN), F32)],
        compiler_params=params(),
        name="patches",
    )(owned)
    grads, scores = pl.pallas_call(
        functools.partial(reward_kernel, row_count, tiles, samples),
        out_shape=[
            jax.ShapeDtypeStruct((tiles, samples, 3, sent_rows, 128), BF16),
            jax.ShapeDtypeStruct((tiles * parts, 128), F32),
        ],
        in_specs=[
            smem,
            pl.BlockSpec(memory_space=pltpu.VMEM),
            pl.BlockSpec(memory_space=pltpu.VMEM),
            pl.BlockSpec(memory_space=pl.ANY),
            pl.BlockSpec(memory_space=pltpu.VMEM),
        ],
        scratch_shapes=[
            pltpu.VMEM(packed.shape, BF16),
            pltpu.SemaphoreType.DMA((3,)),
            frame_scratch,
            flip_scratch,
            pltpu.VMEM((D, 640), BF16),
            pltpu.VMEM((HEADS * 128, D), BF16),
            pltpu.VMEM((NTOK, D), BF16),
            pltpu.VMEM((count, KIN), F32),
            pltpu.VMEM((count, 128), F32),
            pltpu.VMEM((count, D), F32),
            pltpu.VMEM((count, D), BF16),
            pltpu.VMEM((3 * HEADS, count, 128), BF16),
            pltpu.VMEM((HEADS * samples, NTOK, NTOK), F32),
            pltpu.VMEM((3 * HEADS, count, 128), F32),
            pltpu.VMEM((count, D), F32),
            pltpu.VMEM((2, 8, D), F32),
            pltpu.VMEM((8, HEADS * 128), F32),
            pltpu.VMEM((HEADS * samples, 16, 128), BF16),
        ],
        compiler_params=params(),
        name="reward",
    )(group_index, inputs, input_order, packed, head)

    everyone = lax.all_to_all(scores, TILE + ("sample",), split_axis=0, concat_axis=0, tiled=True)
    returned = lax.all_to_all(grads, TILE, split_axis=0, concat_axis=0, tiled=True)
    returned = returned[:SCORED]

    here = lax.axis_index("sample").astype(jnp.int32).reshape(1)
    result = pl.pallas_call(
        functools.partial(restore_kernel, parts),
        grid=(frames,),
        in_specs=[
            smem,
            smem,
            pl.BlockSpec((tiles * parts, 128), lambda t: (0, 0)),
            aligned_spec,
            aligned_spec,
            band_spec,
            sent_spec,
        ],
        out_specs=view_spec,
        scratch_shapes=[
            pltpu.VMEM((row_block, samples * merged // 128, 128), F32),
            pltpu.VMEM((frames + 2, -(-row_count // BACK), 80, 256), BF16),
            pltpu.VMEM((-(-row_count // BACK), BACK * CH, 256), F32),
        ],
        out_shape=jax.ShapeDtypeStruct(view.shape, BF16),
        compiler_params=params(),
        name="restore",
    )(frame_pick, here, everyone, x_aligned, slopes, band, returned)
    result = result.reshape(frames, row_count, merged // 128, samples, 128).transpose(3, 0, 1, 2, 4)
    return with_layout_constraint(result, order).reshape(features.shape)


def solution(mesh):
    tiles, parts = mesh.devices.shape
    split = Mesh(mesh.devices.reshape(tiles // 2, 2, parts), ("chip", "core", "sample"))
    in_specs = (
        P("sample", None, TILE, None),
        P(),
        P(),
        P(None, TILE),
        P("sample", TILE),
        P("sample", TILE),
        P("sample", TILE),
        P(),
        P("sample"),
        P("sample", None),
    )
    out_specs = P("sample", None, TILE, None)
    return jax.shard_map(local, mesh=split, in_specs=in_specs, out_specs=out_specs, check_vma=False)
```

```python
import functools

import jax
import jax.numpy as jnp
from jax import lax
from jax.experimental import pallas as pl
from jax.experimental.pallas import tpu as pltpu
from jax.experimental.layout import Layout, with_layout_constraint
from jax.sharding import Mesh, PartitionSpec as P

SCORED = 8
PATCH = 14
HEADS = 8
HD = 80
GROUP = 4
LOSS_SCALE = 16384.0
SMOOTH = 0.01

TILE = ("chip", "core")
CH = 96
COLS = 112
SPANS = CH // 8
OUT_ROWS = 27 * 16
BACK = 6
EARLY = 3
BACK_ROWS = 3 * 80
NT = 8
NZ = 4
PACK = 1120
CYCLE = [
    (2 * chip + core, z)
    for chip, heights in ((0, (0, 1, 2, 3)), (1, (3, 2, 1, 0)), (3, (0, 1, 2, 3)), (2, (3, 2, 1, 0)))
    for z in heights
    for core in range(2)
]
PLACES = [[CYCLE.index((i, z)) for z in range(NZ)] for i in range(NT)]
STARTS = (0, 48, 96, 112)
KIN = 896
D = 1280
NTOK = 128
F32 = jnp.float32
BF16 = jnp.bfloat16


def lane_iota(rows):
    return lax.broadcasted_iota(jnp.int32, (rows, 128), 1)


def left(value, amount):
    return pltpu.roll(value, 128 - amount, 1)


def sub_iota(rows):
    return lax.broadcasted_iota(jnp.int32, (rows, 128), 0)


def channels_of(raw, at, group, sample):
    start = 8 + 14 * group + sample
    here = raw[at, pl.ds(start, 8, stride=2), :]
    before = raw[at, pl.ds(start - 2, 8, stride=2), :]
    joined = jnp.where(lane_iota(8) < 128 - 16 * sub_iota(8), here, before)
    return pltpu.roll(joined, 0, 1, stride=16, stride_axis=0)


def tiles_of(value):
    turned = jnp.take_along_axis(value, (lane_iota(8) + 16 * sub_iota(8)) % 128, axis=1)
    return jnp.where(lane_iota(8) < COLS - 16 * sub_iota(8), turned, pltpu.roll(turned, 7, 0))


def load_taps(weight_ref, taps):
    taps[...] = jnp.zeros(taps.shape, F32)
    for a in range(3):
        for b in range(3):
            for e in range(3):
                for o in range(3):
                    at = (a * 3 + e) * 3 + o
                    taps[b, at : at + 1, :] = weight_ref[a, b, e, o : o + 1, :].astype(F32)


def row_of(shape, dim):
    at = lax.broadcasted_iota(jnp.int32, shape, dim)
    return ((at.astype(F32) + 0.5) * (1.0 / CH)).astype(jnp.int32)


def banded(taps, row_block):
    inner = row_block * CH
    pick = (
        lax.broadcasted_iota(jnp.int32, (OUT_ROWS, 32), 0) // 16
        == lax.broadcasted_iota(jnp.int32, (OUT_ROWS, 32), 1)
    ).astype(BF16)
    at = lax.broadcasted_iota(jnp.int32, (CH, inner), 1) - CH * row_of((CH, inner), 1)
    grow = (at == lax.broadcasted_iota(jnp.int32, (CH, inner), 0)).astype(BF16)
    shape = (OUT_ROWS, inner)
    p_at = lax.broadcasted_iota(jnp.int32, shape, 0) % 16
    r_at = row_of(shape, 1)
    total = jnp.zeros(shape, F32)
    for b in range(3):
        rows = nn_dot(pick, taps[b].astype(BF16)).astype(BF16)
        total = jnp.where(p_at == r_at + 2 - b, nn_dot(rows, grow), total)
    return total.astype(BF16)


def banded_back(taps):
    inner = BACK * CH

    def column_of(shape, dim):
        at = lax.broadcasted_iota(jnp.int32, shape, dim)
        a = (at >= 80).astype(jnp.int32) + (at >= 160).astype(jnp.int32)
        return a, at - 80 * a

    a, rest = column_of((BACK_ROWS, 32), 0)
    tap = jnp.where(rest // 8 < 9, 9 * a + rest // 8, 31)
    pick = (tap == lax.broadcasted_iota(jnp.int32, (BACK_ROWS, 32), 1)).astype(BF16)
    at = lax.broadcasted_iota(jnp.int32, (inner, CH), 0) - CH * row_of((inner, CH), 0)
    grow = (at == lax.broadcasted_iota(jnp.int32, (inner, CH), 1)).astype(BF16)
    shape = (inner, BACK_ROWS)
    p_at = column_of(shape, 1)[1] % 8
    r_at = row_of(shape, 0)
    total = jnp.zeros(shape, F32)
    for b in range(3):
        rows = nn_dot(pick, taps[b].astype(BF16)).astype(BF16)
        total = jnp.where(p_at == r_at + 2 - b, nt_dot(grow, rows), total)
    return total.astype(BF16)


def half_gains(gain_ref):
    rows = jnp.concatenate([gain_ref[0:1, :], jnp.zeros((1, 128 - CH), F32)], axis=1)
    return 0.5 * jnp.broadcast_to(rows, (128, 128)).T


def entry_of(pick_ref, sample, frame):
    found = jnp.int32(-1)
    for j in range(SCORED):
        found = jnp.where(pick_ref[sample, j] == frame, jnp.int32(j), found)
    return found


def decode_kernel(row_block, pick_ref, x_ref, gain_ref, weight_ref, out_ref, x_out, slope_out, turned_out, band, taps, gains, raw, operand, acc, final):
    t = pl.program_id(0)
    blocks = x_ref.shape[1] // row_block
    rows = out_ref.shape[3]

    @pl.when(t == 0)
    def _():
        load_taps(weight_ref, taps)
        band[...] = banded(taps, row_block)
        turned_out[...] = banded_back(taps)
        gains[...] = half_gains(gain_ref)
        acc[...] = jnp.zeros(acc.shape, F32)
        raw[...] = jnp.zeros(raw.shape, F32)

    for k in range(blocks):

        def one_row(row, at):
            raw[at, 8:176, :] = x_ref[0, k * row_block + row].astype(F32)
            for s in range(2):
                found = [channels_of(raw, at, g, s) for g in range(SPANS)]
                square = found[0] * found[0]
                for g in range(1, SPANS):
                    square = square + found[g] * found[g]
                second = jnp.sum(square, axis=0, keepdims=True) * (1.0 / CH)
                inv = lax.rsqrt(second + 1e-06)
                for m in range(SPANS // 2):
                    x_out[0, k * row_block + row, s, 16 * m : 16 * m + 16, :] = jnp.concatenate(
                        [found[2 * m] * inv, found[2 * m + 1] * inv], axis=0
                    ).astype(BF16)
                    acts, slopes = [], []
                    for g in (2 * m, 2 * m + 1):
                        gain = gains[8 * g : 8 * g + 8, :]
                        half = found[g] * inv * gain
                        th = jnp.tanh(half)
                        rest = half - half * th
                        acts.append(half + half * th)
                        slopes.append((gain * inv) * (1.0 + th) * (1.0 + rest))
                    slope_out[0, k * row_block + row, s, 16 * m : 16 * m + 16, :] = jnp.concatenate(
                        slopes, axis=0
                    ).astype(BF16)
                    start = row * CH + 16 * m
                    operand[k, start : start + 16, 128 * s : 128 * s + 128] = jnp.concatenate(
                        acts, axis=0
                    ).astype(BF16)

        for row in range(row_block):
            one_row(row, row)
        spread = jnp.dot(band[...], operand[k], preferred_element_type=F32)
        lane = lane_iota(48)
        for s in range(2):
            part = spread[:, 128 * s : 128 * s + 128]
            for a in range(3):
                low, mid, high = (part[144 * a + 48 * e : 144 * a + 48 * e + 48] for e in range(3))
                low = jnp.where(lane == 0, 0.0, pltpu.roll(low, 1, 1))
                high = jnp.where(lane == COLS - 1, 0.0, pltpu.roll(high, 127, 1))
                acc[k, 2 - a, s] += low + mid + high

    keep = lane_iota(rows) < COLS
    for s in range(2):
        entry = entry_of(pick_ref, s, t)

        @pl.when(entry >= 0)
        def _():
            for o in range(3):
                final[...] = jnp.zeros(final.shape, F32)
                for k in range(blocks):
                    start = k * row_block
                    final[start : start + 16, :] += acc[k, 0, s, 16 * o : 16 * o + 16, :]
                out_ref[jnp.maximum(entry, 0), s, o] = jnp.where(keep, final[0:rows, :], 0.0).astype(BF16)

    for k in range(blocks):
        acc[k, 0] = acc[k, 1]
        acc[k, 1] = acc[k, 2]
        acc[k, 2] = jnp.zeros(acc.shape[2:], F32)


def cotangents(parts, here, everyone):
    row = lax.broadcasted_iota(jnp.int32, everyone.shape, 0)
    own = jnp.zeros((1, 128), F32)
    layers = []
    for z in range(parts):
        mine = (row % parts == z) & (row < SCORED * parts)
        found = jnp.sum(jnp.where(mine, everyone, 0.0), axis=0, keepdims=True) / SCORED
        own = jnp.where(here == z, found, own)
        layers.append(found)
    prompt = left(own, 2)
    total = jnp.zeros((1, 128), F32)
    square = jnp.zeros((1, 128), F32)
    for found in layers:
        for s in range(2):
            member = prompt == found[:, 2 + s : 3 + s]
            reward = found[:, s : s + 1]
            total = total + jnp.where(member, reward, 0.0)
            square = square + jnp.where(member, reward * reward, 0.0)
    mean = total / GROUP
    second = square / GROUP - mean * mean
    return -LOSS_SCALE * ((own - mean) * lax.rsqrt(second + SMOOTH)) / SCORED


def shift_frames(pick_ref, grad_ref, shifted, row_count, begin, end, scales):
    starts = range(0, row_count, BACK)
    rows = grad_ref.shape[3]
    shifted[...] = jnp.zeros(shifted.shape, BF16)
    lane = lane_iota(rows)
    blank = jnp.zeros((8, 128), F32)

    def one_frame(frame, carry):
        for s in range(2):
            entry = entry_of(pick_ref, s, frame)
            scale = jnp.where(entry >= 0, scales[s], 0.0)
            source = jnp.maximum(entry, 0)
            moved = [[], [], []]
            for o in range(3):
                value = grad_ref[source, s, o].astype(F32) * scale
                value = jnp.where(lane < COLS, value, 0.0)
                for e, turned in enumerate((pltpu.roll(value, 127, 1), value, pltpu.roll(value, 1, 1))):
                    moved[e].append(turned)
            for k, start in enumerate(starts):
                block = [turned[start : start + 8] for some in moved for turned in some]
                shifted[frame, k, :, 128 * s : 128 * s + 128] = jnp.concatenate(
                    block + [blank], axis=0
                ).astype(BF16)
        return carry

    lax.fori_loop(begin, end, one_frame, 0)


def restore_frame(t, x_ref, slope_ref, band, out_ref, back, shifted, coming):
    row_count = x_ref.shape[1]
    for k, start in enumerate(range(0, row_count, BACK)):
        count = min(BACK, row_count - start)
        operand = jnp.concatenate([shifted[t + 2 - a, k] for a in range(3)], axis=0)
        coming[k, 0 : count * CH, :] = nn_dot(band[0 : count * CH, :], operand)
        for local in range(count):
            row = start + local
            for s in range(2):
                outs, units, total = [], [], None
                for m in range(SPANS // 2):
                    pair = x_ref[0, row, s, 16 * m : 16 * m + 16, :].astype(F32)
                    slopes = slope_ref[0, row, s, 16 * m : 16 * m + 16, :].astype(F32)
                    for part in range(2):
                        g = 2 * m + part
                        unit = pair[8 * part : 8 * part + 8]
                        at = local * CH + 8 * g
                        out = coming[k, at : at + 8, 128 * s : 128 * s + 128] * slopes[8 * part : 8 * part + 8]
                        outs.append(out)
                        units.append(unit)
                        total = out * unit if g == 0 else total + out * unit
                factor = jnp.sum(total, axis=0, keepdims=True) * (1.0 / CH)
                for g in range(SPANS):
                    result = tiles_of(outs[g] - units[g] * factor)
                    back[row % back.shape[0], pl.ds(14 * g + s, 7, stride=2), :] = result[0:7]
            out_ref[0, row] = back[row % back.shape[0]].astype(BF16)


def early_kernel(pick_ref, x_ref, slope_ref, band, grad_ref, out_ref, back, shifted, coming):
    t = pl.program_id(0)

    @pl.when(t == 0)
    def _():
        one = jnp.ones((1, 1), F32)
        shift_frames(pick_ref, grad_ref, shifted, x_ref.shape[1], 0, EARLY + 2, (one, one))

    restore_frame(t, x_ref, slope_ref, band, out_ref, back, shifted, coming)


def restore_kernel(parts, pick_ref, here_ref, everyone_ref, early_ref, x_ref, slope_ref, band, grad_ref, out_ref, back, shifted, coming, scaling):
    t = pl.program_id(0)
    row_count = x_ref.shape[1]

    @pl.when(t == 0)
    def _():
        both = cotangents(parts, here_ref[0], everyone_ref[...])
        scales = (both[:, 0:1], both[:, 1:2])
        scaling[...] = jnp.where(sub_iota(8) % 2 == 0, scales[0], scales[1])
        shift_frames(pick_ref, grad_ref, shifted, row_count, EARLY, pl.num_programs(0), scales)

    @pl.when(t < EARLY)
    def _():
        for row in range(row_count):
            value = early_ref[0, row].astype(F32)
            value = value.reshape(value.shape[0] // 8, 8, 128) * scaling[...]
            out_ref[0, row] = value.reshape(early_ref.shape[2:]).astype(BF16)

    @pl.when(t >= EARLY)
    def _():
        restore_frame(t, x_ref, slope_ref, band, out_ref, back, shifted, coming)


def nt_dot(one, two):
    return lax.dot_general(one, two, (((1,), (1,)), ((), ())), preferred_element_type=F32)


def tn_dot(one, two):
    return lax.dot_general(one, two, (((0,), (0,)), ((), ())), preferred_element_type=F32)


def nn_dot(one, two):
    return jnp.dot(one, two, preferred_element_type=F32)


def split_two(value):
    high = value.astype(BF16)
    low = (value - high.astype(F32)).astype(BF16)
    return jnp.concatenate([high, low], axis=0)


def patch_kernel(row_count, tiles, samples, part_ref, inputs_ref, order, frame, flip, patches):
    height = row_count * tiles
    patch_rows = height // PATCH
    lane64 = lane_iota(8) < 64
    inputs = order.shape[1]
    pixel = lax.broadcasted_iota(jnp.int32, (64, inputs), 0)
    column = lax.broadcasted_iota(jnp.int32, (64, inputs), 1)
    for x in range(PATCH):
        order[64 * x : 64 * x + 64, :] = (
            (column == pixel * PATCH + x) & (pixel < 3 * PATCH)
        ).astype(BF16)

    flip[...] = jnp.zeros(flip.shape, F32)
    frame[...] = jnp.zeros(frame.shape, F32)
    for f in range(samples):
        for i in range(tiles):
            at = row_count * i + 7
            for o in range(3):
                frame[f, o, at : at + row_count + 2, :] += part_ref[i, f, o, 0 : row_count + 2, :].astype(F32)
    for f in range(samples):
        for pair in range(patch_rows // 2):
            turn = flip.at[f * (patch_rows // 2) + pair]
            for local in range(2):
                at = 8 + PATCH * (2 * pair + local)
                for o in range(3):
                    turn[0, 64 * local + PATCH * o : 64 * local + PATCH * o + PATCH, :] = (
                        frame[f, o, at : at + PATCH, :].astype(BF16).astype(F32)
                    )
            turn[1] = turn[0].T
            token = f * NTOK + pair * 16
            for y in range(PATCH // 2):
                even = turn[1, pl.ds(2 * y, 8, stride=PATCH), :]
                odd = turn[1, pl.ds(2 * y + 1, 8, stride=PATCH), :]
                patches[token : token + 8, 128 * y : 128 * y + 128] = jnp.where(lane64, even, pltpu.roll(odd, 64, 1))
                patches[token + 8 : token + 16, 128 * y : 128 * y + 128] = jnp.where(lane64, pltpu.roll(even, 64, 1), odd)

    inputs_ref[...] = nn_dot(patches[...].astype(BF16), order[...]).astype(BF16)


def reward_kernel(
    row_count, tiles, samples,
    group_ref, inputs_ref, order, packed_ref, head_ref,
    out_ref, score_ref,
    pack, arrived, frame, flip, embed, outw, place, patches, tokens, normed, normed16, slots, weights, dslots, dnormed, rows8, abar, both, dweights, dlogits,
):
    height = row_count * tiles
    patch_rows = height // PATCH
    lane64 = lane_iota(8) < 64
    lane = lane_iota(NTOK)
    count = samples * NTOK

    copies = []
    for part, (begin, end) in enumerate(((880, 1120), (640, 880), (0, 640))):
        copies.append(
            pltpu.make_async_copy(
                packed_ref.at[:, begin:end, :], pack.at[:, begin:end, :], arrived.at[part]
            )
        )
        copies[-1].start()

    flip[...] = jnp.zeros(flip.shape, F32)
    copies[0].wait()
    copies[1].wait()

    for i in range(NT):
        for z, (begin, height, target) in enumerate(
            ((0, 48, 128 * i), (0, 48, 128 * i + 48), (0, 32, 128 * i + 96), (16, 32, 1024 + 32 * i))
        ):
            source = pack.at[PLACES[i][z]]
            for part in range(5):
                at = 880 + 48 * part + begin
                embed[target : target + height, 128 * part : 128 * part + 128] = source[at : at + height, :]
    lane48 = lane_iota(48)
    for h in range(HEADS):
        outw[128 * h + HD : 128 * h + 128, :] = jnp.zeros((128 - HD, D), BF16)
    for z in range(NZ):
        for i in range(NT):
            source = pack.at[PLACES[i][z]]
            for local in range(2):
                at, begin = 128 * (2 * z + local), 640 + HD * local
                outw[at : at + HD, 128 * i : 128 * i + 128] = source[begin : begin + HD, :]
            place[32 * z : 32 * z + 32, 128 * i : 128 * i + 128] = source[800:832, :]
        for ib in range(2):
            sources = [pack[PLACES[4 * ib + j][z], 832:880, :].astype(F32) for j in range(4)]
            rolled = [[sources[j] if d == 0 else pltpu.roll(sources[j], 32 * d, 1) for d in range(4)] for j in range(4)]
            at = 1024 + 128 * ib
            for q in range(4):
                found = rolled[0][(0 - q) % 4]
                for j in range(1, 4):
                    found = jnp.where(lane48 >= 32 * j, rolled[j][(j - q) % 4], found)
                found = found.astype(BF16)
                for begin, end, row in (
                    ((0, 48, 0),),
                    ((0, 32, 48), (32, 48, 128)),
                    ((0, 48, 144),),
                    ((0, 16, 192),),
                )[q]:
                    row = 256 * z + row
                    outw[row : row + end - begin, at : at + 128] = found[begin:end]
                if q == 3:
                    place[32 * z : 32 * z + 32, at : at + 128] = found[16:48]

    token_value = nt_dot(inputs_ref[...], embed[...])
    rows8[...] = jnp.zeros(rows8.shape, F32)
    abar[...] = jnp.zeros(abar.shape, F32)
    place_value = place[...].astype(F32)
    for f in range(samples):
        value = token_value[f * NTOK : f * NTOK + NTOK] + place_value
        rows8[0, f : f + 1, :] = jnp.mean(value, axis=0, keepdims=True)
        centered = value - jnp.mean(value, axis=-1, keepdims=True)
        scale = lax.rsqrt(jnp.mean(centered * centered, axis=-1, keepdims=True) + 1e-05)
        value = centered * scale
        normed[f * NTOK : f * NTOK + NTOK, :] = value
        normed16[f * NTOK : f * NTOK + NTOK, :] = value.astype(BF16)
        tokens[f * NTOK : f * NTOK + NTOK, :] = jnp.broadcast_to(scale, (NTOK, 128))

    def weight_part(i, z):
        source = pack.at[PLACES[i][z]]
        return jnp.concatenate([source[0:256, :], source[320:576, :]], axis=1)

    def weight_rest(i):
        return jnp.concatenate(
            [
                jnp.concatenate([pack[PLACES[i][z], 256:320, :], pack[PLACES[i][z], 576:640, :]], axis=1)
                for z in range(NZ)
            ],
            axis=0,
        )

    lane_all = lane_iota(count)
    copies[2].wait()
    for i in range(NT):
        mixed = nn_dot(
            normed16[...], jnp.concatenate([weight_part(i, z) for z in range(NZ)] + [weight_rest(i)], axis=0)
        )
        first, second = mixed[:, 0:128], mixed[:, 128:256]
        found = (
            first,
            jnp.where(lane_all < 48, pltpu.roll(first, 48, 1), pltpu.roll(second, 48, 1)),
            pltpu.roll(second, 96, 1),
        )
        for m in range(3):
            slots[3 * i + m] = jnp.where(lane_all < HD, found[m], 0.0).astype(BF16)

    pairs = [(h, f, h * samples + f, slice(f * NTOK, f * NTOK + NTOK)) for h in range(HEADS) for f in range(samples)]
    for h, f, at, span in pairs:
        weights[at] = nt_dot(slots[h, span, :], slots[HEADS + h, span, :]) * HD ** (-0.5)
    logits = weights[...]
    logits = jnp.exp(logits - jnp.max(logits, axis=-1, keepdims=True))
    prob = logits / jnp.sum(logits, axis=-1, keepdims=True)
    weights[...] = prob
    sums = jnp.sum(prob.astype(BF16).astype(F32), axis=1, keepdims=True)
    for h, f, at, span in pairs:
        two = split_two(jnp.broadcast_to(sums[at], (8, 128)))
        both[at] = two
        mean = nn_dot(two, slots[2 * HEADS + h, span, :]) * (1.0 / NTOK)
        abar[f : f + 1, 128 * h : 128 * h + 128] = mean[0:1] + mean[8:9]

    part = nn_dot(split_two(abar[...]), outw[...])
    pooled = rows8[0] + part[0:8] + part[8:16]
    pooled = pooled - jnp.mean(pooled, axis=-1, keepdims=True)
    scale = lax.rsqrt(jnp.mean(pooled * pooled, axis=-1, keepdims=True) + 1e-05)
    pooled = pooled * scale
    head = head_ref[...]
    score = jnp.sum(pooled * head, axis=-1, keepdims=True)
    lane1 = lane_iota(1)
    sent = jnp.zeros((1, 128), F32)
    for f in range(samples):
        sent = jnp.where(lane1 == f, score[f : f + 1], sent)
        sent = jnp.where(lane1 == samples + f, group_ref[f].astype(F32), sent)
    score_ref[...] = jnp.broadcast_to(sent, score_ref.shape)
    dpooled = scale * (
        head - jnp.mean(head, axis=-1, keepdims=True) - pooled * jnp.mean(pooled * head, axis=-1, keepdims=True)
    )
    dres = dpooled * (1.0 / NTOK)
    rows8[1] = dres
    datts = nt_dot(split_two(dres), outw[...])
    datts = (datts[0:8] + datts[8:16]).astype(BF16)

    first_rows = sub_iota(16) % 8 == 0
    for h, f, at, span in pairs:
        datt = datts[:, 128 * h : 128 * h + 128]
        pair = jnp.where(first_rows, jnp.broadcast_to(datt[f : f + 1].astype(F32), (16, 128)), 0.0).astype(BF16)
        dslots[2 * HEADS + h, span, :] = tn_dot(both[at], pair)
        dweight = nt_dot(datt, slots[2 * HEADS + h, span, :])[f : f + 1, :].astype(BF16).astype(F32)
        dweights[at] = jnp.broadcast_to(dweight, (8, 128))
    prob = weights[...]
    dweight = dweights[:, 0:1, :]
    inner = jnp.sum(prob * dweight, axis=-1, keepdims=True)
    dlogits[...] = (prob * (dweight - inner) * HD ** (-0.5)).astype(BF16)
    for h, f, at, span in pairs:
        dslots[h, span, :] = nn_dot(dlogits[at], slots[HEADS + h, span, :])
        dslots[HEADS + h, span, :] = tn_dot(dlogits[at], slots[h, span, :])

    parts = []
    for i in range(NT):
        one, two, three = dslots[3 * i], dslots[3 * i + 1], dslots[3 * i + 2]
        two = pltpu.roll(two, 80, 1)
        three = pltpu.roll(three, 32, 1)
        first = jnp.where(lane_all < HD, one, two)
        second = jnp.where(lane_all < 32, two, jnp.where(lane_all < COLS, three, 0.0))
        parts += [first.astype(BF16), second.astype(BF16)]
    dmixed = jnp.concatenate(parts, axis=1)
    for z in range(NZ):
        wide = jnp.concatenate([weight_part(i, z) for i in range(NT)], axis=1)
        dnormed[:, 256 * z : 256 * z + 256] = nt_dot(dmixed, wide)
    wide = jnp.concatenate([weight_rest(i) for i in range(NT)], axis=1)
    dnormed[:, 1024:1280] = nt_dot(dmixed, wide)

    for f in range(samples):
        span = slice(f * NTOK, f * NTOK + NTOK)
        value, dvalue = normed[span, :], dnormed[span, :]
        scale = tokens[span, 0:1]
        dvalue = scale * (
            dvalue
            - jnp.mean(dvalue, axis=-1, keepdims=True)
            - value * jnp.mean(dvalue * value, axis=-1, keepdims=True)
        )
        normed16[span, :] = (dvalue + rows8[1, f : f + 1, :]).astype(BF16)
    patches[...] = nt_dot(nn_dot(normed16[...], embed[...]).astype(BF16), order[...])

    frame[...] = jnp.zeros(frame.shape, F32)
    rows = out_ref.shape[3]
    for f in range(samples):
        for pair in range(patch_rows // 2):
            turn = flip.at[f * (patch_rows // 2) + pair]
            token = f * NTOK + pair * 16
            for y in range(PATCH // 2):
                one = patches[token : token + 8, 128 * y : 128 * y + 128]
                two = patches[token + 8 : token + 16, 128 * y : 128 * y + 128]
                turn[1, pl.ds(2 * y, 8, stride=PATCH), :] = jnp.where(lane64, one, pltpu.roll(two, 64, 1))
                turn[1, pl.ds(2 * y + 1, 8, stride=PATCH), :] = jnp.where(lane64, pltpu.roll(one, 64, 1), two)
            turn[0] = turn[1].T
            for local in range(2):
                at = 8 + PATCH * (2 * pair + local)
                for o in range(3):
                    frame[f, o, at : at + PATCH, :] = turn[0, 64 * local + PATCH * o : 64 * local + PATCH * o + PATCH, :]
    for f in range(samples):
        for i in range(tiles):
            at = row_count * i + 7
            for o in range(3):
                out_ref[i, f, o] = frame[f, o, at : at + rows, :].astype(BF16)


def pack_part(rows_in, out_part, place_part, embed_part):
    ordered = jnp.concatenate([rows_in[0:128], rows_in[160:288], rows_in[128:160], rows_in[288:320]], axis=0)
    upper = jnp.pad(ordered[:, 128:240], ((0, 0), (0, 16)))
    other = jnp.concatenate([out_part, place_part], axis=0)
    rest = other[:, 128:160].reshape(4, 48, 32)
    rest = jnp.concatenate([rest[q] for q in range(4)], axis=1)
    embed_part = jnp.pad(embed_part, ((0, 0), (0, 640 - embed_part.shape[1])))
    embed_part = embed_part.reshape(48, 5, 128).transpose(1, 0, 2).reshape(240, 128)
    return jnp.concatenate([ordered[:, 0:128], upper, other[:, 0:128], rest, embed_part], axis=0)


def pack_kernel(z_ref, rows_ref, out_ref, place_ref, embed_ref, packed_ref):
    for source, target, count in ((0, 0, 128), (160, 128, 128), (128, 256, 32), (288, 288, 32)):
        packed_ref[target : target + count, :] = rows_ref[source : source + count, 0:128]
        packed_ref[320 + target : 320 + target + count, :] = jnp.concatenate(
            [rows_ref[source : source + count, 128:240], jnp.zeros((count, 16), BF16)], axis=1
        )
    packed_ref[640:800, :] = out_ref[:, 0:128]
    packed_ref[800:832, :] = place_ref[:, 0:128]
    tail = out_ref[:, 128:160].astype(F32)
    last = place_ref[:, 128:160].astype(F32)
    packed_ref[832:880, :] = jnp.concatenate(
        [tail[0:48], tail[48:96], tail[96:144], jnp.concatenate([tail[144:160], last], axis=0)],
        axis=1,
    ).astype(BF16)
    width = embed_ref.shape[1]
    start = pl.multiple_of(jnp.where(z_ref[0] == NZ - 1, STARTS[-1], 48 * z_ref[0]), 16)
    for part in range(5):
        count = min(128, width - 128 * part)
        value = embed_ref[pl.ds(start, 48), 128 * part : 128 * part + count]
        if count < 128:
            value = jnp.concatenate([value, jnp.zeros((48, 128 - count), BF16)], axis=1)
        packed_ref[880 + 48 * part : 928 + 48 * part, :] = value


def packed_weights(patch_embed, position, attend_in, attend_out):
    if lax.axis_size(TILE) == NT and lax.axis_size("sample") == NZ:
        z = lax.axis_index("sample").astype(jnp.int32).reshape(1)
        mine = pl.pallas_call(
            pack_kernel,
            in_specs=[pl.BlockSpec(memory_space=pltpu.SMEM)] + [pl.BlockSpec(memory_space=pltpu.VMEM)] * 4,
            out_shape=jax.ShapeDtypeStruct((PACK, 128), BF16),
            compiler_params=params(),
            name="pack",
        )(z, attend_in, attend_out, position, patch_embed.T)
        group = [i * NZ + z for i, z in CYCLE]
        return lax.all_gather(mine, TILE + ("sample",), axis=0, axis_index_groups=[group])

    def whole(value):
        value = lax.all_gather(value, "sample", axis=0, tiled=True)
        return lax.all_gather(value, TILE, axis=1, tiled=True)

    split = [
        value.reshape(NZ, value.shape[0] // NZ, NT, value.shape[1] // NT).transpose(2, 0, 1, 3)
        for value in (whole(attend_in), whole(attend_out), whole(position))
    ]
    columns = lax.all_gather(patch_embed.T, TILE, axis=0, tiled=True).reshape(NT, D // NT, -1)
    split.append(jnp.stack([columns[:, start : start + 48] for start in STARTS], axis=1))
    packed = jax.vmap(jax.vmap(pack_part))(*split)
    return jnp.stack([packed[i, z] for i, z in CYCLE])


def params(mib=58):
    return pltpu.CompilerParams(vmem_limit_bytes=mib * 1024 * 1024)


def local(
    features,
    norm_gain,
    conv_weight,
    patch_embed,
    position,
    attend_in,
    attend_out,
    reward_head,
    group_index,
    frame_pick,
):
    samples, frames, row_count, merged = features.shape
    tiles, parts = lax.axis_size(TILE), lax.axis_size("sample")
    sent_rows = -(-(row_count + 2) // 16) * 16
    row_block = row_count if row_count <= 14 else 14
    blocks = row_count // row_block
    inner = row_block * CH
    packed = packed_weights(patch_embed, position, attend_in, attend_out)
    order = Layout((1, 2, 3, 0, 4))
    split = (samples, frames, row_count, merged // 128, 128)
    view = with_layout_constraint(features.reshape(split), order).transpose(1, 2, 3, 0, 4)
    view = view.reshape(frames, row_count, samples * merged // 128, 128)
    gain = norm_gain[None, :]

    smem = pl.BlockSpec(memory_space=pltpu.SMEM)
    view_spec = pl.BlockSpec((1,) + view.shape[1:], lambda t: (t, 0, 0, 0))
    gain_spec = pl.BlockSpec((1, CH), lambda t: (0, 0))
    taps_spec = pl.BlockSpec((3, 3, 3, 3, CH), lambda t: (0, 0, 0, 0, 0))
    sent = (SCORED, samples, 3, sent_rows, 128)
    sent_spec = pl.BlockSpec(sent, lambda t: (0, 0, 0, 0, 0))
    aligned = (frames, row_count, samples, CH, 128)
    aligned_spec = pl.BlockSpec((1,) + aligned[1:], lambda t: (t, 0, 0, 0, 0))
    band_spec = pl.BlockSpec((BACK * CH, BACK_ROWS), lambda t: (0, 0))
    decoded, x_aligned, slopes, band = pl.pallas_call(
        functools.partial(decode_kernel, row_block),
        grid=(frames,),
        in_specs=[smem, view_spec, gain_spec, taps_spec],
        out_specs=[sent_spec, aligned_spec, aligned_spec, band_spec],
        scratch_shapes=[
            pltpu.VMEM((OUT_ROWS, inner), BF16),
            pltpu.VMEM((3, 32, CH), F32),
            pltpu.VMEM((128, 128), F32),
            pltpu.VMEM((row_block, 192, 128), F32),
            pltpu.VMEM((blocks, inner, 256), BF16),
            pltpu.VMEM((blocks, 3, samples, 48, 128), F32),
            pltpu.VMEM((sent_rows + 16, 128), F32),
        ],
        out_shape=[
            jax.ShapeDtypeStruct(sent, BF16),
            jax.ShapeDtypeStruct(aligned, BF16),
            jax.ShapeDtypeStruct(aligned, BF16),
            jax.ShapeDtypeStruct((BACK * CH, BACK_ROWS), BF16),
        ],
        compiler_params=params(),
        name="decode",
    )(frame_pick, view, gain, conv_weight)

    if tiles > SCORED:
        decoded = jnp.pad(decoded, ((0, tiles - SCORED),) + ((0, 0),) * 4)
    owned = lax.all_to_all(decoded, TILE, split_axis=0, concat_axis=0, tiled=True)

    head = reward_head.reshape(NT, D // NT)
    head = jnp.concatenate([head[:, :128].reshape(-1), head[:, 128:].reshape(-1)])[None, :]
    height = row_count * tiles
    count = samples * NTOK
    frame_scratch = pltpu.VMEM((samples, 3, height + 48, 128), F32)
    flip_scratch = pltpu.VMEM((samples * height // (2 * PATCH), 2, 128, 128), F32)
    inputs, input_order = pl.pallas_call(
        functools.partial(patch_kernel, row_count, tiles, samples),
        out_shape=[jax.ShapeDtypeStruct((count, 640), BF16), jax.ShapeDtypeStruct((KIN, 640), BF16)],
        scratch_shapes=[frame_scratch, flip_scratch, pltpu.VMEM((count, KIN), F32)],
        compiler_params=params(),
        name="patches",
    )(owned)
    grads, scores = pl.pallas_call(
        functools.partial(reward_kernel, row_count, tiles, samples),
        out_shape=[
            jax.ShapeDtypeStruct((tiles, samples, 3, sent_rows, 128), BF16),
            jax.ShapeDtypeStruct((tiles * parts, 128), F32),
        ],
        in_specs=[
            smem,
            pl.BlockSpec(memory_space=pltpu.VMEM),
            pl.BlockSpec(memory_space=pltpu.VMEM),
            pl.BlockSpec(memory_space=pl.ANY),
            pl.BlockSpec(memory_space=pltpu.VMEM),
        ],
        scratch_shapes=[
            pltpu.VMEM(packed.shape, BF16),
            pltpu.SemaphoreType.DMA((3,)),
            frame_scratch,
            flip_scratch,
            pltpu.VMEM((D, 640), BF16),
            pltpu.VMEM((HEADS * 128, D), BF16),
            pltpu.VMEM((NTOK, D), BF16),
            pltpu.VMEM((count, KIN), F32),
            pltpu.VMEM((count, 128), F32),
            pltpu.VMEM((count, D), F32),
            pltpu.VMEM((count, D), BF16),
            pltpu.VMEM((3 * HEADS, count, 128), BF16),
            pltpu.VMEM((HEADS * samples, NTOK, NTOK), F32),
            pltpu.VMEM((3 * HEADS, count, 128), F32),
            pltpu.VMEM((count, D), F32),
            pltpu.VMEM((2, 8, D), F32),
            pltpu.VMEM((8, HEADS * 128), F32),
            pltpu.VMEM((HEADS * samples, 16, 128), BF16),
            pltpu.VMEM((HEADS * samples, 8, 128), F32),
            pltpu.VMEM((HEADS * samples, NTOK, NTOK), BF16),
        ],
        compiler_params=params(),
        name="reward",
    )(group_index, inputs, input_order, packed, head)

    returned = lax.all_to_all(grads, TILE, split_axis=0, concat_axis=0, tiled=True)
    scores, returned = lax.optimization_barrier((scores, returned))
    everyone = lax.all_to_all(scores, TILE + ("sample",), split_axis=0, concat_axis=0, tiled=True)
    returned = returned[:SCORED]
    here = lax.axis_index("sample").astype(jnp.int32).reshape(1)

    restore_scratch = [
        pltpu.VMEM((row_block, samples * merged // 128, 128), F32),
        pltpu.VMEM((frames + 2, -(-row_count // BACK), 80, 256), BF16),
        pltpu.VMEM((-(-row_count // BACK), BACK * CH, 256), F32),
    ]
    early = pl.pallas_call(
        early_kernel,
        grid=(EARLY,),
        in_specs=[smem, aligned_spec, aligned_spec, band_spec, sent_spec],
        out_specs=view_spec,
        scratch_shapes=restore_scratch,
        out_shape=jax.ShapeDtypeStruct((EARLY,) + view.shape[1:], BF16),
        compiler_params=params(),
        name="early",
    )(frame_pick, x_aligned, slopes, band, returned)
    late_spec = pl.BlockSpec((1,) + aligned[1:], lambda t: (jnp.maximum(t, EARLY), 0, 0, 0, 0))
    result = pl.pallas_call(
        functools.partial(restore_kernel, parts),
        grid=(frames,),
        in_specs=[
            smem,
            smem,
            pl.BlockSpec((tiles * parts, 128), lambda t: (0, 0)),
            pl.BlockSpec((1,) + view.shape[1:], lambda t: (jnp.minimum(t, EARLY - 1), 0, 0, 0)),
            late_spec,
            late_spec,
            band_spec,
            sent_spec,
        ],
        out_specs=view_spec,
        scratch_shapes=restore_scratch + [pltpu.VMEM((8, 128), F32)],
        out_shape=jax.ShapeDtypeStruct(view.shape, BF16),
        compiler_params=params(),
        name="restore",
    )(frame_pick, here, everyone, early, x_aligned, slopes, band, returned)
    result = result.reshape(frames, row_count, merged // 128, samples, 128).transpose(3, 0, 1, 2, 4)
    return with_layout_constraint(result, order).reshape(features.shape)


def solution(mesh):
    tiles, parts = mesh.devices.shape
    split = Mesh(mesh.devices.reshape(tiles // 2, 2, parts), ("chip", "core", "sample"))
    in_specs = (
        P("sample", None, TILE, None),
        P(),
        P(),
        P(None, TILE),
        P("sample", TILE),
        P("sample", TILE),
        P("sample", TILE),
        P(),
        P("sample"),
        P("sample", None),
    )
    out_specs = P("sample", None, TILE, None)
    return jax.shard_map(local, mesh=split, in_specs=in_specs, out_specs=out_specs, check_vma=False)
```

```python
import functools

import jax
import jax.numpy as jnp
from jax import lax
from jax.experimental import pallas as pl
from jax.experimental.pallas import tpu as pltpu
from jax.experimental.layout import Layout, with_layout_constraint
from jax.sharding import Mesh, PartitionSpec as P

SCORED = 8
PATCH = 14
HEADS = 8
HD = 80
GROUP = 4
LOSS_SCALE = 16384.0
SMOOTH = 0.01

TILE = ("chip", "core")
CH = 96
COLS = 112
SPANS = CH // 8
OUT_ROWS = 27 * 16
BACK = 6
EARLY = 3
BACK_ROWS = 3 * 80
NT = 8
NZ = 4
PACK = 1120
CYCLE = [
    (2 * chip + core, z)
    for chip, heights in ((0, (0, 1, 2, 3)), (1, (3, 2, 1, 0)), (3, (0, 1, 2, 3)), (2, (3, 2, 1, 0)))
    for z in heights
    for core in range(2)
]
PLACES = [[CYCLE.index((i, z)) for z in range(NZ)] for i in range(NT)]
STARTS = (0, 48, 96, 112)
KIN = 896
D = 1280
NTOK = 128
F32 = jnp.float32
BF16 = jnp.bfloat16


def lane_iota(rows):
    return lax.broadcasted_iota(jnp.int32, (rows, 128), 1)


def left(value, amount):
    return pltpu.roll(value, 128 - amount, 1)


def sub_iota(rows):
    return lax.broadcasted_iota(jnp.int32, (rows, 128), 0)


def channels_of(raw, at, group, sample):
    start = 8 + 14 * group + sample
    here = raw[at, pl.ds(start, 8, stride=2), :]
    before = raw[at, pl.ds(start - 2, 8, stride=2), :]
    joined = jnp.where(lane_iota(8) < 128 - 16 * sub_iota(8), here, before)
    return pltpu.roll(joined, 0, 1, stride=16, stride_axis=0)


def tiles_of(value):
    turned = jnp.take_along_axis(value, (lane_iota(8) + 16 * sub_iota(8)) % 128, axis=1)
    return jnp.where(lane_iota(8) < COLS - 16 * sub_iota(8), turned, pltpu.roll(turned, 7, 0))


def load_taps(weight_ref, taps):
    taps[...] = jnp.zeros(taps.shape, F32)
    for a in range(3):
        for b in range(3):
            for e in range(3):
                for o in range(3):
                    at = (a * 3 + e) * 3 + o
                    taps[b, at : at + 1, :] = weight_ref[a, b, e, o : o + 1, :].astype(F32)


def row_of(shape, dim):
    at = lax.broadcasted_iota(jnp.int32, shape, dim)
    return ((at.astype(F32) + 0.5) * (1.0 / CH)).astype(jnp.int32)


def banded(taps, row_block):
    inner = row_block * CH
    pick = (
        lax.broadcasted_iota(jnp.int32, (OUT_ROWS, 32), 0) // 16
        == lax.broadcasted_iota(jnp.int32, (OUT_ROWS, 32), 1)
    ).astype(BF16)
    at = lax.broadcasted_iota(jnp.int32, (CH, inner), 1) - CH * row_of((CH, inner), 1)
    grow = (at == lax.broadcasted_iota(jnp.int32, (CH, inner), 0)).astype(BF16)
    shape = (OUT_ROWS, inner)
    p_at = lax.broadcasted_iota(jnp.int32, shape, 0) % 16
    r_at = row_of(shape, 1)
    total = jnp.zeros(shape, F32)
    for b in range(3):
        rows = nn_dot(pick, taps[b].astype(BF16)).astype(BF16)
        total = jnp.where(p_at == r_at + 2 - b, nn_dot(rows, grow), total)
    return total.astype(BF16)


def banded_back(taps):
    inner = BACK * CH

    def column_of(shape, dim):
        at = lax.broadcasted_iota(jnp.int32, shape, dim)
        a = (at >= 80).astype(jnp.int32) + (at >= 160).astype(jnp.int32)
        return a, at - 80 * a

    a, rest = column_of((BACK_ROWS, 32), 0)
    tap = jnp.where(rest // 8 < 9, 9 * a + rest // 8, 31)
    pick = (tap == lax.broadcasted_iota(jnp.int32, (BACK_ROWS, 32), 1)).astype(BF16)
    at = lax.broadcasted_iota(jnp.int32, (inner, CH), 0) - CH * row_of((inner, CH), 0)
    grow = (at == lax.broadcasted_iota(jnp.int32, (inner, CH), 1)).astype(BF16)
    shape = (inner, BACK_ROWS)
    p_at = column_of(shape, 1)[1] % 8
    r_at = row_of(shape, 0)
    total = jnp.zeros(shape, F32)
    for b in range(3):
        rows = nn_dot(pick, taps[b].astype(BF16)).astype(BF16)
        total = jnp.where(p_at == r_at + 2 - b, nt_dot(grow, rows), total)
    return total.astype(BF16)


def half_gains(gain_ref):
    rows = jnp.concatenate([gain_ref[0:1, :], jnp.zeros((1, 128 - CH), F32)], axis=1)
    return 0.5 * jnp.broadcast_to(rows, (128, 128)).T


def entry_of(pick_ref, sample, frame):
    found = jnp.int32(-1)
    for j in range(SCORED):
        found = jnp.where(pick_ref[sample, j] == frame, jnp.int32(j), found)
    return found


def decode_kernel(row_block, pick_ref, x_ref, gain_ref, weight_ref, out_ref, x_out, slope_out, turned_out, band, taps, gains, raw, operand, acc, final):
    t = pl.program_id(0)
    blocks = x_ref.shape[1] // row_block
    rows = out_ref.shape[3]

    @pl.when(t == 0)
    def _():
        load_taps(weight_ref, taps)
        band[...] = banded(taps, row_block)
        turned_out[...] = banded_back(taps)
        gains[...] = half_gains(gain_ref)
        acc[...] = jnp.zeros(acc.shape, F32)
        raw[...] = jnp.zeros(raw.shape, F32)

    for k in range(blocks):

        def one_row(row, at):
            raw[at, 8:176, :] = x_ref[0, k * row_block + row].astype(F32)
            for s in range(2):
                found = [channels_of(raw, at, g, s) for g in range(SPANS)]
                square = found[0] * found[0]
                for g in range(1, SPANS):
                    square = square + found[g] * found[g]
                second = jnp.sum(square, axis=0, keepdims=True) * (1.0 / CH)
                inv = lax.rsqrt(second + 1e-06)
                for m in range(SPANS // 2):
                    x_out[0, k * row_block + row, s, 16 * m : 16 * m + 16, :] = jnp.concatenate(
                        [found[2 * m] * inv, found[2 * m + 1] * inv], axis=0
                    ).astype(BF16)
                    acts, slopes = [], []
                    for g in (2 * m, 2 * m + 1):
                        gain = gains[8 * g : 8 * g + 8, :]
                        half = found[g] * inv * gain
                        th = jnp.tanh(half)
                        rest = half - half * th
                        acts.append(half + half * th)
                        slopes.append((gain * inv) * (1.0 + th) * (1.0 + rest))
                    slope_out[0, k * row_block + row, s, 16 * m : 16 * m + 16, :] = jnp.concatenate(
                        slopes, axis=0
                    ).astype(BF16)
                    start = row * CH + 16 * m
                    operand[k, start : start + 16, 128 * s : 128 * s + 128] = jnp.concatenate(
                        acts, axis=0
                    ).astype(BF16)

        for row in range(row_block):
            one_row(row, row)
        spread = jnp.dot(band[...], operand[k], preferred_element_type=F32)
        lane = lane_iota(48)
        for s in range(2):
            part = spread[:, 128 * s : 128 * s + 128]
            for a in range(3):
                low, mid, high = (part[144 * a + 48 * e : 144 * a + 48 * e + 48] for e in range(3))
                low = jnp.where(lane == 0, 0.0, pltpu.roll(low, 1, 1))
                high = jnp.where(lane == COLS - 1, 0.0, pltpu.roll(high, 127, 1))
                acc[k, 2 - a, s] += low + mid + high

    keep = lane_iota(rows) < COLS
    for s in range(2):
        entry = entry_of(pick_ref, s, t)

        @pl.when(entry >= 0)
        def _():
            for o in range(3):
                final[...] = jnp.zeros(final.shape, F32)
                for k in range(blocks):
                    start = k * row_block
                    final[start : start + 16, :] += acc[k, 0, s, 16 * o : 16 * o + 16, :]
                out_ref[jnp.maximum(entry, 0), s, o] = jnp.where(keep, final[0:rows, :], 0.0).astype(BF16)

    for k in range(blocks):
        acc[k, 0] = acc[k, 1]
        acc[k, 1] = acc[k, 2]
        acc[k, 2] = jnp.zeros(acc.shape[2:], F32)


def cotangents(parts, here, everyone):
    row = lax.broadcasted_iota(jnp.int32, everyone.shape, 0)
    own = jnp.zeros((1, 128), F32)
    layers = []
    for z in range(parts):
        mine = (row % parts == z) & (row < SCORED * parts)
        found = jnp.sum(jnp.where(mine, everyone, 0.0), axis=0, keepdims=True) / SCORED
        own = jnp.where(here == z, found, own)
        layers.append(found)
    prompt = left(own, 2)
    total = jnp.zeros((1, 128), F32)
    square = jnp.zeros((1, 128), F32)
    for found in layers:
        for s in range(2):
            member = prompt == found[:, 2 + s : 3 + s]
            reward = found[:, s : s + 1]
            total = total + jnp.where(member, reward, 0.0)
            square = square + jnp.where(member, reward * reward, 0.0)
    mean = total / GROUP
    second = square / GROUP - mean * mean
    return -LOSS_SCALE * ((own - mean) * lax.rsqrt(second + SMOOTH)) / SCORED


def shift_frames(entry_ref, grad_ref, shifted, row_count, begin, end, scales):
    starts = range(0, row_count, BACK)
    rows = grad_ref.shape[3]
    shifted[...] = jnp.zeros(shifted.shape, BF16)
    lane = lane_iota(rows)
    blank = jnp.zeros((8, 128), F32)

    def one_frame(frame, carry):
        for s in range(2):
            entry = entry_ref[s, frame]
            scale = jnp.where(entry >= 0, scales[s], 0.0)
            source = jnp.maximum(entry, 0)
            moved = [[], [], []]
            for o in range(3):
                value = grad_ref[source, s, o].astype(F32) * scale
                value = jnp.where(lane < COLS, value, 0.0)
                for e, turned in enumerate((pltpu.roll(value, 127, 1), value, pltpu.roll(value, 1, 1))):
                    moved[e].append(turned)
            for k, start in enumerate(starts):
                block = [turned[start : start + 8] for some in moved for turned in some]
                shifted[frame, k, :, 128 * s : 128 * s + 128] = jnp.concatenate(
                    block + [blank], axis=0
                ).astype(BF16)
        return carry

    lax.fori_loop(begin, end, one_frame, 0)


def restore_frame(t, x_ref, slope_ref, band, out_ref, back, shifted, coming, factors):
    row_count = x_ref.shape[1]
    for k, start in enumerate(range(0, row_count, BACK)):
        count = min(BACK, row_count - start)
        operand = jnp.concatenate([shifted[t + 2 - a, k] for a in range(3)], axis=0)
        coming[k, 0 : count * CH, :] = nn_dot(band[0 : count * CH, :], operand)
        places = [(local, s) for local in range(count) for s in range(2)]
        for local, s in places:
            totals = []
            for m in range(SPANS // 2):
                pair = x_ref[0, start + local, s, 16 * m : 16 * m + 16, :].astype(F32)
                slopes = slope_ref[0, start + local, s, 16 * m : 16 * m + 16, :].astype(F32)
                at = local * CH + 16 * m
                out = coming[k, at : at + 16, 128 * s : 128 * s + 128] * slopes
                coming[k, at : at + 16, 128 * s : 128 * s + 128] = out
                out = out * pair
                totals.append(out[0:8] + out[8:16])
            while len(totals) > 1:
                totals = [sum(totals[i + 1 : i + 2], totals[i]) for i in range(0, len(totals), 2)]
            factors[k, local * 2 + s] = totals[0]
        found = jnp.sum(factors[k], axis=1, keepdims=True) * (1.0 / CH)
        for local, s in places:
            row = start + local
            for m in range(SPANS // 2):
                pair = x_ref[0, row, s, 16 * m : 16 * m + 16, :].astype(F32)
                at = local * CH + 16 * m
                result = coming[k, at : at + 16, 128 * s : 128 * s + 128] - pair * found[local * 2 + s]
                for part in range(2):
                    g = 2 * m + part
                    moved = tiles_of(result[8 * part : 8 * part + 8])
                    back[row % back.shape[0], pl.ds(14 * g + s, 7, stride=2), :] = moved[0:7]
        for local in range(count):
            row = start + local
            out_ref[0, row] = back[row % back.shape[0]].astype(BF16)


def early_kernel(entry_ref, x_ref, slope_ref, band, grad_ref, out_ref, back, shifted, coming, factors):
    t = pl.program_id(0)

    @pl.when(t == 0)
    def _():
        one = jnp.ones((1, 1), F32)
        shift_frames(entry_ref, grad_ref, shifted, x_ref.shape[1], 0, EARLY + 2, (one, one))

    restore_frame(t, x_ref, slope_ref, band, out_ref, back, shifted, coming, factors)


def restore_kernel(parts, entry_ref, here_ref, everyone_ref, early_ref, x_ref, slope_ref, band, grad_ref, out_ref, back, shifted, coming, factors, scaling):
    t = pl.program_id(0)
    row_count = x_ref.shape[1]

    @pl.when(t == 0)
    def _():
        both = cotangents(parts, here_ref[0], everyone_ref[...])
        scales = (both[:, 0:1], both[:, 1:2])
        scaling[...] = jnp.where(sub_iota(8) % 2 == 0, scales[0], scales[1])
        shift_frames(entry_ref, grad_ref, shifted, row_count, EARLY, pl.num_programs(0), scales)

    @pl.when(t < EARLY)
    def _():
        for row in range(row_count):
            value = early_ref[0, row].astype(F32)
            value = value.reshape(value.shape[0] // 8, 8, 128) * scaling[...]
            out_ref[0, row] = value.reshape(early_ref.shape[2:]).astype(BF16)

    @pl.when(t >= EARLY)
    def _():
        restore_frame(t, x_ref, slope_ref, band, out_ref, back, shifted, coming, factors)


def nt_dot(one, two):
    return lax.dot_general(one, two, (((1,), (1,)), ((), ())), preferred_element_type=F32)


def tn_dot(one, two):
    return lax.dot_general(one, two, (((0,), (0,)), ((), ())), preferred_element_type=F32)


def nn_dot(one, two):
    return jnp.dot(one, two, preferred_element_type=F32)


def split_two(value):
    high = value.astype(BF16)
    low = (value - high.astype(F32)).astype(BF16)
    return jnp.concatenate([high, low], axis=0)


def patch_kernel(row_count, tiles, samples, part_ref, inputs_ref, order, frame, flip, patches):
    height = row_count * tiles
    patch_rows = height // PATCH
    lane64 = lane_iota(8) < 64
    inputs = order.shape[1]
    pixel = lax.broadcasted_iota(jnp.int32, (64, inputs), 0)
    column = lax.broadcasted_iota(jnp.int32, (64, inputs), 1)
    for x in range(PATCH):
        order[64 * x : 64 * x + 64, :] = (
            (column == pixel * PATCH + x) & (pixel < 3 * PATCH)
        ).astype(BF16)

    flip[...] = jnp.zeros(flip.shape, F32)
    frame[...] = jnp.zeros(frame.shape, F32)
    for f in range(samples):
        for i in range(tiles):
            at = row_count * i + 7
            for o in range(3):
                frame[f, o, at : at + row_count + 2, :] += part_ref[i, f, o, 0 : row_count + 2, :].astype(F32)
    for f in range(samples):
        for pair in range(patch_rows // 2):
            turn = flip.at[f * (patch_rows // 2) + pair]
            for local in range(2):
                at = 8 + PATCH * (2 * pair + local)
                for o in range(3):
                    turn[0, 64 * local + PATCH * o : 64 * local + PATCH * o + PATCH, :] = (
                        frame[f, o, at : at + PATCH, :].astype(BF16).astype(F32)
                    )
            turn[1] = turn[0].T
            token = f * NTOK + pair * 16
            for y in range(PATCH // 2):
                even = turn[1, pl.ds(2 * y, 8, stride=PATCH), :]
                odd = turn[1, pl.ds(2 * y + 1, 8, stride=PATCH), :]
                patches[token : token + 8, 128 * y : 128 * y + 128] = jnp.where(lane64, even, pltpu.roll(odd, 64, 1))
                patches[token + 8 : token + 16, 128 * y : 128 * y + 128] = jnp.where(lane64, pltpu.roll(even, 64, 1), odd)

    inputs_ref[...] = nn_dot(patches[...].astype(BF16), order[...]).astype(BF16)


def reward_kernel(
    row_count, tiles, samples,
    group_ref, inputs_ref, order, packed_ref, head_ref,
    out_ref, score_ref,
    pack, arrived, frame, flip, embed, outw, place, patches, tokens, normed, normed16, slots, weights, dslots, dnormed, rows8, abar, both, dweights, dlogits,
):
    height = row_count * tiles
    patch_rows = height // PATCH
    lane64 = lane_iota(8) < 64
    lane = lane_iota(NTOK)
    count = samples * NTOK

    copies = []
    for part, (begin, end) in enumerate(((880, 1120), (640, 880), (0, 640))):
        copies.append(
            pltpu.make_async_copy(
                packed_ref.at[:, begin:end, :], pack.at[:, begin:end, :], arrived.at[part]
            )
        )
        copies[-1].start()

    flip[...] = jnp.zeros(flip.shape, F32)
    copies[0].wait()
    copies[1].wait()

    for i in range(NT):
        for z, (begin, height, target) in enumerate(
            ((0, 48, 128 * i), (0, 48, 128 * i + 48), (0, 32, 128 * i + 96), (16, 32, 1024 + 32 * i))
        ):
            source = pack.at[PLACES[i][z]]
            for part in range(5):
                at = 880 + 48 * part + begin
                embed[target : target + height, 128 * part : 128 * part + 128] = source[at : at + height, :]
    lane48 = lane_iota(48)
    for h in range(HEADS):
        outw[128 * h + HD : 128 * h + 128, :] = jnp.zeros((128 - HD, D), BF16)
    for z in range(NZ):
        for i in range(NT):
            source = pack.at[PLACES[i][z]]
            for local in range(2):
                at, begin = 128 * (2 * z + local), 640 + HD * local
                outw[at : at + HD, 128 * i : 128 * i + 128] = source[begin : begin + HD, :]
            place[32 * z : 32 * z + 32, 128 * i : 128 * i + 128] = source[800:832, :]
        for ib in range(2):
            sources = [pack[PLACES[4 * ib + j][z], 832:880, :].astype(F32) for j in range(4)]
            rolled = [[sources[j] if d == 0 else pltpu.roll(sources[j], 32 * d, 1) for d in range(4)] for j in range(4)]
            at = 1024 + 128 * ib
            for q in range(4):
                found = rolled[0][(0 - q) % 4]
                for j in range(1, 4):
                    found = jnp.where(lane48 >= 32 * j, rolled[j][(j - q) % 4], found)
                found = found.astype(BF16)
                for begin, end, row in (
                    ((0, 48, 0),),
                    ((0, 32, 48), (32, 48, 128)),
                    ((0, 48, 144),),
                    ((0, 16, 192),),
                )[q]:
                    row = 256 * z + row
                    outw[row : row + end - begin, at : at + 128] = found[begin:end]
                if q == 3:
                    place[32 * z : 32 * z + 32, at : at + 128] = found[16:48]

    token_value = nt_dot(inputs_ref[...], embed[...])
    rows8[...] = jnp.zeros(rows8.shape, F32)
    abar[...] = jnp.zeros(abar.shape, F32)
    place_value = place[...].astype(F32)
    for f in range(samples):
        value = token_value[f * NTOK : f * NTOK + NTOK] + place_value
        rows8[0, f : f + 1, :] = jnp.mean(value, axis=0, keepdims=True)
        centered = value - jnp.mean(value, axis=-1, keepdims=True)
        scale = lax.rsqrt(jnp.mean(centered * centered, axis=-1, keepdims=True) + 1e-05)
        value = centered * scale
        normed[f * NTOK : f * NTOK + NTOK, :] = value
        normed16[f * NTOK : f * NTOK + NTOK, :] = value.astype(BF16)
        tokens[f * NTOK : f * NTOK + NTOK, :] = jnp.broadcast_to(scale, (NTOK, 128))

    def weight_part(i, z):
        source = pack.at[PLACES[i][z]]
        return jnp.concatenate([source[0:256, :], source[320:576, :]], axis=1)

    def weight_rest(i):
        return jnp.concatenate(
            [
                jnp.concatenate([pack[PLACES[i][z], 256:320, :], pack[PLACES[i][z], 576:640, :]], axis=1)
                for z in range(NZ)
            ],
            axis=0,
        )

    lane_all = lane_iota(count)
    copies[2].wait()
    for i in range(NT):
        mixed = nn_dot(
            normed16[...], jnp.concatenate([weight_part(i, z) for z in range(NZ)] + [weight_rest(i)], axis=0)
        )
        first, second = mixed[:, 0:128], mixed[:, 128:256]
        found = (
            first,
            jnp.where(lane_all < 48, pltpu.roll(first, 48, 1), pltpu.roll(second, 48, 1)),
            pltpu.roll(second, 96, 1),
        )
        for m in range(3):
            slots[3 * i + m] = jnp.where(lane_all < HD, found[m], 0.0).astype(BF16)

    pairs = [(h, f, h * samples + f, slice(f * NTOK, f * NTOK + NTOK)) for h in range(HEADS) for f in range(samples)]
    for h, f, at, span in pairs:
        weights[at] = nt_dot(slots[h, span, :], slots[HEADS + h, span, :]) * HD ** (-0.5)
    logits = weights[...]
    logits = jnp.exp(logits - jnp.max(logits, axis=-1, keepdims=True))
    prob = logits / jnp.sum(logits, axis=-1, keepdims=True)
    weights[...] = prob
    sums = jnp.sum(prob.astype(BF16).astype(F32), axis=1, keepdims=True)
    for h, f, at, span in pairs:
        two = split_two(jnp.broadcast_to(sums[at], (8, 128)))
        both[at] = two
        mean = nn_dot(two, slots[2 * HEADS + h, span, :]) * (1.0 / NTOK)
        abar[f : f + 1, 128 * h : 128 * h + 128] = mean[0:1] + mean[8:9]

    part = nn_dot(split_two(abar[...]), outw[...])
    pooled = rows8[0] + part[0:8] + part[8:16]
    pooled = pooled - jnp.mean(pooled, axis=-1, keepdims=True)
    scale = lax.rsqrt(jnp.mean(pooled * pooled, axis=-1, keepdims=True) + 1e-05)
    pooled = pooled * scale
    head = head_ref[...]
    score = jnp.sum(pooled * head, axis=-1, keepdims=True)
    lane1 = lane_iota(1)
    sent = jnp.zeros((1, 128), F32)
    for f in range(samples):
        sent = jnp.where(lane1 == f, score[f : f + 1], sent)
        sent = jnp.where(lane1 == samples + f, group_ref[f].astype(F32), sent)
    score_ref[...] = jnp.broadcast_to(sent, score_ref.shape)
    dpooled = scale * (
        head - jnp.mean(head, axis=-1, keepdims=True) - pooled * jnp.mean(pooled * head, axis=-1, keepdims=True)
    )
    dres = dpooled * (1.0 / NTOK)
    rows8[1] = dres
    datts = nt_dot(split_two(dres), outw[...])
    datts = (datts[0:8] + datts[8:16]).astype(BF16)

    first_rows = sub_iota(16) % 8 == 0
    for h, f, at, span in pairs:
        datt = datts[:, 128 * h : 128 * h + 128]
        pair = jnp.where(first_rows, jnp.broadcast_to(datt[f : f + 1].astype(F32), (16, 128)), 0.0).astype(BF16)
        dslots[2 * HEADS + h, span, :] = tn_dot(both[at], pair)
        dweight = nt_dot(datt, slots[2 * HEADS + h, span, :])[f : f + 1, :].astype(BF16).astype(F32)
        dweights[at] = jnp.broadcast_to(dweight, (8, 128))
    prob = weights[...]
    dweight = dweights[:, 0:1, :]
    inner = jnp.sum(prob * dweight, axis=-1, keepdims=True)
    dlogits[...] = (prob * (dweight - inner) * HD ** (-0.5)).astype(BF16)
    for h, f, at, span in pairs:
        dslots[h, span, :] = nn_dot(dlogits[at], slots[HEADS + h, span, :])
        dslots[HEADS + h, span, :] = tn_dot(dlogits[at], slots[h, span, :])

    parts = []
    for i in range(NT):
        one, two, three = dslots[3 * i], dslots[3 * i + 1], dslots[3 * i + 2]
        two = pltpu.roll(two, 80, 1)
        three = pltpu.roll(three, 32, 1)
        first = jnp.where(lane_all < HD, one, two)
        second = jnp.where(lane_all < 32, two, jnp.where(lane_all < COLS, three, 0.0))
        parts += [first.astype(BF16), second.astype(BF16)]
    dmixed = jnp.concatenate(parts, axis=1)
    for z in range(NZ):
        wide = jnp.concatenate([weight_part(i, z) for i in range(NT)], axis=1)
        dnormed[:, 256 * z : 256 * z + 256] = nt_dot(dmixed, wide)
    wide = jnp.concatenate([weight_rest(i) for i in range(NT)], axis=1)
    dnormed[:, 1024:1280] = nt_dot(dmixed, wide)

    for f in range(samples):
        span = slice(f * NTOK, f * NTOK + NTOK)
        value, dvalue = normed[span, :], dnormed[span, :]
        scale = tokens[span, 0:1]
        dvalue = scale * (
            dvalue
            - jnp.mean(dvalue, axis=-1, keepdims=True)
            - value * jnp.mean(dvalue * value, axis=-1, keepdims=True)
        )
        normed16[span, :] = (dvalue + rows8[1, f : f + 1, :]).astype(BF16)
    patches[...] = nt_dot(nn_dot(normed16[...], embed[...]).astype(BF16), order[...])

    frame[...] = jnp.zeros(frame.shape, F32)
    rows = out_ref.shape[3]
    for f in range(samples):
        for pair in range(patch_rows // 2):
            turn = flip.at[f * (patch_rows // 2) + pair]
            token = f * NTOK + pair * 16
            for y in range(PATCH // 2):
                one = patches[token : token + 8, 128 * y : 128 * y + 128]
                two = patches[token + 8 : token + 16, 128 * y : 128 * y + 128]
                turn[1, pl.ds(2 * y, 8, stride=PATCH), :] = jnp.where(lane64, one, pltpu.roll(two, 64, 1))
                turn[1, pl.ds(2 * y + 1, 8, stride=PATCH), :] = jnp.where(lane64, pltpu.roll(one, 64, 1), two)
            turn[0] = turn[1].T
            for local in range(2):
                at = 8 + PATCH * (2 * pair + local)
                for o in range(3):
                    frame[f, o, at : at + PATCH, :] = turn[0, 64 * local + PATCH * o : 64 * local + PATCH * o + PATCH, :]
    for f in range(samples):
        for i in range(tiles):
            at = row_count * i + 7
            for o in range(3):
                out_ref[i, f, o] = frame[f, o, at : at + rows, :].astype(BF16)


def pack_part(rows_in, out_part, place_part, embed_part):
    ordered = jnp.concatenate([rows_in[0:128], rows_in[160:288], rows_in[128:160], rows_in[288:320]], axis=0)
    upper = jnp.pad(ordered[:, 128:240], ((0, 0), (0, 16)))
    other = jnp.concatenate([out_part, place_part], axis=0)
    rest = other[:, 128:160].reshape(4, 48, 32)
    rest = jnp.concatenate([rest[q] for q in range(4)], axis=1)
    embed_part = jnp.pad(embed_part, ((0, 0), (0, 640 - embed_part.shape[1])))
    embed_part = embed_part.reshape(48, 5, 128).transpose(1, 0, 2).reshape(240, 128)
    return jnp.concatenate([ordered[:, 0:128], upper, other[:, 0:128], rest, embed_part], axis=0)


def pack_kernel(z_ref, rows_ref, out_ref, place_ref, embed_ref, packed_ref):
    for source, target, count in ((0, 0, 128), (160, 128, 128), (128, 256, 32), (288, 288, 32)):
        packed_ref[target : target + count, :] = rows_ref[source : source + count, 0:128]
        packed_ref[320 + target : 320 + target + count, :] = jnp.concatenate(
            [rows_ref[source : source + count, 128:240], jnp.zeros((count, 16), BF16)], axis=1
        )
    packed_ref[640:800, :] = out_ref[:, 0:128]
    packed_ref[800:832, :] = place_ref[:, 0:128]
    tail = out_ref[:, 128:160].astype(F32)
    last = place_ref[:, 128:160].astype(F32)
    packed_ref[832:880, :] = jnp.concatenate(
        [tail[0:48], tail[48:96], tail[96:144], jnp.concatenate([tail[144:160], last], axis=0)],
        axis=1,
    ).astype(BF16)
    width = embed_ref.shape[1]
    start = pl.multiple_of(jnp.where(z_ref[0] == NZ - 1, STARTS[-1], 48 * z_ref[0]), 16)
    for part in range(5):
        count = min(128, width - 128 * part)
        value = embed_ref[pl.ds(start, 48), 128 * part : 128 * part + count]
        if count < 128:
            value = jnp.concatenate([value, jnp.zeros((48, 128 - count), BF16)], axis=1)
        packed_ref[880 + 48 * part : 928 + 48 * part, :] = value


def packed_weights(patch_embed, position, attend_in, attend_out):
    if lax.axis_size(TILE) == NT and lax.axis_size("sample") == NZ:
        z = lax.axis_index("sample").astype(jnp.int32).reshape(1)
        mine = pl.pallas_call(
            pack_kernel,
            in_specs=[pl.BlockSpec(memory_space=pltpu.SMEM)] + [pl.BlockSpec(memory_space=pltpu.VMEM)] * 4,
            out_shape=jax.ShapeDtypeStruct((PACK, 128), BF16),
            compiler_params=params(),
            name="pack",
        )(z, attend_in, attend_out, position, patch_embed.T)
        group = [i * NZ + z for i, z in CYCLE]
        return lax.all_gather(mine, TILE + ("sample",), axis=0, axis_index_groups=[group])

    def whole(value):
        value = lax.all_gather(value, "sample", axis=0, tiled=True)
        return lax.all_gather(value, TILE, axis=1, tiled=True)

    split = [
        value.reshape(NZ, value.shape[0] // NZ, NT, value.shape[1] // NT).transpose(2, 0, 1, 3)
        for value in (whole(attend_in), whole(attend_out), whole(position))
    ]
    columns = lax.all_gather(patch_embed.T, TILE, axis=0, tiled=True).reshape(NT, D // NT, -1)
    split.append(jnp.stack([columns[:, start : start + 48] for start in STARTS], axis=1))
    packed = jax.vmap(jax.vmap(pack_part))(*split)
    return jnp.stack([packed[i, z] for i, z in CYCLE])


def params(mib=58):
    return pltpu.CompilerParams(vmem_limit_bytes=mib * 1024 * 1024)


def local(
    features,
    norm_gain,
    conv_weight,
    patch_embed,
    position,
    attend_in,
    attend_out,
    reward_head,
    group_index,
    frame_pick,
):
    samples, frames, row_count, merged = features.shape
    tiles, parts = lax.axis_size(TILE), lax.axis_size("sample")
    sent_rows = -(-(row_count + 2) // 16) * 16
    row_block = row_count if row_count <= 14 else 14
    blocks = row_count // row_block
    inner = row_block * CH
    packed = packed_weights(patch_embed, position, attend_in, attend_out)
    order = Layout((1, 2, 3, 0, 4))
    split = (samples, frames, row_count, merged // 128, 128)
    view = with_layout_constraint(features.reshape(split), order).transpose(1, 2, 3, 0, 4)
    view = view.reshape(frames, row_count, samples * merged // 128, 128)
    gain = norm_gain[None, :]

    smem = pl.BlockSpec(memory_space=pltpu.SMEM)
    view_spec = pl.BlockSpec((1,) + view.shape[1:], lambda t: (t, 0, 0, 0))
    gain_spec = pl.BlockSpec((1, CH), lambda t: (0, 0))
    taps_spec = pl.BlockSpec((3, 3, 3, 3, CH), lambda t: (0, 0, 0, 0, 0))
    sent = (SCORED, samples, 3, sent_rows, 128)
    sent_spec = pl.BlockSpec(sent, lambda t: (0, 0, 0, 0, 0))
    aligned = (frames, row_count, samples, CH, 128)
    aligned_spec = pl.BlockSpec((1,) + aligned[1:], lambda t: (t, 0, 0, 0, 0))
    band_spec = pl.BlockSpec((BACK * CH, BACK_ROWS), lambda t: (0, 0))
    decoded, x_aligned, slopes, band = pl.pallas_call(
        functools.partial(decode_kernel, row_block),
        grid=(frames,),
        in_specs=[smem, view_spec, gain_spec, taps_spec],
        out_specs=[sent_spec, aligned_spec, aligned_spec, band_spec],
        scratch_shapes=[
            pltpu.VMEM((OUT_ROWS, inner), BF16),
            pltpu.VMEM((3, 32, CH), F32),
            pltpu.VMEM((128, 128), F32),
            pltpu.VMEM((row_block, 192, 128), F32),
            pltpu.VMEM((blocks, inner, 256), BF16),
            pltpu.VMEM((blocks, 3, samples, 48, 128), F32),
            pltpu.VMEM((sent_rows + 16, 128), F32),
        ],
        out_shape=[
            jax.ShapeDtypeStruct(sent, BF16),
            jax.ShapeDtypeStruct(aligned, BF16),
            jax.ShapeDtypeStruct(aligned, BF16),
            jax.ShapeDtypeStruct((BACK * CH, BACK_ROWS), BF16),
        ],
        compiler_params=params(),
        name="decode",
    )(frame_pick, view, gain, conv_weight)

    if tiles > SCORED:
        decoded = jnp.pad(decoded, ((0, tiles - SCORED),) + ((0, 0),) * 4)
    owned = lax.all_to_all(decoded, TILE, split_axis=0, concat_axis=0, tiled=True)

    head = reward_head.reshape(NT, D // NT)
    head = jnp.concatenate([head[:, :128].reshape(-1), head[:, 128:].reshape(-1)])[None, :]
    height = row_count * tiles
    count = samples * NTOK
    frame_scratch = pltpu.VMEM((samples, 3, height + 48, 128), F32)
    flip_scratch = pltpu.VMEM((samples * height // (2 * PATCH), 2, 128, 128), F32)
    inputs, input_order = pl.pallas_call(
        functools.partial(patch_kernel, row_count, tiles, samples),
        out_shape=[jax.ShapeDtypeStruct((count, 640), BF16), jax.ShapeDtypeStruct((KIN, 640), BF16)],
        scratch_shapes=[frame_scratch, flip_scratch, pltpu.VMEM((count, KIN), F32)],
        compiler_params=params(),
        name="patches",
    )(owned)
    grads, scores = pl.pallas_call(
        functools.partial(reward_kernel, row_count, tiles, samples),
        out_shape=[
            jax.ShapeDtypeStruct((tiles, samples, 3, sent_rows, 128), BF16),
            jax.ShapeDtypeStruct((tiles * parts, 128), F32),
        ],
        in_specs=[
            smem,
            pl.BlockSpec(memory_space=pltpu.VMEM),
            pl.BlockSpec(memory_space=pltpu.VMEM),
            pl.BlockSpec(memory_space=pl.ANY),
            pl.BlockSpec(memory_space=pltpu.VMEM),
        ],
        scratch_shapes=[
            pltpu.VMEM(packed.shape, BF16),
            pltpu.SemaphoreType.DMA((3,)),
            frame_scratch,
            flip_scratch,
            pltpu.VMEM((D, 640), BF16),
            pltpu.VMEM((HEADS * 128, D), BF16),
            pltpu.VMEM((NTOK, D), BF16),
            pltpu.VMEM((count, KIN), F32),
            pltpu.VMEM((count, 128), F32),
            pltpu.VMEM((count, D), F32),
            pltpu.VMEM((count, D), BF16),
            pltpu.VMEM((3 * HEADS, count, 128), BF16),
            pltpu.VMEM((HEADS * samples, NTOK, NTOK), F32),
            pltpu.VMEM((3 * HEADS, count, 128), F32),
            pltpu.VMEM((count, D), F32),
            pltpu.VMEM((2, 8, D), F32),
            pltpu.VMEM((8, HEADS * 128), F32),
            pltpu.VMEM((HEADS * samples, 16, 128), BF16),
            pltpu.VMEM((HEADS * samples, 8, 128), F32),
            pltpu.VMEM((HEADS * samples, NTOK, NTOK), BF16),
        ],
        compiler_params=params(),
        name="reward",
    )(group_index, inputs, input_order, packed, head)

    returned = lax.all_to_all(grads, TILE, split_axis=0, concat_axis=0, tiled=True)
    picks, scores = lax.optimization_barrier((frame_pick, scores))
    is_entry = picks[:, None, :] == jnp.arange(frames, dtype=jnp.int32)[None, :, None]
    entry = jnp.max(jnp.where(is_entry, jnp.arange(SCORED, dtype=jnp.int32)[None, None, :], -1), axis=2)
    scores, returned = lax.optimization_barrier((scores, returned))
    everyone = lax.all_to_all(scores, TILE + ("sample",), split_axis=0, concat_axis=0, tiled=True)
    returned = returned[:SCORED]
    here = lax.axis_index("sample").astype(jnp.int32).reshape(1)

    restore_scratch = [
        pltpu.VMEM((row_block, samples * merged // 128, 128), F32),
        pltpu.VMEM((frames + 2, -(-row_count // BACK), 80, 256), BF16),
        pltpu.VMEM((-(-row_count // BACK), BACK * CH, 256), F32),
        pltpu.VMEM((-(-row_count // BACK), BACK * 2, 8, 128), F32),
    ]
    early = pl.pallas_call(
        early_kernel,
        grid=(EARLY,),
        in_specs=[smem, aligned_spec, aligned_spec, band_spec, sent_spec],
        out_specs=view_spec,
        scratch_shapes=restore_scratch,
        out_shape=jax.ShapeDtypeStruct((EARLY,) + view.shape[1:], BF16),
        compiler_params=params(),
        name="early",
    )(entry, x_aligned, slopes, band, returned)
    late_spec = pl.BlockSpec((1,) + aligned[1:], lambda t: (jnp.maximum(t, EARLY), 0, 0, 0, 0))
    result = pl.pallas_call(
        functools.partial(restore_kernel, parts),
        grid=(frames,),
        in_specs=[
            smem,
            smem,
            pl.BlockSpec((tiles * parts, 128), lambda t: (0, 0)),
            pl.BlockSpec((1,) + view.shape[1:], lambda t: (jnp.minimum(t, EARLY - 1), 0, 0, 0)),
            late_spec,
            late_spec,
            band_spec,
            sent_spec,
        ],
        out_specs=view_spec,
        scratch_shapes=restore_scratch + [pltpu.VMEM((8, 128), F32)],
        out_shape=jax.ShapeDtypeStruct(view.shape, BF16),
        compiler_params=params(),
        name="restore",
    )(entry, here, everyone, early, x_aligned, slopes, band, returned)
    result = result.reshape(frames, row_count, merged // 128, samples, 128).transpose(3, 0, 1, 2, 4)
    return with_layout_constraint(result, order).reshape(features.shape)


def solution(mesh):
    tiles, parts = mesh.devices.shape
    split = Mesh(mesh.devices.reshape(tiles // 2, 2, parts), ("chip", "core", "sample"))
    in_specs = (
        P("sample", None, TILE, None),
        P(),
        P(),
        P(None, TILE),
        P("sample", TILE),
        P("sample", TILE),
        P("sample", TILE),
        P(),
        P("sample"),
        P("sample", None),
    )
    out_specs = P("sample", None, TILE, None)
    return jax.shard_map(local, mesh=split, in_specs=in_specs, out_specs=out_specs, check_vma=False)
```

```python
import functools

import jax
import jax.numpy as jnp
from jax import lax
from jax.experimental import pallas as pl
from jax.experimental.pallas import tpu as pltpu
from jax.experimental.layout import Layout, with_layout_constraint
from jax.sharding import Mesh, PartitionSpec as P

SCORED = 8
PATCH = 14
HEADS = 8
HD = 80
GROUP = 4
LOSS_SCALE = 16384.0
SMOOTH = 0.01

TILE = ("chip", "core")
CH = 96
COLS = 112
SPANS = CH // 8
OUT_ROWS = 27 * 16
BACK = 6
EARLY = 2
BACK_ROWS = 3 * 80
NT = 8
NZ = 4
PACK = 1088
CYCLE = [
    (2 * chip + core, z)
    for chip, heights in ((0, (0, 1, 2, 3)), (1, (3, 2, 1, 0)), (3, (0, 1, 2, 3)), (2, (3, 2, 1, 0)))
    for z in heights
    for core in range(2)
]
PLACES = [[CYCLE.index((i, z)) for z in range(NZ)] for i in range(NT)]
KIN = 896
D = 1280
NTOK = 128
F32 = jnp.float32
BF16 = jnp.bfloat16


def lane_iota(rows):
    return lax.broadcasted_iota(jnp.int32, (rows, 128), 1)


def left(value, amount):
    return pltpu.roll(value, 128 - amount, 1)


def sub_iota(rows):
    return lax.broadcasted_iota(jnp.int32, (rows, 128), 0)


def channels_of(raw, at, group, sample):
    start = 8 + 14 * group + sample
    here = raw[at, pl.ds(start, 8, stride=2), :]
    before = raw[at, pl.ds(start - 2, 8, stride=2), :]
    joined = jnp.where(lane_iota(8) < 128 - 16 * sub_iota(8), here, before)
    return pltpu.roll(joined, 0, 1, stride=16, stride_axis=0)


def tiles_of(value):
    turned = jnp.take_along_axis(value, (lane_iota(8) + 16 * sub_iota(8)) % 128, axis=1)
    return jnp.where(lane_iota(8) < COLS - 16 * sub_iota(8), turned, pltpu.roll(turned, 7, 0))


def load_taps(weight_ref, taps):
    taps[...] = jnp.zeros(taps.shape, F32)
    for a in range(3):
        for b in range(3):
            for e in range(3):
                for o in range(3):
                    at = (a * 3 + e) * 3 + o
                    taps[b, at : at + 1, :] = weight_ref[a, b, e, o : o + 1, :].astype(F32)


def row_of(shape, dim):
    at = lax.broadcasted_iota(jnp.int32, shape, dim)
    return ((at.astype(F32) + 0.5) * (1.0 / CH)).astype(jnp.int32)


def banded(taps, row_block):
    inner = row_block * CH
    pick = (
        lax.broadcasted_iota(jnp.int32, (OUT_ROWS, 32), 0) // 16
        == lax.broadcasted_iota(jnp.int32, (OUT_ROWS, 32), 1)
    ).astype(BF16)
    at = lax.broadcasted_iota(jnp.int32, (CH, inner), 1) - CH * row_of((CH, inner), 1)
    grow = (at == lax.broadcasted_iota(jnp.int32, (CH, inner), 0)).astype(BF16)
    shape = (OUT_ROWS, inner)
    p_at = lax.broadcasted_iota(jnp.int32, shape, 0) % 16
    r_at = row_of(shape, 1)
    total = jnp.zeros(shape, F32)
    for b in range(3):
        rows = nn_dot(pick, taps[b].astype(BF16)).astype(BF16)
        total = jnp.where(p_at == r_at + 2 - b, nn_dot(rows, grow), total)
    return total.astype(BF16)


def banded_back(taps):
    inner = BACK * CH

    def column_of(shape, dim):
        at = lax.broadcasted_iota(jnp.int32, shape, dim)
        a = (at >= 80).astype(jnp.int32) + (at >= 160).astype(jnp.int32)
        return a, at - 80 * a

    a, rest = column_of((BACK_ROWS, 32), 0)
    tap = jnp.where(rest // 8 < 9, 9 * a + rest // 8, 31)
    pick = (tap == lax.broadcasted_iota(jnp.int32, (BACK_ROWS, 32), 1)).astype(BF16)
    at = lax.broadcasted_iota(jnp.int32, (inner, CH), 0) - CH * row_of((inner, CH), 0)
    grow = (at == lax.broadcasted_iota(jnp.int32, (inner, CH), 1)).astype(BF16)
    shape = (inner, BACK_ROWS)
    p_at = column_of(shape, 1)[1] % 8
    r_at = row_of(shape, 0)
    total = jnp.zeros(shape, F32)
    for b in range(3):
        rows = nn_dot(pick, taps[b].astype(BF16)).astype(BF16)
        total = jnp.where(p_at == r_at + 2 - b, nt_dot(grow, rows), total)
    return total.astype(BF16)


def half_gains(gain_ref):
    rows = jnp.concatenate([gain_ref[0:1, :], jnp.zeros((1, 128 - CH), F32)], axis=1)
    return 0.5 * jnp.broadcast_to(rows, (128, 128)).T


def entry_of(pick_ref, sample, frame):
    found = jnp.int32(-1)
    for j in range(SCORED):
        found = jnp.where(pick_ref[sample, j] == frame, jnp.int32(j), found)
    return found


def decode_kernel(row_block, pick_ref, x_ref, gain_ref, weight_ref, out_ref, x_out, slope_out, turned_out, band, taps, gains, raw, operand, acc, final):
    t = pl.program_id(0)
    blocks = x_ref.shape[1] // row_block
    rows = out_ref.shape[3]

    @pl.when(t == 0)
    def _():
        load_taps(weight_ref, taps)
        band[...] = banded(taps, row_block)
        turned_out[...] = banded_back(taps)
        gains[...] = half_gains(gain_ref)
        acc[...] = jnp.zeros(acc.shape, F32)
        raw[...] = jnp.zeros(raw.shape, F32)

    for k in range(blocks):

        def one_row(row, at):
            raw[at, 8:176, :] = x_ref[0, k * row_block + row].astype(F32)
            for s in range(2):
                found = [channels_of(raw, at, g, s) for g in range(SPANS)]
                square = found[0] * found[0]
                for g in range(1, SPANS):
                    square = square + found[g] * found[g]
                second = jnp.sum(square, axis=0, keepdims=True) * (1.0 / CH)
                inv = lax.rsqrt(second + 1e-06)
                for m in range(SPANS // 2):
                    x_out[0, k * row_block + row, s, 16 * m : 16 * m + 16, :] = jnp.concatenate(
                        [found[2 * m] * inv, found[2 * m + 1] * inv], axis=0
                    ).astype(BF16)
                    acts, slopes = [], []
                    for g in (2 * m, 2 * m + 1):
                        gain = gains[8 * g : 8 * g + 8, :]
                        half = found[g] * inv * gain
                        th = jnp.tanh(half)
                        rest = half - half * th
                        acts.append(half + half * th)
                        slopes.append((gain * inv) * (1.0 + th) * (1.0 + rest))
                    slope_out[0, k * row_block + row, s, 16 * m : 16 * m + 16, :] = jnp.concatenate(
                        slopes, axis=0
                    ).astype(BF16)
                    start = row * CH + 16 * m
                    operand[k, start : start + 16, 128 * s : 128 * s + 128] = jnp.concatenate(
                        acts, axis=0
                    ).astype(BF16)

        for row in range(row_block):
            one_row(row, row)
        spread = jnp.dot(band[...], operand[k], preferred_element_type=F32)
        lane = lane_iota(48)
        for s in range(2):
            part = spread[:, 128 * s : 128 * s + 128]
            for a in range(3):
                low, mid, high = (part[144 * a + 48 * e : 144 * a + 48 * e + 48] for e in range(3))
                low = jnp.where(lane == 0, 0.0, pltpu.roll(low, 1, 1))
                high = jnp.where(lane == COLS - 1, 0.0, pltpu.roll(high, 127, 1))
                acc[k, 2 - a, s] += low + mid + high

    keep = lane_iota(rows) < COLS
    for s in range(2):
        entry = entry_of(pick_ref, s, t)

        @pl.when(entry >= 0)
        def _():
            for o in range(3):
                final[...] = jnp.zeros(final.shape, F32)
                for k in range(blocks):
                    start = k * row_block
                    final[start : start + 16, :] += acc[k, 0, s, 16 * o : 16 * o + 16, :]
                out_ref[jnp.maximum(entry, 0), s, o] = jnp.where(keep, final[0:rows, :], 0.0).astype(BF16)

    for k in range(blocks):
        acc[k, 0] = acc[k, 1]
        acc[k, 1] = acc[k, 2]
        acc[k, 2] = jnp.zeros(acc.shape[2:], F32)


def cotangents(parts, here, everyone):
    row = lax.broadcasted_iota(jnp.int32, everyone.shape, 0)
    own = jnp.zeros((1, 128), F32)
    layers = []
    for z in range(parts):
        mine = (row % parts == z) & (row < SCORED * parts)
        found = jnp.sum(jnp.where(mine, everyone, 0.0), axis=0, keepdims=True) / SCORED
        own = jnp.where(here == z, found, own)
        layers.append(found)
    prompt = left(own, 2)
    total = jnp.zeros((1, 128), F32)
    square = jnp.zeros((1, 128), F32)
    for found in layers:
        for s in range(2):
            member = prompt == found[:, 2 + s : 3 + s]
            reward = found[:, s : s + 1]
            total = total + jnp.where(member, reward, 0.0)
            square = square + jnp.where(member, reward * reward, 0.0)
    mean = total / GROUP
    second = square / GROUP - mean * mean
    return -LOSS_SCALE * ((own - mean) * lax.rsqrt(second + SMOOTH)) / SCORED


def shift_frames(entry_ref, grad_ref, shifted, row_count, begin, end, scales):
    starts = range(0, row_count, BACK)
    rows = grad_ref.shape[3]
    shifted[...] = jnp.zeros(shifted.shape, BF16)
    lane = lane_iota(rows)
    blank = jnp.zeros((8, 128), F32)

    def one_frame(frame, carry):
        for s in range(2):
            entry = entry_ref[s, frame]
            scale = jnp.where(entry >= 0, scales[s], 0.0)
            source = jnp.maximum(entry, 0)
            moved = [[], [], []]
            for o in range(3):
                value = grad_ref[source, s, o].astype(F32) * scale
                value = jnp.where(lane < COLS, value, 0.0)
                for e, turned in enumerate((pltpu.roll(value, 127, 1), value, pltpu.roll(value, 1, 1))):
                    moved[e].append(turned)
            for k, start in enumerate(starts):
                block = [turned[start : start + 8] for some in moved for turned in some]
                shifted[frame, k, :, 128 * s : 128 * s + 128] = jnp.concatenate(
                    block + [blank], axis=0
                ).astype(BF16)
        return carry

    lax.fori_loop(begin, end, one_frame, 0)


def restore_frame(t, x_ref, slope_ref, band, out_ref, back, shifted, coming, factors):
    row_count = x_ref.shape[1]
    for k, start in enumerate(range(0, row_count, BACK)):
        count = min(BACK, row_count - start)
        operand = jnp.concatenate([shifted[t + 2 - a, k] for a in range(3)], axis=0)
        coming[k, 0 : count * CH, :] = nn_dot(band[0 : count * CH, :], operand)
        places = [(local, s) for local in range(count) for s in range(2)]
        for local, s in places:
            totals = []
            for m in range(SPANS // 2):
                pair = x_ref[0, start + local, s, 16 * m : 16 * m + 16, :].astype(F32)
                slopes = slope_ref[0, start + local, s, 16 * m : 16 * m + 16, :].astype(F32)
                at = local * CH + 16 * m
                out = coming[k, at : at + 16, 128 * s : 128 * s + 128] * slopes
                coming[k, at : at + 16, 128 * s : 128 * s + 128] = out
                out = out * pair
                totals.append(out[0:8] + out[8:16])
            while len(totals) > 1:
                totals = [sum(totals[i + 1 : i + 2], totals[i]) for i in range(0, len(totals), 2)]
            factors[k, local * 2 + s] = totals[0]
        found = jnp.sum(factors[k], axis=1, keepdims=True) * (1.0 / CH)
        for local, s in places:
            row = start + local
            for m in range(SPANS // 2):
                pair = x_ref[0, row, s, 16 * m : 16 * m + 16, :].astype(F32)
                at = local * CH + 16 * m
                result = coming[k, at : at + 16, 128 * s : 128 * s + 128] - pair * found[local * 2 + s]
                for part in range(2):
                    g = 2 * m + part
                    moved = tiles_of(result[8 * part : 8 * part + 8])
                    back[row % back.shape[0], pl.ds(14 * g + s, 7, stride=2), :] = moved[0:7]
        for local in range(count):
            row = start + local
            out_ref[0, row] = back[row % back.shape[0]].astype(BF16)


def early_kernel(entry_ref, x_ref, slope_ref, band, grad_ref, out_ref, back, shifted, coming, factors):
    t = pl.program_id(0)

    @pl.when(t == 0)
    def _():
        one = jnp.ones((1, 1), F32)
        shift_frames(entry_ref, grad_ref, shifted, x_ref.shape[1], 0, EARLY + 2, (one, one))

    restore_frame(t, x_ref, slope_ref, band, out_ref, back, shifted, coming, factors)


def restore_kernel(parts, entry_ref, here_ref, everyone_ref, early_ref, x_ref, slope_ref, band, grad_ref, out_ref, back, shifted, coming, factors, scaling):
    t = pl.program_id(0)
    row_count = x_ref.shape[1]

    @pl.when(t == 0)
    def _():
        both = cotangents(parts, here_ref[0], everyone_ref[...])
        scales = (both[:, 0:1], both[:, 1:2])
        scaling[...] = jnp.where(sub_iota(8) % 2 == 0, scales[0], scales[1])
        shift_frames(entry_ref, grad_ref, shifted, row_count, EARLY, pl.num_programs(0), scales)

    @pl.when(t < EARLY)
    def _():
        for row in range(row_count):
            value = early_ref[0, row].astype(F32)
            value = value.reshape(value.shape[0] // 8, 8, 128) * scaling[...]
            out_ref[0, row] = value.reshape(early_ref.shape[2:]).astype(BF16)

    @pl.when(t >= EARLY)
    def _():
        restore_frame(t, x_ref, slope_ref, band, out_ref, back, shifted, coming, factors)


def nt_dot(one, two):
    return lax.dot_general(one, two, (((1,), (1,)), ((), ())), preferred_element_type=F32)


def tn_dot(one, two):
    return lax.dot_general(one, two, (((0,), (0,)), ((), ())), preferred_element_type=F32)


def nn_dot(one, two):
    return jnp.dot(one, two, preferred_element_type=F32)


def split_two(value):
    high = value.astype(BF16)
    low = (value - high.astype(F32)).astype(BF16)
    return jnp.concatenate([high, low], axis=0)


def patch_kernel(row_count, tiles, samples, part_ref, inputs_ref, order, frame, flip, patches):
    height = row_count * tiles
    patch_rows = height // PATCH
    lane64 = lane_iota(8) < 64
    inputs = order.shape[1]
    pixel = lax.broadcasted_iota(jnp.int32, (64, inputs), 0)
    column = lax.broadcasted_iota(jnp.int32, (64, inputs), 1)
    for x in range(PATCH):
        order[64 * x : 64 * x + 64, :] = (
            (column == pixel * PATCH + x) & (pixel < 3 * PATCH)
        ).astype(BF16)

    flip[...] = jnp.zeros(flip.shape, F32)
    frame[...] = jnp.zeros(frame.shape, F32)
    for f in range(samples):
        for i in range(tiles):
            at = row_count * i + 7
            for o in range(3):
                frame[f, o, at : at + row_count + 2, :] += part_ref[i, f, o, 0 : row_count + 2, :].astype(F32)
    for f in range(samples):
        for pair in range(patch_rows // 2):
            turn = flip.at[f * (patch_rows // 2) + pair]
            for local in range(2):
                at = 8 + PATCH * (2 * pair + local)
                for o in range(3):
                    turn[0, 64 * local + PATCH * o : 64 * local + PATCH * o + PATCH, :] = (
                        frame[f, o, at : at + PATCH, :].astype(BF16).astype(F32)
                    )
            turn[1] = turn[0].T
            token = f * NTOK + pair * 16
            for y in range(PATCH // 2):
                even = turn[1, pl.ds(2 * y, 8, stride=PATCH), :]
                odd = turn[1, pl.ds(2 * y + 1, 8, stride=PATCH), :]
                patches[token : token + 8, 128 * y : 128 * y + 128] = jnp.where(lane64, even, pltpu.roll(odd, 64, 1))
                patches[token + 8 : token + 16, 128 * y : 128 * y + 128] = jnp.where(lane64, pltpu.roll(even, 64, 1), odd)

    inputs_ref[...] = nn_dot(patches[...].astype(BF16), order[...]).astype(BF16)


def reward_kernel(
    row_count, tiles, samples,
    group_ref, inputs_ref, order, packed_ref, head_ref,
    out_ref, score_ref,
    pack, arrived, frame, flip, embed, outw, place, patches, tokens, normed, normed16, slots, weights, dslots, dnormed, rows8, abar, both, dweights, dlogits,
):
    height = row_count * tiles
    patch_rows = height // PATCH
    lane64 = lane_iota(8) < 64
    lane = lane_iota(NTOK)
    count = samples * NTOK

    copies = []
    for part, (begin, end) in enumerate(((880, 1088), (640, 880), (0, 640))):
        copies.append(
            pltpu.make_async_copy(
                packed_ref.at[:, begin:end, :], pack.at[:, begin:end, :], arrived.at[part]
            )
        )
        copies[-1].start()

    flip[...] = jnp.zeros(flip.shape, F32)
    copies[0].wait()
    copies[1].wait()

    for i in range(NT):
        for z in range(NZ):
            source = pack.at[PLACES[i][z]]
            embed[128 * i : 128 * i + 128, 128 * z : 128 * z + 128] = source[880:1008, :]
            embed[1024 + 32 * i : 1056 + 32 * i, 128 * z : 128 * z + 128] = source[1008:1040, :]
        last = [pack[PLACES[i][z], 1040:1088, :].astype(F32)[0:40] for z in range(NZ)]
        last = jnp.concatenate(last, axis=0).astype(BF16)
        embed[128 * i : 128 * i + 128, 512:640] = last[0:128]
        embed[1024 + 32 * i : 1056 + 32 * i, 512:640] = last[128:160]
    lane48 = lane_iota(48)
    for h in range(HEADS):
        outw[128 * h + HD : 128 * h + 128, :] = jnp.zeros((128 - HD, D), BF16)
    for z in range(NZ):
        for i in range(NT):
            source = pack.at[PLACES[i][z]]
            for local in range(2):
                at, begin = 128 * (2 * z + local), 640 + HD * local
                outw[at : at + HD, 128 * i : 128 * i + 128] = source[begin : begin + HD, :]
            place[32 * z : 32 * z + 32, 128 * i : 128 * i + 128] = source[800:832, :]
        for ib in range(2):
            sources = [pack[PLACES[4 * ib + j][z], 832:880, :].astype(F32) for j in range(4)]
            rolled = [[sources[j] if d == 0 else pltpu.roll(sources[j], 32 * d, 1) for d in range(4)] for j in range(4)]
            at = 1024 + 128 * ib
            for q in range(4):
                found = rolled[0][(0 - q) % 4]
                for j in range(1, 4):
                    found = jnp.where(lane48 >= 32 * j, rolled[j][(j - q) % 4], found)
                found = found.astype(BF16)
                for begin, end, row in (
                    ((0, 48, 0),),
                    ((0, 32, 48), (32, 48, 128)),
                    ((0, 48, 144),),
                    ((0, 16, 192),),
                )[q]:
                    row = 256 * z + row
                    outw[row : row + end - begin, at : at + 128] = found[begin:end]
                if q == 3:
                    place[32 * z : 32 * z + 32, at : at + 128] = found[16:48]

    token_value = nt_dot(inputs_ref[...], embed[...])
    rows8[...] = jnp.zeros(rows8.shape, F32)
    abar[...] = jnp.zeros(abar.shape, F32)
    place_value = place[...].astype(F32)
    for f in range(samples):
        value = token_value[f * NTOK : f * NTOK + NTOK] + place_value
        rows8[0, f : f + 1, :] = jnp.mean(value, axis=0, keepdims=True)
        centered = value - jnp.mean(value, axis=-1, keepdims=True)
        scale = lax.rsqrt(jnp.mean(centered * centered, axis=-1, keepdims=True) + 1e-05)
        value = centered * scale
        normed[f * NTOK : f * NTOK + NTOK, :] = value
        normed16[f * NTOK : f * NTOK + NTOK, :] = value.astype(BF16)
        tokens[f * NTOK : f * NTOK + NTOK, :] = jnp.broadcast_to(scale, (NTOK, 128))

    def weight_part(i, z):
        source = pack.at[PLACES[i][z]]
        return jnp.concatenate([source[0:256, :], source[320:576, :]], axis=1)

    def weight_rest(i):
        return jnp.concatenate(
            [
                jnp.concatenate([pack[PLACES[i][z], 256:320, :], pack[PLACES[i][z], 576:640, :]], axis=1)
                for z in range(NZ)
            ],
            axis=0,
        )

    lane_all = lane_iota(count)
    copies[2].wait()
    for i in range(NT):
        mixed = nn_dot(
            normed16[...], jnp.concatenate([weight_part(i, z) for z in range(NZ)] + [weight_rest(i)], axis=0)
        )
        first, second = mixed[:, 0:128], mixed[:, 128:256]
        found = (
            first,
            jnp.where(lane_all < 48, pltpu.roll(first, 48, 1), pltpu.roll(second, 48, 1)),
            pltpu.roll(second, 96, 1),
        )
        for m in range(3):
            slots[3 * i + m] = jnp.where(lane_all < HD, found[m], 0.0).astype(BF16)

    pairs = [(h, f, h * samples + f, slice(f * NTOK, f * NTOK + NTOK)) for h in range(HEADS) for f in range(samples)]
    for h, f, at, span in pairs:
        weights[at] = nt_dot(slots[h, span, :], slots[HEADS + h, span, :]) * HD ** (-0.5)
    logits = weights[...]
    logits = jnp.exp(logits - jnp.max(logits, axis=-1, keepdims=True))
    prob = logits / jnp.sum(logits, axis=-1, keepdims=True)
    weights[...] = prob
    sums = jnp.sum(prob.astype(BF16).astype(F32), axis=1, keepdims=True)
    for h, f, at, span in pairs:
        two = split_two(jnp.broadcast_to(sums[at], (8, 128)))
        both[at] = two
        mean = nn_dot(two, slots[2 * HEADS + h, span, :]) * (1.0 / NTOK)
        abar[f : f + 1, 128 * h : 128 * h + 128] = mean[0:1] + mean[8:9]

    part = nn_dot(split_two(abar[...]), outw[...])
    pooled = rows8[0] + part[0:8] + part[8:16]
    pooled = pooled - jnp.mean(pooled, axis=-1, keepdims=True)
    scale = lax.rsqrt(jnp.mean(pooled * pooled, axis=-1, keepdims=True) + 1e-05)
    pooled = pooled * scale
    head = head_ref[...]
    score = jnp.sum(pooled * head, axis=-1, keepdims=True)
    lane1 = lane_iota(1)
    sent = jnp.zeros((1, 128), F32)
    for f in range(samples):
        sent = jnp.where(lane1 == f, score[f : f + 1], sent)
        sent = jnp.where(lane1 == samples + f, group_ref[f].astype(F32), sent)
    score_ref[...] = jnp.broadcast_to(sent, score_ref.shape)
    dpooled = scale * (
        head - jnp.mean(head, axis=-1, keepdims=True) - pooled * jnp.mean(pooled * head, axis=-1, keepdims=True)
    )
    dres = dpooled * (1.0 / NTOK)
    rows8[1] = dres
    datts = nt_dot(split_two(dres), outw[...])
    datts = (datts[0:8] + datts[8:16]).astype(BF16)

    first_rows = sub_iota(16) % 8 == 0
    for h, f, at, span in pairs:
        datt = datts[:, 128 * h : 128 * h + 128]
        pair = jnp.where(first_rows, jnp.broadcast_to(datt[f : f + 1].astype(F32), (16, 128)), 0.0).astype(BF16)
        dslots[2 * HEADS + h, span, :] = tn_dot(both[at], pair)
        dweight = nt_dot(datt, slots[2 * HEADS + h, span, :])[f : f + 1, :].astype(BF16).astype(F32)
        dweights[at] = jnp.broadcast_to(dweight, (8, 128))
    prob = weights[...]
    dweight = dweights[:, 0:1, :]
    inner = jnp.sum(prob * dweight, axis=-1, keepdims=True)
    dlogits[...] = (prob * (dweight - inner) * HD ** (-0.5)).astype(BF16)
    for h, f, at, span in pairs:
        dslots[h, span, :] = nn_dot(dlogits[at], slots[HEADS + h, span, :])
        dslots[HEADS + h, span, :] = tn_dot(dlogits[at], slots[h, span, :])

    parts = []
    for i in range(NT):
        one, two, three = dslots[3 * i], dslots[3 * i + 1], dslots[3 * i + 2]
        two = pltpu.roll(two, 80, 1)
        three = pltpu.roll(three, 32, 1)
        first = jnp.where(lane_all < HD, one, two)
        second = jnp.where(lane_all < 32, two, jnp.where(lane_all < COLS, three, 0.0))
        parts += [first.astype(BF16), second.astype(BF16)]
    dmixed = jnp.concatenate(parts, axis=1)
    for z in range(NZ):
        wide = jnp.concatenate([weight_part(i, z) for i in range(NT)], axis=1)
        dnormed[:, 256 * z : 256 * z + 256] = nt_dot(dmixed, wide)
    wide = jnp.concatenate([weight_rest(i) for i in range(NT)], axis=1)
    dnormed[:, 1024:1280] = nt_dot(dmixed, wide)

    for f in range(samples):
        span = slice(f * NTOK, f * NTOK + NTOK)
        value, dvalue = normed[span, :], dnormed[span, :]
        scale = tokens[span, 0:1]
        dvalue = scale * (
            dvalue
            - jnp.mean(dvalue, axis=-1, keepdims=True)
            - value * jnp.mean(dvalue * value, axis=-1, keepdims=True)
        )
        normed16[span, :] = (dvalue + rows8[1, f : f + 1, :]).astype(BF16)
    patches[...] = nt_dot(nn_dot(normed16[...], embed[...]).astype(BF16), order[...])

    frame[...] = jnp.zeros(frame.shape, F32)
    rows = out_ref.shape[3]
    for f in range(samples):
        for pair in range(patch_rows // 2):
            turn = flip.at[f * (patch_rows // 2) + pair]
            token = f * NTOK + pair * 16
            for y in range(PATCH // 2):
                one = patches[token : token + 8, 128 * y : 128 * y + 128]
                two = patches[token + 8 : token + 16, 128 * y : 128 * y + 128]
                turn[1, pl.ds(2 * y, 8, stride=PATCH), :] = jnp.where(lane64, one, pltpu.roll(two, 64, 1))
                turn[1, pl.ds(2 * y + 1, 8, stride=PATCH), :] = jnp.where(lane64, pltpu.roll(one, 64, 1), two)
            turn[0] = turn[1].T
            for local in range(2):
                at = 8 + PATCH * (2 * pair + local)
                for o in range(3):
                    frame[f, o, at : at + PATCH, :] = turn[0, 64 * local + PATCH * o : 64 * local + PATCH * o + PATCH, :]
    for f in range(samples):
        for i in range(tiles):
            at = row_count * i + 7
            for o in range(3):
                out_ref[i, f, o] = frame[f, o, at : at + rows, :].astype(BF16)


def pack_part(rows_in, out_part, place_part, embed_part):
    ordered = jnp.concatenate([rows_in[0:128], rows_in[160:288], rows_in[128:160], rows_in[288:320]], axis=0)
    upper = jnp.pad(ordered[:, 128:240], ((0, 0), (0, 16)))
    other = jnp.concatenate([out_part, place_part], axis=0)
    rest = other[:, 128:160].reshape(4, 48, 32)
    rest = jnp.concatenate([rest[q] for q in range(4)], axis=1)
    return jnp.concatenate([ordered[:, 0:128], upper, other[:, 0:128], rest, embed_part], axis=0)


def pack_kernel(z_ref, rows_ref, out_ref, place_ref, embed_ref, packed_ref):
    for source, target, count in ((0, 0, 128), (160, 128, 128), (128, 256, 32), (288, 288, 32)):
        packed_ref[target : target + count, :] = rows_ref[source : source + count, 0:128]
        packed_ref[320 + target : 320 + target + count, :] = jnp.concatenate(
            [rows_ref[source : source + count, 128:240], jnp.zeros((count, 16), BF16)], axis=1
        )
    packed_ref[640:800, :] = out_ref[:, 0:128]
    packed_ref[800:832, :] = place_ref[:, 0:128]
    tail = out_ref[:, 128:160].astype(F32)
    last = place_ref[:, 128:160].astype(F32)
    packed_ref[832:880, :] = jnp.concatenate(
        [tail[0:48], tail[48:96], tail[96:144], jnp.concatenate([tail[144:160], last], axis=0)],
        axis=1,
    ).astype(BF16)
    at = pl.multiple_of(128 * z_ref[0], 128)
    packed_ref[880:1040, :] = embed_ref[:, pl.ds(at, 128)]
    width = embed_ref.shape[1] - 512
    last = jnp.concatenate([embed_ref[:, 512:].astype(F32), jnp.zeros((160, 128 - width), F32)], axis=1)
    quarter = last[0:40]
    for z in range(1, NZ):
        quarter = jnp.where(z_ref[0] == z, last[40 * z : 40 * z + 40], quarter)
    packed_ref[1040:1088, :] = jnp.concatenate([quarter, jnp.zeros((8, 128), F32)], axis=0).astype(BF16)


def packed_weights(patch_embed, position, attend_in, attend_out):
    if lax.axis_size(TILE) == NT and lax.axis_size("sample") == NZ:
        z = lax.axis_index("sample").astype(jnp.int32).reshape(1)
        mine = pl.pallas_call(
            pack_kernel,
            in_specs=[pl.BlockSpec(memory_space=pltpu.SMEM)] + [pl.BlockSpec(memory_space=pltpu.VMEM)] * 4,
            out_shape=jax.ShapeDtypeStruct((PACK, 128), BF16),
            compiler_params=params(),
            name="pack",
        )(z, attend_in, attend_out, position, patch_embed.T)
        group = [i * NZ + z for i, z in CYCLE]
        return lax.all_gather(mine, TILE + ("sample",), axis=0, axis_index_groups=[group])

    def whole(value):
        value = lax.all_gather(value, "sample", axis=0, tiled=True)
        return lax.all_gather(value, TILE, axis=1, tiled=True)

    split = [
        value.reshape(NZ, value.shape[0] // NZ, NT, value.shape[1] // NT).transpose(2, 0, 1, 3)
        for value in (whole(attend_in), whole(attend_out), whole(position))
    ]
    columns = lax.all_gather(patch_embed.T, TILE, axis=0, tiled=True).reshape(NT, D // NT, -1)
    columns = jnp.pad(columns, ((0, 0), (0, 0), (0, 640 - columns.shape[2])))
    split.append(
        jnp.stack(
            [
                jnp.pad(
                    jnp.concatenate(
                        [columns[:, :, 128 * z : 128 * z + 128], columns[:, 40 * z : 40 * z + 40, 512:]], axis=1
                    ),
                    ((0, 0), (0, 8), (0, 0)),
                )
                for z in range(NZ)
            ],
            axis=1,
        )
    )
    packed = jax.vmap(jax.vmap(pack_part))(*split)
    return jnp.stack([packed[i, z] for i, z in CYCLE])


def params(mib=58):
    return pltpu.CompilerParams(vmem_limit_bytes=mib * 1024 * 1024)


def local(
    features,
    norm_gain,
    conv_weight,
    patch_embed,
    position,
    attend_in,
    attend_out,
    reward_head,
    group_index,
    frame_pick,
):
    samples, frames, row_count, merged = features.shape
    tiles, parts = lax.axis_size(TILE), lax.axis_size("sample")
    sent_rows = -(-(row_count + 2) // 16) * 16
    row_block = row_count if row_count <= 14 else 14
    blocks = row_count // row_block
    inner = row_block * CH
    packed = packed_weights(patch_embed, position, attend_in, attend_out)
    order = Layout((1, 2, 3, 0, 4))
    split = (samples, frames, row_count, merged // 128, 128)
    view = with_layout_constraint(features.reshape(split), order).transpose(1, 2, 3, 0, 4)
    view = view.reshape(frames, row_count, samples * merged // 128, 128)
    gain = norm_gain[None, :]

    smem = pl.BlockSpec(memory_space=pltpu.SMEM)
    view_spec = pl.BlockSpec((1,) + view.shape[1:], lambda t: (t, 0, 0, 0))
    gain_spec = pl.BlockSpec((1, CH), lambda t: (0, 0))
    taps_spec = pl.BlockSpec((3, 3, 3, 3, CH), lambda t: (0, 0, 0, 0, 0))
    sent = (SCORED, samples, 3, sent_rows, 128)
    sent_spec = pl.BlockSpec(sent, lambda t: (0, 0, 0, 0, 0))
    aligned = (frames, row_count, samples, CH, 128)
    aligned_spec = pl.BlockSpec((1,) + aligned[1:], lambda t: (t, 0, 0, 0, 0))
    band_spec = pl.BlockSpec((BACK * CH, BACK_ROWS), lambda t: (0, 0))
    decoded, x_aligned, slopes, band = pl.pallas_call(
        functools.partial(decode_kernel, row_block),
        grid=(frames,),
        in_specs=[smem, view_spec, gain_spec, taps_spec],
        out_specs=[sent_spec, aligned_spec, aligned_spec, band_spec],
        scratch_shapes=[
            pltpu.VMEM((OUT_ROWS, inner), BF16),
            pltpu.VMEM((3, 32, CH), F32),
            pltpu.VMEM((128, 128), F32),
            pltpu.VMEM((row_block, 192, 128), F32),
            pltpu.VMEM((blocks, inner, 256), BF16),
            pltpu.VMEM((blocks, 3, samples, 48, 128), F32),
            pltpu.VMEM((sent_rows + 16, 128), F32),
        ],
        out_shape=[
            jax.ShapeDtypeStruct(sent, BF16),
            jax.ShapeDtypeStruct(aligned, BF16),
            jax.ShapeDtypeStruct(aligned, BF16),
            jax.ShapeDtypeStruct((BACK * CH, BACK_ROWS), BF16),
        ],
        compiler_params=params(),
        name="decode",
    )(frame_pick, view, gain, conv_weight)

    if tiles > SCORED:
        decoded = jnp.pad(decoded, ((0, tiles - SCORED),) + ((0, 0),) * 4)
    owned = lax.all_to_all(decoded, TILE, split_axis=0, concat_axis=0, tiled=True)

    head = reward_head.reshape(NT, D // NT)
    head = jnp.concatenate([head[:, :128].reshape(-1), head[:, 128:].reshape(-1)])[None, :]
    height = row_count * tiles
    count = samples * NTOK
    frame_scratch = pltpu.VMEM((samples, 3, height + 48, 128), F32)
    flip_scratch = pltpu.VMEM((samples * height // (2 * PATCH), 2, 128, 128), F32)
    inputs, input_order = pl.pallas_call(
        functools.partial(patch_kernel, row_count, tiles, samples),
        out_shape=[jax.ShapeDtypeStruct((count, 640), BF16), jax.ShapeDtypeStruct((KIN, 640), BF16)],
        scratch_shapes=[frame_scratch, flip_scratch, pltpu.VMEM((count, KIN), F32)],
        compiler_params=params(),
        name="patches",
    )(owned)
    grads, scores = pl.pallas_call(
        functools.partial(reward_kernel, row_count, tiles, samples),
        out_shape=[
            jax.ShapeDtypeStruct((tiles, samples, 3, sent_rows, 128), BF16),
            jax.ShapeDtypeStruct((tiles * parts, 128), F32),
        ],
        in_specs=[
            smem,
            pl.BlockSpec(memory_space=pltpu.VMEM),
            pl.BlockSpec(memory_space=pltpu.VMEM),
            pl.BlockSpec(memory_space=pl.ANY),
            pl.BlockSpec(memory_space=pltpu.VMEM),
        ],
        scratch_shapes=[
            pltpu.VMEM(packed.shape, BF16),
            pltpu.SemaphoreType.DMA((3,)),
            frame_scratch,
            flip_scratch,
            pltpu.VMEM((D, 640), BF16),
            pltpu.VMEM((HEADS * 128, D), BF16),
            pltpu.VMEM((NTOK, D), BF16),
            pltpu.VMEM((count, KIN), F32),
            pltpu.VMEM((count, 128), F32),
            pltpu.VMEM((count, D), F32),
            pltpu.VMEM((count, D), BF16),
            pltpu.VMEM((3 * HEADS, count, 128), BF16),
            pltpu.VMEM((HEADS * samples, NTOK, NTOK), F32),
            pltpu.VMEM((3 * HEADS, count, 128), F32),
            pltpu.VMEM((count, D), F32),
            pltpu.VMEM((2, 8, D), F32),
            pltpu.VMEM((8, HEADS * 128), F32),
            pltpu.VMEM((HEADS * samples, 16, 128), BF16),
            pltpu.VMEM((HEADS * samples, 8, 128), F32),
            pltpu.VMEM((HEADS * samples, NTOK, NTOK), BF16),
        ],
        compiler_params=params(),
        name="reward",
    )(group_index, inputs, input_order, packed, head)

    returned = lax.all_to_all(grads, TILE, split_axis=0, concat_axis=0, tiled=True)
    picks, scores = lax.optimization_barrier((frame_pick, scores))
    is_entry = picks[:, None, :] == jnp.arange(frames, dtype=jnp.int32)[None, :, None]
    entry = jnp.max(jnp.where(is_entry, jnp.arange(SCORED, dtype=jnp.int32)[None, None, :], -1), axis=2)
    scores, returned = lax.optimization_barrier((scores, returned))
    everyone = lax.all_to_all(scores, TILE + ("sample",), split_axis=0, concat_axis=0, tiled=True)
    returned = returned[:SCORED]
    here = lax.axis_index("sample").astype(jnp.int32).reshape(1)

    restore_scratch = [
        pltpu.VMEM((row_block, samples * merged // 128, 128), F32),
        pltpu.VMEM((frames + 2, -(-row_count // BACK), 80, 256), BF16),
        pltpu.VMEM((-(-row_count // BACK), BACK * CH, 256), F32),
        pltpu.VMEM((-(-row_count // BACK), BACK * 2, 8, 128), F32),
    ]
    early = pl.pallas_call(
        early_kernel,
        grid=(EARLY,),
        in_specs=[smem, aligned_spec, aligned_spec, band_spec, sent_spec],
        out_specs=view_spec,
        scratch_shapes=restore_scratch,
        out_shape=jax.ShapeDtypeStruct((EARLY,) + view.shape[1:], BF16),
        compiler_params=params(),
        name="early",
    )(entry, x_aligned, slopes, band, returned)
    late_spec = pl.BlockSpec((1,) + aligned[1:], lambda t: (jnp.maximum(t, EARLY), 0, 0, 0, 0))
    result = pl.pallas_call(
        functools.partial(restore_kernel, parts),
        grid=(frames,),
        in_specs=[
            smem,
            smem,
            pl.BlockSpec((tiles * parts, 128), lambda t: (0, 0)),
            pl.BlockSpec((1,) + view.shape[1:], lambda t: (jnp.minimum(t, EARLY - 1), 0, 0, 0)),
            late_spec,
            late_spec,
            band_spec,
            sent_spec,
        ],
        out_specs=view_spec,
        scratch_shapes=restore_scratch + [pltpu.VMEM((8, 128), F32)],
        out_shape=jax.ShapeDtypeStruct(view.shape, BF16),
        compiler_params=params(),
        name="restore",
    )(entry, here, everyone, early, x_aligned, slopes, band, returned)
    result = result.reshape(frames, row_count, merged // 128, samples, 128).transpose(3, 0, 1, 2, 4)
    return with_layout_constraint(result, order).reshape(features.shape)


def solution(mesh):
    tiles, parts = mesh.devices.shape
    split = Mesh(mesh.devices.reshape(tiles // 2, 2, parts), ("chip", "core", "sample"))
    in_specs = (
        P("sample", None, TILE, None),
        P(),
        P(),
        P(None, TILE),
        P("sample", TILE),
        P("sample", TILE),
        P("sample", TILE),
        P(),
        P("sample"),
        P("sample", None),
    )
    out_specs = P("sample", None, TILE, None)
    return jax.shard_map(local, mesh=split, in_specs=in_specs, out_specs=out_specs, check_vma=False)
```
